32 devices in a mesh: img: 8 (over y, x, core), band: 4 (over z).
Axes of the slice: x: 2, y: 2, z: 4, core: 2. Of those that a mesh axis runs over, the one named last changes fastest.
Arguments:
- inputs: bfloat16 [32, 1024, 1152], P('img', 'band'), may hold values from -17 to 17
- condition: bfloat16 [32, 1152], P('img'), may hold values from -17 to 17
- valid_rows: int32 [32], P('img'), may hold values from 960 to 1024, as said below
- cotangent: bfloat16 [32, 1024, 1152], P('img', 'band'), may hold values from -17 to 17
- ada_weight: float32 [1152, 6912], P('band', 'img'), may hold values from -0.1875 to 0.1875
- qkv_weight: float32 [1152, 3456], P('band', 'img'), may hold values from -0.1875 to 0.1875
- out_weight: float32 [1152, 1152], P('band', 'img'), may hold values from -1 to 1
- up_weight: float32 [1152, 4608], P('band', 'img'), may hold values from -0.1875 to 0.1875
- down_weight: float32 [4608, 1152], P('band', 'img'), may hold values from -0.09375 to 0.09375
- biases: float32 [14, 1152], P(None, 'img'), may hold values from -3 to 3
- ada_first: float32 [1152, 6912], P('band', 'img'), may hold values from -0.00030517578 to 0.00030517578
- qkv_first: float32 [1152, 3456], P('band', 'img'), may hold values from -0.00030517578 to 0.00030517578
- out_first: float32 [1152, 1152], P('band', 'img'), may hold values from -6.1035156e-05 to 6.1035156e-05
- up_first: float32 [1152, 4608], P('band', 'img'), may hold values from -3.0517578e-05 to 3.0517578e-05
- down_first: float32 [4608, 1152], P('band', 'img'), may hold values from -7.6293945e-05 to 7.6293945e-05
- bias_first: float32 [14, 1152], P(None, 'img'), may hold values from -0.00030517578 to 0.00030517578
- ada_second: float32 [1152, 6912], P('band', 'img'), may hold values from 2.0917e-11 to 3.34672e-10
- qkv_second: float32 [1152, 3456], P('band', 'img'), may hold values from 2.0917e-11 to 3.34672e-10
- out_second: float32 [1152, 1152], P('band', 'img'), may hold values from 2.4263723e-12 to 9.621821e-12
- up_second: float32 [1152, 4608], P('band', 'img'), may hold values from 4.6017405e-13 to 1.8406962e-12
- down_second: float32 [4608, 1152], P('band', 'img'), may hold values from 3.6813924e-12 to 1.46419e-11
- bias_second: float32 [14, 1152], P(None, 'img'), may hold values from 2.0917e-11 to 3.34672e-10
Outputs:
- output: bfloat16 [32, 1024, 1152], P('img', 'band')
- input_grad: float32 [32, 1024, 1152], P('img', 'band')
- grad_norm: float32 [], replicated
- ada_new: float32 [1152, 6912], P('band', 'img')
- qkv_new: float32 [1152, 3456], P('band', 'img')
- out_new: float32 [1152, 1152], P('band', 'img')
- up_new: float32 [1152, 4608], P('band', 'img')
- down_new: float32 [4608, 1152], P('band', 'img')
- bias_new: float32 [14, 1152], P(None, 'img')
- ada_first_new: float32 [1152, 6912], P('band', 'img')
- qkv_first_new: float32 [1152, 3456], P('band', 'img')
- out_first_new: float32 [1152, 1152], P('band', 'img')
- up_first_new: float32 [1152, 4608], P('band', 'img')
- down_first_new: float32 [4608, 1152], P('band', 'img')
- bias_first_new: float32 [14, 1152], P(None, 'img')
- ada_second_new: float32 [1152, 6912], P('band', 'img')
- qkv_second_new: float32 [1152, 3456], P('band', 'img')
- out_second_new: float32 [1152, 1152], P('band', 'img')
- up_second_new: float32 [1152, 4608], P('band', 'img')
- down_second_new: float32 [4608, 1152], P('band', 'img')
- bias_second_new: float32 [14, 1152], P(None, 'img')
- branch_bias_grad: float32 [1152], P('img')
The draws below stay inside these ranges and needn't reach their ends.
Inputs may be any that keep to these rules, and one draw needn't show every extreme that they name: Rows of an image at or past valid_rows are padding; among the 4 images of each index of img one has 1024 real rows and one has 960.
All inputs are finite; a program needn't handle non-finite values.
Results may differ from the reference program's by a relative error of at most 0.02.
The reference program's roundings to bfloat16 on the way count: a program that leaves them out, or rounds other values in their place, can miss the bound.
Values may be sent and summed in bfloat16 or wider, within the bound.
A program may use at most 448 MiB of HBM per device.

```python
import math
from functools import partial
import jax
import jax.numpy as jnp
from jax import lax

D = 1152
HEADS = 16
HEAD_DIM = 72
FF = 4608
L = 1024
IMG_DEV = 4
STEP = 10
IMAGES = 32
PARAMS = 23904000


def feature_scale(key, feature_count, top_ratio):
    factor = jax.random.uniform(key, (feature_count,), jnp.float32, 0.7, 1.4)
    return jnp.exp(jnp.linspace(0.0, math.log(top_ratio), feature_count)) * factor


def draw_inputs(key, part):
    key = jax.random.fold_in(key, 11)
    base_key, scale_key = jax.random.split(key)
    base_values = jax.random.truncated_normal(base_key, -4.0, 4.0, (IMAGES, L, D), jnp.float32)
    return (base_values * feature_scale(scale_key, D, 3.0)).astype(jnp.bfloat16)


def draw_condition(key, part):
    key = jax.random.fold_in(key, 12)
    base_key, scale_key = jax.random.split(key)
    base_values = jax.random.truncated_normal(base_key, -4.0, 4.0, (IMAGES, D), jnp.float32)
    return (base_values * feature_scale(scale_key, D, 3.0)).astype(jnp.bfloat16)


def draw_cotangent(key, part):
    key = jax.random.fold_in(key, 13)
    base_key, scale_key = jax.random.split(key)
    base_values = jax.random.truncated_normal(base_key, -4.0, 4.0, (IMAGES, L, D), jnp.float32)
    return (base_values * feature_scale(scale_key, D, 3.0)).astype(jnp.bfloat16)


def draw_valid_rows(key, part):
    key = jax.random.fold_in(key, 14)
    aspect_key, full_key, short_key = jax.random.split(key, 3)
    groups = IMAGES // IMG_DEV
    aspect_kind = jax.random.randint(aspect_key, (groups, IMG_DEV), 0, 3)
    short_rows = L - L // 16
    lengths = jnp.where(aspect_kind == 1, short_rows, L)
    chosen_full = jax.random.randint(full_key, (groups, 1), 0, IMG_DEV)
    chosen_short = (chosen_full + jax.random.randint(short_key, (groups, 1), 1, IMG_DEV)) % IMG_DEV
    column_index = jnp.arange(IMG_DEV)[None, :]
    lengths = jnp.where(column_index == chosen_full, L, lengths)
    lengths = jnp.where(column_index == chosen_short, short_rows, lengths)
    return lengths.reshape(IMAGES).astype(jnp.int32)


def block_levels(key, dims, pieces, low, largest):
    def one(axis_at, parts):
        draws = jax.random.uniform(jax.random.fold_in(jax.random.fold_in(key, 6), axis_at), (parts,), jnp.float32, low / len(pieces), largest / len(pieces))
        return jnp.repeat(jnp.exp(draws), dims[axis_at] // parts).reshape((-1,) + (1,) * (len(dims) - axis_at - 1))

    loudness = one(*pieces[0])
    for cut in pieces[1:]:
        loudness = loudness * one(*cut)
    return loudness


def noise(key, dims, scale, most, shards=(), held_as=jnp.bfloat16):
    entries = scale * jax.random.normal(key, dims, jnp.float32)
    if shards:
        entries = entries * block_levels(key, dims, shards, -0.22, 0.18)
    return jnp.clip(entries, -most, most).astype(held_as)


def setup_inputs(seed: int = 0) -> dict:
    seeds = jax.random.split(jax.random.key(seed), 23)
    return {
        "inputs": draw_inputs(jax.random.fold_in(seeds[22], 71), 0),
        "condition": draw_condition(jax.random.fold_in(seeds[22], 71), 0),
        "valid_rows": draw_valid_rows(jax.random.fold_in(seeds[22], 71), 0),
        "cotangent": draw_cotangent(jax.random.fold_in(seeds[22], 71), 0),
        "ada_weight": noise(seeds[4], (D, 6 * D), D ** -0.5, 0.1875, ((0, 4), (1, 8)), jnp.float32),
        "qkv_weight": noise(seeds[5], (D, 3 * D), D ** -0.5, 0.1875, ((0, 4), (1, 8)), jnp.float32),
        "out_weight": noise(seeds[6], (D, D), (D // 32) ** -0.5, 1.0, ((0, 4), (1, 8)), jnp.float32),
        "up_weight": noise(seeds[7], (D, FF), D ** -0.5, 0.1875, ((0, 4), (1, 8)), jnp.float32),
        "down_weight": noise(seeds[8], (FF, D), FF ** -0.5, 0.09375, ((0, 4), (1, 8)), jnp.float32),
        "biases": noise(seeds[9], (14, D), 0.5, 3.0, ((1, 8),), jnp.float32),
        "ada_first": noise(seeds[10], (D, 6 * D), (0.11 * PARAMS ** -0.5), 0.00030517578, ((0, 4), (1, 8)), jnp.float32),
        "qkv_first": noise(seeds[11], (D, 3 * D), (0.11 * PARAMS ** -0.5), 0.00030517578, ((0, 4), (1, 8)), jnp.float32),
        "out_first": noise(seeds[12], (D, D), (0.022 * PARAMS ** -0.5), 6.103515625e-05, ((0, 4), (1, 8)), jnp.float32),
        "up_first": noise(seeds[13], (D, FF), (0.0095 * PARAMS ** -0.5), 3.0517578125e-05, ((0, 4), (1, 8)), jnp.float32),
        "down_first": noise(seeds[14], (FF, D), (0.027 * PARAMS ** -0.5), 7.62939453125e-05, ((0, 4), (1, 8)), jnp.float32),
        "bias_first": noise(seeds[15], (14, D), (0.11 * PARAMS ** -0.5), 0.00030517578, ((1, 8),), jnp.float32),
        "ada_second": jnp.clip(jnp.exp(math.log(3.346720123253988e-10) - 2.7725887 * jax.random.uniform(seeds[16], (D, 6 * D), jnp.float32) ** block_levels(seeds[16], (D, 6 * D), ((0, 4), (1, 8)), -0.2, 0.2)), 2.0917000770337424e-11, 3.346720123253988e-10),
        "qkv_second": jnp.clip(jnp.exp(math.log(3.346720123253988e-10) - 2.7725887 * jax.random.uniform(seeds[17], (D, 3 * D), jnp.float32) ** block_levels(seeds[17], (D, 3 * D), ((0, 4), (1, 8)), -0.2, 0.2)), 2.0917000770337424e-11, 3.346720123253988e-10),
        "out_second": jnp.clip(jnp.exp(math.log(9.62182070129991e-12) - 1.3776363 * jax.random.uniform(seeds[18], (D, D), jnp.float32) ** block_levels(seeds[18], (D, D), ((0, 4), (1, 8)), -0.2, 0.2)), 2.4263722541578714e-12, 9.62182070129991e-12),
        "up_second": jnp.clip(jnp.exp(math.log(1.8406962152411888e-12) - 1.3862944 * jax.random.uniform(seeds[19], (D, FF), jnp.float32) ** block_levels(seeds[19], (D, FF), ((0, 4), (1, 8)), -0.2, 0.2)), 4.601740538102972e-13, 1.8406962152411888e-12),
        "down_second": jnp.clip(jnp.exp(math.log(1.4641900539236197e-11) - 1.3805963 * jax.random.uniform(seeds[20], (FF, D), jnp.float32) ** block_levels(seeds[20], (FF, D), ((0, 4), (1, 8)), -0.2, 0.2)), 3.6813924304823775e-12, 1.4641900539236197e-11),
        "bias_second": jnp.clip(jnp.exp(math.log(3.346720123253988e-10) - 2.7725887 * jax.random.uniform(seeds[21], (14, D), jnp.float32) ** block_levels(seeds[21], (14, D), ((1, 8),), -0.2, 0.2)), 2.0917000770337424e-11, 3.346720123253988e-10),
    }


@jax.custom_vjp
def low(v):
    return lax.optimization_barrier(v.astype(jnp.bfloat16)).astype(jnp.float32)

@jax.custom_vjp
def low_back(v):
    return v

def low_keep(v):
    return (low(v), None)

def low_pass(kept, grad):
    return (grad,)

def back_keep(v):
    return (v, None)

def back_low(kept, grad):
    return (low(grad),)
low.defvjp(low_keep, low_pass)
low_back.defvjp(back_keep, back_low)
norm_eps = 1e-06
beta_one = 0.9
beta_two = 0.999
adam_eps = 1e-08
learn_rate = 0.03
out_rate = 0.25
bias_rate = 0.4
clip_norm = 1.0
very_low = -1000000000.0

def matmul(first_op, second_op):
    return jnp.dot(first_op, second_op, precision=lax.Precision.HIGHEST, preferred_element_type=jnp.float32)

def normalize(values):
    centre = values - lax.optimization_barrier(jnp.mean(values, axis=-1, keepdims=True))
    return centre * lax.rsqrt(lax.optimization_barrier(jnp.mean(centre * centre, axis=-1, keepdims=True)) + norm_eps)

def image_block(weights, carried):
    qkv_w, out_w, up_w, down_w, bias_rows = weights
    tokens_in, modulation, key_mask = carried
    features = tokens_in.shape[-1]
    length = tokens_in.shape[0]
    mod_parts = modulation.reshape(6, features)
    first_in = low(normalize(tokens_in) * (1.0 + mod_parts[1]) + mod_parts[0])
    qkv_bias = jnp.concatenate([bias_rows[6], jnp.zeros((features,), jnp.float32), bias_rows[7]])
    projected = low_back(low(matmul(first_in, qkv_w) + qkv_bias))
    queries = projected[:, :features].reshape(length, HEADS, HEAD_DIM)
    keys_all = projected[:, features:2 * features].reshape(length, HEADS, HEAD_DIM)
    values_all = projected[:, 2 * features:].reshape(length, HEADS, HEAD_DIM)
    raw_scores = jnp.einsum('qhd,khd->hqk', queries, keys_all, precision=lax.Precision.HIGHEST)
    scores = low_back(raw_scores) * HEAD_DIM ** (-0.5) + jnp.where(key_mask, 0.0, very_low)[None, None, :]
    probs_full = jax.nn.softmax(scores, axis=-1)
    mixed = jnp.einsum('hqk,khd->qhd', low(probs_full), values_all, precision=lax.Precision.HIGHEST)
    mixed = low_back(low(mixed.reshape(length, features)))
    attended = low_back(matmul(mixed, out_w) + bias_rows[8])
    middle = tokens_in + mod_parts[2] * attended
    second_in = low(normalize(middle) * (1.0 + mod_parts[4]) + mod_parts[3])
    hidden_pre = low_back(matmul(second_in, up_w) + bias_rows[9:13].reshape(-1))
    hidden = low(jax.nn.gelu(hidden_pre, approximate=True))
    branch = low_back(matmul(hidden, down_w) + bias_rows[13])
    return middle + mod_parts[5] * branch

def adam_update(weight, first_old, second_old, gradient, factor, rate):
    clipped = gradient * factor
    first_new = beta_one * first_old + (1.0 - beta_one) * clipped
    second_new = beta_two * second_old + (1.0 - beta_two) * clipped * clipped
    first_hat = first_new / (1.0 - beta_one ** STEP)
    second_hat = second_new / (1.0 - beta_two ** STEP)
    return (weight - rate * first_hat / (jnp.sqrt(second_hat) + adam_eps), first_new, second_new)

def reference(inputs, condition, valid_rows, cotangent, ada_weight, qkv_weight, out_weight, up_weight, down_weight, biases, ada_first, qkv_first, out_first, up_first, down_first, bias_first, ada_second, qkv_second, out_second, up_second, down_second, bias_second):
    positions = jnp.arange(L, dtype=jnp.int32)
    key_masks = positions[None, :] < valid_rows[:, None]
    silu_cond = low(jax.nn.silu(condition.astype(jnp.float32)))

    def forward(tokens_all, ada_w, qkv_w, out_w, up_w, down_w, bias_rows):
        ada_w = low(ada_w)
        qkv_w = low(qkv_w)
        out_w = low(out_w)
        up_w = low(up_w)
        down_w = low(down_w)
        bias_rows = low(bias_rows)
        modulation = matmul(silu_cond, ada_w) + bias_rows[0:6].reshape(-1)
        block = jax.checkpoint(partial(image_block, (qkv_w, out_w, up_w, down_w, bias_rows)))

        def scan_step(state, carried):
            return (state, block(carried))
        state, outputs = lax.scan(scan_step, jnp.zeros((), jnp.float32), (tokens_all, modulation, key_masks))
        return outputs
    result, pullback = jax.vjp(forward, inputs.astype(jnp.float32), ada_weight, qkv_weight, out_weight, up_weight, down_weight, biases)
    row_mask = key_masks.astype(jnp.float32)[:, :, None]
    gradients = pullback(cotangent.astype(jnp.float32) * row_mask)
    squares = jnp.zeros((), jnp.float32)
    for gradient in gradients[1:]:
        squares = squares + jnp.sum(gradient * gradient)
    grad_norm = jnp.sqrt(squares)
    factor = clip_norm / jnp.maximum(grad_norm, clip_norm)
    ada_new, ada_first_new, ada_second_new = adam_update(ada_weight, ada_first, ada_second, gradients[1], factor, learn_rate)
    qkv_new, qkv_first_new, qkv_second_new = adam_update(qkv_weight, qkv_first, qkv_second, gradients[2], factor, learn_rate)
    out_new, out_first_new, out_second_new = adam_update(out_weight, out_first, out_second, gradients[3], factor, out_rate)
    up_new, up_first_new, up_second_new = adam_update(up_weight, up_first, up_second, gradients[4], factor, learn_rate)
    down_new, down_first_new, down_second_new = adam_update(down_weight, down_first, down_second, gradients[5], factor, learn_rate)
    bias_new, bias_first_new, bias_second_new = adam_update(biases, bias_first, bias_second, gradients[6], factor, bias_rate)
    branch_bias_grad = gradients[6][13] * factor
    return (result.astype(jnp.bfloat16), gradients[0], grad_norm, ada_new, qkv_new, out_new, up_new, down_new, bias_new, ada_first_new, qkv_first_new, out_first_new, up_first_new, down_first_new, bias_first_new, ada_second_new, qkv_second_new, out_second_new, up_second_new, down_second_new, bias_second_new, branch_bias_grad)
```

```python
import jax
import jax.numpy as jnp
from jax import lax
from jax.sharding import PartitionSpec as P

HEADS = 16
HEAD_DIM = 72
L = 1024
STEP = 10


norm_eps = 1e-06
beta_one = 0.9
beta_two = 0.999
adam_eps = 1e-08
learn_rate = 0.03
out_rate = 0.25
bias_rate = 0.4
clip_norm = 1.0
very_low = -1000000000.0


def normalize_keep(values):
    centre = values - jnp.mean(values, axis=-1, keepdims=True)
    inverse = lax.rsqrt(jnp.mean(centre * centre, axis=-1, keepdims=True) + norm_eps)
    return (centre * inverse, inverse)


def normalize_back(normed, inverse, incoming):
    return inverse * (
        incoming
        - jnp.mean(incoming, axis=-1, keepdims=True)
        - normed * jnp.mean(incoming * normed, axis=-1, keepdims=True)
    )


def smooth_gate(values):
    return jax.nn.gelu(values, approximate=True)


def adam_update(weight, first_old, second_old, gradient, factor, rate):
    clipped = gradient * factor
    first_new = beta_one * first_old + (1.0 - beta_one) * clipped
    second_new = beta_two * second_old + (1.0 - beta_two) * clipped * clipped
    first_hat = first_new / (1.0 - beta_one**STEP)
    second_hat = second_new / (1.0 - beta_two**STEP)
    return (weight - rate * first_hat / (jnp.sqrt(second_hat) + adam_eps), first_new, second_new)


def attention_forward(query_heads, key_heads, value_heads, key_bias, score_scale):
    scores = (
        jnp.einsum("iqhd,ikhd->ihqk", query_heads, key_heads, preferred_element_type=jnp.float32)
        * score_scale
        + key_bias
    )
    top_score = jnp.max(scores, axis=-1, keepdims=True)
    log_total = top_score + jnp.log(jnp.sum(jnp.exp(scores - top_score), axis=-1, keepdims=True))
    probs_low = jnp.exp(scores - log_total).astype(jnp.bfloat16)
    mixed = jnp.einsum(
        "ihqk,ikhd->iqhd", probs_low, value_heads, preferred_element_type=jnp.float32
    )
    return (mixed, log_total)


def attention_backward(
    query_heads, key_heads, value_heads, key_bias, score_scale, log_total, mixed_heads_grad
):
    scores = (
        jnp.einsum("iqhd,ikhd->ihqk", query_heads, key_heads, preferred_element_type=jnp.float32)
        * score_scale
        + key_bias
    )
    probs_full = jnp.exp(scores - log_total)
    prob_grad = jnp.einsum(
        "iqhd,ikhd->ihqk", mixed_heads_grad, value_heads, preferred_element_type=jnp.float32
    )
    inner_sum = jnp.sum(probs_full * prob_grad, axis=-1, keepdims=True)
    score_grad = (probs_full * (prob_grad - inner_sum) * score_scale).astype(jnp.bfloat16)
    query_grad = jnp.einsum(
        "ihqk,ikhd->iqhd", score_grad, key_heads, preferred_element_type=jnp.float32
    )
    key_part = jnp.einsum(
        "ihqk,iqhd->ikhd", score_grad, query_heads, preferred_element_type=jnp.float32
    )
    value_part = jnp.einsum(
        "ihqk,iqhd->ikhd",
        probs_full.astype(jnp.bfloat16),
        mixed_heads_grad,
        preferred_element_type=jnp.float32,
    )
    return (query_grad, key_part, value_part)


def body(
    inputs,
    condition,
    valid_rows,
    cotangent,
    ada_weight,
    qkv_weight,
    out_weight,
    up_weight,
    down_weight,
    biases,
    ada_first,
    qkv_first,
    out_first,
    up_first,
    down_first,
    bias_first,
    ada_second,
    qkv_second,
    out_second,
    up_second,
    down_second,
    bias_second,
):
    images, local_rows, features = inputs.shape
    length = L
    head_count = HEADS
    head_size = HEAD_DIM
    score_scale = head_size ** (-0.5)
    band_count = lax.axis_size("band")
    img_count = lax.axis_size("img")
    band_rank = lax.axis_index("band")
    img_rank = lax.axis_index("img")
    own = max(1, images // band_count)
    split = max(1, band_count // images)
    mates = band_count // split
    image_rows = length // split
    exchange_groups = None
    share_groups = None
    if split > 1:
        exchange_groups = [[g * mates + m for m in range(mates)] for g in range(split)]
        share_groups = [[g * mates + m for g in range(split)] for m in range(mates)]
    low_type = jnp.bfloat16

    def to_images(rows):
        return lax.all_to_all(rows, "band", split_axis=0, concat_axis=1, axis_index_groups=exchange_groups, tiled=True)

    def to_bands(whole):
        return lax.all_to_all(whole, "band", split_axis=1, concat_axis=0, axis_index_groups=exchange_groups, tiled=True)

    def gather_weight(weight):
        rows = lax.all_gather(weight.astype(low_type), "band", axis=0, tiled=True)
        return lax.all_gather(rows, "img", axis=1, tiled=True)

    def scatter_grad(grad):
        columns = lax.psum_scatter(grad.astype(low_type), "img", scatter_dimension=1, tiled=True)
        return lax.psum_scatter(columns, "band", scatter_dimension=0, tiled=True).astype(jnp.float32)

    condition_all = lax.all_gather(condition, "img", axis=0, tiled=True)
    tokens_low = to_images(inputs)
    bias_vals = lax.all_gather(biases.astype(low_type), "img", axis=1, tiled=True).astype(
        jnp.float32
    )
    qkv_full = gather_weight(qkv_weight)
    out_full = gather_weight(out_weight)
    up_full = gather_weight(up_weight)
    cotangent_low = to_images(cotangent)
    down_full = gather_weight(down_weight)

    silu_all = jax.nn.silu(condition_all.astype(jnp.float32)).astype(low_type)
    ada_rows = ada_weight.shape[0]
    silu_rows = lax.dynamic_slice_in_dim(silu_all, band_rank * ada_rows, ada_rows, axis=1)
    mod_partial = jnp.dot(
        silu_rows, ada_weight.astype(low_type), preferred_element_type=jnp.float32
    )
    ada_columns = mod_partial.shape[1]
    mod_sent = jnp.tile(
        mod_partial.reshape(img_count, 1, images * ada_columns), (1, split, 1)
    )
    mod_pieces = lax.all_to_all(
        mod_sent.reshape(img_count * band_count, own * ada_columns),
        ("img", "band"),
        split_axis=0,
        concat_axis=0,
        tiled=True,
    ).reshape(img_count, band_count, own, ada_columns)
    modulation = (
        jnp.sum(mod_pieces, axis=1).transpose(1, 0, 2).reshape(own, img_count * ada_columns)
        + bias_vals[0:6].reshape(-1)
    )
    mod_parts = modulation.reshape(own, 6, 1, features)
    shift_one = mod_parts[:, 0]
    scale_one = mod_parts[:, 1]
    gate_one = mod_parts[:, 2]
    shift_two = mod_parts[:, 3]
    scale_two = mod_parts[:, 4]
    gate_two = mod_parts[:, 5]
    valid_own = lax.dynamic_slice_in_dim(valid_rows, lax.rem(band_rank, mates) * own, own, axis=0)
    key_mask = jnp.arange(length, dtype=jnp.int32)[None, :] < valid_own[:, None]
    positions = lax.div(band_rank, mates) * image_rows + jnp.arange(image_rows, dtype=jnp.int32)
    row_mask = (positions[None, :] < valid_own[:, None]).astype(jnp.float32)[:, :, None]
    key_bias = jnp.where(key_mask, 0.0, very_low).astype(jnp.float32)[:, None, None, :]
    tokens_in = tokens_low.astype(jnp.float32)
    normed_one, inverse_one = normalize_keep(tokens_in)
    first_in = (normed_one * (1.0 + scale_one) + shift_one).astype(jnp.bfloat16)
    grad_out = cotangent_low.astype(jnp.float32) * row_mask
    qkv_bias = jnp.concatenate([bias_vals[6], jnp.zeros((features,), jnp.float32), bias_vals[7]])
    projected = (
        jnp.einsum("ird,de->ire", first_in, qkv_full, preferred_element_type=jnp.float32) + qkv_bias
    ).astype(jnp.bfloat16)
    query_heads = projected[..., :features].reshape(own, image_rows, head_count, head_size)
    keys_values = projected[..., features:]
    if split > 1:
        keys_values = lax.all_gather(
            keys_values, "band", axis=1, axis_index_groups=share_groups, tiled=True
        )
    key_heads = keys_values[..., :features].reshape(own, length, head_count, head_size)
    value_heads = keys_values[..., features:].reshape(own, length, head_count, head_size)
    mixed, log_total = attention_forward(query_heads, key_heads, value_heads, key_bias, score_scale)
    mixed = mixed.reshape(own, image_rows, features).astype(jnp.bfloat16)
    attended = (
        jnp.einsum("ird,de->ire", mixed, out_full, preferred_element_type=jnp.float32)
        + bias_vals[8]
    )
    middle = tokens_in + gate_one * attended
    normed_two, inverse_two = normalize_keep(middle)
    second_in = (normed_two * (1.0 + scale_two) + shift_two).astype(jnp.bfloat16)
    hidden_pre = jnp.einsum(
        "ird,df->irf", second_in, up_full, preferred_element_type=jnp.float32
    ) + bias_vals[9:13].reshape(-1)
    hidden, gelu_back = jax.vjp(smooth_gate, hidden_pre)
    hidden_low = hidden.astype(jnp.bfloat16)
    branch = (
        jnp.einsum("irf,fd->ird", hidden_low, down_full, preferred_element_type=jnp.float32)
        + bias_vals[13]
    )
    output = to_bands((middle + gate_two * branch).astype(jnp.bfloat16))
    branch_grad = (gate_two * grad_out).astype(jnp.bfloat16)
    gate_two_grad = jnp.sum(grad_out * branch, axis=1)
    down_shard = scatter_grad(
        jnp.einsum("irf,ird->fd", hidden_low, branch_grad, preferred_element_type=jnp.float32)
    )
    hidden_grad = jnp.einsum(
        "ird,fd->irf", branch_grad, down_full, preferred_element_type=jnp.float32
    )
    pre_grad = gelu_back(hidden_grad)[0].astype(jnp.bfloat16)
    up_shard = scatter_grad(
        jnp.einsum("ird,irf->df", second_in, pre_grad, preferred_element_type=jnp.float32)
    )
    second_grad = jnp.einsum("irf,df->ird", pre_grad, up_full, preferred_element_type=jnp.float32)
    shift_two_grad = jnp.sum(second_grad, axis=1)
    scale_two_grad = jnp.sum(second_grad * normed_two, axis=1)
    middle_grad = grad_out + normalize_back(
        normed_two, inverse_two, second_grad * (1.0 + scale_two)
    )
    attended_grad = (gate_one * middle_grad).astype(jnp.bfloat16)
    gate_one_grad = jnp.sum(middle_grad * attended, axis=1)
    out_shard = scatter_grad(
        jnp.einsum("ird,ire->de", mixed, attended_grad, preferred_element_type=jnp.float32)
    )
    mixed_grad = jnp.einsum(
        "ire,de->ird", attended_grad, out_full, preferred_element_type=jnp.float32
    ).astype(jnp.bfloat16)
    mixed_heads_grad = mixed_grad.reshape(own, image_rows, head_count, head_size)
    query_part, key_part, value_part = attention_backward(
        query_heads, key_heads, value_heads, key_bias, score_scale, log_total, mixed_heads_grad
    )
    query_grad = query_part.reshape(own, image_rows, features).astype(jnp.bfloat16)
    key_part = key_part.reshape(own, length, features)
    value_part = value_part.reshape(own, length, features)
    if split > 1:
        key_part, value_part = (
            lax.psum_scatter(
                part, "band", scatter_dimension=1, axis_index_groups=share_groups, tiled=True
            )
            for part in (key_part, value_part)
        )
    key_grad_low = key_part.astype(jnp.bfloat16)
    value_grad_low = value_part.astype(jnp.bfloat16)
    qkv_grad = jnp.concatenate([query_grad, key_grad_low, value_grad_low], axis=-1)
    qkv_shard = scatter_grad(
        jnp.einsum("ird,ire->de", first_in, qkv_grad, preferred_element_type=jnp.float32)
    )
    first_grad = jnp.einsum("ire,de->ird", qkv_grad, qkv_full, preferred_element_type=jnp.float32)
    shift_one_grad = jnp.sum(first_grad, axis=1)
    scale_one_grad = jnp.sum(first_grad * normed_one, axis=1)
    input_grad = to_bands(
        (
            middle_grad
            + normalize_back(normed_one, inverse_one, first_grad * (1.0 + scale_one))
        ).astype(low_type)
    ).astype(jnp.float32)
    mod_grad = jnp.stack(
        [
            shift_one_grad,
            scale_one_grad,
            gate_one_grad,
            shift_two_grad,
            scale_two_grad,
            gate_two_grad,
        ],
        axis=1,
    )
    row_sums = jnp.concatenate(
        [
            jnp.sum(query_grad.astype(jnp.float32), axis=(0, 1))[None],
            jnp.sum(value_grad_low.astype(jnp.float32), axis=(0, 1))[None],
            jnp.sum(attended_grad.astype(jnp.float32), axis=(0, 1))[None],
            jnp.sum(pre_grad.astype(jnp.float32), axis=(0, 1)).reshape(4, features),
            jnp.sum(branch_grad.astype(jnp.float32), axis=(0, 1))[None],
        ],
        axis=0,
    )
    mod_all = lax.all_gather(
        mod_grad.reshape(own, 6 * features), ("img", "band"), axis=0, tiled=True
    )
    bias_columns = biases.shape[1]
    mod_columns = lax.dynamic_slice_in_dim(mod_all, img_rank * ada_columns, ada_columns, axis=1)
    silu_terms = jnp.tile(
        silu_rows.astype(jnp.float32).reshape(img_count, 1, images, ada_rows), (1, split, 1, 1)
    ).reshape(img_count * band_count * own, ada_rows)
    ada_shard = jnp.einsum(
        "id,ie->de",
        silu_terms,
        mod_columns,
        precision=lax.Precision.HIGHEST,
    )
    mod_sums = lax.dynamic_slice_in_dim(
        jnp.sum(mod_all, axis=0).reshape(6, features),
        img_rank * bias_columns,
        bias_columns,
        axis=1,
    )
    sums_shard = lax.psum(
        lax.psum_scatter(row_sums, "img", scatter_dimension=1, tiled=True), "band"
    )
    bias_total = jnp.concatenate([mod_sums, sums_shard], axis=0)
    shards = (ada_shard, qkv_shard, out_shard, up_shard, down_shard)
    squares = jnp.sum(bias_total * bias_total) / band_count
    for shard_grad in shards:
        squares = squares + jnp.sum(shard_grad * shard_grad)
    squares_total = lax.psum(squares, ("img", "band"))
    grad_norm = jnp.sqrt(squares_total)
    factor = clip_norm / jnp.maximum(grad_norm, clip_norm)
    ada_new, ada_first_new, ada_second_new = adam_update(
        ada_weight, ada_first, ada_second, shards[0], factor, learn_rate
    )
    qkv_new, qkv_first_new, qkv_second_new = adam_update(
        qkv_weight, qkv_first, qkv_second, shards[1], factor, learn_rate
    )
    out_new, out_first_new, out_second_new = adam_update(
        out_weight, out_first, out_second, shards[2], factor, out_rate
    )
    up_new, up_first_new, up_second_new = adam_update(
        up_weight, up_first, up_second, shards[3], factor, learn_rate
    )
    down_new, down_first_new, down_second_new = adam_update(
        down_weight, down_first, down_second, shards[4], factor, learn_rate
    )
    bias_new, bias_first_new, bias_second_new = adam_update(
        biases, bias_first, bias_second, bias_total, factor, bias_rate
    )
    branch_bias_grad = bias_total[13] * factor
    return (
        output,
        input_grad,
        grad_norm,
        ada_new,
        qkv_new,
        out_new,
        up_new,
        down_new,
        bias_new,
        ada_first_new,
        qkv_first_new,
        out_first_new,
        up_first_new,
        down_first_new,
        bias_first_new,
        ada_second_new,
        qkv_second_new,
        out_second_new,
        up_second_new,
        down_second_new,
        bias_second_new,
        branch_bias_grad,
    )


def solution(mesh):
    return jax.shard_map(
        body,
        mesh=mesh,
        in_specs=(
            P("img", "band", None),
            P("img", None),
            P("img"),
            P("img", "band", None),
            P("band", "img"),
            P("band", "img"),
            P("band", "img"),
            P("band", "img"),
            P("band", "img"),
            P(None, "img"),
            P("band", "img"),
            P("band", "img"),
            P("band", "img"),
            P("band", "img"),
            P("band", "img"),
            P(None, "img"),
            P("band", "img"),
            P("band", "img"),
            P("band", "img"),
            P("band", "img"),
            P("band", "img"),
            P(None, "img"),
        ),
        out_specs=(
            P("img", "band", None),
            P("img", "band", None),
            P(),
            P("band", "img"),
            P("band", "img"),
            P("band", "img"),
            P("band", "img"),
            P("band", "img"),
            P(None, "img"),
            P("band", "img"),
            P("band", "img"),
            P("band", "img"),
            P("band", "img"),
            P("band", "img"),
            P(None, "img"),
            P("band", "img"),
            P("band", "img"),
            P("band", "img"),
            P("band", "img"),
            P("band", "img"),
            P(None, "img"),
            P("img"),
        ),
        check_vma=False,
    )
```

```python
import functools

import jax
import jax.numpy as jnp
from jax import lax
from jax.experimental import pallas as pl
from jax.experimental.pallas import tpu as pltpu
from jax.sharding import PartitionSpec as P

HEADS = 16
HEAD_DIM = 72
L = 1024
STEP = 10


norm_eps = 1e-06
beta_one = 0.9
beta_two = 0.999
adam_eps = 1e-08
learn_rate = 0.03
out_rate = 0.25
bias_rate = 0.4
clip_norm = 1.0
very_low = -1000000000.0


def normalize_keep(values):
    centre = values - jnp.mean(values, axis=-1, keepdims=True)
    inverse = lax.rsqrt(jnp.mean(centre * centre, axis=-1, keepdims=True) + norm_eps)
    return (centre * inverse, inverse)


def normalize_back(normed, inverse, incoming):
    return inverse * (
        incoming
        - jnp.mean(incoming, axis=-1, keepdims=True)
        - normed * jnp.mean(incoming * normed, axis=-1, keepdims=True)
    )


def smooth_gate(values):
    return jax.nn.gelu(values, approximate=True)


def adam_update(weight, first_old, second_old, gradient, factor, rate):
    clipped = gradient * factor
    first_new = beta_one * first_old + (1.0 - beta_one) * clipped
    second_new = beta_two * second_old + (1.0 - beta_two) * clipped * clipped
    first_hat = first_new / (1.0 - beta_one**STEP)
    second_hat = second_new / (1.0 - beta_two**STEP)
    return (weight - rate * first_hat / (jnp.sqrt(second_hat) + adam_eps), first_new, second_new)


WINDOW = 256
CONTRACT_LAST = (((1,), (1,)), ((), ()))
LOG2_E = 1.4426950408889634


def head_window(head, features):
    start = head * HEAD_DIM
    base = pl.multiple_of(jnp.minimum(start // 128 * 128, features - WINDOW), 128)
    lane = lax.broadcasted_iota(jnp.int32, (1, WINDOW), 1)
    inside = (lane >= start - base) & (lane < start - base + HEAD_DIM)
    return base, inside


def attention_forward_kernel(
    query_ref, keyval_ref, bias_ref, mixed_ref, log_ref, scaled, value_t, mixed_t, *, features, shift, block
):
    length = keyval_ref.shape[0]
    rows = mixed_ref.shape[0]
    scaled[...] = (query_ref[:, :features].astype(jnp.float32) * (HEAD_DIM**-0.5 * LOG2_E)).astype(
        jnp.bfloat16
    )

    @pl.loop(0, features // 128)
    def _(tile):
        columns = pl.ds(pl.multiple_of(tile * 128, 128), 128)
        source = pl.ds(pl.multiple_of(shift + features + tile * 128, 128), 128)
        value_t[columns, :] = keyval_ref[:, source].astype(jnp.float32).T

    @pl.loop(0, HEADS)
    def _(head):
        base, inside = head_window(head, features)
        head_rows = pl.ds(pl.multiple_of(head * HEAD_DIM, 8), HEAD_DIM)
        query = scaled[:, pl.ds(base, WINDOW)]
        ones = jnp.ones((8, block), jnp.float32)
        top = None
        for at in range(0, length, block):
            key = keyval_ref[pl.ds(at, block), pl.ds(pl.multiple_of(base + shift, 128), WINDOW)]
            key = jnp.where(inside, key, jnp.zeros_like(key))
            scores = lax.dot_general(key, query, CONTRACT_LAST, preferred_element_type=jnp.float32)
            if at + block == length:
                scores = scores + bias_ref[pl.ds(at, block), :]
            block_top = jnp.max(scores, axis=0, keepdims=True)
            value = jnp.concatenate([value_t[head_rows, pl.ds(at, block)], ones], axis=0).astype(jnp.bfloat16)
            if top is None:
                top = block_top
                probs = jnp.exp2(scores - top).astype(jnp.bfloat16)
                total = jnp.dot(value, probs, preferred_element_type=jnp.float32)
            else:
                new_top = jnp.maximum(top, block_top)
                fade = jnp.exp2(top - new_top)
                top = new_top
                probs = jnp.exp2(scores - top).astype(jnp.bfloat16)
                total = total * fade + jnp.dot(value, probs, preferred_element_type=jnp.float32)
        weight = total[HEAD_DIM : HEAD_DIM + 1]
        mixed_t[head_rows, :] = total[:HEAD_DIM] * (1.0 / weight)
        log_ref[pl.ds(head, 1), :] = top + jnp.log2(weight)

    @pl.loop(0, features // 128)
    def _(tile):
        columns = pl.ds(pl.multiple_of(tile * 128, 128), 128)
        mixed_ref[:, columns] = mixed_t[columns, :].T.astype(jnp.bfloat16)


def attention_forward(query, keyval, key_bias, features, shift, block):
    rows, length = query.shape[0], keyval.shape[0]
    return pl.pallas_call(
        functools.partial(attention_forward_kernel, features=features, shift=shift, block=block),
        out_shape=(
            jax.ShapeDtypeStruct((rows, features), jnp.bfloat16),
            jax.ShapeDtypeStruct((HEADS, rows), jnp.float32),
        ),
        scratch_shapes=[
            pltpu.VMEM((rows, features), jnp.bfloat16),
            pltpu.VMEM((features, length), jnp.float32),
            pltpu.VMEM((features, rows), jnp.float32),
        ],
        compiler_params=pltpu.CompilerParams(vmem_limit_bytes=56 * 2**20),
    )(query, keyval, key_bias)


def attention_backward_kernel(
    query_ref, keyval_ref, bias_ref, mixed_ref, grad_ref, log_ref, out_ref, keyval_grad_ref,
    scaled, key_t, wide_t, *, features, shift, out_shift, block
):
    length = keyval_ref.shape[0]
    rows = mixed_ref.shape[0]
    scale = HEAD_DIM**-0.5
    scaled[...] = (query_ref[:, :features].astype(jnp.float32) * (scale * LOG2_E)).astype(jnp.bfloat16)

    @pl.loop(0, features // 128)
    def _(tile):
        columns = pl.ds(pl.multiple_of(tile * 128, 128), 128)
        key_t[columns, :] = keyval_ref[:, pl.ds(pl.multiple_of(shift + tile * 128, 128), 128)].astype(jnp.float32).T
        wide_t[columns, :] = (
            mixed_ref[:, columns].astype(jnp.float32) * grad_ref[:, columns].astype(jnp.float32)
        ).T

    @pl.loop(0, HEADS)
    def _(head):
        base, inside = head_window(head, features)
        head_rows = pl.ds(pl.multiple_of(head * HEAD_DIM, 8), HEAD_DIM)
        window = pl.ds(base, WINDOW)
        delta = jnp.sum(wide_t[head_rows, :], axis=0, keepdims=True)
        log_total = log_ref[pl.ds(head, 1), :]
        query = query_ref[:, window]
        query_scaled = scaled[:, window]
        grad = grad_ref[:, window]
        query_grad = None
        for at in range(0, length, block):
            here = pl.ds(at, block)
            key_window = pl.ds(pl.multiple_of(base + shift, 128), WINDOW)
            value_window = pl.ds(pl.multiple_of(base + shift + features, 128), WINDOW)
            key = keyval_ref[here, key_window]
            value = keyval_ref[here, value_window]
            key = jnp.where(inside, key, jnp.zeros_like(key))
            value = jnp.where(inside, value, jnp.zeros_like(value))
            scores = lax.dot_general(key, query_scaled, CONTRACT_LAST, preferred_element_type=jnp.float32)
            if at + block == length:
                scores = scores + bias_ref[here, :]
            probs = jnp.exp2(scores - log_total)
            prob_grad = lax.dot_general(value, grad, CONTRACT_LAST, preferred_element_type=jnp.float32)
            score_grad = (probs * (prob_grad - delta)).astype(jnp.bfloat16)
            value_grad = jnp.dot(probs.astype(jnp.bfloat16), grad, preferred_element_type=jnp.float32)
            key_grad = jnp.dot(score_grad, query, preferred_element_type=jnp.float32) * scale
            key_out = pl.ds(pl.multiple_of(base + out_shift, 128), WINDOW)
            value_out = pl.ds(pl.multiple_of(base + out_shift + features, 128), WINDOW)
            keyval_grad_ref[here, key_out] = jnp.where(inside, key_grad.astype(jnp.bfloat16), keyval_grad_ref[here, key_out])
            keyval_grad_ref[here, value_out] = jnp.where(inside, value_grad.astype(jnp.bfloat16), keyval_grad_ref[here, value_out])
            part = jnp.dot(
                key_t[head_rows, here].astype(jnp.bfloat16), score_grad, preferred_element_type=jnp.float32
            )
            query_grad = part if query_grad is None else query_grad + part
        wide_t[head_rows, :] = query_grad * scale

    @pl.loop(0, features // 128)
    def _(tile):
        columns = pl.ds(pl.multiple_of(tile * 128, 128), 128)
        out_ref[:, columns] = wide_t[columns, :].T.astype(jnp.bfloat16)


def attention_backward(query, keyval, key_bias, mixed, grad, log_total, features, block):
    rows, length = query.shape[0], keyval.shape[0]
    shared = query is keyval
    scratch = [
        pltpu.VMEM((rows, features), jnp.bfloat16),
        pltpu.VMEM((features, length), jnp.float32),
        pltpu.VMEM((features, rows), jnp.float32),
    ]
    params = pltpu.CompilerParams(vmem_limit_bytes=56 * 2**20)
    if shared:

        def shared_kernel(both_ref, bias_ref, mixed_ref, grad_ref, log_ref, out_ref, *held):
            attention_backward_kernel(
                both_ref, both_ref, bias_ref, mixed_ref, grad_ref, log_ref, out_ref, out_ref, *held,
                features=features, shift=features, out_shift=features, block=block,
            )

        return pl.pallas_call(
            shared_kernel,
            out_shape=jax.ShapeDtypeStruct((rows, 3 * features), jnp.bfloat16),
            scratch_shapes=scratch,
            compiler_params=params,
        )(query, key_bias, mixed, grad, log_total)
    return pl.pallas_call(
        functools.partial(
            attention_backward_kernel, features=features, shift=0, out_shift=0, block=block
        ),
        out_shape=(
            jax.ShapeDtypeStruct((rows, features), jnp.bfloat16),
            jax.ShapeDtypeStruct((length, 2 * features), jnp.bfloat16),
        ),
        scratch_shapes=scratch,
        compiler_params=params,
    )(query, keyval, key_bias, mixed, grad, log_total)


def body(
    inputs,
    condition,
    valid_rows,
    cotangent,
    ada_weight,
    qkv_weight,
    out_weight,
    up_weight,
    down_weight,
    biases,
    ada_first,
    qkv_first,
    out_first,
    up_first,
    down_first,
    bias_first,
    ada_second,
    qkv_second,
    out_second,
    up_second,
    down_second,
    bias_second,
):
    images, local_rows, features = inputs.shape
    length = L
    head_count = HEADS
    head_size = HEAD_DIM
    score_scale = head_size ** (-0.5)
    band_count = lax.axis_size("band")
    img_count = lax.axis_size("img")
    band_rank = lax.axis_index("band")
    img_rank = lax.axis_index("img")
    own = max(1, images // band_count)
    split = max(1, band_count // images)
    mates = band_count // split
    image_rows = length // split
    exchange_groups = None
    share_groups = None
    if split > 1:
        exchange_groups = [[g * mates + m for m in range(mates)] for g in range(split)]
        share_groups = [[g * mates + m for g in range(split)] for m in range(mates)]
    low_type = jnp.bfloat16

    def to_images(rows):
        return lax.all_to_all(rows, "band", split_axis=0, concat_axis=1, axis_index_groups=exchange_groups, tiled=True)

    def to_bands(whole):
        cut = whole.reshape(own, mates, local_rows, features).transpose(1, 0, 2, 3)
        back = lax.all_to_all(
            cut, "band", split_axis=0, concat_axis=0, axis_index_groups=exchange_groups, tiled=True
        )
        return back.reshape(images, local_rows, features)

    def after(value, *earlier):
        return lax.optimization_barrier((value,) + earlier)[0]

    def sum_everywhere(partial):
        sent = jnp.broadcast_to(partial, (img_count * band_count, 128))
        got = lax.all_to_all(sent, ("img", "band"), split_axis=0, concat_axis=0, tiled=True)
        return jnp.sum(got[:, 0])

    def gather_weight(weight):
        rows = lax.all_gather(weight.astype(low_type), "band", axis=0, tiled=True)
        return lax.all_gather(rows, "img", axis=1, tiled=True)

    def scatter_grad(grad):
        columns = lax.psum_scatter(grad, "img", scatter_dimension=1, tiled=True)
        return lax.psum_scatter(columns, "band", scatter_dimension=0, tiled=True).astype(jnp.float32)

    bias_rows, bias_columns = biases.shape
    small = lax.all_gather(
        jnp.concatenate([condition.reshape(1, -1), biases.astype(low_type).reshape(1, -1)], axis=1),
        "img",
        axis=0,
        tiled=True,
    )
    condition_all = small[:, : images * features].reshape(img_count * images, features)
    bias_vals = (
        small[:, images * features :]
        .astype(jnp.float32)
        .reshape(img_count, bias_rows, bias_columns)
        .transpose(1, 0, 2)
        .reshape(bias_rows, features)
    )
    tokens_low = to_images(inputs)
    qkv_full = gather_weight(qkv_weight)
    out_full = gather_weight(out_weight)
    up_full = gather_weight(up_weight)
    down_full = gather_weight(down_weight)

    silu_all = jax.nn.silu(condition_all.astype(jnp.float32)).astype(low_type)
    ada_rows = ada_weight.shape[0]
    silu_rows = lax.dynamic_slice_in_dim(silu_all, band_rank * ada_rows, ada_rows, axis=1)
    mod_partial = jnp.dot(
        silu_rows, ada_weight.astype(low_type), preferred_element_type=jnp.float32
    )
    ada_columns = mod_partial.shape[1]
    mod_sent = jnp.tile(
        mod_partial.reshape(img_count, 1, images * ada_columns), (1, split, 1)
    )
    mod_pieces = lax.all_to_all(
        mod_sent.reshape(img_count * band_count, own * ada_columns),
        ("img", "band"),
        split_axis=0,
        concat_axis=0,
        tiled=True,
    ).reshape(img_count, band_count, own, ada_columns)
    modulation = (
        jnp.sum(mod_pieces, axis=1).transpose(1, 0, 2).reshape(own, img_count * ada_columns)
        + bias_vals[0:6].reshape(-1)
    )
    mod_parts = modulation.reshape(own, 6, 1, features)
    shift_one = mod_parts[:, 0]
    scale_one = mod_parts[:, 1]
    gate_one = mod_parts[:, 2]
    shift_two = mod_parts[:, 3]
    scale_two = mod_parts[:, 4]
    gate_two = mod_parts[:, 5]
    valid_own = lax.dynamic_slice_in_dim(valid_rows, lax.rem(band_rank, mates) * own, own, axis=0)
    key_mask = jnp.arange(length, dtype=jnp.int32)[None, :] < valid_own[:, None]
    positions = lax.div(band_rank, mates) * image_rows + jnp.arange(image_rows, dtype=jnp.int32)
    row_mask = (positions[None, :] < valid_own[:, None]).astype(jnp.float32)[:, :, None]
    tokens_in = tokens_low.astype(jnp.float32)
    normed_one, inverse_one = normalize_keep(tokens_in)
    first_in = (normed_one * (1.0 + scale_one) + shift_one).astype(jnp.bfloat16)
    cotangent_low = to_images(after(cotangent, tokens_low))
    grad_out = cotangent_low.astype(jnp.float32) * row_mask
    qkv_bias = jnp.concatenate([bias_vals[6], jnp.zeros((features,), jnp.float32), bias_vals[7]])
    projected = (
        jnp.einsum("ird,de->ire", first_in, qkv_full, preferred_element_type=jnp.float32) + qkv_bias
    ).astype(jnp.bfloat16)
    key_bias = jnp.where(key_mask, 0.0, very_low).astype(jnp.float32)[:, :, None]
    queries = [projected[i] for i in range(own)]
    if split > 1:
        keys_values = lax.all_gather(
            projected[..., features:], "band", axis=1, axis_index_groups=share_groups, tiled=True
        )
        keys_values = [keys_values[i] for i in range(own)]
        key_shift = 0
    else:
        keys_values = queries
        key_shift = features
    mixed, log_total = zip(
        *[
            attention_forward(queries[i], keys_values[i], key_bias[i], features, key_shift, 512)
            for i in range(own)
        ]
    )
    mixed_parts = mixed
    mixed = jnp.stack(mixed)
    attended = (
        jnp.einsum("ird,de->ire", mixed, out_full, preferred_element_type=jnp.float32)
        + bias_vals[8]
    )
    middle = tokens_in + gate_one * attended
    normed_two, inverse_two = normalize_keep(middle)
    second_in = (normed_two * (1.0 + scale_two) + shift_two).astype(jnp.bfloat16)
    hidden_pre = jnp.einsum(
        "ird,df->irf", second_in, up_full, preferred_element_type=jnp.float32
    ) + bias_vals[9:13].reshape(-1)
    hidden, gelu_back = jax.vjp(smooth_gate, hidden_pre)
    hidden_low = hidden.astype(jnp.bfloat16)
    branch = (
        jnp.einsum("irf,fd->ird", hidden_low, down_full, preferred_element_type=jnp.float32)
        + bias_vals[13]
    )
    output = to_bands((middle + gate_two * branch).astype(jnp.bfloat16))
    branch_grad = (gate_two * grad_out).astype(jnp.bfloat16)
    gate_two_grad = jnp.sum(grad_out * branch, axis=1)
    down_grad = jnp.einsum(
        "irf,ird->fd", hidden_low, branch_grad, preferred_element_type=jnp.float32
    ).astype(low_type)
    down_shard = scatter_grad(down_grad)
    hidden_grad = jnp.einsum(
        "ird,fd->irf",
        after(branch_grad, down_grad),
        down_full,
        preferred_element_type=jnp.float32,
    )
    pre_grad = gelu_back(hidden_grad)[0].astype(jnp.bfloat16)
    up_grad = jnp.einsum(
        "ird,irf->df", second_in, pre_grad, preferred_element_type=jnp.float32
    ).astype(low_type)
    up_shard = scatter_grad(up_grad)
    second_grad = jnp.einsum("irf,df->ird", after(pre_grad, up_grad), up_full, preferred_element_type=jnp.float32)
    shift_two_grad = jnp.sum(second_grad, axis=1)
    scale_two_grad = jnp.sum(second_grad * normed_two, axis=1)
    middle_grad = grad_out + normalize_back(
        normed_two, inverse_two, second_grad * (1.0 + scale_two)
    )
    attended_grad = (gate_one * middle_grad).astype(jnp.bfloat16)
    gate_one_grad = jnp.sum(middle_grad * attended, axis=1)
    out_grad = jnp.einsum(
        "ird,ire->de", mixed, attended_grad, preferred_element_type=jnp.float32
    ).astype(low_type)
    out_shard = scatter_grad(out_grad)
    mixed_grad = jnp.einsum(
        "ire,de->ird", after(attended_grad, out_grad), out_full, preferred_element_type=jnp.float32
    ).astype(jnp.bfloat16)
    attention_grads = [
        attention_backward(
            queries[i], keys_values[i], key_bias[i], mixed_parts[i], mixed_grad[i], log_total[i],
            features, 512,
        )
        for i in range(own)
    ]
    if split > 1:
        shared_grads = lax.psum_scatter(
            jnp.stack([pair[1] for pair in attention_grads]),
            "band",
            scatter_dimension=1,
            axis_index_groups=share_groups,
            tiled=True,
        )
        qkv_grad = jnp.concatenate(
            [jnp.stack([pair[0] for pair in attention_grads]), shared_grads], axis=-1
        )
    else:
        qkv_grad = jnp.stack(attention_grads)
    qkv_sums = jnp.sum(qkv_grad.astype(jnp.float32), axis=(0, 1))
    qkv_weight_grad = jnp.einsum(
        "ird,ire->de", first_in, qkv_grad, preferred_element_type=jnp.float32
    ).astype(low_type)
    qkv_shard = scatter_grad(qkv_weight_grad)
    first_grad = jnp.einsum("ire,de->ird", after(qkv_grad, qkv_weight_grad), qkv_full, preferred_element_type=jnp.float32)
    shift_one_grad = jnp.sum(first_grad, axis=1)
    scale_one_grad = jnp.sum(first_grad * normed_one, axis=1)
    input_grad = to_bands(
        (
            middle_grad
            + normalize_back(normed_one, inverse_one, first_grad * (1.0 + scale_one))
        ).astype(low_type)
    ).astype(jnp.float32)
    mod_grad = jnp.stack(
        [
            shift_one_grad,
            scale_one_grad,
            gate_one_grad,
            shift_two_grad,
            scale_two_grad,
            gate_two_grad,
        ],
        axis=1,
    )
    row_sums = jnp.concatenate(
        [
            qkv_sums[:features][None],
            qkv_sums[2 * features :][None],
            jnp.sum(attended_grad.astype(jnp.float32), axis=(0, 1))[None],
            jnp.sum(pre_grad.astype(jnp.float32), axis=(0, 1)).reshape(4, features),
            jnp.sum(branch_grad.astype(jnp.float32), axis=(0, 1))[None],
        ],
        axis=0,
    )
    pieces = jnp.concatenate(
        [
            mod_grad.reshape(own, img_count, ada_columns)
            .transpose(1, 0, 2)
            .reshape(img_count, own * ada_columns),
            jnp.concatenate([jnp.sum(mod_grad, axis=0).reshape(6, features), row_sums], axis=0)
            .reshape(bias_rows, img_count, bias_columns)
            .transpose(1, 0, 2)
            .reshape(img_count, -1),
        ],
        axis=1,
    )
    sent = jnp.broadcast_to(pieces[:, None], (img_count, band_count, pieces.shape[1])).reshape(
        img_count * band_count, -1
    )
    got = lax.all_to_all(sent, ("img", "band"), split_axis=0, concat_axis=0, tiled=True)
    mod_columns = got[:, : own * ada_columns].reshape(-1, ada_columns)
    silu_terms = jnp.tile(
        silu_rows.astype(jnp.float32).reshape(img_count, 1, images, ada_rows), (1, split, 1, 1)
    ).reshape(img_count * band_count * own, ada_rows)
    ada_shard = jnp.einsum(
        "id,ie->de",
        silu_terms,
        mod_columns,
        precision=lax.Precision.HIGHEST,
    )
    bias_total = jnp.sum(got[:, own * ada_columns :], axis=0).reshape(bias_rows, bias_columns)
    shards = (ada_shard, qkv_shard, out_shard, up_shard, down_shard)
    squares = jnp.sum(bias_total * bias_total) / band_count
    for shard_grad in shards:
        squares = squares + jnp.sum(shard_grad * shard_grad)
    squares_total = sum_everywhere(squares)
    grad_norm = jnp.sqrt(squares_total)
    factor = clip_norm / jnp.maximum(grad_norm, clip_norm)
    ada_new, ada_first_new, ada_second_new = adam_update(
        ada_weight, ada_first, ada_second, shards[0], factor, learn_rate
    )
    qkv_new, qkv_first_new, qkv_second_new = adam_update(
        qkv_weight, qkv_first, qkv_second, shards[1], factor, learn_rate
    )
    out_new, out_first_new, out_second_new = adam_update(
        out_weight, out_first, out_second, shards[2], factor, out_rate
    )
    up_new, up_first_new, up_second_new = adam_update(
        up_weight, up_first, up_second, shards[3], factor, learn_rate
    )
    down_new, down_first_new, down_second_new = adam_update(
        down_weight, down_first, down_second, shards[4], factor, learn_rate
    )
    bias_new, bias_first_new, bias_second_new = adam_update(
        biases, bias_first, bias_second, bias_total, factor, bias_rate
    )
    branch_bias_grad = bias_total[13] * factor
    return (
        output,
        input_grad,
        grad_norm,
        ada_new,
        qkv_new,
        out_new,
        up_new,
        down_new,
        bias_new,
        ada_first_new,
        qkv_first_new,
        out_first_new,
        up_first_new,
        down_first_new,
        bias_first_new,
        ada_second_new,
        qkv_second_new,
        out_second_new,
        up_second_new,
        down_second_new,
        bias_second_new,
        branch_bias_grad,
    )


def solution(mesh):
    return jax.shard_map(
        body,
        mesh=mesh,
        in_specs=(
            P("img", "band", None),
            P("img", None),
            P("img"),
            P("img", "band", None),
            P("band", "img"),
            P("band", "img"),
            P("band", "img"),
            P("band", "img"),
            P("band", "img"),
            P(None, "img"),
            P("band", "img"),
            P("band", "img"),
            P("band", "img"),
            P("band", "img"),
            P("band", "img"),
            P(None, "img"),
            P("band", "img"),
            P("band", "img"),
            P("band", "img"),
            P("band", "img"),
            P("band", "img"),
            P(None, "img"),
        ),
        out_specs=(
            P("img", "band", None),
            P("img", "band", None),
            P(),
            P("band", "img"),
            P("band", "img"),
            P("band", "img"),
            P("band", "img"),
            P("band", "img"),
            P(None, "img"),
            P("band", "img"),
            P("band", "img"),
            P("band", "img"),
            P("band", "img"),
            P("band", "img"),
            P(None, "img"),
            P("band", "img"),
            P("band", "img"),
            P("band", "img"),
            P("band", "img"),
            P("band", "img"),
            P(None, "img"),
            P("img"),
        ),
        check_vma=False,
    )
```

```python
import functools

import jax
import jax.numpy as jnp
from jax import lax
from jax.experimental import pallas as pl
from jax.experimental.pallas import tpu as pltpu
from jax.sharding import PartitionSpec as P

HEADS = 16
HEAD_DIM = 72
L = 1024
STEP = 10


norm_eps = 1e-06
beta_one = 0.9
beta_two = 0.999
adam_eps = 1e-08
learn_rate = 0.03
out_rate = 0.25
bias_rate = 0.4
clip_norm = 1.0
very_low = -1000000000.0


def normalize_keep(values):
    centre = values - jnp.mean(values, axis=-1, keepdims=True)
    inverse = lax.rsqrt(jnp.mean(centre * centre, axis=-1, keepdims=True) + norm_eps)
    return (centre * inverse, inverse)


def normalize_back(normed, inverse, incoming):
    return inverse * (
        incoming
        - jnp.mean(incoming, axis=-1, keepdims=True)
        - normed * jnp.mean(incoming * normed, axis=-1, keepdims=True)
    )


def smooth_gate(values):
    return jax.nn.gelu(values, approximate=True)


def adam_update(weight, first_old, second_old, gradient, factor, rate):
    clipped = gradient * factor
    first_new = beta_one * first_old + (1.0 - beta_one) * clipped
    second_new = beta_two * second_old + (1.0 - beta_two) * clipped * clipped
    first_hat = first_new / (1.0 - beta_one**STEP)
    second_hat = second_new / (1.0 - beta_two**STEP)
    return (weight - rate * first_hat / (jnp.sqrt(second_hat) + adam_eps), first_new, second_new)


WINDOW = 256
CONTRACT_LAST = (((1,), (1,)), ((), ()))
LOG2_E = 1.4426950408889634


def head_window(head, features):
    start = head * HEAD_DIM
    base = pl.multiple_of(jnp.minimum(start // 128 * 128, features - WINDOW), 128)
    lane = lax.broadcasted_iota(jnp.int32, (1, WINDOW), 1)
    inside = (lane >= start - base) & (lane < start - base + HEAD_DIM)
    return base, inside


def attention_forward_kernel(
    query_ref, keyval_ref, bias_ref, mixed_ref, log_ref, scaled, value_t, mixed_t, *, features, shift, block
):
    length = keyval_ref.shape[0]
    rows = mixed_ref.shape[0]
    scaled[...] = (query_ref[:, :features].astype(jnp.float32) * (HEAD_DIM**-0.5 * LOG2_E)).astype(
        jnp.bfloat16
    )

    @pl.loop(0, features // 128)
    def _(tile):
        columns = pl.ds(pl.multiple_of(tile * 128, 128), 128)
        source = pl.ds(pl.multiple_of(shift + features + tile * 128, 128), 128)
        value_t[columns, :] = keyval_ref[:, source].astype(jnp.float32).T

    @pl.loop(0, HEADS)
    def _(head):
        base, inside = head_window(head, features)
        head_rows = pl.ds(pl.multiple_of(head * HEAD_DIM, 8), HEAD_DIM)
        query = scaled[:, pl.ds(base, WINDOW)]
        ones = jnp.ones((8, block), jnp.float32)
        top = None
        for at in range(0, length, block):
            key = keyval_ref[pl.ds(at, block), pl.ds(pl.multiple_of(base + shift, 128), WINDOW)]
            key = jnp.where(inside, key, jnp.zeros_like(key))
            scores = lax.dot_general(key, query, CONTRACT_LAST, preferred_element_type=jnp.float32)
            if at + block == length:
                scores = scores + bias_ref[pl.ds(at, block), :]
            block_top = jnp.max(scores, axis=0, keepdims=True)
            value = jnp.concatenate([value_t[head_rows, pl.ds(at, block)], ones], axis=0).astype(jnp.bfloat16)
            if top is None:
                top = block_top
                probs = jnp.exp2(scores - top).astype(jnp.bfloat16)
                total = jnp.dot(value, probs, preferred_element_type=jnp.float32)
            else:
                new_top = jnp.maximum(top, block_top)
                fade = jnp.exp2(top - new_top)
                top = new_top
                probs = jnp.exp2(scores - top).astype(jnp.bfloat16)
                total = total * fade + jnp.dot(value, probs, preferred_element_type=jnp.float32)
        weight = total[HEAD_DIM : HEAD_DIM + 1]
        mixed_t[head_rows, :] = total[:HEAD_DIM] * (1.0 / weight)
        log_ref[pl.ds(head, 1), :] = top + jnp.log2(weight)

    @pl.loop(0, features // 128)
    def _(tile):
        columns = pl.ds(pl.multiple_of(tile * 128, 128), 128)
        mixed_ref[:, columns] = mixed_t[columns, :].T.astype(jnp.bfloat16)


def attention_forward(query, keyval, key_bias, features, shift, block):
    rows, length = query.shape[0], keyval.shape[0]
    return pl.pallas_call(
        functools.partial(attention_forward_kernel, features=features, shift=shift, block=block),
        out_shape=(
            jax.ShapeDtypeStruct((rows, features), jnp.bfloat16),
            jax.ShapeDtypeStruct((HEADS, rows), jnp.float32),
        ),
        scratch_shapes=[
            pltpu.VMEM((rows, features), jnp.bfloat16),
            pltpu.VMEM((features, length), jnp.float32),
            pltpu.VMEM((features, rows), jnp.float32),
        ],
        compiler_params=pltpu.CompilerParams(vmem_limit_bytes=56 * 2**20),
    )(query, keyval, key_bias)


def attention_backward_kernel(
    query_ref, keyval_ref, bias_ref, mixed_ref, grad_ref, log_ref, out_ref, keyval_grad_ref,
    scaled, key_t, wide_t, *, features, shift, out_shift, block
):
    length = keyval_ref.shape[0]
    rows = mixed_ref.shape[0]
    scale = HEAD_DIM**-0.5
    scaled[...] = (query_ref[:, :features].astype(jnp.float32) * (scale * LOG2_E)).astype(jnp.bfloat16)

    @pl.loop(0, features // 128)
    def _(tile):
        columns = pl.ds(pl.multiple_of(tile * 128, 128), 128)
        key_t[columns, :] = keyval_ref[:, pl.ds(pl.multiple_of(shift + tile * 128, 128), 128)].astype(jnp.float32).T
        wide_t[columns, :] = (
            mixed_ref[:, columns].astype(jnp.float32) * grad_ref[:, columns].astype(jnp.float32)
        ).T

    @pl.loop(0, HEADS)
    def _(head):
        base, inside = head_window(head, features)
        head_rows = pl.ds(pl.multiple_of(head * HEAD_DIM, 8), HEAD_DIM)
        window = pl.ds(base, WINDOW)
        delta = jnp.sum(wide_t[head_rows, :], axis=0, keepdims=True)
        log_total = log_ref[pl.ds(head, 1), :]
        query = query_ref[:, window]
        query_scaled = scaled[:, window]
        grad = grad_ref[:, window]
        query_grad = None
        for at in range(0, length, block):
            here = pl.ds(at, block)
            key_window = pl.ds(pl.multiple_of(base + shift, 128), WINDOW)
            value_window = pl.ds(pl.multiple_of(base + shift + features, 128), WINDOW)
            key = keyval_ref[here, key_window]
            value = keyval_ref[here, value_window]
            key = jnp.where(inside, key, jnp.zeros_like(key))
            value = jnp.where(inside, value, jnp.zeros_like(value))
            scores = lax.dot_general(key, query_scaled, CONTRACT_LAST, preferred_element_type=jnp.float32)
            if at + block == length:
                scores = scores + bias_ref[here, :]
            probs = jnp.exp2(scores - log_total)
            prob_grad = lax.dot_general(value, grad, CONTRACT_LAST, preferred_element_type=jnp.float32)
            score_grad = (probs * (prob_grad - delta)).astype(jnp.bfloat16)
            value_grad = jnp.dot(probs.astype(jnp.bfloat16), grad, preferred_element_type=jnp.float32)
            key_grad = jnp.dot(score_grad, query, preferred_element_type=jnp.float32) * scale
            key_out = pl.ds(pl.multiple_of(base + out_shift, 128), WINDOW)
            value_out = pl.ds(pl.multiple_of(base + out_shift + features, 128), WINDOW)
            keyval_grad_ref[here, key_out] = jnp.where(inside, key_grad.astype(jnp.bfloat16), keyval_grad_ref[here, key_out])
            keyval_grad_ref[here, value_out] = jnp.where(inside, value_grad.astype(jnp.bfloat16), keyval_grad_ref[here, value_out])
            part = jnp.dot(
                key_t[head_rows, here].astype(jnp.bfloat16), score_grad, preferred_element_type=jnp.float32
            )
            query_grad = part if query_grad is None else query_grad + part
        wide_t[head_rows, :] = query_grad * scale

    @pl.loop(0, features // 128)
    def _(tile):
        columns = pl.ds(pl.multiple_of(tile * 128, 128), 128)
        out_ref[:, columns] = wide_t[columns, :].T.astype(jnp.bfloat16)


def attention_backward(query, keyval, key_bias, mixed, grad, log_total, features, block):
    rows, length = query.shape[0], keyval.shape[0]
    shared = query is keyval
    scratch = [
        pltpu.VMEM((rows, features), jnp.bfloat16),
        pltpu.VMEM((features, length), jnp.float32),
        pltpu.VMEM((features, rows), jnp.float32),
    ]
    params = pltpu.CompilerParams(vmem_limit_bytes=56 * 2**20)
    if shared:

        def shared_kernel(both_ref, bias_ref, mixed_ref, grad_ref, log_ref, out_ref, *held):
            attention_backward_kernel(
                both_ref, both_ref, bias_ref, mixed_ref, grad_ref, log_ref, out_ref, out_ref, *held,
                features=features, shift=features, out_shift=features, block=block,
            )

        return pl.pallas_call(
            shared_kernel,
            out_shape=jax.ShapeDtypeStruct((rows, 3 * features), jnp.bfloat16),
            scratch_shapes=scratch,
            compiler_params=params,
        )(query, key_bias, mixed, grad, log_total)
    return pl.pallas_call(
        functools.partial(
            attention_backward_kernel, features=features, shift=0, out_shift=0, block=block
        ),
        out_shape=(
            jax.ShapeDtypeStruct((rows, features), jnp.bfloat16),
            jax.ShapeDtypeStruct((length, 2 * features), jnp.bfloat16),
        ),
        scratch_shapes=scratch,
        compiler_params=params,
    )(query, keyval, key_bias, mixed, grad, log_total)


MESH = pl.DeviceIdType.MESH


def flip(index, bit):
    return index + bit - 2 * bit * lax.rem(lax.div(index, bit), 2)


def start_kernel(
    wide_ref, tall_ref, tokens_ref,
    qkv_ref, out_ref, up_ref, down_ref, rows_ref,
    held, turned, line_send, line_recv, row_send, row_recv, flat_send, flat_recv, local_sem,
    *, bands, qkv_part, out_part,
):
    img, band = lax.axis_index("img"), lax.axis_index("band")
    depth, width = wide_ref.shape
    tall_rows, tall_width = tall_ref.shape
    row_block = tokens_ref.shape[1]
    lanes = 128
    first = -(-(qkv_part + out_part) // lanes) * lanes
    beside_x, beside_y, sibling = flip(img, 2), flip(img, 4), flip(img, 1)
    across = flip(beside_x, 4)

    barrier = pltpu.get_barrier_semaphore()
    for other in (beside_x, beside_y, sibling):
        pl.semaphore_signal(barrier, inc=1, device_id={"img": other}, device_id_type=MESH)
    for step in range(1, bands):
        pl.semaphore_signal(
            barrier, inc=1, device_id={"band": lax.rem(band + step, bands)}, device_id_type=MESH
        )
    pl.semaphore_wait(barrier, 3 + bands - 1)

    def piece(part, owner):
        if part == 2:
            return down_ref.at[:, pl.ds(pl.multiple_of(owner * tall_width, lanes), tall_width)]
        span = pl.ds(0, first) if part == 0 else pl.ds(first, width - first)
        return held.at[pl.ds(pl.multiple_of(owner * depth, 16), depth), span]

    def line_copy(part, way, step, owner, toward):
        view = piece(part, owner)
        return pltpu.make_async_remote_copy(
            src_ref=view, dst_ref=view,
            send_sem=line_send.at[part, way, step], recv_sem=line_recv.at[part, way, step],
            device_id={"band": toward}, device_id_type=MESH,
        )

    def line_sends(part, step, act):
        for way, sign in ((0, 1), (1, -1)):
            owner, toward = band - sign * step, band + sign

            @pl.when((owner >= 0) & (owner < bands) & (toward >= 0) & (toward < bands))
            def _():
                act(line_copy(part, way, step, owner, toward))

    def line_arrivals(part, step):
        for way, sign in ((0, 1), (1, -1)):
            owner = band - sign * (step + 1)

            @pl.when((owner >= 0) & (owner < bands))
            def _():
                line_copy(part, way, step, owner, band - sign).wait_recv()

    def row_copy(step):
        target = lax.rem(band + step, bands)
        return pltpu.make_async_remote_copy(
            src_ref=tokens_ref.at[target],
            dst_ref=rows_ref.at[pl.ds(pl.multiple_of(band * row_block, 16), row_block), :],
            send_sem=row_send.at[step - 1], recv_sem=row_recv.at[step - 1],
            device_id={"band": target}, device_id_type=MESH,
        )

    def row_arrival(step):
        source = lax.rem(band + bands - step, bands)
        view = rows_ref.at[pl.ds(pl.multiple_of(source * row_block, 16), row_block), :]
        return pltpu.make_async_remote_copy(
            src_ref=view, dst_ref=view,
            send_sem=row_send.at[step - 1], recv_sem=row_recv.at[step - 1],
            device_id={"band": source}, device_id_type=MESH,
        )

    def qkv_rows(owner, start=0, count=qkv_part):
        return qkv_ref.at[pl.ds(pl.multiple_of(owner * qkv_part + start, 16), count), :]

    def out_rows(owner):
        return out_ref.at[pl.ds(pl.multiple_of(owner * out_part, 16), out_part), :]

    half = (qkv_part + out_part) // 2
    own_qkv, own_out = turned.at[pl.ds(0, qkv_part), :], turned.at[pl.ds(qkv_part, out_part), :]
    plan = [
        (own_qkv, qkv_rows(img), beside_x, qkv_rows(beside_x)),
        (own_out, out_rows(img), beside_x, out_rows(beside_x)),
        (own_qkv, qkv_rows(img), beside_y, qkv_rows(beside_y)),
        (own_out, out_rows(img), beside_y, out_rows(beside_y)),
        (own_qkv, qkv_rows(img), sibling, qkv_rows(sibling)),
        (own_out, out_rows(img), sibling, out_rows(sibling)),
    ]
    for owner, toward, whole in ((beside_x, beside_y, True), (beside_y, beside_x, False)):
        if whole:
            view = qkv_rows(owner, 0, half)
            plan.append((view, view, toward, qkv_rows(across, 0, half)))
        else:
            rest = qkv_part - half
            view = qkv_rows(owner, half, rest)
            plan.append((view, view, toward, qkv_rows(across, half, rest)))
            plan.append((out_rows(owner), out_rows(owner), toward, out_rows(across)))
    for owner in (beside_x, beside_y):
        plan.append((qkv_rows(owner), qkv_rows(owner), sibling, qkv_rows(flip(owner, 1))))
        plan.append((out_rows(owner), out_rows(owner), sibling, out_rows(flip(owner, 1))))
    far = flip(across, 1)
    plan.append((qkv_rows(across, 0, half), qkv_rows(across, 0, half), sibling, qkv_rows(far, 0, half)))
    rest = qkv_part - half
    plan.append((qkv_rows(across, half, rest), qkv_rows(across, half, rest), sibling, qkv_rows(far, half, rest)))
    plan.append((out_rows(across), out_rows(across), sibling, out_rows(far)))

    def flat_copy(at):
        source, target, toward, _ = plan[at]
        return pltpu.make_async_remote_copy(
            src_ref=source, dst_ref=target, send_sem=flat_send.at[at], recv_sem=flat_recv.at[at],
            device_id={"img": toward}, device_id_type=MESH,
        )

    def flat_arrival(at):
        landing = plan[at][3]
        pltpu.make_async_remote_copy(
            src_ref=landing, dst_ref=landing, send_sem=flat_send.at[at], recv_sem=flat_recv.at[at],
            device_id={"img": sibling}, device_id_type=MESH,
        ).wait_recv()

    def turn(tile):
        span = pl.ds(pl.multiple_of(tile * lanes, lanes), lanes)
        turned[span, :] = held[:, span].astype(jnp.float32).T.astype(jnp.bfloat16)

    start = lambda copy: copy.start()
    own_rows = pltpu.make_async_copy(
        tokens_ref.at[band],
        rows_ref.at[pl.ds(pl.multiple_of(band * row_block, 16), row_block), :],
        local_sem.at[0],
    )
    own_rows.start()
    held[pl.ds(pl.multiple_of(band * depth, 16), depth), :] = wide_ref[...]
    down_ref[:, pl.ds(pl.multiple_of(band * tall_width, lanes), tall_width)] = tall_ref[...]
    line_sends(0, 0, start)
    for step in range(bands - 1):
        line_arrivals(0, step)
        if step < bands - 2:
            line_sends(0, step + 1, start)
    line_sends(1, 0, start)
    line_sends(2, 0, start)
    for step in range(1, bands):
        row_copy(step).start()
    pl.loop(0, first // lanes)(turn)
    keep_qkv = pltpu.make_async_copy(own_qkv, qkv_rows(img), local_sem.at[1])
    keep_out = pltpu.make_async_copy(own_out, out_rows(img), local_sem.at[2])
    for at in range(6):
        flat_copy(at).start()
    keep_qkv.start()
    keep_out.start()
    for step in range(bands - 2):
        for part in (1, 2):
            line_arrivals(part, step)
            line_sends(part, step + 1, start)
    for arrived, sent in (((0, 1), (6, 9, 10)), ((2, 3), (7, 8, 11, 12))):
        for at in arrived:
            flat_arrival(at)
        for at in sent:
            flat_copy(at).start()
    for at in (6, 7, 8):
        flat_arrival(at)
        flat_copy(at + 7).start()
    for part in (1, 2):
        line_arrivals(part, bands - 2)
    pl.loop(first // lanes, width // lanes)(turn)
    up_ref[...] = turned[pl.ds(qkv_part + out_part, width - qkv_part - out_part), :]
    for part in range(3):
        for step in range(bands - 1):
            line_sends(part, step, lambda copy: copy.wait_send())
    for at in (4, 5, 9, 10, 11, 12, 13, 14, 15):
        flat_arrival(at)
    for at in range(16):
        flat_copy(at).wait_send()
    for step in range(1, bands):
        row_copy(step).wait_send()
        row_arrival(step).wait_recv()
    own_rows.wait()
    keep_qkv.wait()
    keep_out.wait()


def start_exchange(wide, tall, tokens, bands, imgs, qkv_part, out_part):
    depth, width = wide.shape
    up_part = width - qkv_part - out_part
    low = jnp.bfloat16
    anywhere, vmem = pl.BlockSpec(memory_space=pl.ANY), pl.BlockSpec(memory_space=pltpu.VMEM)
    features = depth * bands
    return pl.pallas_call(
        functools.partial(start_kernel, bands=bands, qkv_part=qkv_part, out_part=out_part),
        out_shape=(
            jax.ShapeDtypeStruct((qkv_part * imgs, features), low),
            jax.ShapeDtypeStruct((out_part * imgs, features), low),
            jax.ShapeDtypeStruct((up_part, features), low),
            jax.ShapeDtypeStruct((tall.shape[0], tall.shape[1] * bands), low),
            jax.ShapeDtypeStruct((tokens.shape[1] * bands, tokens.shape[2]), low),
        ),
        in_specs=[vmem, vmem, anywhere],
        out_specs=(anywhere, anywhere, vmem, vmem, anywhere),
        scratch_shapes=[
            pltpu.VMEM((features, width), low),
            pltpu.VMEM((width, features), low),
            pltpu.SemaphoreType.DMA((3, 2, bands - 1)),
            pltpu.SemaphoreType.DMA((3, 2, bands - 1)),
            pltpu.SemaphoreType.DMA((bands - 1,)),
            pltpu.SemaphoreType.DMA((bands - 1,)),
            pltpu.SemaphoreType.DMA((16,)),
            pltpu.SemaphoreType.DMA((16,)),
            pltpu.SemaphoreType.DMA((3,)),
        ],
        compiler_params=pltpu.CompilerParams(
            collective_id=0, has_side_effects=True, vmem_limit_bytes=40 * 2**20
        ),
    )(wide, tall, tokens)


def body(
    inputs,
    condition,
    valid_rows,
    cotangent,
    ada_weight,
    qkv_weight,
    out_weight,
    up_weight,
    down_weight,
    biases,
    ada_first,
    qkv_first,
    out_first,
    up_first,
    down_first,
    bias_first,
    ada_second,
    qkv_second,
    out_second,
    up_second,
    down_second,
    bias_second,
):
    images, local_rows, features = inputs.shape
    length = L
    head_count = HEADS
    head_size = HEAD_DIM
    score_scale = head_size ** (-0.5)
    band_count = lax.axis_size("band")
    img_count = lax.axis_size("img")
    band_rank = lax.axis_index("band")
    img_rank = lax.axis_index("img")
    own = max(1, images // band_count)
    split = max(1, band_count // images)
    mates = band_count // split
    image_rows = length // split
    exchange_groups = None
    share_groups = None
    if split > 1:
        exchange_groups = [[g * mates + m for m in range(mates)] for g in range(split)]
        share_groups = [[g * mates + m for g in range(split)] for m in range(mates)]
    low_type = jnp.bfloat16

    def to_images(rows):
        return lax.all_to_all(rows, "band", split_axis=0, concat_axis=1, axis_index_groups=exchange_groups, tiled=True)

    def to_bands(whole):
        cut = whole.reshape(own, mates, local_rows, features).transpose(1, 0, 2, 3)
        back = lax.all_to_all(
            cut, "band", split_axis=0, concat_axis=0, axis_index_groups=exchange_groups, tiled=True
        )
        return back.reshape(images, local_rows, features)

    def after(value, *earlier):
        return lax.optimization_barrier((value,) + earlier)[0]

    def sum_everywhere(partial):
        sent = jnp.broadcast_to(partial, (img_count * band_count, 128))
        got = lax.all_to_all(sent, ("img", "band"), split_axis=0, concat_axis=0, tiled=True)
        return jnp.sum(got[:, 0])

    qkv_part, out_part = qkv_weight.shape[1], out_weight.shape[1]

    bias_rows, bias_columns = biases.shape
    small = lax.all_gather(
        jnp.concatenate([condition.reshape(1, -1), biases.astype(low_type).reshape(1, -1)], axis=1),
        "img",
        axis=0,
        tiled=True,
    )
    condition_all = small[:, : images * features].reshape(img_count * images, features)
    bias_vals = (
        small[:, images * features :]
        .astype(jnp.float32)
        .reshape(img_count, bias_rows, bias_columns)
        .transpose(1, 0, 2)
        .reshape(bias_rows, features)
    )
    wide = jnp.concatenate([qkv_weight, out_weight, up_weight], axis=1).astype(low_type)
    tall = down_weight.T.astype(low_type)
    if img_count == 8 and own == 1 and split == 1:
        qkv_full, out_full, up_rows, down_rows, tokens_low = start_exchange(
            wide, tall, inputs, band_count, img_count, qkv_part, out_part
        )
        tokens_low = tokens_low.reshape(own, image_rows, features)
    else:
        turned = lax.all_gather(wide, "band", axis=0, tiled=True).T
        qkv_full = lax.all_gather(turned[:qkv_part], "img", axis=0, tiled=True)
        out_full = lax.all_gather(
            turned[qkv_part : qkv_part + out_part], "img", axis=0, tiled=True
        )
        up_rows = turned[qkv_part + out_part :]
        down_rows = lax.all_gather(tall, "band", axis=1, tiled=True)
        tokens_low = to_images(inputs)
    up_full = lax.all_gather(up_rows, "img", axis=0, tiled=True)
    down_full = lax.all_gather(after(down_rows, up_rows), "img", axis=0, tiled=True)

    silu_all = jax.nn.silu(condition_all.astype(jnp.float32)).astype(low_type)
    ada_rows = ada_weight.shape[0]
    silu_rows = lax.dynamic_slice_in_dim(silu_all, band_rank * ada_rows, ada_rows, axis=1)
    mod_partial = jnp.dot(
        silu_rows, ada_weight.astype(low_type), preferred_element_type=jnp.float32
    )
    ada_columns = mod_partial.shape[1]
    mod_sent = jnp.tile(
        mod_partial.reshape(img_count, 1, images * ada_columns), (1, split, 1)
    )
    mod_pieces = lax.all_to_all(
        mod_sent.reshape(img_count * band_count, own * ada_columns),
        ("img", "band"),
        split_axis=0,
        concat_axis=0,
        tiled=True,
    ).reshape(img_count, band_count, own, ada_columns)
    modulation = (
        jnp.sum(mod_pieces, axis=1).transpose(1, 0, 2).reshape(own, img_count * ada_columns)
        + bias_vals[0:6].reshape(-1)
    )
    mod_parts = modulation.reshape(own, 6, 1, features)
    shift_one = mod_parts[:, 0]
    scale_one = mod_parts[:, 1]
    gate_one = mod_parts[:, 2]
    shift_two = mod_parts[:, 3]
    scale_two = mod_parts[:, 4]
    gate_two = mod_parts[:, 5]
    valid_own = lax.dynamic_slice_in_dim(valid_rows, lax.rem(band_rank, mates) * own, own, axis=0)
    key_mask = jnp.arange(length, dtype=jnp.int32)[None, :] < valid_own[:, None]
    positions = lax.div(band_rank, mates) * image_rows + jnp.arange(image_rows, dtype=jnp.int32)
    row_mask = (positions[None, :] < valid_own[:, None]).astype(jnp.float32)[:, :, None]
    tokens_in = tokens_low.astype(jnp.float32)
    normed_one, inverse_one = normalize_keep(tokens_in)
    first_in = (normed_one * (1.0 + scale_one) + shift_one).astype(jnp.bfloat16)
    cotangent_low = to_images(after(cotangent, tokens_low))
    grad_out = cotangent_low.astype(jnp.float32) * row_mask
    qkv_bias = jnp.concatenate([bias_vals[6], jnp.zeros((features,), jnp.float32), bias_vals[7]])
    projected = (
        jnp.einsum("ird,ed->ire", first_in, qkv_full, preferred_element_type=jnp.float32) + qkv_bias
    ).astype(jnp.bfloat16)
    key_bias = jnp.where(key_mask, 0.0, very_low).astype(jnp.float32)[:, :, None]
    queries = [projected[i] for i in range(own)]
    if split > 1:
        keys_values = lax.all_gather(
            projected[..., features:], "band", axis=1, axis_index_groups=share_groups, tiled=True
        )
        keys_values = [keys_values[i] for i in range(own)]
        key_shift = 0
    else:
        keys_values = queries
        key_shift = features
    mixed, log_total = zip(
        *[
            attention_forward(queries[i], keys_values[i], key_bias[i], features, key_shift, 512)
            for i in range(own)
        ]
    )
    mixed_parts = mixed
    mixed = jnp.stack(mixed)
    attended = (
        jnp.einsum("ird,ed->ire", mixed, out_full, preferred_element_type=jnp.float32)
        + bias_vals[8]
    )
    middle = tokens_in + gate_one * attended
    normed_two, inverse_two = normalize_keep(middle)
    second_in = (normed_two * (1.0 + scale_two) + shift_two).astype(jnp.bfloat16)
    hidden_pre = jnp.einsum(
        "ird,fd->irf", second_in, up_full, preferred_element_type=jnp.float32
    ) + bias_vals[9:13].reshape(-1)
    hidden, gelu_back = jax.vjp(smooth_gate, hidden_pre)
    hidden_low = hidden.astype(jnp.bfloat16)
    branch = (
        jnp.einsum("irf,df->ird", hidden_low, down_full, preferred_element_type=jnp.float32)
        + bias_vals[13]
    )
    output = to_bands((middle + gate_two * branch).astype(jnp.bfloat16))
    branch_grad = (gate_two * grad_out).astype(jnp.bfloat16)
    gate_two_grad = jnp.sum(grad_out * branch, axis=1)
    down_grad = jnp.einsum(
        "ird,irf->df", branch_grad, hidden_low, preferred_element_type=jnp.float32
    ).astype(low_type)
    down_sum = lax.psum_scatter(down_grad, "img", scatter_dimension=0, tiled=True)
    hidden_grad = jnp.einsum(
        "ird,df->irf",
        after(branch_grad, down_grad),
        down_full,
        preferred_element_type=jnp.float32,
    )
    pre_grad = gelu_back(hidden_grad)[0].astype(jnp.bfloat16)
    up_grad = jnp.einsum(
        "irf,ird->fd", pre_grad, second_in, preferred_element_type=jnp.float32
    ).astype(low_type)
    up_sum = lax.psum_scatter(up_grad, "img", scatter_dimension=0, tiled=True)
    second_grad = jnp.einsum("irf,fd->ird", after(pre_grad, up_grad), up_full, preferred_element_type=jnp.float32)
    shift_two_grad = jnp.sum(second_grad, axis=1)
    scale_two_grad = jnp.sum(second_grad * normed_two, axis=1)
    middle_grad = grad_out + normalize_back(
        normed_two, inverse_two, second_grad * (1.0 + scale_two)
    )
    attended_grad = (gate_one * middle_grad).astype(jnp.bfloat16)
    gate_one_grad = jnp.sum(middle_grad * attended, axis=1)
    out_grad = jnp.einsum(
        "ire,ird->ed", attended_grad, mixed, preferred_element_type=jnp.float32
    ).astype(low_type)
    out_sum = lax.psum_scatter(out_grad, "img", scatter_dimension=0, tiled=True)
    mixed_grad = jnp.einsum(
        "ire,ed->ird", after(attended_grad, out_grad), out_full, preferred_element_type=jnp.float32
    ).astype(jnp.bfloat16)
    attention_grads = [
        attention_backward(
            queries[i], keys_values[i], key_bias[i], mixed_parts[i], mixed_grad[i], log_total[i],
            features, 512,
        )
        for i in range(own)
    ]
    if split > 1:
        shared_grads = lax.psum_scatter(
            jnp.stack([pair[1] for pair in attention_grads]),
            "band",
            scatter_dimension=1,
            axis_index_groups=share_groups,
            tiled=True,
        )
        qkv_grad = jnp.concatenate(
            [jnp.stack([pair[0] for pair in attention_grads]), shared_grads], axis=-1
        )
    else:
        qkv_grad = jnp.stack(attention_grads)
    qkv_sums = jnp.sum(qkv_grad.astype(jnp.float32), axis=(0, 1))
    qkv_weight_grad = jnp.einsum(
        "ire,ird->ed", qkv_grad, first_in, preferred_element_type=jnp.float32
    ).astype(low_type)
    qkv_sum = lax.psum_scatter(qkv_weight_grad, "img", scatter_dimension=0, tiled=True)
    first_grad = jnp.einsum("ire,ed->ird", after(qkv_grad, qkv_weight_grad), qkv_full, preferred_element_type=jnp.float32)
    shift_one_grad = jnp.sum(first_grad, axis=1)
    scale_one_grad = jnp.sum(first_grad * normed_one, axis=1)
    input_grad = to_bands(
        (
            middle_grad
            + normalize_back(normed_one, inverse_one, first_grad * (1.0 + scale_one))
        ).astype(low_type)
    ).astype(jnp.float32)
    mod_grad = jnp.stack(
        [
            shift_one_grad,
            scale_one_grad,
            gate_one_grad,
            shift_two_grad,
            scale_two_grad,
            gate_two_grad,
        ],
        axis=1,
    )
    row_sums = jnp.concatenate(
        [
            qkv_sums[:features][None],
            qkv_sums[2 * features :][None],
            jnp.sum(attended_grad.astype(jnp.float32), axis=(0, 1))[None],
            jnp.sum(pre_grad.astype(jnp.float32), axis=(0, 1)).reshape(4, features),
            jnp.sum(branch_grad.astype(jnp.float32), axis=(0, 1))[None],
        ],
        axis=0,
    )
    pieces = jnp.concatenate(
        [
            mod_grad.reshape(own, img_count, ada_columns)
            .transpose(1, 0, 2)
            .reshape(img_count, own * ada_columns),
            jnp.concatenate([jnp.sum(mod_grad, axis=0).reshape(6, features), row_sums], axis=0)
            .reshape(bias_rows, img_count, bias_columns)
            .transpose(1, 0, 2)
            .reshape(img_count, -1),
        ],
        axis=1,
    )
    sent = jnp.broadcast_to(pieces[:, None], (img_count, band_count, pieces.shape[1])).reshape(
        img_count * band_count, -1
    )
    got = lax.all_to_all(sent, ("img", "band"), split_axis=0, concat_axis=0, tiled=True)
    mod_columns = got[:, : own * ada_columns].reshape(-1, ada_columns)
    silu_terms = jnp.tile(
        silu_rows.astype(jnp.float32).reshape(img_count, 1, images, ada_rows), (1, split, 1, 1)
    ).reshape(img_count * band_count * own, ada_rows)
    ada_shard = jnp.einsum(
        "id,ie->de",
        silu_terms,
        mod_columns,
        precision=lax.Precision.HIGHEST,
    )
    bias_total = jnp.sum(got[:, own * ada_columns :], axis=0).reshape(bias_rows, bias_columns)
    down_shard = lax.psum_scatter(down_sum, "band", scatter_dimension=1, tiled=True).T.astype(
        jnp.float32
    )
    wide_shard = lax.psum_scatter(
        jnp.concatenate([qkv_sum, out_sum, up_sum], axis=0).T,
        "band",
        scatter_dimension=0,
        tiled=True,
    ).astype(jnp.float32)
    qkv_shard = wide_shard[:, :qkv_part]
    out_shard = wide_shard[:, qkv_part : qkv_part + out_part]
    up_shard = wide_shard[:, qkv_part + out_part :]
    shards = (ada_shard, qkv_shard, out_shard, up_shard, down_shard)
    squares = jnp.sum(bias_total * bias_total) / band_count
    for shard_grad in shards:
        squares = squares + jnp.sum(shard_grad * shard_grad)
    squares_total = sum_everywhere(squares)
    grad_norm = jnp.sqrt(squares_total)
    factor = clip_norm / jnp.maximum(grad_norm, clip_norm)
    ada_new, ada_first_new, ada_second_new = adam_update(
        ada_weight, ada_first, ada_second, shards[0], factor, learn_rate
    )
    qkv_new, qkv_first_new, qkv_second_new = adam_update(
        qkv_weight, qkv_first, qkv_second, shards[1], factor, learn_rate
    )
    out_new, out_first_new, out_second_new = adam_update(
        out_weight, out_first, out_second, shards[2], factor, out_rate
    )
    up_new, up_first_new, up_second_new = adam_update(
        up_weight, up_first, up_second, shards[3], factor, learn_rate
    )
    down_new, down_first_new, down_second_new = adam_update(
        down_weight, down_first, down_second, shards[4], factor, learn_rate
    )
    bias_new, bias_first_new, bias_second_new = adam_update(
        biases, bias_first, bias_second, bias_total, factor, bias_rate
    )
    branch_bias_grad = bias_total[13] * factor
    return (
        output,
        input_grad,
        grad_norm,
        ada_new,
        qkv_new,
        out_new,
        up_new,
        down_new,
        bias_new,
        ada_first_new,
        qkv_first_new,
        out_first_new,
        up_first_new,
        down_first_new,
        bias_first_new,
        ada_second_new,
        qkv_second_new,
        out_second_new,
        up_second_new,
        down_second_new,
        bias_second_new,
        branch_bias_grad,
    )


def solution(mesh):
    return jax.shard_map(
        body,
        mesh=mesh,
        in_specs=(
            P("img", "band", None),
            P("img", None),
            P("img"),
            P("img", "band", None),
            P("band", "img"),
            P("band", "img"),
            P("band", "img"),
            P("band", "img"),
            P("band", "img"),
            P(None, "img"),
            P("band", "img"),
            P("band", "img"),
            P("band", "img"),
            P("band", "img"),
            P("band", "img"),
            P(None, "img"),
            P("band", "img"),
            P("band", "img"),
            P("band", "img"),
            P("band", "img"),
            P("band", "img"),
            P(None, "img"),
        ),
        out_specs=(
            P("img", "band", None),
            P("img", "band", None),
            P(),
            P("band", "img"),
            P("band", "img"),
            P("band", "img"),
            P("band", "img"),
            P("band", "img"),
            P(None, "img"),
            P("band", "img"),
            P("band", "img"),
            P("band", "img"),
            P("band", "img"),
            P("band", "img"),
            P(None, "img"),
            P("band", "img"),
            P("band", "img"),
            P("band", "img"),
            P("band", "img"),
            P("band", "img"),
            P(None, "img"),
            P("img"),
        ),
        check_vma=False,
    )
```

```python
import functools

import jax
import jax.numpy as jnp
from jax import lax
from jax.experimental import pallas as pl
from jax.experimental.pallas import tpu as pltpu
from jax.sharding import PartitionSpec as P

HEADS = 16
HEAD_DIM = 72
L = 1024
STEP = 10


norm_eps = 1e-06
beta_one = 0.9
beta_two = 0.999
adam_eps = 1e-08
learn_rate = 0.03
out_rate = 0.25
bias_rate = 0.4
clip_norm = 1.0
very_low = -1000000000.0


def normalize_keep(values):
    centre = values - jnp.mean(values, axis=-1, keepdims=True)
    inverse = lax.rsqrt(jnp.mean(centre * centre, axis=-1, keepdims=True) + norm_eps)
    return (centre * inverse, inverse)


def normalize_back(normed, inverse, incoming):
    return inverse * (
        incoming
        - jnp.mean(incoming, axis=-1, keepdims=True)
        - normed * jnp.mean(incoming * normed, axis=-1, keepdims=True)
    )


def smooth_gate(values):
    return jax.nn.gelu(values, approximate=True)


def adam_update(weight, first_old, second_old, gradient, factor, rate):
    clipped = gradient * factor
    first_new = beta_one * first_old + (1.0 - beta_one) * clipped
    second_new = beta_two * second_old + (1.0 - beta_two) * clipped * clipped
    first_hat = first_new / (1.0 - beta_one**STEP)
    second_hat = second_new / (1.0 - beta_two**STEP)
    return (weight - rate * first_hat / (jnp.sqrt(second_hat) + adam_eps), first_new, second_new)


WINDOW = 256
CONTRACT_LAST = (((1,), (1,)), ((), ()))
LOG2_E = 1.4426950408889634


def head_window(head, features):
    start = head * HEAD_DIM
    base = pl.multiple_of(jnp.minimum(start // 128 * 128, features - WINDOW), 128)
    lane = lax.broadcasted_iota(jnp.int32, (1, WINDOW), 1)
    inside = (lane >= start - base) & (lane < start - base + HEAD_DIM)
    return base, inside


def attention_forward_kernel(
    query_ref, keyval_ref, bias_ref, mixed_ref, log_ref, scaled, value_t, mixed_t, *, features, shift, block
):
    length = keyval_ref.shape[0]
    rows = mixed_ref.shape[0]
    scaled[...] = (query_ref[:, :features].astype(jnp.float32) * (HEAD_DIM**-0.5 * LOG2_E)).astype(
        jnp.bfloat16
    )

    @pl.loop(0, features // 128)
    def _(tile):
        columns = pl.ds(pl.multiple_of(tile * 128, 128), 128)
        source = pl.ds(pl.multiple_of(shift + features + tile * 128, 128), 128)
        value_t[columns, :] = keyval_ref[:, source].astype(jnp.float32).T

    @pl.loop(0, HEADS)
    def _(head):
        base, inside = head_window(head, features)
        head_rows = pl.ds(pl.multiple_of(head * HEAD_DIM, 8), HEAD_DIM)
        query = scaled[:, pl.ds(base, WINDOW)]
        ones = jnp.ones((8, block), jnp.float32)
        top = None
        for at in range(0, length, block):
            key = keyval_ref[pl.ds(at, block), pl.ds(pl.multiple_of(base + shift, 128), WINDOW)]
            key = jnp.where(inside, key, jnp.zeros_like(key))
            scores = lax.dot_general(key, query, CONTRACT_LAST, preferred_element_type=jnp.float32)
            if at + block == length:
                scores = scores + bias_ref[pl.ds(at, block), :]
            block_top = jnp.max(scores, axis=0, keepdims=True)
            value = jnp.concatenate([value_t[head_rows, pl.ds(at, block)], ones], axis=0).astype(jnp.bfloat16)
            if top is None:
                top = block_top
                probs = jnp.exp2(scores - top).astype(jnp.bfloat16)
                total = jnp.dot(value, probs, preferred_element_type=jnp.float32)
            else:
                new_top = jnp.maximum(top, block_top)
                fade = jnp.exp2(top - new_top)
                top = new_top
                probs = jnp.exp2(scores - top).astype(jnp.bfloat16)
                total = total * fade + jnp.dot(value, probs, preferred_element_type=jnp.float32)
        weight = total[HEAD_DIM : HEAD_DIM + 1]
        mixed_t[head_rows, :] = total[:HEAD_DIM] * (1.0 / weight)
        log_ref[pl.ds(head, 1), :] = top + jnp.log2(weight)

    @pl.loop(0, features // 128)
    def _(tile):
        columns = pl.ds(pl.multiple_of(tile * 128, 128), 128)
        mixed_ref[:, columns] = mixed_t[columns, :].T.astype(jnp.bfloat16)


def attention_forward(query, keyval, key_bias, features, shift, block):
    rows, length = query.shape[0], keyval.shape[0]
    return pl.pallas_call(
        functools.partial(attention_forward_kernel, features=features, shift=shift, block=block),
        out_shape=(
            jax.ShapeDtypeStruct((rows, features), jnp.bfloat16),
            jax.ShapeDtypeStruct((HEADS, rows), jnp.float32),
        ),
        scratch_shapes=[
            pltpu.VMEM((rows, features), jnp.bfloat16),
            pltpu.VMEM((features, length), jnp.float32),
            pltpu.VMEM((features, rows), jnp.float32),
        ],
        compiler_params=pltpu.CompilerParams(vmem_limit_bytes=56 * 2**20),
    )(query, keyval, key_bias)


def attention_backward_kernel(
    query_ref, keyval_ref, bias_ref, mixed_ref, grad_ref, log_ref, out_ref, keyval_grad_ref,
    scaled, key_t, wide_t, *, features, shift, out_shift, block
):
    length = keyval_ref.shape[0]
    rows = mixed_ref.shape[0]
    scale = HEAD_DIM**-0.5
    scaled[...] = (query_ref[:, :features].astype(jnp.float32) * (scale * LOG2_E)).astype(jnp.bfloat16)

    @pl.loop(0, features // 128)
    def _(tile):
        columns = pl.ds(pl.multiple_of(tile * 128, 128), 128)
        key_t[columns, :] = keyval_ref[:, pl.ds(pl.multiple_of(shift + tile * 128, 128), 128)].astype(jnp.float32).T
        wide_t[columns, :] = (
            mixed_ref[:, columns].astype(jnp.float32) * grad_ref[:, columns].astype(jnp.float32)
        ).T

    @pl.loop(0, HEADS)
    def _(head):
        base, inside = head_window(head, features)
        head_rows = pl.ds(pl.multiple_of(head * HEAD_DIM, 8), HEAD_DIM)
        window = pl.ds(base, WINDOW)
        delta = jnp.sum(wide_t[head_rows, :], axis=0, keepdims=True)
        log_total = log_ref[pl.ds(head, 1), :]
        query = query_ref[:, window]
        query_scaled = scaled[:, window]
        grad = grad_ref[:, window]
        query_grad = None
        for at in range(0, length, block):
            here = pl.ds(at, block)
            key_window = pl.ds(pl.multiple_of(base + shift, 128), WINDOW)
            value_window = pl.ds(pl.multiple_of(base + shift + features, 128), WINDOW)
            key = keyval_ref[here, key_window]
            value = keyval_ref[here, value_window]
            key = jnp.where(inside, key, jnp.zeros_like(key))
            value = jnp.where(inside, value, jnp.zeros_like(value))
            scores = lax.dot_general(key, query_scaled, CONTRACT_LAST, preferred_element_type=jnp.float32)
            if at + block == length:
                scores = scores + bias_ref[here, :]
            probs = jnp.exp2(scores - log_total)
            prob_grad = lax.dot_general(value, grad, CONTRACT_LAST, preferred_element_type=jnp.float32)
            score_grad = (probs * (prob_grad - delta)).astype(jnp.bfloat16)
            value_grad = jnp.dot(probs.astype(jnp.bfloat16), grad, preferred_element_type=jnp.float32)
            key_grad = jnp.dot(score_grad, query, preferred_element_type=jnp.float32) * scale
            key_out = pl.ds(pl.multiple_of(base + out_shift, 128), WINDOW)
            value_out = pl.ds(pl.multiple_of(base + out_shift + features, 128), WINDOW)
            keyval_grad_ref[here, key_out] = jnp.where(inside, key_grad.astype(jnp.bfloat16), keyval_grad_ref[here, key_out])
            keyval_grad_ref[here, value_out] = jnp.where(inside, value_grad.astype(jnp.bfloat16), keyval_grad_ref[here, value_out])
            part = jnp.dot(
                key_t[head_rows, here].astype(jnp.bfloat16), score_grad, preferred_element_type=jnp.float32
            )
            query_grad = part if query_grad is None else query_grad + part
        wide_t[head_rows, :] = query_grad * scale

    @pl.loop(0, features // 128)
    def _(tile):
        columns = pl.ds(pl.multiple_of(tile * 128, 128), 128)
        out_ref[:, columns] = wide_t[columns, :].T.astype(jnp.bfloat16)


def attention_backward(query, keyval, key_bias, mixed, grad, log_total, features, block):
    rows, length = query.shape[0], keyval.shape[0]
    shared = query is keyval
    scratch = [
        pltpu.VMEM((rows, features), jnp.bfloat16),
        pltpu.VMEM((features, length), jnp.float32),
        pltpu.VMEM((features, rows), jnp.float32),
    ]
    params = pltpu.CompilerParams(vmem_limit_bytes=56 * 2**20)
    if shared:

        def shared_kernel(both_ref, bias_ref, mixed_ref, grad_ref, log_ref, out_ref, *held):
            attention_backward_kernel(
                both_ref, both_ref, bias_ref, mixed_ref, grad_ref, log_ref, out_ref, out_ref, *held,
                features=features, shift=features, out_shift=features, block=block,
            )

        return pl.pallas_call(
            shared_kernel,
            out_shape=jax.ShapeDtypeStruct((rows, 3 * features), jnp.bfloat16),
            scratch_shapes=scratch,
            compiler_params=params,
        )(query, key_bias, mixed, grad, log_total)
    return pl.pallas_call(
        functools.partial(
            attention_backward_kernel, features=features, shift=0, out_shift=0, block=block
        ),
        out_shape=(
            jax.ShapeDtypeStruct((rows, features), jnp.bfloat16),
            jax.ShapeDtypeStruct((length, 2 * features), jnp.bfloat16),
        ),
        scratch_shapes=scratch,
        compiler_params=params,
    )(query, keyval, key_bias, mixed, grad, log_total)


MESH = pl.DeviceIdType.MESH


def flip(index, bit):
    return index + bit - 2 * bit * lax.rem(lax.div(index, bit), 2)


def start_kernel(
    wide_ref, tall_ref, tokens_ref,
    qkv_ref, out_ref, up_ref, down_ref, rows_ref,
    held, turned, line_send, line_recv, row_send, row_recv, flat_send, flat_recv, local_sem,
    *, bands, qkv_part, out_part,
):
    img, band = lax.axis_index("img"), lax.axis_index("band")
    depth, width = wide_ref.shape
    tall_rows, tall_width = tall_ref.shape
    row_block = tokens_ref.shape[1]
    lanes = 128
    first = -(-(qkv_part + out_part) // lanes) * lanes
    beside_x, beside_y, sibling = flip(img, 2), flip(img, 4), flip(img, 1)
    across = flip(beside_x, 4)

    barrier = pltpu.get_barrier_semaphore()
    for other in (beside_x, beside_y, sibling):
        pl.semaphore_signal(barrier, inc=1, device_id={"img": other}, device_id_type=MESH)
    for step in range(1, bands):
        pl.semaphore_signal(
            barrier, inc=1, device_id={"band": lax.rem(band + step, bands)}, device_id_type=MESH
        )
    pl.semaphore_wait(barrier, 3 + bands - 1)

    def piece(part, owner):
        if part == 2:
            return down_ref.at[:, pl.ds(pl.multiple_of(owner * tall_width, lanes), tall_width)]
        span = pl.ds(0, first) if part == 0 else pl.ds(first, width - first)
        return held.at[pl.ds(pl.multiple_of(owner * depth, 16), depth), span]

    def line_copy(part, way, step, owner, toward):
        view = piece(part, owner)
        return pltpu.make_async_remote_copy(
            src_ref=view, dst_ref=view,
            send_sem=line_send.at[part, way, step], recv_sem=line_recv.at[part, way, step],
            device_id={"band": toward}, device_id_type=MESH,
        )

    def line_sends(part, step, act):
        for way, sign in ((0, 1), (1, -1)):
            owner, toward = band - sign * step, band + sign

            @pl.when((owner >= 0) & (owner < bands) & (toward >= 0) & (toward < bands))
            def _():
                act(line_copy(part, way, step, owner, toward))

    def line_arrivals(part, step):
        for way, sign in ((0, 1), (1, -1)):
            owner = band - sign * (step + 1)

            @pl.when((owner >= 0) & (owner < bands))
            def _():
                line_copy(part, way, step, owner, band - sign).wait_recv()

    def row_copy(step):
        target = lax.rem(band + step, bands)
        return pltpu.make_async_remote_copy(
            src_ref=tokens_ref.at[target],
            dst_ref=rows_ref.at[pl.ds(pl.multiple_of(band * row_block, 16), row_block), :],
            send_sem=row_send.at[step - 1], recv_sem=row_recv.at[step - 1],
            device_id={"band": target}, device_id_type=MESH,
        )

    def row_arrival(step):
        source = lax.rem(band + bands - step, bands)
        view = rows_ref.at[pl.ds(pl.multiple_of(source * row_block, 16), row_block), :]
        return pltpu.make_async_remote_copy(
            src_ref=view, dst_ref=view,
            send_sem=row_send.at[step - 1], recv_sem=row_recv.at[step - 1],
            device_id={"band": source}, device_id_type=MESH,
        )

    def qkv_rows(owner, start=0, count=qkv_part):
        return qkv_ref.at[pl.ds(pl.multiple_of(owner * qkv_part + start, 16), count), :]

    def out_rows(owner):
        return out_ref.at[pl.ds(pl.multiple_of(owner * out_part, 16), out_part), :]

    half = (qkv_part + out_part) // 2
    own_qkv, own_out = turned.at[pl.ds(0, qkv_part), :], turned.at[pl.ds(qkv_part, out_part), :]
    plan = [
        (own_qkv, qkv_rows(img), beside_x, qkv_rows(beside_x)),
        (own_out, out_rows(img), beside_x, out_rows(beside_x)),
        (own_qkv, qkv_rows(img), beside_y, qkv_rows(beside_y)),
        (own_out, out_rows(img), beside_y, out_rows(beside_y)),
        (own_qkv, qkv_rows(img), sibling, qkv_rows(sibling)),
        (own_out, out_rows(img), sibling, out_rows(sibling)),
    ]
    for owner, toward, whole in ((beside_x, beside_y, True), (beside_y, beside_x, False)):
        if whole:
            view = qkv_rows(owner, 0, half)
            plan.append((view, view, toward, qkv_rows(across, 0, half)))
        else:
            rest = qkv_part - half
            view = qkv_rows(owner, half, rest)
            plan.append((view, view, toward, qkv_rows(across, half, rest)))
            plan.append((out_rows(owner), out_rows(owner), toward, out_rows(across)))
    for owner in (beside_x, beside_y):
        plan.append((qkv_rows(owner), qkv_rows(owner), sibling, qkv_rows(flip(owner, 1))))
        plan.append((out_rows(owner), out_rows(owner), sibling, out_rows(flip(owner, 1))))
    far = flip(across, 1)
    plan.append((qkv_rows(across, 0, half), qkv_rows(across, 0, half), sibling, qkv_rows(far, 0, half)))
    rest = qkv_part - half
    plan.append((qkv_rows(across, half, rest), qkv_rows(across, half, rest), sibling, qkv_rows(far, half, rest)))
    plan.append((out_rows(across), out_rows(across), sibling, out_rows(far)))

    def flat_copy(at):
        source, target, toward, _ = plan[at]
        return pltpu.make_async_remote_copy(
            src_ref=source, dst_ref=target, send_sem=flat_send.at[at], recv_sem=flat_recv.at[at],
            device_id={"img": toward}, device_id_type=MESH,
        )

    def flat_arrival(at):
        landing = plan[at][3]
        pltpu.make_async_remote_copy(
            src_ref=landing, dst_ref=landing, send_sem=flat_send.at[at], recv_sem=flat_recv.at[at],
            device_id={"img": sibling}, device_id_type=MESH,
        ).wait_recv()

    def turn(tile):
        span = pl.ds(pl.multiple_of(tile * lanes, lanes), lanes)
        turned[span, :] = held[:, span].astype(jnp.float32).T.astype(jnp.bfloat16)

    start = lambda copy: copy.start()
    own_rows = pltpu.make_async_copy(
        tokens_ref.at[band],
        rows_ref.at[pl.ds(pl.multiple_of(band * row_block, 16), row_block), :],
        local_sem.at[0],
    )
    own_rows.start()
    held[pl.ds(pl.multiple_of(band * depth, 16), depth), :] = wide_ref[...]
    down_ref[:, pl.ds(pl.multiple_of(band * tall_width, lanes), tall_width)] = tall_ref[...]
    line_sends(0, 0, start)
    for step in range(bands - 1):
        line_arrivals(0, step)
        if step < bands - 2:
            line_sends(0, step + 1, start)
    line_sends(1, 0, start)
    line_sends(2, 0, start)
    for step in range(1, bands):
        row_copy(step).start()
    pl.loop(0, first // lanes)(turn)
    keep_qkv = pltpu.make_async_copy(own_qkv, qkv_rows(img), local_sem.at[1])
    keep_out = pltpu.make_async_copy(own_out, out_rows(img), local_sem.at[2])
    for at in range(6):
        flat_copy(at).start()
    keep_qkv.start()
    keep_out.start()
    for step in range(bands - 2):
        for part in (1, 2):
            line_arrivals(part, step)
            line_sends(part, step + 1, start)
    for arrived, sent in (((0, 1), (6, 9, 10)), ((2, 3), (7, 8, 11, 12))):
        for at in arrived:
            flat_arrival(at)
        for at in sent:
            flat_copy(at).start()
    for at in (6, 7, 8):
        flat_arrival(at)
        flat_copy(at + 7).start()
    for part in (1, 2):
        line_arrivals(part, bands - 2)
    pl.loop(first // lanes, width // lanes)(turn)
    up_ref[...] = turned[pl.ds(qkv_part + out_part, width - qkv_part - out_part), :]
    for part in range(3):
        for step in range(bands - 1):
            line_sends(part, step, lambda copy: copy.wait_send())
    for at in (4, 5, 9, 10, 11, 12, 13, 14, 15):
        flat_arrival(at)
    for at in range(16):
        flat_copy(at).wait_send()
    for step in range(1, bands):
        row_copy(step).wait_send()
        row_arrival(step).wait_recv()
    own_rows.wait()
    keep_qkv.wait()
    keep_out.wait()


def start_exchange(wide, tall, tokens, bands, imgs, qkv_part, out_part):
    depth, width = wide.shape
    up_part = width - qkv_part - out_part
    low = jnp.bfloat16
    anywhere, vmem = pl.BlockSpec(memory_space=pl.ANY), pl.BlockSpec(memory_space=pltpu.VMEM)
    features = depth * bands
    return pl.pallas_call(
        functools.partial(start_kernel, bands=bands, qkv_part=qkv_part, out_part=out_part),
        out_shape=(
            jax.ShapeDtypeStruct((qkv_part * imgs, features), low),
            jax.ShapeDtypeStruct((out_part * imgs, features), low),
            jax.ShapeDtypeStruct((up_part, features), low),
            jax.ShapeDtypeStruct((tall.shape[0], tall.shape[1] * bands), low),
            jax.ShapeDtypeStruct((tokens.shape[1] * bands, tokens.shape[2]), low),
        ),
        in_specs=[vmem, vmem, anywhere],
        out_specs=(anywhere, anywhere, vmem, vmem, anywhere),
        scratch_shapes=[
            pltpu.VMEM((features, width), low),
            pltpu.VMEM((width, features), low),
            pltpu.SemaphoreType.DMA((3, 2, bands - 1)),
            pltpu.SemaphoreType.DMA((3, 2, bands - 1)),
            pltpu.SemaphoreType.DMA((bands - 1,)),
            pltpu.SemaphoreType.DMA((bands - 1,)),
            pltpu.SemaphoreType.DMA((16,)),
            pltpu.SemaphoreType.DMA((16,)),
            pltpu.SemaphoreType.DMA((3,)),
        ],
        compiler_params=pltpu.CompilerParams(
            collective_id=0, has_side_effects=True, vmem_limit_bytes=40 * 2**20
        ),
    )(wide, tall, tokens)


def add_low(left, right):
    return (left.astype(jnp.float32) + right.astype(jnp.float32)).astype(jnp.bfloat16)


def tail_kernel(
    qkv_ref, out_ref, up_ref, down_ref, rows_ref,
    wide_ref, tall_ref, back_ref,
    own, from_core, first_x, first_y, last_x, last_y, turned, held, tall, held_in, tall_in,
    core_send, core_recv, flat_send, flat_recv, line_send, line_recv, row_send, row_recv, local_sem,
    *, bands, early,
):
    img, band = lax.axis_index("img"), lax.axis_index("band")
    qkv_part, out_part = own.shape[1], out_ref.shape[0]
    width = turned.shape[0]
    depth, tall_width = wide_ref.shape[0], tall_ref.shape[1]
    row_block = back_ref.shape[1]
    half = first_x.shape[1]
    lanes = 128
    first = -(-(qkv_part + out_part) // lanes) * lanes
    beside_x, beside_y, sibling = flip(img, 2), flip(img, 4), flip(img, 1)
    chips = (img, beside_x, beside_y, flip(beside_x, 4))
    upper, lower = pl.ds(0, half), pl.ds(half, qkv_part - half)

    barrier = pltpu.get_barrier_semaphore()
    for other in (beside_x, beside_y, sibling):
        pl.semaphore_signal(barrier, inc=1, device_id={"img": other}, device_id_type=MESH)
    for step in range(1, bands):
        pl.semaphore_signal(
            barrier, inc=1, device_id={"band": lax.rem(band + step, bands)}, device_id_type=MESH
        )
    pl.semaphore_wait(barrier, 3 + bands - 1)

    def qkv_rows(owner):
        return qkv_ref.at[pl.ds(pl.multiple_of(owner * qkv_part, 16), qkv_part), :]

    def core_copy(at):
        return pltpu.make_async_remote_copy(
            src_ref=qkv_rows(flip(chips[at], 1)), dst_ref=from_core.at[at],
            send_sem=core_send.at[at], recv_sem=core_recv.at[at],
            device_id={"img": sibling}, device_id_type=MESH,
        )

    def own_copy(at):
        return pltpu.make_async_copy(qkv_rows(chips[at]), own.at[at], local_sem.at[at])

    plan = (
        (own.at[1, upper], first_x.at[0], beside_x),
        (own.at[3, upper], first_x.at[1], beside_x),
        (own.at[2, lower], first_y.at[0], beside_y),
        (own.at[3, lower], first_y.at[1], beside_y),
        (own.at[2, upper], last_y, beside_y),
        (own.at[1, lower], last_x, beside_x),
    )

    def flat_copy(at):
        source, target, toward = plan[at]
        return pltpu.make_async_remote_copy(
            src_ref=source, dst_ref=target, send_sem=flat_send.at[at], recv_sem=flat_recv.at[at],
            device_id={"img": toward}, device_id_type=MESH,
        )

    def row_span(owner):
        return pl.ds(pl.multiple_of(owner * row_block, 16), row_block)

    def row_copy(step):
        target = lax.rem(band + step, bands)
        return pltpu.make_async_remote_copy(
            src_ref=rows_ref.at[row_span(target), :], dst_ref=back_ref.at[band],
            send_sem=row_send.at[step - 1], recv_sem=row_recv.at[step - 1],
            device_id={"band": target}, device_id_type=MESH,
        )

    def row_arrival(step):
        source = lax.rem(band + bands - step, bands)
        return pltpu.make_async_remote_copy(
            src_ref=back_ref.at[source], dst_ref=back_ref.at[source],
            send_sem=row_send.at[step - 1], recv_sem=row_recv.at[step - 1],
            device_id={"band": source}, device_id_type=MESH,
        )

    def piece(part, owner, way=None):
        if part == 2:
            span = pl.ds(pl.multiple_of(owner * tall_width, lanes), tall_width)
            return tall.at[:, span] if way is None else tall_in.at[way, :, span]
        span = pl.ds(0, first) if part == 0 else pl.ds(first, width - first)
        down = pl.ds(pl.multiple_of(owner * depth, 16), depth)
        return held.at[down, span] if way is None else held_in.at[way, down, span]

    def line_copy(part, way, owner, toward):
        return pltpu.make_async_remote_copy(
            src_ref=piece(part, owner), dst_ref=piece(part, owner, way),
            send_sem=line_send.at[part, way, owner], recv_sem=line_recv.at[part, way, owner],
            device_id={"band": toward}, device_id_type=MESH,
        )

    def line_ends(part):
        for step in range(bands - 1):

            @pl.when(band == 0)
            def _():
                line_copy(part, 0, bands - 1 - step, band + 1).start()

            @pl.when(band == bands - 1)
            def _():
                line_copy(part, 1, step, band - 1).start()

    def line_round(part, step):
        for way, owner, sign in ((0, bands - 1 - step, 1), (1, step, -1)):

            @pl.when((sign * (owner - band) > 0) & (band > 0) & (band < bands - 1))
            def _():
                copy = line_copy(part, way, owner, band + sign)
                copy.wait_recv()
                mine = piece(part, owner)
                mine[...] = add_low(mine[...], piece(part, owner, way)[...])
                copy.start()

    def line_finish(part, target, span):
        total = piece(part, band)[...].astype(jnp.float32)
        target[:, span] = total
        for way, sign in ((0, 1), (1, -1)):

            @pl.when((band - sign >= 0) & (band - sign < bands))
            def _():
                line_copy(part, way, band, band - sign).wait_recv()
                target[:, span] += piece(part, band, way)[...].astype(jnp.float32)

    def line_sent(part):
        for way, sign in ((0, 1), (1, -1)):
            for owner in range(bands):

                @pl.when(sign * (owner - band) > 0)
                def _():
                    line_copy(part, way, owner, band + sign).wait_send()

    def turn(tile):
        span = pl.ds(pl.multiple_of(tile * lanes, lanes), lanes)
        held[:, span] = turned[span, :].astype(jnp.float32).T.astype(jnp.bfloat16)

    order = (3, 1, 2, 0)
    for at in order:
        core_copy(at).start()
    for at in order:
        own_copy(at).start()
    turned[pl.ds(qkv_part, out_part), :] = out_ref[...]
    turned[pl.ds(qkv_part + out_part, width - qkv_part - out_part), :] = up_ref[...]
    pl.loop(first // lanes, width // lanes)(turn)
    tall[...] = down_ref[...]
    line_ends(1)
    line_ends(2)
    keep = pltpu.make_async_copy(rows_ref.at[row_span(band), :], back_ref.at[band], local_sem.at[4])
    keep.start()
    for step in range(1, bands):
        row_copy(step).start()
    for at in order:
        own_copy(at).wait()
        core_copy(at).wait_recv()
        own[at] = add_low(own[at], from_core[at])
        for ready in {3: (1, 3), 1: (0,), 2: (2,), 0: ()}[at]:
            flat_copy(ready).start()
    flat_copy(1).wait_recv()
    own[2, upper] = add_low(own[2, upper], first_x[1])
    flat_copy(4).start()
    flat_copy(3).wait_recv()
    own[1, lower] = add_low(own[1, lower], first_y[1])
    flat_copy(5).start()
    for part in early:
        line_round(part, 0)
    flat_copy(0).wait_recv()
    flat_copy(2).wait_recv()
    flat_copy(4).wait_recv()
    flat_copy(5).wait_recv()
    turned[upper, :] = (
        own[0, upper].astype(jnp.float32)
        + first_x[0].astype(jnp.float32)
        + last_y[...].astype(jnp.float32)
    ).astype(jnp.bfloat16)
    turned[lower, :] = (
        own[0, lower].astype(jnp.float32)
        + first_y[0].astype(jnp.float32)
        + last_x[...].astype(jnp.float32)
    ).astype(jnp.bfloat16)
    pl.loop(0, first // lanes)(turn)
    line_ends(0)
    for step in range(bands - 1):
        for part in (1, 2, 0):
            if step > 0 or part not in early:
                line_round(part, step)
    line_finish(1, wide_ref, pl.ds(first, width - first))
    line_finish(2, tall_ref, pl.ds(0, tall_width))
    line_finish(0, wide_ref, pl.ds(0, first))
    for part in range(3):
        line_sent(part)
    for at in range(4):
        core_copy(at).wait_send()
    for at in range(6):
        flat_copy(at).wait_send()
    for step in range(1, bands):
        row_copy(step).wait_send()
        row_arrival(step).wait_recv()
    keep.wait()


def tail_exchange(qkv_grad, out_sum, up_sum, down_sum, rows, bands, imgs):
    low = jnp.bfloat16
    qkv_part, features = qkv_grad.shape[0] // imgs, qkv_grad.shape[1]
    out_part, up_part = out_sum.shape[0], up_sum.shape[0]
    width = qkv_part + out_part + up_part
    tall_rows, tall_width = down_sum.shape[0], down_sum.shape[1] // bands
    half = -(-qkv_part // 32) * 16
    anywhere, vmem = pl.BlockSpec(memory_space=pl.ANY), pl.BlockSpec(memory_space=pltpu.VMEM)
    return pl.pallas_call(
        functools.partial(tail_kernel, bands=bands, early=(1, 2)),
        out_shape=(
            jax.ShapeDtypeStruct((features // bands, width), jnp.float32),
            jax.ShapeDtypeStruct((tall_rows, tall_width), jnp.float32),
            jax.ShapeDtypeStruct((bands, rows.shape[0] // bands, features), low),
        ),
        in_specs=[anywhere, vmem, vmem, vmem, anywhere],
        out_specs=(vmem, vmem, anywhere),
        scratch_shapes=[
            pltpu.VMEM((4, qkv_part, features), low),
            pltpu.VMEM((4, qkv_part, features), low),
            pltpu.VMEM((2, half, features), low),
            pltpu.VMEM((2, qkv_part - half, features), low),
            pltpu.VMEM((qkv_part - half, features), low),
            pltpu.VMEM((half, features), low),
            pltpu.VMEM((width, features), low),
            pltpu.VMEM((features, width), low),
            pltpu.VMEM((tall_rows, tall_width * bands), low),
            pltpu.VMEM((2, features, width), low),
            pltpu.VMEM((2, tall_rows, tall_width * bands), low),
            pltpu.SemaphoreType.DMA((4,)),
            pltpu.SemaphoreType.DMA((4,)),
            pltpu.SemaphoreType.DMA((6,)),
            pltpu.SemaphoreType.DMA((6,)),
            pltpu.SemaphoreType.DMA((3, 2, bands)),
            pltpu.SemaphoreType.DMA((3, 2, bands)),
            pltpu.SemaphoreType.DMA((bands - 1,)),
            pltpu.SemaphoreType.DMA((bands - 1,)),
            pltpu.SemaphoreType.DMA((5,)),
        ],
        compiler_params=pltpu.CompilerParams(
            collective_id=1, has_side_effects=True, vmem_limit_bytes=50 * 2**20
        ),
    )(qkv_grad, out_sum, up_sum, down_sum, rows)


def body(
    inputs,
    condition,
    valid_rows,
    cotangent,
    ada_weight,
    qkv_weight,
    out_weight,
    up_weight,
    down_weight,
    biases,
    ada_first,
    qkv_first,
    out_first,
    up_first,
    down_first,
    bias_first,
    ada_second,
    qkv_second,
    out_second,
    up_second,
    down_second,
    bias_second,
):
    images, local_rows, features = inputs.shape
    length = L
    head_count = HEADS
    head_size = HEAD_DIM
    score_scale = head_size ** (-0.5)
    band_count = lax.axis_size("band")
    img_count = lax.axis_size("img")
    band_rank = lax.axis_index("band")
    img_rank = lax.axis_index("img")
    own = max(1, images // band_count)
    split = max(1, band_count // images)
    mates = band_count // split
    image_rows = length // split
    exchange_groups = None
    share_groups = None
    if split > 1:
        exchange_groups = [[g * mates + m for m in range(mates)] for g in range(split)]
        share_groups = [[g * mates + m for g in range(split)] for m in range(mates)]
    low_type = jnp.bfloat16

    def to_images(rows):
        return lax.all_to_all(rows, "band", split_axis=0, concat_axis=1, axis_index_groups=exchange_groups, tiled=True)

    def to_bands(whole):
        cut = whole.reshape(own, mates, local_rows, features).transpose(1, 0, 2, 3)
        back = lax.all_to_all(
            cut, "band", split_axis=0, concat_axis=0, axis_index_groups=exchange_groups, tiled=True
        )
        return back.reshape(images, local_rows, features)

    def after(value, *earlier):
        return lax.optimization_barrier((value,) + earlier)[0]

    def sum_everywhere(partial):
        sent = jnp.broadcast_to(partial, (img_count * band_count, 128))
        got = lax.all_to_all(sent, ("img", "band"), split_axis=0, concat_axis=0, tiled=True)
        return jnp.sum(got[:, 0])

    qkv_part, out_part = qkv_weight.shape[1], out_weight.shape[1]

    bias_rows, bias_columns = biases.shape
    small = lax.all_gather(
        jnp.concatenate([condition.reshape(1, -1), biases.astype(low_type).reshape(1, -1)], axis=1),
        "img",
        axis=0,
        tiled=True,
    )
    condition_all = small[:, : images * features].reshape(img_count * images, features)
    bias_vals = (
        small[:, images * features :]
        .astype(jnp.float32)
        .reshape(img_count, bias_rows, bias_columns)
        .transpose(1, 0, 2)
        .reshape(bias_rows, features)
    )
    wide = jnp.concatenate([qkv_weight, out_weight, up_weight], axis=1).astype(low_type)
    tall = down_weight.T.astype(low_type)
    if img_count == 8 and own == 1 and split == 1:
        qkv_full, out_full, up_rows, down_rows, tokens_low = start_exchange(
            wide, tall, inputs, band_count, img_count, qkv_part, out_part
        )
        tokens_low = tokens_low.reshape(own, image_rows, features)
    else:
        turned = lax.all_gather(wide, "band", axis=0, tiled=True).T
        qkv_full = lax.all_gather(turned[:qkv_part], "img", axis=0, tiled=True)
        out_full = lax.all_gather(
            turned[qkv_part : qkv_part + out_part], "img", axis=0, tiled=True
        )
        up_rows = turned[qkv_part + out_part :]
        down_rows = lax.all_gather(tall, "band", axis=1, tiled=True)
        tokens_low = to_images(inputs)
    up_full = lax.all_gather(up_rows, "img", axis=0, tiled=True)
    down_full = lax.all_gather(after(down_rows, up_rows), "img", axis=0, tiled=True)

    silu_all = jax.nn.silu(condition_all.astype(jnp.float32)).astype(low_type)
    ada_rows = ada_weight.shape[0]
    silu_rows = lax.dynamic_slice_in_dim(silu_all, band_rank * ada_rows, ada_rows, axis=1)
    mod_partial = jnp.dot(
        silu_rows, ada_weight.astype(low_type), preferred_element_type=jnp.float32
    )
    ada_columns = mod_partial.shape[1]
    mod_sent = jnp.tile(
        mod_partial.reshape(img_count, 1, images * ada_columns), (1, split, 1)
    )
    mod_pieces = lax.all_to_all(
        mod_sent.reshape(img_count * band_count, own * ada_columns),
        ("img", "band"),
        split_axis=0,
        concat_axis=0,
        tiled=True,
    ).reshape(img_count, band_count, own, ada_columns)
    modulation = (
        jnp.sum(mod_pieces, axis=1).transpose(1, 0, 2).reshape(own, img_count * ada_columns)
        + bias_vals[0:6].reshape(-1)
    )
    mod_parts = modulation.reshape(own, 6, 1, features)
    shift_one = mod_parts[:, 0]
    scale_one = mod_parts[:, 1]
    gate_one = mod_parts[:, 2]
    shift_two = mod_parts[:, 3]
    scale_two = mod_parts[:, 4]
    gate_two = mod_parts[:, 5]
    valid_own = lax.dynamic_slice_in_dim(valid_rows, lax.rem(band_rank, mates) * own, own, axis=0)
    key_mask = jnp.arange(length, dtype=jnp.int32)[None, :] < valid_own[:, None]
    positions = lax.div(band_rank, mates) * image_rows + jnp.arange(image_rows, dtype=jnp.int32)
    row_mask = (positions[None, :] < valid_own[:, None]).astype(jnp.float32)[:, :, None]
    tokens_in = tokens_low.astype(jnp.float32)
    normed_one, inverse_one = normalize_keep(tokens_in)
    first_in = (normed_one * (1.0 + scale_one) + shift_one).astype(jnp.bfloat16)
    cotangent_low = to_images(after(cotangent, tokens_low))
    grad_out = cotangent_low.astype(jnp.float32) * row_mask
    qkv_bias = jnp.concatenate([bias_vals[6], jnp.zeros((features,), jnp.float32), bias_vals[7]])
    projected = (
        jnp.einsum("ird,ed->ire", first_in, qkv_full, preferred_element_type=jnp.float32) + qkv_bias
    ).astype(jnp.bfloat16)
    key_bias = jnp.where(key_mask, 0.0, very_low).astype(jnp.float32)[:, :, None]
    queries = [projected[i] for i in range(own)]
    if split > 1:
        keys_values = lax.all_gather(
            projected[..., features:], "band", axis=1, axis_index_groups=share_groups, tiled=True
        )
        keys_values = [keys_values[i] for i in range(own)]
        key_shift = 0
    else:
        keys_values = queries
        key_shift = features
    mixed, log_total = zip(
        *[
            attention_forward(queries[i], keys_values[i], key_bias[i], features, key_shift, 512)
            for i in range(own)
        ]
    )
    mixed_parts = mixed
    mixed = jnp.stack(mixed)
    attended = (
        jnp.einsum("ird,ed->ire", mixed, out_full, preferred_element_type=jnp.float32)
        + bias_vals[8]
    )
    middle = tokens_in + gate_one * attended
    normed_two, inverse_two = normalize_keep(middle)
    second_in = (normed_two * (1.0 + scale_two) + shift_two).astype(jnp.bfloat16)
    hidden_pre = jnp.einsum(
        "ird,fd->irf", second_in, up_full, preferred_element_type=jnp.float32
    ) + bias_vals[9:13].reshape(-1)
    hidden, gelu_back = jax.vjp(smooth_gate, hidden_pre)
    hidden_low = hidden.astype(jnp.bfloat16)
    branch = (
        jnp.einsum("irf,df->ird", hidden_low, down_full, preferred_element_type=jnp.float32)
        + bias_vals[13]
    )
    output = to_bands((middle + gate_two * branch).astype(jnp.bfloat16))
    branch_grad = (gate_two * grad_out).astype(jnp.bfloat16)
    gate_two_grad = jnp.sum(grad_out * branch, axis=1)
    down_grad = jnp.einsum(
        "ird,irf->df", branch_grad, hidden_low, preferred_element_type=jnp.float32
    ).astype(low_type)
    down_sum = lax.psum_scatter(down_grad, "img", scatter_dimension=0, tiled=True)
    hidden_grad = jnp.einsum(
        "ird,df->irf",
        after(branch_grad, down_grad),
        down_full,
        preferred_element_type=jnp.float32,
    )
    pre_grad = gelu_back(hidden_grad)[0].astype(jnp.bfloat16)
    up_grad = jnp.einsum(
        "irf,ird->fd", pre_grad, second_in, preferred_element_type=jnp.float32
    ).astype(low_type)
    up_sum = lax.psum_scatter(after(up_grad, down_sum), "img", scatter_dimension=0, tiled=True)
    second_grad = jnp.einsum("irf,fd->ird", after(pre_grad, up_grad), up_full, preferred_element_type=jnp.float32)
    shift_two_grad = jnp.sum(second_grad, axis=1)
    scale_two_grad = jnp.sum(second_grad * normed_two, axis=1)
    middle_grad = grad_out + normalize_back(
        normed_two, inverse_two, second_grad * (1.0 + scale_two)
    )
    attended_grad = (gate_one * middle_grad).astype(jnp.bfloat16)
    gate_one_grad = jnp.sum(middle_grad * attended, axis=1)
    out_grad = jnp.einsum(
        "ire,ird->ed", attended_grad, mixed, preferred_element_type=jnp.float32
    ).astype(low_type)
    out_sum = lax.psum_scatter(after(out_grad, up_sum), "img", scatter_dimension=0, tiled=True)
    mixed_grad = jnp.einsum(
        "ire,ed->ird", after(attended_grad, out_grad), out_full, preferred_element_type=jnp.float32
    ).astype(jnp.bfloat16)
    attention_grads = [
        attention_backward(
            queries[i], keys_values[i], key_bias[i], mixed_parts[i], mixed_grad[i], log_total[i],
            features, 512,
        )
        for i in range(own)
    ]
    if split > 1:
        shared_grads = lax.psum_scatter(
            jnp.stack([pair[1] for pair in attention_grads]),
            "band",
            scatter_dimension=1,
            axis_index_groups=share_groups,
            tiled=True,
        )
        qkv_grad = jnp.concatenate(
            [jnp.stack([pair[0] for pair in attention_grads]), shared_grads], axis=-1
        )
    else:
        qkv_grad = jnp.stack(attention_grads)
    qkv_sums = jnp.sum(qkv_grad.astype(jnp.float32), axis=(0, 1))
    qkv_weight_grad = jnp.einsum(
        "ire,ird->ed", qkv_grad, first_in, preferred_element_type=jnp.float32
    ).astype(low_type)
    first_grad = jnp.einsum("ire,ed->ird", after(qkv_grad, qkv_weight_grad), qkv_full, preferred_element_type=jnp.float32)
    shift_one_grad = jnp.sum(first_grad, axis=1)
    scale_one_grad = jnp.sum(first_grad * normed_one, axis=1)
    input_grad_low = (
        middle_grad + normalize_back(normed_one, inverse_one, first_grad * (1.0 + scale_one))
    ).astype(low_type)
    mod_grad = jnp.stack(
        [
            shift_one_grad,
            scale_one_grad,
            gate_one_grad,
            shift_two_grad,
            scale_two_grad,
            gate_two_grad,
        ],
        axis=1,
    )
    row_sums = jnp.concatenate(
        [
            qkv_sums[:features][None],
            qkv_sums[2 * features :][None],
            jnp.sum(attended_grad.astype(jnp.float32), axis=(0, 1))[None],
            jnp.sum(pre_grad.astype(jnp.float32), axis=(0, 1)).reshape(4, features),
            jnp.sum(branch_grad.astype(jnp.float32), axis=(0, 1))[None],
        ],
        axis=0,
    )
    pieces = jnp.concatenate(
        [
            mod_grad.reshape(own, img_count, ada_columns)
            .transpose(1, 0, 2)
            .reshape(img_count, own * ada_columns),
            jnp.concatenate([jnp.sum(mod_grad, axis=0).reshape(6, features), row_sums], axis=0)
            .reshape(bias_rows, img_count, bias_columns)
            .transpose(1, 0, 2)
            .reshape(img_count, -1),
        ],
        axis=1,
    )
    sent = jnp.broadcast_to(pieces[:, None], (img_count, band_count, pieces.shape[1])).reshape(
        img_count * band_count, -1
    )
    got = lax.all_to_all(sent, ("img", "band"), split_axis=0, concat_axis=0, tiled=True)
    mod_columns = got[:, : own * ada_columns].reshape(-1, ada_columns)
    silu_terms = jnp.tile(
        silu_rows.astype(jnp.float32).reshape(img_count, 1, images, ada_rows), (1, split, 1, 1)
    ).reshape(img_count * band_count * own, ada_rows)
    ada_shard = jnp.einsum(
        "id,ie->de",
        silu_terms,
        mod_columns,
        precision=lax.Precision.HIGHEST,
    )
    bias_total = jnp.sum(got[:, own * ada_columns :], axis=0).reshape(bias_rows, bias_columns)
    if img_count == 8 and own == 1 and split == 1:
        wide_shard, tall_shard, input_grad_low = tail_exchange(
            qkv_weight_grad, out_sum, up_sum, down_sum, input_grad_low[0], band_count, img_count
        )
    else:
        qkv_sum = lax.psum_scatter(qkv_weight_grad, "img", scatter_dimension=0, tiled=True)
        tall_shard = lax.psum_scatter(down_sum, "band", scatter_dimension=1, tiled=True).astype(
            jnp.float32
        )
        wide_shard = lax.psum_scatter(
            jnp.concatenate([qkv_sum, out_sum, up_sum], axis=0).T,
            "band",
            scatter_dimension=0,
            tiled=True,
        ).astype(jnp.float32)
        input_grad_low = to_bands(input_grad_low)
    input_grad = input_grad_low.astype(jnp.float32)
    down_shard = tall_shard.T
    qkv_shard = wide_shard[:, :qkv_part]
    out_shard = wide_shard[:, qkv_part : qkv_part + out_part]
    up_shard = wide_shard[:, qkv_part + out_part :]
    shards = (ada_shard, qkv_shard, out_shard, up_shard, down_shard)
    squares = jnp.sum(bias_total * bias_total) / band_count
    for shard_grad in shards:
        squares = squares + jnp.sum(shard_grad * shard_grad)
    squares_total = sum_everywhere(squares)
    grad_norm = jnp.sqrt(squares_total)
    factor = clip_norm / jnp.maximum(grad_norm, clip_norm)
    ada_new, ada_first_new, ada_second_new = adam_update(
        ada_weight, ada_first, ada_second, shards[0], factor, learn_rate
    )
    qkv_new, qkv_first_new, qkv_second_new = adam_update(
        qkv_weight, qkv_first, qkv_second, shards[1], factor, learn_rate
    )
    out_new, out_first_new, out_second_new = adam_update(
        out_weight, out_first, out_second, shards[2], factor, out_rate
    )
    up_new, up_first_new, up_second_new = adam_update(
        up_weight, up_first, up_second, shards[3], factor, learn_rate
    )
    down_new, down_first_new, down_second_new = adam_update(
        down_weight, down_first, down_second, shards[4], factor, learn_rate
    )
    bias_new, bias_first_new, bias_second_new = adam_update(
        biases, bias_first, bias_second, bias_total, factor, bias_rate
    )
    branch_bias_grad = bias_total[13] * factor
    return (
        output,
        input_grad,
        grad_norm,
        ada_new,
        qkv_new,
        out_new,
        up_new,
        down_new,
        bias_new,
        ada_first_new,
        qkv_first_new,
        out_first_new,
        up_first_new,
        down_first_new,
        bias_first_new,
        ada_second_new,
        qkv_second_new,
        out_second_new,
        up_second_new,
        down_second_new,
        bias_second_new,
        branch_bias_grad,
    )


def solution(mesh):
    return jax.shard_map(
        body,
        mesh=mesh,
        in_specs=(
            P("img", "band", None),
            P("img", None),
            P("img"),
            P("img", "band", None),
            P("band", "img"),
            P("band", "img"),
            P("band", "img"),
            P("band", "img"),
            P("band", "img"),
            P(None, "img"),
            P("band", "img"),
            P("band", "img"),
            P("band", "img"),
            P("band", "img"),
            P("band", "img"),
            P(None, "img"),
            P("band", "img"),
            P("band", "img"),
            P("band", "img"),
            P("band", "img"),
            P("band", "img"),
            P(None, "img"),
        ),
        out_specs=(
            P("img", "band", None),
            P("img", "band", None),
            P(),
            P("band", "img"),
            P("band", "img"),
            P("band", "img"),
            P("band", "img"),
            P("band", "img"),
            P(None, "img"),
            P("band", "img"),
            P("band", "img"),
            P("band", "img"),
            P("band", "img"),
            P("band", "img"),
            P(None, "img"),
            P("band", "img"),
            P("band", "img"),
            P("band", "img"),
            P("band", "img"),
            P("band", "img"),
            P(None, "img"),
            P("img"),
        ),
        check_vma=False,
    )
```

```python
import functools

import jax
import jax.numpy as jnp
from jax import lax
from jax.experimental import pallas as pl
from jax.experimental.pallas import tpu as pltpu
from jax.sharding import PartitionSpec as P

HEADS = 16
HEAD_DIM = 72
L = 1024
STEP = 10


norm_eps = 1e-06
beta_one = 0.9
beta_two = 0.999
adam_eps = 1e-08
learn_rate = 0.03
out_rate = 0.25
bias_rate = 0.4
clip_norm = 1.0
very_low = -1000000000.0


def normalize_keep(values):
    centre = values - jnp.mean(values, axis=-1, keepdims=True)
    inverse = lax.rsqrt(jnp.mean(centre * centre, axis=-1, keepdims=True) + norm_eps)
    return (centre * inverse, inverse)


def normalize_back(normed, inverse, incoming):
    return inverse * (
        incoming
        - jnp.mean(incoming, axis=-1, keepdims=True)
        - normed * jnp.mean(incoming * normed, axis=-1, keepdims=True)
    )


def smooth_gate(values):
    return jax.nn.gelu(values, approximate=True)


def adam_update(weight, first_old, second_old, gradient, factor, rate):
    clipped = gradient * factor
    first_new = beta_one * first_old + (1.0 - beta_one) * clipped
    second_new = beta_two * second_old + (1.0 - beta_two) * clipped * clipped
    first_hat = first_new / (1.0 - beta_one**STEP)
    second_hat = second_new / (1.0 - beta_two**STEP)
    return (weight - rate * first_hat / (jnp.sqrt(second_hat) + adam_eps), first_new, second_new)


WINDOW = 256
CONTRACT_LAST = (((1,), (1,)), ((), ()))
LOG2_E = 1.4426950408889634


FORWARD_US, BACKWARD_US, START_US, TAIL_US = 37, 57, 115, 110


def expected(microseconds):
    moved = int(microseconds * 3.2e6)
    return pl.CostEstimate(flops=0, bytes_accessed=moved, transcendentals=0)


def head_window(head, features):
    start = head * HEAD_DIM
    base = pl.multiple_of(jnp.minimum(start // 128 * 128, features - WINDOW), 128)
    lane = lax.broadcasted_iota(jnp.int32, (1, WINDOW), 1)
    inside = (lane >= start - base) & (lane < start - base + HEAD_DIM)
    return base, inside


def attention_forward_kernel(
    query_ref, keyval_ref, bias_ref, mixed_ref, log_ref, scaled, value_t, mixed_t, *, features, shift, block
):
    length = keyval_ref.shape[0]
    rows = mixed_ref.shape[0]
    scaled[...] = (query_ref[:, :features].astype(jnp.float32) * (HEAD_DIM**-0.5 * LOG2_E)).astype(
        jnp.bfloat16
    )

    @pl.loop(0, features // 128)
    def _(tile):
        columns = pl.ds(pl.multiple_of(tile * 128, 128), 128)
        source = pl.ds(pl.multiple_of(shift + features + tile * 128, 128), 128)
        value_t[columns, :] = keyval_ref[:, source].astype(jnp.float32).T

    @pl.loop(0, HEADS)
    def _(head):
        base, inside = head_window(head, features)
        head_rows = pl.ds(pl.multiple_of(head * HEAD_DIM, 8), HEAD_DIM)
        query = scaled[:, pl.ds(base, WINDOW)]
        ones = jnp.ones((8, block), jnp.float32)
        top = None
        for at in range(0, length, block):
            key = keyval_ref[pl.ds(at, block), pl.ds(pl.multiple_of(base + shift, 128), WINDOW)]
            key = jnp.where(inside, key, jnp.zeros_like(key))
            scores = lax.dot_general(key, query, CONTRACT_LAST, preferred_element_type=jnp.float32)
            if at + block == length:
                scores = scores + bias_ref[pl.ds(at, block), :]
            block_top = jnp.max(scores, axis=0, keepdims=True)
            value = jnp.concatenate([value_t[head_rows, pl.ds(at, block)], ones], axis=0).astype(jnp.bfloat16)
            if top is None:
                top = block_top
                probs = jnp.exp2(scores - top).astype(jnp.bfloat16)
                total = jnp.dot(value, probs, preferred_element_type=jnp.float32)
            else:
                new_top = jnp.maximum(top, block_top)
                fade = jnp.exp2(top - new_top)
                top = new_top
                probs = jnp.exp2(scores - top).astype(jnp.bfloat16)
                total = total * fade + jnp.dot(value, probs, preferred_element_type=jnp.float32)
        weight = total[HEAD_DIM : HEAD_DIM + 1]
        mixed_t[head_rows, :] = total[:HEAD_DIM] * (1.0 / weight)
        log_ref[pl.ds(head, 1), :] = top + jnp.log2(weight)

    @pl.loop(0, features // 128)
    def _(tile):
        columns = pl.ds(pl.multiple_of(tile * 128, 128), 128)
        mixed_ref[:, columns] = mixed_t[columns, :].T.astype(jnp.bfloat16)


def attention_forward(query, keyval, key_bias, features, shift, block):
    rows, length = query.shape[0], keyval.shape[0]
    return pl.pallas_call(
        functools.partial(attention_forward_kernel, features=features, shift=shift, block=block),
        out_shape=(
            jax.ShapeDtypeStruct((rows, features), jnp.bfloat16),
            jax.ShapeDtypeStruct((HEADS, rows), jnp.float32),
        ),
        scratch_shapes=[
            pltpu.VMEM((rows, features), jnp.bfloat16),
            pltpu.VMEM((features, length), jnp.float32),
            pltpu.VMEM((features, rows), jnp.float32),
        ],
        cost_estimate=expected(FORWARD_US),
        compiler_params=pltpu.CompilerParams(vmem_limit_bytes=56 * 2**20),
    )(query, keyval, key_bias)


MESH = pl.DeviceIdType.MESH


def exchange_rows(rows_ref, back_ref, send, recv, local_sem, *, bands):
    band = lax.axis_index("band")
    block = back_ref.shape[1]
    barrier = pltpu.get_barrier_semaphore()
    for step in range(1, bands):
        pl.semaphore_signal(
            barrier, inc=1, device_id={"band": lax.rem(band + step, bands)}, device_id_type=MESH
        )
    pl.semaphore_wait(barrier, bands - 1)

    def span(owner):
        return rows_ref.at[pl.ds(pl.multiple_of(owner * block, 16), block), :]

    def sent(step):
        target = lax.rem(band + step, bands)
        return pltpu.make_async_remote_copy(
            src_ref=span(target), dst_ref=back_ref.at[band],
            send_sem=send.at[step], recv_sem=recv.at[step],
            device_id={"band": target}, device_id_type=MESH,
        )

    keep = pltpu.make_async_copy(span(band), back_ref.at[band], local_sem)
    keep.start()
    for step in range(1, bands):
        sent(step).start()

    def finish():
        keep.wait()
        for step in range(1, bands):
            sent(step).wait_send()
            source = lax.rem(band + bands - step, bands)
            pltpu.make_async_remote_copy(
                src_ref=back_ref.at[source], dst_ref=back_ref.at[source],
                send_sem=send.at[step], recv_sem=recv.at[step],
                device_id={"band": source}, device_id_type=MESH,
            ).wait_recv()

    return finish


def attention_backward_kernel(
    query_ref, keyval_ref, bias_ref, mixed_ref, grad_ref, log_ref, out_ref, keyval_grad_ref,
    scaled, key_t, wide_t, *, features, shift, out_shift, block
):
    length = keyval_ref.shape[0]
    rows = mixed_ref.shape[0]
    scale = HEAD_DIM**-0.5
    scaled[...] = (query_ref[:, :features].astype(jnp.float32) * (scale * LOG2_E)).astype(jnp.bfloat16)

    @pl.loop(0, features // 128)
    def _(tile):
        columns = pl.ds(pl.multiple_of(tile * 128, 128), 128)
        key_t[columns, :] = keyval_ref[:, pl.ds(pl.multiple_of(shift + tile * 128, 128), 128)].astype(jnp.float32).T
        wide_t[columns, :] = (
            mixed_ref[:, columns].astype(jnp.float32) * grad_ref[:, columns].astype(jnp.float32)
        ).T

    @pl.loop(0, HEADS)
    def _(head):
        base, inside = head_window(head, features)
        head_rows = pl.ds(pl.multiple_of(head * HEAD_DIM, 8), HEAD_DIM)
        window = pl.ds(base, WINDOW)
        delta = jnp.sum(wide_t[head_rows, :], axis=0, keepdims=True)
        log_total = log_ref[pl.ds(head, 1), :]
        query = query_ref[:, window]
        query_scaled = scaled[:, window]
        grad = grad_ref[:, window]
        query_grad = None
        for at in range(0, length, block):
            here = pl.ds(at, block)
            key_window = pl.ds(pl.multiple_of(base + shift, 128), WINDOW)
            value_window = pl.ds(pl.multiple_of(base + shift + features, 128), WINDOW)
            key = keyval_ref[here, key_window]
            value = keyval_ref[here, value_window]
            key = jnp.where(inside, key, jnp.zeros_like(key))
            value = jnp.where(inside, value, jnp.zeros_like(value))
            scores = lax.dot_general(key, query_scaled, CONTRACT_LAST, preferred_element_type=jnp.float32)
            if at + block == length:
                scores = scores + bias_ref[here, :]
            probs = jnp.exp2(scores - log_total)
            prob_grad = lax.dot_general(value, grad, CONTRACT_LAST, preferred_element_type=jnp.float32)
            score_grad = (probs * (prob_grad - delta)).astype(jnp.bfloat16)
            value_grad = jnp.dot(probs.astype(jnp.bfloat16), grad, preferred_element_type=jnp.float32)
            key_grad = jnp.dot(score_grad, query, preferred_element_type=jnp.float32) * scale
            key_out = pl.ds(pl.multiple_of(base + out_shift, 128), WINDOW)
            value_out = pl.ds(pl.multiple_of(base + out_shift + features, 128), WINDOW)
            keyval_grad_ref[here, key_out] = jnp.where(inside, key_grad.astype(jnp.bfloat16), keyval_grad_ref[here, key_out])
            keyval_grad_ref[here, value_out] = jnp.where(inside, value_grad.astype(jnp.bfloat16), keyval_grad_ref[here, value_out])
            part = jnp.dot(
                key_t[head_rows, here].astype(jnp.bfloat16), score_grad, preferred_element_type=jnp.float32
            )
            query_grad = part if query_grad is None else query_grad + part
        wide_t[head_rows, :] = query_grad * scale

    @pl.loop(0, features // 128)
    def _(tile):
        columns = pl.ds(pl.multiple_of(tile * 128, 128), 128)
        out_ref[:, columns] = wide_t[columns, :].T.astype(jnp.bfloat16)


def attention_backward(
    query, keyval, key_bias, mixed, grad, log_total, features, block, exchanged, known, bands
):
    rows, length = query.shape[0], keyval.shape[0]
    shared = exchanged is not None
    scratch = [
        pltpu.VMEM((rows, features), jnp.bfloat16),
        pltpu.VMEM((features, length), jnp.float32),
        pltpu.VMEM((features, rows), jnp.float32),
    ]
    params = pltpu.CompilerParams(vmem_limit_bytes=56 * 2**20)
    if shared:

        def shared_kernel(both_ref, bias_ref, mixed_ref, grad_ref, log_ref, rows_ref, known_ref, out_ref, back_ref, kept_ref, *held):
            kept_ref[...] = known_ref[...]
            finish = exchange_rows(rows_ref, back_ref, *held[3:], bands=bands)
            attention_backward_kernel(
                both_ref, both_ref, bias_ref, mixed_ref, grad_ref, log_ref, out_ref, out_ref, *held[:3],
                features=features, shift=features, out_shift=features, block=block,
            )
            finish()

        anywhere, vmem = pl.BlockSpec(memory_space=pl.ANY), pl.BlockSpec(memory_space=pltpu.VMEM)
        return pl.pallas_call(
            shared_kernel,
            out_shape=(
                jax.ShapeDtypeStruct((rows, 3 * features), jnp.bfloat16),
                jax.ShapeDtypeStruct((bands, rows // bands, features), jnp.bfloat16),
                jax.ShapeDtypeStruct(known.shape, jnp.float32),
            ),
            in_specs=[vmem] * 5 + [anywhere, vmem],
            out_specs=(vmem, anywhere, vmem),
            scratch_shapes=scratch
            + [
                pltpu.SemaphoreType.DMA((bands,)),
                pltpu.SemaphoreType.DMA((bands,)),
                pltpu.SemaphoreType.DMA(()),
            ],
            cost_estimate=expected(BACKWARD_US),
            compiler_params=pltpu.CompilerParams(
                collective_id=2, has_side_effects=True, vmem_limit_bytes=56 * 2**20
            ),
        )(query, key_bias, mixed, grad, log_total, exchanged, known)
    return pl.pallas_call(
        functools.partial(
            attention_backward_kernel, features=features, shift=0, out_shift=0, block=block
        ),
        out_shape=(
            jax.ShapeDtypeStruct((rows, features), jnp.bfloat16),
            jax.ShapeDtypeStruct((length, 2 * features), jnp.bfloat16),
        ),
        scratch_shapes=scratch,
        compiler_params=params,
    )(query, keyval, key_bias, mixed, grad, log_total)


def flip(index, bit):
    return index + bit - 2 * bit * lax.rem(lax.div(index, bit), 2)


def start_kernel(
    wide_ref, tall_ref, tokens_ref,
    qkv_ref, out_ref, up_ref, down_ref, rows_ref,
    held, turned, line_send, line_recv, row_send, row_recv, flat_send, flat_recv, local_sem,
    *, bands, qkv_part, out_part,
):
    img, band = lax.axis_index("img"), lax.axis_index("band")
    depth, width = wide_ref.shape
    tall_rows, tall_width = tall_ref.shape
    row_block = tokens_ref.shape[1]
    lanes = 128
    first = -(-(qkv_part + out_part) // lanes) * lanes
    beside_x, beside_y, sibling = flip(img, 2), flip(img, 4), flip(img, 1)
    across = flip(beside_x, 4)

    barrier = pltpu.get_barrier_semaphore()
    for other in (beside_x, beside_y, sibling):
        pl.semaphore_signal(barrier, inc=1, device_id={"img": other}, device_id_type=MESH)
    for step in range(1, bands):
        pl.semaphore_signal(
            barrier, inc=1, device_id={"band": lax.rem(band + step, bands)}, device_id_type=MESH
        )
    pl.semaphore_wait(barrier, 3 + bands - 1)

    def piece(part, owner):
        if part == 2:
            return down_ref.at[:, pl.ds(pl.multiple_of(owner * tall_width, lanes), tall_width)]
        span = pl.ds(0, first) if part == 0 else pl.ds(first, width - first)
        return held.at[pl.ds(pl.multiple_of(owner * depth, 16), depth), span]

    def line_copy(part, way, step, owner, toward):
        view = piece(part, owner)
        return pltpu.make_async_remote_copy(
            src_ref=view, dst_ref=view,
            send_sem=line_send.at[part, way, step], recv_sem=line_recv.at[part, way, step],
            device_id={"band": toward}, device_id_type=MESH,
        )

    def line_sends(part, step, act):
        for way, sign in ((0, 1), (1, -1)):
            owner, toward = band - sign * step, band + sign

            @pl.when((owner >= 0) & (owner < bands) & (toward >= 0) & (toward < bands))
            def _():
                act(line_copy(part, way, step, owner, toward))

    def line_arrivals(part, step):
        for way, sign in ((0, 1), (1, -1)):
            owner = band - sign * (step + 1)

            @pl.when((owner >= 0) & (owner < bands))
            def _():
                line_copy(part, way, step, owner, band - sign).wait_recv()

    def row_copy(step):
        target = lax.rem(band + step, bands)
        return pltpu.make_async_remote_copy(
            src_ref=tokens_ref.at[target],
            dst_ref=rows_ref.at[pl.ds(pl.multiple_of(band * row_block, 16), row_block), :],
            send_sem=row_send.at[step - 1], recv_sem=row_recv.at[step - 1],
            device_id={"band": target}, device_id_type=MESH,
        )

    def row_arrival(step):
        source = lax.rem(band + bands - step, bands)
        view = rows_ref.at[pl.ds(pl.multiple_of(source * row_block, 16), row_block), :]
        return pltpu.make_async_remote_copy(
            src_ref=view, dst_ref=view,
            send_sem=row_send.at[step - 1], recv_sem=row_recv.at[step - 1],
            device_id={"band": source}, device_id_type=MESH,
        )

    def qkv_rows(owner, start=0, count=qkv_part):
        return qkv_ref.at[pl.ds(pl.multiple_of(owner * qkv_part + start, 16), count), :]

    def out_rows(owner):
        return out_ref.at[pl.ds(pl.multiple_of(owner * out_part, 16), out_part), :]

    half = (qkv_part + out_part) // 2
    own_qkv, own_out = turned.at[pl.ds(0, qkv_part), :], turned.at[pl.ds(qkv_part, out_part), :]
    plan = [
        (own_qkv, qkv_rows(img), beside_x, qkv_rows(beside_x)),
        (own_out, out_rows(img), beside_x, out_rows(beside_x)),
        (own_qkv, qkv_rows(img), beside_y, qkv_rows(beside_y)),
        (own_out, out_rows(img), beside_y, out_rows(beside_y)),
        (own_qkv, qkv_rows(img), sibling, qkv_rows(sibling)),
        (own_out, out_rows(img), sibling, out_rows(sibling)),
    ]
    for owner, toward, whole in ((beside_x, beside_y, True), (beside_y, beside_x, False)):
        if whole:
            view = qkv_rows(owner, 0, half)
            plan.append((view, view, toward, qkv_rows(across, 0, half)))
        else:
            rest = qkv_part - half
            view = qkv_rows(owner, half, rest)
            plan.append((view, view, toward, qkv_rows(across, half, rest)))
            plan.append((out_rows(owner), out_rows(owner), toward, out_rows(across)))
    for owner in (beside_x, beside_y):
        plan.append((qkv_rows(owner), qkv_rows(owner), sibling, qkv_rows(flip(owner, 1))))
        plan.append((out_rows(owner), out_rows(owner), sibling, out_rows(flip(owner, 1))))
    far = flip(across, 1)
    plan.append((qkv_rows(across, 0, half), qkv_rows(across, 0, half), sibling, qkv_rows(far, 0, half)))
    rest = qkv_part - half
    plan.append((qkv_rows(across, half, rest), qkv_rows(across, half, rest), sibling, qkv_rows(far, half, rest)))
    plan.append((out_rows(across), out_rows(across), sibling, out_rows(far)))

    def flat_copy(at):
        source, target, toward, _ = plan[at]
        return pltpu.make_async_remote_copy(
            src_ref=source, dst_ref=target, send_sem=flat_send.at[at], recv_sem=flat_recv.at[at],
            device_id={"img": toward}, device_id_type=MESH,
        )

    def flat_arrival(at):
        landing = plan[at][3]
        pltpu.make_async_remote_copy(
            src_ref=landing, dst_ref=landing, send_sem=flat_send.at[at], recv_sem=flat_recv.at[at],
            device_id={"img": sibling}, device_id_type=MESH,
        ).wait_recv()

    def turn(tile):
        span = pl.ds(pl.multiple_of(tile * lanes, lanes), lanes)
        turned[span, :] = held[:, span].astype(jnp.float32).T.astype(jnp.bfloat16)

    start = lambda copy: copy.start()
    own_rows = pltpu.make_async_copy(
        tokens_ref.at[band],
        rows_ref.at[pl.ds(pl.multiple_of(band * row_block, 16), row_block), :],
        local_sem.at[0],
    )
    own_rows.start()
    held[pl.ds(pl.multiple_of(band * depth, 16), depth), :] = wide_ref[...]
    down_ref[:, pl.ds(pl.multiple_of(band * tall_width, lanes), tall_width)] = tall_ref[...]
    line_sends(0, 0, start)
    for step in range(bands - 1):
        line_arrivals(0, step)
        if step < bands - 2:
            line_sends(0, step + 1, start)
    line_sends(1, 0, start)
    line_sends(2, 0, start)
    for step in range(1, bands):
        row_copy(step).start()
    pl.loop(0, first // lanes)(turn)
    keep_qkv = pltpu.make_async_copy(own_qkv, qkv_rows(img), local_sem.at[1])
    keep_out = pltpu.make_async_copy(own_out, out_rows(img), local_sem.at[2])
    for at in range(6):
        flat_copy(at).start()
    keep_qkv.start()
    keep_out.start()
    for step in range(bands - 2):
        for part in (1, 2):
            line_arrivals(part, step)
            line_sends(part, step + 1, start)
    for arrived, sent in (((0, 1), (6, 9, 10)), ((2, 3), (7, 8, 11, 12))):
        for at in arrived:
            flat_arrival(at)
        for at in sent:
            flat_copy(at).start()
    for at in (6, 7, 8):
        flat_arrival(at)
        flat_copy(at + 7).start()
    for part in (1, 2):
        line_arrivals(part, bands - 2)
    pl.loop(first // lanes, width // lanes)(turn)
    up_ref[...] = turned[pl.ds(qkv_part + out_part, width - qkv_part - out_part), :]
    for part in range(3):
        for step in range(bands - 1):
            line_sends(part, step, lambda copy: copy.wait_send())
    for at in (4, 5, 9, 10, 11, 12, 13, 14, 15):
        flat_arrival(at)
    for at in range(16):
        flat_copy(at).wait_send()
    for step in range(1, bands):
        row_copy(step).wait_send()
        row_arrival(step).wait_recv()
    own_rows.wait()
    keep_qkv.wait()
    keep_out.wait()


def start_exchange(wide, tall, tokens, bands, imgs, qkv_part, out_part):
    depth, width = wide.shape
    up_part = width - qkv_part - out_part
    low = jnp.bfloat16
    anywhere, vmem = pl.BlockSpec(memory_space=pl.ANY), pl.BlockSpec(memory_space=pltpu.VMEM)
    features = depth * bands
    return pl.pallas_call(
        functools.partial(start_kernel, bands=bands, qkv_part=qkv_part, out_part=out_part),
        out_shape=(
            jax.ShapeDtypeStruct((qkv_part * imgs, features), low),
            jax.ShapeDtypeStruct((out_part * imgs, features), low),
            jax.ShapeDtypeStruct((up_part, features), low),
            jax.ShapeDtypeStruct((tall.shape[0], tall.shape[1] * bands), low),
            jax.ShapeDtypeStruct((tokens.shape[1] * bands, tokens.shape[2]), low),
        ),
        in_specs=[vmem, vmem, anywhere],
        out_specs=(anywhere, anywhere, vmem, vmem, anywhere),
        scratch_shapes=[
            pltpu.VMEM((features, width), low),
            pltpu.VMEM((width, features), low),
            pltpu.SemaphoreType.DMA((3, 2, bands - 1)),
            pltpu.SemaphoreType.DMA((3, 2, bands - 1)),
            pltpu.SemaphoreType.DMA((bands - 1,)),
            pltpu.SemaphoreType.DMA((bands - 1,)),
            pltpu.SemaphoreType.DMA((16,)),
            pltpu.SemaphoreType.DMA((16,)),
            pltpu.SemaphoreType.DMA((3,)),
        ],
        cost_estimate=expected(START_US),
        compiler_params=pltpu.CompilerParams(
            collective_id=0, has_side_effects=True, vmem_limit_bytes=40 * 2**20
        ),
    )(wide, tall, tokens)


def add_low(left, right):
    return (left.astype(jnp.float32) + right.astype(jnp.float32)).astype(jnp.bfloat16)


def tail_kernel(
    qkv_ref, out_ref, up_ref, rows_ref, pieces_ref, silu_ref, known_ref,
    wide_ref, back_ref, ada_ref, bias_ref, squares_ref,
    pieces, terms, square_flat, square_line, small_send, small_recv,
    own, from_core, first_x, first_y, last_x, last_y, turned, held, held_in,
    core_send, core_recv, flat_send, flat_recv, line_send, line_recv, row_send, row_recv, local_sem,
    *, imgs, bands,
):
    img, band = lax.axis_index("img"), lax.axis_index("band")
    qkv_part, out_part = qkv_ref.shape[0] // imgs, out_ref.shape[0] // imgs
    both = own.shape[1]
    depth, width = wide_ref.shape
    row_block = back_ref.shape[1]
    half = first_x.shape[1]
    lanes = 128
    beside_x, beside_y, sibling = flip(img, 2), flip(img, 4), flip(img, 1)
    chips = (img, beside_x, beside_y, flip(beside_x, 4))
    upper, lower = pl.ds(0, half), pl.ds(half, both - half)
    spans = (pl.ds(0, qkv_part), pl.ds(qkv_part, out_part))

    barrier = pltpu.get_barrier_semaphore()
    for step in range(1, imgs):
        other = lax.rem(img + step, imgs)
        pl.semaphore_signal(barrier, inc=1, device_id={"img": other}, device_id_type=MESH)
    for step in range(1, bands):
        pl.semaphore_signal(
            barrier, inc=1, device_id={"band": lax.rem(band + step, bands)}, device_id_type=MESH
        )
    pl.semaphore_wait(barrier, imgs + bands - 2)

    def grad_rows(kind, owner):
        source, count = ((qkv_ref, qkv_part), (out_ref, out_part))[kind]
        return source.at[pl.ds(pl.multiple_of(owner * count, 16), count), :]

    def core_copy(kind, at):
        return pltpu.make_async_remote_copy(
            src_ref=grad_rows(kind, flip(chips[at], 1)), dst_ref=from_core.at[at, spans[kind]],
            send_sem=core_send.at[kind, at], recv_sem=core_recv.at[kind, at],
            device_id={"img": sibling}, device_id_type=MESH,
        )

    def own_copy(kind, at):
        return pltpu.make_async_copy(
            grad_rows(kind, chips[at]), own.at[at, spans[kind]], local_sem.at[4 * kind + at]
        )

    plan = (
        (own.at[1, upper], first_x.at[0], beside_x),
        (own.at[3, upper], first_x.at[1], beside_x),
        (own.at[2, lower], first_y.at[0], beside_y),
        (own.at[3, lower], first_y.at[1], beside_y),
        (own.at[2, upper], last_y, beside_y),
        (own.at[1, lower], last_x, beside_x),
    )

    def flat_copy(at):
        source, target, toward = plan[at]
        return pltpu.make_async_remote_copy(
            src_ref=source, dst_ref=target, send_sem=flat_send.at[at], recv_sem=flat_recv.at[at],
            device_id={"img": toward}, device_id_type=MESH,
        )

    def row_span(owner):
        return pl.ds(pl.multiple_of(owner * row_block, 16), row_block)

    def row_copy(step):
        target = lax.rem(band + step, bands)
        return pltpu.make_async_remote_copy(
            src_ref=rows_ref.at[row_span(target), :], dst_ref=back_ref.at[band],
            send_sem=row_send.at[step - 1], recv_sem=row_recv.at[step - 1],
            device_id={"band": target}, device_id_type=MESH,
        )

    def row_arrival(step):
        source = lax.rem(band + bands - step, bands)
        return pltpu.make_async_remote_copy(
            src_ref=back_ref.at[source], dst_ref=back_ref.at[source],
            send_sem=row_send.at[step - 1], recv_sem=row_recv.at[step - 1],
            device_id={"band": source}, device_id_type=MESH,
        )

    first = -(-both // lanes) * lanes
    parts = (pl.ds(0, first), pl.ds(first, width - first))

    def piece(part, owner, way=None):
        down = pl.ds(pl.multiple_of(owner * depth, 16), depth)
        return held.at[down, parts[part]] if way is None else held_in.at[way, down, parts[part]]

    def line_copy(part, way, owner, toward):
        return pltpu.make_async_remote_copy(
            src_ref=piece(part, owner), dst_ref=piece(part, owner, way),
            send_sem=line_send.at[part, way, owner], recv_sem=line_recv.at[part, way, owner],
            device_id={"band": toward}, device_id_type=MESH,
        )

    def line_ends(part):
        for step in range(bands - 1):

            @pl.when(band == 0)
            def _():
                line_copy(part, 0, bands - 1 - step, band + 1).start()

            @pl.when(band == bands - 1)
            def _():
                line_copy(part, 1, step, band - 1).start()

    def line_round(part, step):
        for way, owner, sign in ((0, bands - 1 - step, 1), (1, step, -1)):

            @pl.when((sign * (owner - band) > 0) & (band > 0) & (band < bands - 1))
            def _():
                copy = line_copy(part, way, owner, band + sign)
                copy.wait_recv()
                mine = piece(part, owner)
                mine[...] = add_low(mine[...], piece(part, owner, way)[...])
                copy.start()

    def line_finish(part):
        span = parts[part]
        wide_ref[:, span] = piece(part, band)[...].astype(jnp.float32)
        for way, sign in ((0, 1), (1, -1)):

            @pl.when((band - sign >= 0) & (band - sign < bands))
            def _():
                line_copy(part, way, band, band - sign).wait_recv()
                wide_ref[:, span] += piece(part, band, way)[...].astype(jnp.float32)

    def line_sent(part):
        for way, sign in ((0, 1), (1, -1)):
            for owner in range(bands):

                @pl.when(sign * (owner - band) > 0)
                def _():
                    line_copy(part, way, owner, band + sign).wait_send()

    def turn(tile):
        span = pl.ds(pl.multiple_of(tile * lanes, lanes), lanes)
        held[:, span] = turned[span, :].astype(jnp.float32).T.astype(jnp.bfloat16)

    def small_copy(source, target, kind, step, axis, toward):
        return pltpu.make_async_remote_copy(
            src_ref=source, dst_ref=target,
            send_sem=small_send.at[kind, step], recv_sem=small_recv.at[kind, step],
            device_id={axis: toward}, device_id_type=MESH,
        )

    def piece_flat(step):
        other = lax.rem(img + step, imgs)
        return small_copy(pieces_ref.at[other], pieces.at[band, img], 0, step, "img", other)

    def piece_line(step):
        other = lax.rem(band + step, bands)
        return small_copy(pieces.at[band], pieces.at[band], 1, step, "band", other)

    def square_one(step):
        other = lax.rem(img + step, imgs)
        return small_copy(square_flat.at[img], square_flat.at[img], 2, step, "img", other)

    def square_two(step):
        other = lax.rem(band + step, bands)
        return small_copy(square_line.at[band], square_line.at[band], 3, step, "band", other)

    def arrival(view, kind, step, axis):
        me, count = (img, imgs) if axis == "img" else (band, bands)
        small_copy(view, view, kind, step, axis, lax.rem(me + count - step, count)).wait_recv()

    order = (3, 1, 2, 0)
    for step in range(1, imgs):
        piece_flat(step).start()
    keep_piece = pltpu.make_async_copy(pieces_ref.at[img], pieces.at[band, img], local_sem.at[9])
    keep_piece.start()
    for at in order:
        core_copy(0, at).start()
        core_copy(1, at).start()
    for at in order:
        own_copy(0, at).start()
        own_copy(1, at).start()
    keep = pltpu.make_async_copy(rows_ref.at[row_span(band), :], back_ref.at[band], local_sem.at[8])
    keep.start()
    turned[pl.ds(both, width - both), :] = up_ref[...]
    pl.loop(first // lanes, width // lanes)(turn)
    line_ends(1)
    keep_piece.wait()
    for step in range(1, imgs):
        arrival(pieces.at[band, lax.rem(img + imgs - step, imgs)], 0, step, "img")
    for step in range(1, bands):
        piece_line(step).start()
    for step in range(1, bands):
        row_copy(step).start()
    for at in order:
        for kind in range(2):
            own_copy(kind, at).wait()
            core_copy(kind, at).wait_recv()
        own[at] = add_low(own[at], from_core[at])
        for ready in {3: (1, 3), 1: (0,), 2: (2,), 0: ()}[at]:
            flat_copy(ready).start()
    flat_copy(1).wait_recv()
    own[2, upper] = add_low(own[2, upper], first_x[1])
    flat_copy(4).start()
    flat_copy(3).wait_recv()
    own[1, lower] = add_low(own[1, lower], first_y[1])
    flat_copy(5).start()
    line_round(1, 0)
    flat_copy(0).wait_recv()
    flat_copy(2).wait_recv()
    flat_copy(4).wait_recv()
    flat_copy(5).wait_recv()
    turned[upper, :] = (
        own[0, upper].astype(jnp.float32)
        + first_x[0].astype(jnp.float32)
        + last_y[...].astype(jnp.float32)
    ).astype(jnp.bfloat16)
    turned[lower, :] = (
        own[0, lower].astype(jnp.float32)
        + first_y[0].astype(jnp.float32)
        + last_x[...].astype(jnp.float32)
    ).astype(jnp.bfloat16)
    pl.loop(0, first // lanes)(turn)
    line_ends(0)
    for step in range(1, bands):
        arrival(pieces.at[lax.rem(band + bands - step, bands)], 1, step, "band")
    for image in range(imgs):
        for at in range(bands):
            terms[pl.ds(image * bands + at, 1), :] = pieces[at, image]
    columns = ada_ref.shape[1]
    ada = lax.dot_general(
        silu_ref[...], terms[:, pl.ds(0, columns)], (((1,), (0,)), ((), ())),
        precision=lax.Precision.HIGHEST, preferred_element_type=jnp.float32,
    )
    ada_ref[...] = ada
    bias_rows, bias_columns = bias_ref.shape
    bias = jnp.sum(terms[:, pl.ds(columns, bias_rows * bias_columns)], axis=0, keepdims=True)
    for at in range(bias_rows):
        bias_ref[pl.ds(at, 1), :] = bias[:, at * bias_columns : (at + 1) * bias_columns]
    squares = jnp.sum(ada * ada, axis=0, keepdims=True)
    squares = jnp.sum(squares, axis=1, keepdims=True)
    squares += jnp.sum(bias * bias, axis=1, keepdims=True) / bands
    for step in range(bands - 1):
        line_round(0, step)
        if step > 0:
            line_round(1, step)
    line_finish(1)
    line_finish(0)
    rows = jnp.sum(wide_ref[...] * wide_ref[...], axis=0, keepdims=True)
    squares += jnp.sum(rows, axis=1, keepdims=True) + known_ref[0:1, 0:1]
    square_flat[img] = jnp.broadcast_to(squares, square_flat.shape[1:])
    for step in range(1, imgs):
        square_one(step).start()
    for step in range(1, imgs):
        arrival(square_flat.at[lax.rem(img + imgs - step, imgs)], 2, step, "img")
    total = square_flat[0]
    for at in range(1, imgs):
        total += square_flat[at]
    square_line[band] = total
    for step in range(1, bands):
        square_two(step).start()
    for step in range(1, bands):
        arrival(square_line.at[lax.rem(band + bands - step, bands)], 3, step, "band")
    total = square_line[0]
    for at in range(1, bands):
        total += square_line[at]
    squares_ref[...] = total
    line_sent(0)
    line_sent(1)
    for step in range(1, imgs):
        piece_flat(step).wait_send()
        square_one(step).wait_send()
    for step in range(1, bands):
        piece_line(step).wait_send()
        square_two(step).wait_send()
    for at in range(4):
        core_copy(0, at).wait_send()
        core_copy(1, at).wait_send()
    for at in range(6):
        flat_copy(at).wait_send()
    for step in range(1, bands):
        row_copy(step).wait_send()
        row_arrival(step).wait_recv()
    keep.wait()


def tail_exchange(qkv_grad, out_grad, up_sum, rows, pieces, silu, known, bias_shape, bands, imgs):
    low = jnp.bfloat16
    features = qkv_grad.shape[1]
    both = (qkv_grad.shape[0] + out_grad.shape[0]) // imgs
    width = both + up_sum.shape[0]
    half = -(-both // 32) * 16
    ada_columns = pieces.shape[2] - bias_shape[0] * bias_shape[1]
    anywhere, vmem = pl.BlockSpec(memory_space=pl.ANY), pl.BlockSpec(memory_space=pltpu.VMEM)
    return pl.pallas_call(
        functools.partial(tail_kernel, imgs=imgs, bands=bands),
        out_shape=(
            jax.ShapeDtypeStruct((features // bands, width), jnp.float32),
            jax.ShapeDtypeStruct((bands, rows.shape[0] // bands, features), low),
            jax.ShapeDtypeStruct((silu.shape[0], ada_columns), jnp.float32),
            jax.ShapeDtypeStruct(bias_shape, jnp.float32),
            jax.ShapeDtypeStruct((8, 128), jnp.float32),
        ),
        in_specs=[anywhere, anywhere, vmem, anywhere, vmem, vmem, vmem],
        out_specs=(vmem, anywhere, vmem, vmem, vmem),
        scratch_shapes=[
            pltpu.VMEM((bands,) + pieces.shape, jnp.float32),
            pltpu.VMEM((bands * imgs, pieces.shape[2]), jnp.float32),
            pltpu.VMEM((imgs, 8, 128), jnp.float32),
            pltpu.VMEM((bands, 8, 128), jnp.float32),
            pltpu.SemaphoreType.DMA((4, imgs)),
            pltpu.SemaphoreType.DMA((4, imgs)),
            pltpu.VMEM((4, both, features), low),
            pltpu.VMEM((4, both, features), low),
            pltpu.VMEM((2, half, features), low),
            pltpu.VMEM((2, both - half, features), low),
            pltpu.VMEM((both - half, features), low),
            pltpu.VMEM((half, features), low),
            pltpu.VMEM((width, features), low),
            pltpu.VMEM((features, width), low),
            pltpu.VMEM((2, features, width), low),
            pltpu.SemaphoreType.DMA((2, 4)),
            pltpu.SemaphoreType.DMA((2, 4)),
            pltpu.SemaphoreType.DMA((6,)),
            pltpu.SemaphoreType.DMA((6,)),
            pltpu.SemaphoreType.DMA((2, 2, bands)),
            pltpu.SemaphoreType.DMA((2, 2, bands)),
            pltpu.SemaphoreType.DMA((bands - 1,)),
            pltpu.SemaphoreType.DMA((bands - 1,)),
            pltpu.SemaphoreType.DMA((10,)),
        ],
        cost_estimate=expected(TAIL_US),
        compiler_params=pltpu.CompilerParams(
            collective_id=1, has_side_effects=True, vmem_limit_bytes=50 * 2**20
        ),
    )(qkv_grad, out_grad, up_sum, rows, pieces, silu, known)


def adam_kernel(*refs):
    squares_ref, wide_ref, tall_ref, ada_ref, bias_ref = refs[:5]
    sources, results = refs[5:23], refs[23:]
    norm = jnp.sqrt(squares_ref[0:1, 0:1])
    factor = clip_norm / jnp.maximum(norm, clip_norm)
    qkv_part = sources[3].shape[1]
    both = qkv_part + sources[6].shape[1]
    rates = (learn_rate, learn_rate, out_rate, learn_rate, learn_rate, bias_rate)

    def update(which, rows, gradient):
        weight_ref, first_ref, second_ref = sources[3 * which : 3 * which + 3]
        new = adam_update(
            weight_ref[rows, :], first_ref[rows, :], second_ref[rows, :], gradient, factor, rates[which]
        )
        for into, value in zip(results[3 * which : 3 * which + 3], new):
            into[rows, :] = value

    depth = wide_ref.shape[0]
    block = next(rows for rows in (32, 16, 8) if depth % rows == 0)

    @pl.loop(0, depth // block)
    def _(step):
        rows = pl.ds(pl.multiple_of(step * block, block), block)
        update(0, rows, ada_ref[rows, :])
        update(1, rows, wide_ref[rows, :qkv_part])
        update(2, rows, wide_ref[rows, qkv_part:both])
        update(3, rows, wide_ref[rows, both:])

    tall_width = sources[12].shape[0]
    whole = tall_width // 128 * 128

    @pl.loop(0, tall_width // 128)
    def _(step):
        rows = pl.ds(pl.multiple_of(step * 128, 128), 128)
        update(4, rows, tall_ref[:, rows].T)

    if whole < tall_width:
        update(4, pl.ds(whole, tall_width - whole), tall_ref[:, whole:].T)
    update(5, slice(None), bias_ref[...])
    results[18][...] = bias_ref[pl.ds(13, 1), :] * factor


def adam_all(squares, wide, tall, ada, bias, groups):
    flat = [array for group in groups for array in group]
    return pl.pallas_call(
        adam_kernel,
        out_shape=[jax.ShapeDtypeStruct(array.shape, jnp.float32) for array in flat]
        + [jax.ShapeDtypeStruct((1, bias.shape[1]), jnp.float32)],
        compiler_params=pltpu.CompilerParams(vmem_limit_bytes=50 * 2**20),
    )(squares, wide, tall, ada, bias, *flat)


def body(
    inputs,
    condition,
    valid_rows,
    cotangent,
    ada_weight,
    qkv_weight,
    out_weight,
    up_weight,
    down_weight,
    biases,
    ada_first,
    qkv_first,
    out_first,
    up_first,
    down_first,
    bias_first,
    ada_second,
    qkv_second,
    out_second,
    up_second,
    down_second,
    bias_second,
):
    images, local_rows, features = inputs.shape
    length = L
    head_count = HEADS
    head_size = HEAD_DIM
    score_scale = head_size ** (-0.5)
    band_count = lax.axis_size("band")
    img_count = lax.axis_size("img")
    band_rank = lax.axis_index("band")
    img_rank = lax.axis_index("img")
    own = max(1, images // band_count)
    split = max(1, band_count // images)
    mates = band_count // split
    image_rows = length // split
    exchange_groups = None
    share_groups = None
    if split > 1:
        exchange_groups = [[g * mates + m for m in range(mates)] for g in range(split)]
        share_groups = [[g * mates + m for g in range(split)] for m in range(mates)]
    low_type = jnp.bfloat16

    def to_images(rows):
        return lax.all_to_all(rows, "band", split_axis=0, concat_axis=1, axis_index_groups=exchange_groups, tiled=True)

    def to_bands(whole):
        cut = whole.reshape(own, mates, local_rows, features).transpose(1, 0, 2, 3)
        back = lax.all_to_all(
            cut, "band", split_axis=0, concat_axis=0, axis_index_groups=exchange_groups, tiled=True
        )
        return back.reshape(images, local_rows, features)

    def after(value, *earlier):
        return lax.optimization_barrier((value,) + earlier)[0]

    def sum_everywhere(partial):
        sent = jnp.broadcast_to(partial, (img_count * band_count, 128))
        got = lax.all_to_all(sent, ("img", "band"), split_axis=0, concat_axis=0, tiled=True)
        return jnp.sum(got[:, 0])

    qkv_part, out_part = qkv_weight.shape[1], out_weight.shape[1]

    bias_rows, bias_columns = biases.shape
    small = lax.all_gather(
        jnp.concatenate([condition.reshape(1, -1), biases.astype(low_type).reshape(1, -1)], axis=1),
        "img",
        axis=0,
        tiled=True,
    )
    condition_all = small[:, : images * features].reshape(img_count * images, features)
    bias_vals = (
        small[:, images * features :]
        .astype(jnp.float32)
        .reshape(img_count, bias_rows, bias_columns)
        .transpose(1, 0, 2)
        .reshape(bias_rows, features)
    )
    wide = jnp.concatenate([qkv_weight, out_weight, up_weight], axis=1).astype(low_type)
    tall = down_weight.T.astype(low_type)
    if img_count == 8 and own == 1 and split == 1:
        qkv_full, out_full, up_rows, down_rows, tokens_low = start_exchange(
            wide, tall, inputs, band_count, img_count, qkv_part, out_part
        )
        tokens_low = tokens_low.reshape(own, image_rows, features)
    else:
        turned = lax.all_gather(wide, "band", axis=0, tiled=True).T
        qkv_full = lax.all_gather(turned[:qkv_part], "img", axis=0, tiled=True)
        out_full = lax.all_gather(
            turned[qkv_part : qkv_part + out_part], "img", axis=0, tiled=True
        )
        up_rows = turned[qkv_part + out_part :]
        down_rows = lax.all_gather(tall, "band", axis=1, tiled=True)
        tokens_low = to_images(inputs)
    up_full = lax.all_gather(up_rows, "img", axis=0, tiled=True)
    down_full = lax.all_gather(after(down_rows, up_rows), "img", axis=0, tiled=True)

    silu_all = jax.nn.silu(condition_all.astype(jnp.float32)).astype(low_type)
    ada_rows = ada_weight.shape[0]
    silu_rows = lax.dynamic_slice_in_dim(silu_all, band_rank * ada_rows, ada_rows, axis=1)
    mod_partial = jnp.dot(
        silu_rows, ada_weight.astype(low_type), preferred_element_type=jnp.float32
    )
    ada_columns = mod_partial.shape[1]
    mod_sent = jnp.tile(
        mod_partial.reshape(img_count, 1, images * ada_columns), (1, split, 1)
    )
    mod_pieces = lax.all_to_all(
        mod_sent.reshape(img_count * band_count, own * ada_columns),
        ("img", "band"),
        split_axis=0,
        concat_axis=0,
        tiled=True,
    ).reshape(img_count, band_count, own, ada_columns)
    modulation = (
        jnp.sum(mod_pieces, axis=1).transpose(1, 0, 2).reshape(own, img_count * ada_columns)
        + bias_vals[0:6].reshape(-1)
    )
    mod_parts = modulation.reshape(own, 6, 1, features)
    shift_one = mod_parts[:, 0]
    scale_one = mod_parts[:, 1]
    gate_one = mod_parts[:, 2]
    shift_two = mod_parts[:, 3]
    scale_two = mod_parts[:, 4]
    gate_two = mod_parts[:, 5]
    valid_own = lax.dynamic_slice_in_dim(valid_rows, lax.rem(band_rank, mates) * own, own, axis=0)
    key_mask = jnp.arange(length, dtype=jnp.int32)[None, :] < valid_own[:, None]
    positions = lax.div(band_rank, mates) * image_rows + jnp.arange(image_rows, dtype=jnp.int32)
    row_mask = (positions[None, :] < valid_own[:, None]).astype(jnp.float32)[:, :, None]
    tokens_in = tokens_low.astype(jnp.float32)
    normed_one, inverse_one = normalize_keep(tokens_in)
    first_in = (normed_one * (1.0 + scale_one) + shift_one).astype(jnp.bfloat16)
    cotangent_low = to_images(after(cotangent, tokens_low))
    grad_out = cotangent_low.astype(jnp.float32) * row_mask
    qkv_bias = jnp.concatenate([bias_vals[6], jnp.zeros((features,), jnp.float32), bias_vals[7]])
    projected = (
        jnp.einsum("ird,ed->ire", first_in, qkv_full, preferred_element_type=jnp.float32) + qkv_bias
    ).astype(jnp.bfloat16)
    key_bias = jnp.where(key_mask, 0.0, very_low).astype(jnp.float32)[:, :, None]
    queries = [projected[i] for i in range(own)]
    if split > 1:
        keys_values = lax.all_gather(
            projected[..., features:], "band", axis=1, axis_index_groups=share_groups, tiled=True
        )
        keys_values = [keys_values[i] for i in range(own)]
        key_shift = 0
    else:
        keys_values = queries
        key_shift = features
    mixed, log_total = zip(
        *[
            attention_forward(queries[i], keys_values[i], key_bias[i], features, key_shift, 512)
            for i in range(own)
        ]
    )
    mixed_parts = mixed
    mixed = jnp.stack(mixed)
    attended = (
        jnp.einsum("ird,ed->ire", mixed, out_full, preferred_element_type=jnp.float32)
        + bias_vals[8]
    )
    middle = tokens_in + gate_one * attended
    normed_two, inverse_two = normalize_keep(middle)
    second_in = (normed_two * (1.0 + scale_two) + shift_two).astype(jnp.bfloat16)
    hidden_pre = jnp.einsum(
        "ird,fd->irf", second_in, up_full, preferred_element_type=jnp.float32
    ) + bias_vals[9:13].reshape(-1)
    hidden, gelu_back = jax.vjp(smooth_gate, hidden_pre)
    hidden_low = hidden.astype(jnp.bfloat16)
    branch = (
        jnp.einsum("irf,df->ird", hidden_low, down_full, preferred_element_type=jnp.float32)
        + bias_vals[13]
    )
    output_low = (middle + gate_two * branch).astype(jnp.bfloat16)
    branch_grad = (gate_two * grad_out).astype(jnp.bfloat16)
    gate_two_grad = jnp.sum(grad_out * branch, axis=1)
    down_grad = jnp.einsum(
        "ird,irf->df", branch_grad, hidden_low, preferred_element_type=jnp.float32
    ).astype(low_type)
    down_sum = lax.psum_scatter(down_grad, "img", scatter_dimension=0, tiled=True)
    hidden_grad = jnp.einsum(
        "ird,df->irf",
        after(branch_grad, down_grad),
        down_full,
        preferred_element_type=jnp.float32,
    )
    pre_grad = gelu_back(hidden_grad)[0].astype(jnp.bfloat16)
    up_grad = jnp.einsum(
        "irf,ird->fd", pre_grad, second_in, preferred_element_type=jnp.float32
    ).astype(low_type)
    up_sum = lax.psum_scatter(up_grad, "img", scatter_dimension=0, tiled=True)
    second_grad = jnp.einsum("irf,fd->ird", after(pre_grad, up_grad), up_full, preferred_element_type=jnp.float32)
    shift_two_grad = jnp.sum(second_grad, axis=1)
    scale_two_grad = jnp.sum(second_grad * normed_two, axis=1)
    middle_grad = grad_out + normalize_back(
        normed_two, inverse_two, second_grad * (1.0 + scale_two)
    )
    attended_grad = (gate_one * middle_grad).astype(jnp.bfloat16)
    gate_one_grad = jnp.sum(middle_grad * attended, axis=1)
    out_grad = jnp.einsum(
        "ire,ird->ed", attended_grad, mixed, preferred_element_type=jnp.float32
    ).astype(low_type)
    mixed_grad = jnp.einsum(
        "ire,ed->ird", after(attended_grad, out_grad), out_full, preferred_element_type=jnp.float32
    ).astype(jnp.bfloat16)
    tall_cut = down_sum.reshape(down_sum.shape[0], band_count, -1).transpose(1, 0, 2)
    tall_shard = jnp.sum(
        lax.all_to_all(tall_cut, "band", split_axis=0, concat_axis=0, tiled=True).astype(jnp.float32),
        axis=0,
    )
    hosted = img_count == 8 and own == 1 and split == 1
    tall_squares = jnp.broadcast_to(jnp.sum(tall_shard * tall_shard), (8, 128))
    attention_grads = [
        attention_backward(
            queries[i], keys_values[i], key_bias[i], mixed_parts[i], mixed_grad[i], log_total[i],
            features, 512, output_low[i] if hosted else None, tall_squares, band_count,
        )
        for i in range(own)
    ]
    if hosted:
        output, tall_squares = attention_grads[0][1:]
    else:
        output = to_bands(output_low)
    if split > 1:
        shared_grads = lax.psum_scatter(
            jnp.stack([pair[1] for pair in attention_grads]),
            "band",
            scatter_dimension=1,
            axis_index_groups=share_groups,
            tiled=True,
        )
        qkv_grad = jnp.concatenate(
            [jnp.stack([pair[0] for pair in attention_grads]), shared_grads], axis=-1
        )
    elif hosted:
        qkv_grad = attention_grads[0][0][None]
    else:
        qkv_grad = jnp.stack([jnp.concatenate(pair, axis=-1) for pair in attention_grads])
    qkv_sums = jnp.sum(qkv_grad.astype(jnp.float32), axis=(0, 1))
    qkv_weight_grad = jnp.einsum(
        "ire,ird->ed", qkv_grad, first_in, preferred_element_type=jnp.float32
    ).astype(low_type)
    first_grad = jnp.einsum("ire,ed->ird", after(qkv_grad, qkv_weight_grad), qkv_full, preferred_element_type=jnp.float32)
    shift_one_grad = jnp.sum(first_grad, axis=1)
    scale_one_grad = jnp.sum(first_grad * normed_one, axis=1)
    input_grad_low = (
        middle_grad + normalize_back(normed_one, inverse_one, first_grad * (1.0 + scale_one))
    ).astype(low_type)
    mod_grad = jnp.stack(
        [
            shift_one_grad,
            scale_one_grad,
            gate_one_grad,
            shift_two_grad,
            scale_two_grad,
            gate_two_grad,
        ],
        axis=1,
    )
    row_sums = jnp.concatenate(
        [
            qkv_sums[:features][None],
            qkv_sums[2 * features :][None],
            jnp.sum(attended_grad.astype(jnp.float32), axis=(0, 1))[None],
            jnp.sum(pre_grad.astype(jnp.float32), axis=(0, 1)).reshape(4, features),
            jnp.sum(branch_grad.astype(jnp.float32), axis=(0, 1))[None],
        ],
        axis=0,
    )
    pieces = jnp.concatenate(
        [
            mod_grad.reshape(own, img_count, ada_columns)
            .transpose(1, 0, 2)
            .reshape(img_count, own * ada_columns),
            jnp.concatenate([jnp.sum(mod_grad, axis=0).reshape(6, features), row_sums], axis=0)
            .reshape(bias_rows, img_count, bias_columns)
            .transpose(1, 0, 2)
            .reshape(img_count, -1),
        ],
        axis=1,
    )
    silu_terms = jnp.tile(
        silu_rows.astype(jnp.float32).reshape(img_count, 1, images, ada_rows), (1, split, 1, 1)
    ).reshape(img_count * band_count * own, ada_rows)
    if img_count == 8 and own == 1 and split == 1:
        wide_shard, input_grad_low, ada_shard, bias_total, squares_total = tail_exchange(
            qkv_weight_grad,
            out_grad,
            up_sum,
            input_grad_low[0],
            pieces[:, None],
            silu_terms.T,
            tall_squares,
            biases.shape,
            band_count,
            img_count,
        )
    else:
        sent = jnp.broadcast_to(
            pieces[:, None], (img_count, band_count, pieces.shape[1])
        ).reshape(img_count * band_count, -1)
        got = lax.all_to_all(sent, ("img", "band"), split_axis=0, concat_axis=0, tiled=True)
        ada_shard = jnp.einsum(
            "id,ie->de",
            silu_terms,
            got[:, : own * ada_columns].reshape(-1, ada_columns),
            precision=lax.Precision.HIGHEST,
        )
        bias_total = jnp.sum(got[:, own * ada_columns :], axis=0).reshape(bias_rows, bias_columns)
        qkv_sum = lax.psum_scatter(qkv_weight_grad, "img", scatter_dimension=0, tiled=True)
        out_sum = lax.psum_scatter(out_grad, "img", scatter_dimension=0, tiled=True)
        wide_shard = lax.psum_scatter(
            jnp.concatenate([qkv_sum, out_sum, up_sum], axis=0).T,
            "band",
            scatter_dimension=0,
            tiled=True,
        ).astype(jnp.float32)
        input_grad_low = to_bands(input_grad_low)
        squares = tall_squares[0, 0] + jnp.sum(bias_total * bias_total) / band_count
        for shard_grad in (ada_shard, wide_shard):
            squares = squares + jnp.sum(shard_grad * shard_grad)
        squares_total = jnp.broadcast_to(sum_everywhere(squares), (8, 128))
    input_grad = input_grad_low.astype(jnp.float32)
    grad_norm = jnp.sqrt(squares_total[0, 0])
    groups = (
        (ada_weight, ada_first, ada_second),
        (qkv_weight, qkv_first, qkv_second),
        (out_weight, out_first, out_second),
        (up_weight, up_first, up_second),
        (down_weight, down_first, down_second),
        (biases, bias_first, bias_second),
    )
    updated = adam_all(squares_total, wide_shard, tall_shard, ada_shard, bias_total, groups)
    ada_new, ada_first_new, ada_second_new = updated[0:3]
    qkv_new, qkv_first_new, qkv_second_new = updated[3:6]
    out_new, out_first_new, out_second_new = updated[6:9]
    up_new, up_first_new, up_second_new = updated[9:12]
    down_new, down_first_new, down_second_new = updated[12:15]
    bias_new, bias_first_new, bias_second_new = updated[15:18]
    branch_bias_grad = updated[18][0]
    return (
        output,
        input_grad,
        grad_norm,
        ada_new,
        qkv_new,
        out_new,
        up_new,
        down_new,
        bias_new,
        ada_first_new,
        qkv_first_new,
        out_first_new,
        up_first_new,
        down_first_new,
        bias_first_new,
        ada_second_new,
        qkv_second_new,
        out_second_new,
        up_second_new,
        down_second_new,
        bias_second_new,
        branch_bias_grad,
    )


def solution(mesh):
    return jax.shard_map(
        body,
        mesh=mesh,
        in_specs=(
            P("img", "band", None),
            P("img", None),
            P("img"),
            P("img", "band", None),
            P("band", "img"),
            P("band", "img"),
            P("band", "img"),
            P("band", "img"),
            P("band", "img"),
            P(None, "img"),
            P("band", "img"),
            P("band", "img"),
            P("band", "img"),
            P("band", "img"),
            P("band", "img"),
            P(None, "img"),
            P("band", "img"),
            P("band", "img"),
            P("band", "img"),
            P("band", "img"),
            P("band", "img"),
            P(None, "img"),
        ),
        out_specs=(
            P("img", "band", None),
            P("img", "band", None),
            P(),
            P("band", "img"),
            P("band", "img"),
            P("band", "img"),
            P("band", "img"),
            P("band", "img"),
            P(None, "img"),
            P("band", "img"),
            P("band", "img"),
            P("band", "img"),
            P("band", "img"),
            P("band", "img"),
            P(None, "img"),
            P("band", "img"),
            P("band", "img"),
            P("band", "img"),
            P("band", "img"),
            P("band", "img"),
            P(None, "img"),
            P("img"),
        ),
        check_vma=False,
    )
```

```python
import functools

import jax
import jax.numpy as jnp
from jax import lax
from jax.experimental import pallas as pl
from jax.experimental.pallas import tpu as pltpu
from jax.sharding import PartitionSpec as P

HEADS = 16
HEAD_DIM = 72
L = 1024
STEP = 10


norm_eps = 1e-06
beta_one = 0.9
beta_two = 0.999
adam_eps = 1e-08
learn_rate = 0.03
out_rate = 0.25
bias_rate = 0.4
clip_norm = 1.0
very_low = -1000000000.0


def normalize_keep(values):
    centre = values - jnp.mean(values, axis=-1, keepdims=True)
    inverse = lax.rsqrt(jnp.mean(centre * centre, axis=-1, keepdims=True) + norm_eps)
    return (centre * inverse, inverse)


def normalize_back(normed, inverse, incoming):
    return inverse * (
        incoming
        - jnp.mean(incoming, axis=-1, keepdims=True)
        - normed * jnp.mean(incoming * normed, axis=-1, keepdims=True)
    )


def smooth_gate(values):
    return jax.nn.gelu(values, approximate=True)


def adam_update(weight, first_old, second_old, gradient, factor, rate):
    clipped = gradient * factor
    first_new = beta_one * first_old + (1.0 - beta_one) * clipped
    second_new = beta_two * second_old + (1.0 - beta_two) * clipped * clipped
    first_hat = first_new / (1.0 - beta_one**STEP)
    second_hat = second_new / (1.0 - beta_two**STEP)
    return (weight - rate * first_hat / (jnp.sqrt(second_hat) + adam_eps), first_new, second_new)


WINDOW = 256
CONTRACT_LAST = (((1,), (1,)), ((), ()))
LOG2_E = 1.4426950408889634


FORWARD_US, BACKWARD_US, START_US, TAIL_US = 37, 57, 115, 110


def expected(microseconds):
    moved = int(microseconds * 3.2e6)
    return pl.CostEstimate(flops=0, bytes_accessed=moved, transcendentals=0)


def head_window(head, features):
    start = head * HEAD_DIM
    base = pl.multiple_of(jnp.minimum(start // 128 * 128, features - WINDOW), 128)
    lane = lax.broadcasted_iota(jnp.int32, (1, WINDOW), 1)
    inside = (lane >= start - base) & (lane < start - base + HEAD_DIM)
    return base, inside


def attention_forward_kernel(
    query_ref, keyval_ref, bias_ref, mixed_ref, log_ref, scaled, value_t, mixed_t, *, features, shift, block
):
    length = keyval_ref.shape[0]
    rows = mixed_ref.shape[0]
    scaled[...] = (query_ref[:, :features].astype(jnp.float32) * (HEAD_DIM**-0.5 * LOG2_E)).astype(
        jnp.bfloat16
    )

    @pl.loop(0, features // 128)
    def _(tile):
        columns = pl.ds(pl.multiple_of(tile * 128, 128), 128)
        source = pl.ds(pl.multiple_of(shift + features + tile * 128, 128), 128)
        value_t[columns, :] = keyval_ref[:, source].astype(jnp.float32).T

    @pl.loop(0, HEADS)
    def _(head):
        base, inside = head_window(head, features)
        head_rows = pl.ds(pl.multiple_of(head * HEAD_DIM, 8), HEAD_DIM)
        query = scaled[:, pl.ds(base, WINDOW)]
        ones = jnp.ones((8, block), jnp.float32)
        top = None
        for at in range(0, length, block):
            key = keyval_ref[pl.ds(at, block), pl.ds(pl.multiple_of(base + shift, 128), WINDOW)]
            key = jnp.where(inside, key, jnp.zeros_like(key))
            scores = lax.dot_general(key, query, CONTRACT_LAST, preferred_element_type=jnp.float32)
            if at + block == length:
                scores = scores + bias_ref[pl.ds(at, block), :]
            block_top = jnp.max(scores, axis=0, keepdims=True)
            value = jnp.concatenate([value_t[head_rows, pl.ds(at, block)], ones], axis=0).astype(jnp.bfloat16)
            if top is None:
                top = block_top
                probs = jnp.exp2(scores - top).astype(jnp.bfloat16)
                total = jnp.dot(value, probs, preferred_element_type=jnp.float32)
            else:
                new_top = jnp.maximum(top, block_top)
                fade = jnp.exp2(top - new_top)
                top = new_top
                probs = jnp.exp2(scores - top).astype(jnp.bfloat16)
                total = total * fade + jnp.dot(value, probs, preferred_element_type=jnp.float32)
        weight = total[HEAD_DIM : HEAD_DIM + 1]
        mixed_t[head_rows, :] = total[:HEAD_DIM] * (1.0 / weight)
        log_ref[pl.ds(head, 1), :] = top + jnp.log2(weight)

    @pl.loop(0, features // 128)
    def _(tile):
        columns = pl.ds(pl.multiple_of(tile * 128, 128), 128)
        mixed_ref[:, columns] = mixed_t[columns, :].T.astype(jnp.bfloat16)


def attention_forward(query, keyval, key_bias, features, shift, block):
    rows, length = query.shape[0], keyval.shape[0]
    return pl.pallas_call(
        functools.partial(attention_forward_kernel, features=features, shift=shift, block=block),
        out_shape=(
            jax.ShapeDtypeStruct((rows, features), jnp.bfloat16),
            jax.ShapeDtypeStruct((HEADS, rows), jnp.float32),
        ),
        scratch_shapes=[
            pltpu.VMEM((rows, features), jnp.bfloat16),
            pltpu.VMEM((features, length), jnp.float32),
            pltpu.VMEM((features, rows), jnp.float32),
        ],
        cost_estimate=expected(FORWARD_US),
        compiler_params=pltpu.CompilerParams(vmem_limit_bytes=56 * 2**20),
    )(query, keyval, key_bias)


MESH = pl.DeviceIdType.MESH


def exchange_rows(rows_ref, back_ref, send, recv, local_sem, *, bands):
    band = lax.axis_index("band")
    block = back_ref.shape[1]
    barrier = pltpu.get_barrier_semaphore()
    for step in range(1, bands):
        pl.semaphore_signal(
            barrier, inc=1, device_id={"band": lax.rem(band + step, bands)}, device_id_type=MESH
        )
    pl.semaphore_wait(barrier, bands - 1)

    def span(owner):
        return rows_ref.at[pl.ds(pl.multiple_of(owner * block, 16), block), :]

    def sent(step):
        target = lax.rem(band + step, bands)
        return pltpu.make_async_remote_copy(
            src_ref=span(target), dst_ref=back_ref.at[band],
            send_sem=send.at[step], recv_sem=recv.at[step],
            device_id={"band": target}, device_id_type=MESH,
        )

    keep = pltpu.make_async_copy(span(band), back_ref.at[band], local_sem)
    keep.start()
    for step in range(1, bands):
        sent(step).start()

    def finish():
        keep.wait()
        for step in range(1, bands):
            sent(step).wait_send()
            source = lax.rem(band + bands - step, bands)
            pltpu.make_async_remote_copy(
                src_ref=back_ref.at[source], dst_ref=back_ref.at[source],
                send_sem=send.at[step], recv_sem=recv.at[step],
                device_id={"band": source}, device_id_type=MESH,
            ).wait_recv()

    return finish


def attention_backward_kernel(
    query_ref, keyval_ref, bias_ref, mixed_ref, grad_ref, log_ref, out_ref, keyval_grad_ref,
    scaled, key_t, wide_t, *, features, shift, out_shift, block
):
    length = keyval_ref.shape[0]
    rows = mixed_ref.shape[0]
    scale = HEAD_DIM**-0.5
    scaled[...] = (query_ref[:, :features].astype(jnp.float32) * (scale * LOG2_E)).astype(jnp.bfloat16)

    @pl.loop(0, features // 128)
    def _(tile):
        columns = pl.ds(pl.multiple_of(tile * 128, 128), 128)
        key_t[columns, :] = keyval_ref[:, pl.ds(pl.multiple_of(shift + tile * 128, 128), 128)].astype(jnp.float32).T
        wide_t[columns, :] = (
            mixed_ref[:, columns].astype(jnp.float32) * grad_ref[:, columns].astype(jnp.float32)
        ).T

    @pl.loop(0, HEADS)
    def _(head):
        base, inside = head_window(head, features)
        head_rows = pl.ds(pl.multiple_of(head * HEAD_DIM, 8), HEAD_DIM)
        window = pl.ds(base, WINDOW)
        delta = jnp.sum(wide_t[head_rows, :], axis=0, keepdims=True)
        log_total = log_ref[pl.ds(head, 1), :]
        query = query_ref[:, window]
        query_scaled = scaled[:, window]
        grad = grad_ref[:, window]
        query_grad = None
        for at in range(0, length, block):
            here = pl.ds(at, block)
            key_window = pl.ds(pl.multiple_of(base + shift, 128), WINDOW)
            value_window = pl.ds(pl.multiple_of(base + shift + features, 128), WINDOW)
            key = keyval_ref[here, key_window]
            value = keyval_ref[here, value_window]
            key = jnp.where(inside, key, jnp.zeros_like(key))
            value = jnp.where(inside, value, jnp.zeros_like(value))
            scores = lax.dot_general(key, query_scaled, CONTRACT_LAST, preferred_element_type=jnp.float32)
            if at + block == length:
                scores = scores + bias_ref[here, :]
            probs = jnp.exp2(scores - log_total)
            prob_grad = lax.dot_general(value, grad, CONTRACT_LAST, preferred_element_type=jnp.float32)
            score_grad = (probs * (prob_grad - delta)).astype(jnp.bfloat16)
            value_grad = jnp.dot(probs.astype(jnp.bfloat16), grad, preferred_element_type=jnp.float32)
            key_grad = jnp.dot(score_grad, query, preferred_element_type=jnp.float32) * scale
            key_out = pl.ds(pl.multiple_of(base + out_shift, 128), WINDOW)
            value_out = pl.ds(pl.multiple_of(base + out_shift + features, 128), WINDOW)
            keyval_grad_ref[here, key_out] = jnp.where(inside, key_grad.astype(jnp.bfloat16), keyval_grad_ref[here, key_out])
            keyval_grad_ref[here, value_out] = jnp.where(inside, value_grad.astype(jnp.bfloat16), keyval_grad_ref[here, value_out])
            part = jnp.dot(
                key_t[head_rows, here].astype(jnp.bfloat16), score_grad, preferred_element_type=jnp.float32
            )
            query_grad = part if query_grad is None else query_grad + part
        wide_t[head_rows, :] = query_grad * scale

    @pl.loop(0, features // 128)
    def _(tile):
        columns = pl.ds(pl.multiple_of(tile * 128, 128), 128)
        out_ref[:, columns] = wide_t[columns, :].T.astype(jnp.bfloat16)


def attention_backward(
    query, keyval, key_bias, mixed, grad, log_total, features, block, exchanged, known, bands
):
    rows, length = query.shape[0], keyval.shape[0]
    shared = exchanged is not None
    scratch = [
        pltpu.VMEM((rows, features), jnp.bfloat16),
        pltpu.VMEM((features, length), jnp.float32),
        pltpu.VMEM((features, rows), jnp.float32),
    ]
    params = pltpu.CompilerParams(vmem_limit_bytes=56 * 2**20)
    if shared:

        def shared_kernel(both_ref, bias_ref, mixed_ref, grad_ref, log_ref, rows_ref, known_ref, out_ref, back_ref, kept_ref, *held):
            kept_ref[...] = known_ref[...]
            finish = exchange_rows(rows_ref, back_ref, *held[3:], bands=bands)
            attention_backward_kernel(
                both_ref, both_ref, bias_ref, mixed_ref, grad_ref, log_ref, out_ref, out_ref, *held[:3],
                features=features, shift=features, out_shift=features, block=block,
            )
            finish()

        anywhere, vmem = pl.BlockSpec(memory_space=pl.ANY), pl.BlockSpec(memory_space=pltpu.VMEM)
        return pl.pallas_call(
            shared_kernel,
            out_shape=(
                jax.ShapeDtypeStruct((rows, 3 * features), jnp.bfloat16),
                jax.ShapeDtypeStruct((bands, rows // bands, features), jnp.bfloat16),
                jax.ShapeDtypeStruct(known.shape, jnp.float32),
            ),
            in_specs=[vmem] * 5 + [anywhere, vmem],
            out_specs=(vmem, anywhere, vmem),
            scratch_shapes=scratch
            + [
                pltpu.SemaphoreType.DMA((bands,)),
                pltpu.SemaphoreType.DMA((bands,)),
                pltpu.SemaphoreType.DMA(()),
            ],
            cost_estimate=expected(BACKWARD_US),
            compiler_params=pltpu.CompilerParams(
                collective_id=2, has_side_effects=True, vmem_limit_bytes=56 * 2**20
            ),
        )(query, key_bias, mixed, grad, log_total, exchanged, known)
    return pl.pallas_call(
        functools.partial(
            attention_backward_kernel, features=features, shift=0, out_shift=0, block=block
        ),
        out_shape=(
            jax.ShapeDtypeStruct((rows, features), jnp.bfloat16),
            jax.ShapeDtypeStruct((length, 2 * features), jnp.bfloat16),
        ),
        scratch_shapes=scratch,
        compiler_params=params,
    )(query, keyval, key_bias, mixed, grad, log_total)


def flip(index, bit):
    return index + bit - 2 * bit * lax.rem(lax.div(index, bit), 2)


def start_kernel(
    wide_ref, tall_ref, tokens_ref, told_ref, ada_ref,
    qkv_ref, out_ref, up_ref, down_ref, rows_ref, heard_ref, silu_ref, mod_ref,
    partial, summed, banded, small_send, small_recv,
    held, turned, line_send, line_recv, row_send, row_recv, flat_send, flat_recv, local_sem,
    *, imgs, bands, qkv_part, out_part,
):
    img, band = lax.axis_index("img"), lax.axis_index("band")
    depth, width = wide_ref.shape
    tall_rows, tall_width = tall_ref.shape
    row_block = tokens_ref.shape[1]
    lanes = 128
    first = -(-(qkv_part + out_part) // lanes) * lanes
    beside_x, beside_y, sibling = flip(img, 2), flip(img, 4), flip(img, 1)
    across = flip(beside_x, 4)

    barrier = pltpu.get_barrier_semaphore()
    for step in range(1, imgs):
        other = lax.rem(img + step, imgs)
        pl.semaphore_signal(barrier, inc=1, device_id={"img": other}, device_id_type=MESH)
    for step in range(1, bands):
        pl.semaphore_signal(
            barrier, inc=1, device_id={"band": lax.rem(band + step, bands)}, device_id_type=MESH
        )
    pl.semaphore_wait(barrier, imgs + bands - 2)

    def piece(part, owner):
        if part == 2:
            return down_ref.at[:, pl.ds(pl.multiple_of(owner * tall_width, lanes), tall_width)]
        span = pl.ds(0, first) if part == 0 else pl.ds(first, width - first)
        return held.at[pl.ds(pl.multiple_of(owner * depth, 16), depth), span]

    def line_copy(part, way, step, owner, toward):
        view = piece(part, owner)
        return pltpu.make_async_remote_copy(
            src_ref=view, dst_ref=view,
            send_sem=line_send.at[part, way, step], recv_sem=line_recv.at[part, way, step],
            device_id={"band": toward}, device_id_type=MESH,
        )

    def line_sends(part, step, act):
        for way, sign in ((0, 1), (1, -1)):
            owner, toward = band - sign * step, band + sign

            @pl.when((owner >= 0) & (owner < bands) & (toward >= 0) & (toward < bands))
            def _():
                act(line_copy(part, way, step, owner, toward))

    def line_arrivals(part, step):
        for way, sign in ((0, 1), (1, -1)):
            owner = band - sign * (step + 1)

            @pl.when((owner >= 0) & (owner < bands))
            def _():
                line_copy(part, way, step, owner, band - sign).wait_recv()

    def row_copy(step):
        target = lax.rem(band + step, bands)
        return pltpu.make_async_remote_copy(
            src_ref=tokens_ref.at[target],
            dst_ref=rows_ref.at[pl.ds(pl.multiple_of(band * row_block, 16), row_block), :],
            send_sem=row_send.at[step - 1], recv_sem=row_recv.at[step - 1],
            device_id={"band": target}, device_id_type=MESH,
        )

    def row_arrival(step):
        source = lax.rem(band + bands - step, bands)
        view = rows_ref.at[pl.ds(pl.multiple_of(source * row_block, 16), row_block), :]
        return pltpu.make_async_remote_copy(
            src_ref=view, dst_ref=view,
            send_sem=row_send.at[step - 1], recv_sem=row_recv.at[step - 1],
            device_id={"band": source}, device_id_type=MESH,
        )

    def qkv_rows(owner, start=0, count=qkv_part):
        return qkv_ref.at[pl.ds(pl.multiple_of(owner * qkv_part + start, 16), count), :]

    def out_rows(owner):
        return out_ref.at[pl.ds(pl.multiple_of(owner * out_part, 16), out_part), :]

    half = (qkv_part + out_part) // 2
    own_qkv, own_out = turned.at[pl.ds(0, qkv_part), :], turned.at[pl.ds(qkv_part, out_part), :]
    plan = [
        (own_qkv, qkv_rows(img), beside_x, qkv_rows(beside_x)),
        (own_out, out_rows(img), beside_x, out_rows(beside_x)),
        (own_qkv, qkv_rows(img), beside_y, qkv_rows(beside_y)),
        (own_out, out_rows(img), beside_y, out_rows(beside_y)),
        (own_qkv, qkv_rows(img), sibling, qkv_rows(sibling)),
        (own_out, out_rows(img), sibling, out_rows(sibling)),
    ]
    for owner, toward, whole in ((beside_x, beside_y, True), (beside_y, beside_x, False)):
        if whole:
            view = qkv_rows(owner, 0, half)
            plan.append((view, view, toward, qkv_rows(across, 0, half)))
        else:
            rest = qkv_part - half
            view = qkv_rows(owner, half, rest)
            plan.append((view, view, toward, qkv_rows(across, half, rest)))
            plan.append((out_rows(owner), out_rows(owner), toward, out_rows(across)))
    for owner in (beside_x, beside_y):
        plan.append((qkv_rows(owner), qkv_rows(owner), sibling, qkv_rows(flip(owner, 1))))
        plan.append((out_rows(owner), out_rows(owner), sibling, out_rows(flip(owner, 1))))
    far = flip(across, 1)
    plan.append((qkv_rows(across, 0, half), qkv_rows(across, 0, half), sibling, qkv_rows(far, 0, half)))
    rest = qkv_part - half
    plan.append((qkv_rows(across, half, rest), qkv_rows(across, half, rest), sibling, qkv_rows(far, half, rest)))
    plan.append((out_rows(across), out_rows(across), sibling, out_rows(far)))

    def flat_copy(at):
        source, target, toward, _ = plan[at]
        return pltpu.make_async_remote_copy(
            src_ref=source, dst_ref=target, send_sem=flat_send.at[at], recv_sem=flat_recv.at[at],
            device_id={"img": toward}, device_id_type=MESH,
        )

    def flat_arrival(at):
        landing = plan[at][3]
        pltpu.make_async_remote_copy(
            src_ref=landing, dst_ref=landing, send_sem=flat_send.at[at], recv_sem=flat_recv.at[at],
            device_id={"img": sibling}, device_id_type=MESH,
        ).wait_recv()

    def turn(tile):
        span = pl.ds(pl.multiple_of(tile * lanes, lanes), lanes)
        turned[span, :] = held[:, span].astype(jnp.float32).T.astype(jnp.bfloat16)

    start = lambda copy: copy.start()
    own_rows = pltpu.make_async_copy(
        tokens_ref.at[band],
        rows_ref.at[pl.ds(pl.multiple_of(band * row_block, 16), row_block), :],
        local_sem.at[0],
    )
    own_rows.start()

    def small_copy(source, target, kind, step, axis, toward):
        return pltpu.make_async_remote_copy(
            src_ref=source, dst_ref=target,
            send_sem=small_send.at[kind, step], recv_sem=small_recv.at[kind, step],
            device_id={axis: toward}, device_id_type=MESH,
        )

    def told(step):
        return small_copy(told_ref, heard_ref.at[img], 0, step, "img", lax.rem(img + step, imgs))

    def partial_copy(step):
        other = lax.rem(img + step, imgs)
        return small_copy(partial.at[other], summed.at[img], 1, step, "img", other)

    def banded_copy(step):
        other = lax.rem(band + step, bands)
        return small_copy(summed.at[:, other], banded.at[band], 2, step, "band", other)

    def arrival(view, kind, step, axis):
        me, count = (img, imgs) if axis == "img" else (band, bands)
        small_copy(view, view, kind, step, axis, lax.rem(me + count - step, count)).wait_recv()

    for step in range(1, imgs):
        told(step).start()
    held[pl.ds(pl.multiple_of(band * depth, 16), depth), :] = wide_ref[...]
    down_ref[:, pl.ds(pl.multiple_of(band * tall_width, lanes), tall_width)] = tall_ref[...]
    line_sends(0, 0, start)
    heard_ref[img] = told_ref[...]
    for step in range(bands - 1):
        line_arrivals(0, step)
        if step < bands - 2:
            line_sends(0, step + 1, start)
    line_sends(1, 0, start)
    line_sends(2, 0, start)
    for step in range(1, bands):
        row_copy(step).start()
    pl.loop(0, first // lanes)(turn)
    keep_qkv = pltpu.make_async_copy(own_qkv, qkv_rows(img), local_sem.at[1])
    keep_out = pltpu.make_async_copy(own_out, out_rows(img), local_sem.at[2])
    for at in range(6):
        flat_copy(at).start()
    keep_qkv.start()
    keep_out.start()
    for step in range(1, imgs):
        arrival(heard_ref.at[lax.rem(img + imgs - step, imgs)], 0, step, "img")
    images = partial.shape[1]
    for other in range(imgs):
        for image in range(images):
            silu_ref[pl.ds(other * images + image, 1), :] = heard_ref[
                other, :, pl.ds(image * depth, depth)
            ]
    products = jnp.dot(
        silu_ref[...].astype(jnp.bfloat16), ada_ref[...], preferred_element_type=jnp.float32
    )
    for other in range(imgs):
        for image in range(images):
            at = other * images + image
            partial[other, image] = products[at : at + 1, :]
    for step in range(1, imgs):
        partial_copy(step).start()
    summed[img] = partial[img]
    for step in range(bands - 2):
        for part in (1, 2):
            line_arrivals(part, step)
            line_sends(part, step + 1, start)
    for arrived, sent in (((0, 1), (6, 9, 10)), ((2, 3), (7, 8, 11, 12))):
        for at in arrived:
            flat_arrival(at)
        for at in sent:
            flat_copy(at).start()
    for step in range(1, imgs):
        arrival(summed.at[lax.rem(img + imgs - step, imgs)], 1, step, "img")
    for step in range(1, bands):
        banded_copy(step).start()
    banded[band] = summed[:, band]
    for at in (6, 7, 8):
        flat_arrival(at)
        flat_copy(at + 7).start()
    for part in (1, 2):
        line_arrivals(part, bands - 2)
    pl.loop(first // lanes, width // lanes)(turn)
    up_ref[...] = turned[pl.ds(qkv_part + out_part, width - qkv_part - out_part), :]
    for step in range(1, bands):
        arrival(banded.at[lax.rem(band + bands - step, bands)], 2, step, "band")
    total = banded[0]
    for at in range(1, bands):
        total += banded[at]
    mod_ref[...] = total
    for part in range(3):
        for step in range(bands - 1):
            line_sends(part, step, lambda copy: copy.wait_send())
    for at in (4, 5, 9, 10, 11, 12, 13, 14, 15):
        flat_arrival(at)
    for at in range(16):
        flat_copy(at).wait_send()
    for step in range(1, bands):
        row_copy(step).wait_send()
        row_arrival(step).wait_recv()
        banded_copy(step).wait_send()
    for step in range(1, imgs):
        told(step).wait_send()
        partial_copy(step).wait_send()
    own_rows.wait()
    keep_qkv.wait()
    keep_out.wait()


def start_exchange(wide, tall, tokens, told, ada, bands, imgs, qkv_part, out_part):
    depth, width = wide.shape
    up_part = width - qkv_part - out_part
    low = jnp.bfloat16
    anywhere, vmem = pl.BlockSpec(memory_space=pl.ANY), pl.BlockSpec(memory_space=pltpu.VMEM)
    features = depth * bands
    images = tokens.shape[0]
    ada_columns = ada.shape[1]
    return pl.pallas_call(
        functools.partial(
            start_kernel, imgs=imgs, bands=bands, qkv_part=qkv_part, out_part=out_part
        ),
        out_shape=(
            jax.ShapeDtypeStruct((qkv_part * imgs, features), low),
            jax.ShapeDtypeStruct((out_part * imgs, features), low),
            jax.ShapeDtypeStruct((up_part, features), low),
            jax.ShapeDtypeStruct((tall.shape[0], tall.shape[1] * bands), low),
            jax.ShapeDtypeStruct((tokens.shape[1] * bands, tokens.shape[2]), low),
            jax.ShapeDtypeStruct((imgs,) + told.shape, jnp.float32),
            jax.ShapeDtypeStruct((imgs * images, depth), jnp.float32),
            jax.ShapeDtypeStruct((imgs, 1, ada_columns), jnp.float32),
        ),
        in_specs=[vmem, vmem, anywhere, vmem, vmem],
        out_specs=(anywhere, anywhere, vmem, vmem, anywhere, vmem, vmem, vmem),
        scratch_shapes=[
            pltpu.VMEM((imgs, images, 1, ada_columns), jnp.float32),
            pltpu.VMEM((imgs, images, 1, ada_columns), jnp.float32),
            pltpu.VMEM((bands, imgs, 1, ada_columns), jnp.float32),
            pltpu.SemaphoreType.DMA((3, imgs)),
            pltpu.SemaphoreType.DMA((3, imgs)),
            pltpu.VMEM((features, width), low),
            pltpu.VMEM((width, features), low),
            pltpu.SemaphoreType.DMA((3, 2, bands - 1)),
            pltpu.SemaphoreType.DMA((3, 2, bands - 1)),
            pltpu.SemaphoreType.DMA((bands - 1,)),
            pltpu.SemaphoreType.DMA((bands - 1,)),
            pltpu.SemaphoreType.DMA((16,)),
            pltpu.SemaphoreType.DMA((16,)),
            pltpu.SemaphoreType.DMA((3,)),
        ],
        cost_estimate=expected(START_US),
        compiler_params=pltpu.CompilerParams(
            collective_id=0, has_side_effects=True, vmem_limit_bytes=48 * 2**20
        ),
    )(wide, tall, tokens, told, ada)


def add_low(left, right):
    return (left.astype(jnp.float32) + right.astype(jnp.float32)).astype(jnp.bfloat16)


def tail_kernel(
    qkv_ref, out_ref, up_ref, rows_ref, pieces_ref, silu_ref, known_ref,
    wide_ref, back_ref, ada_ref, bias_ref, squares_ref,
    pieces, terms, square_flat, square_line, small_send, small_recv,
    own, from_core, first_x, first_y, last_x, last_y, turned, held, held_in,
    core_send, core_recv, flat_send, flat_recv, line_send, line_recv, row_send, row_recv, local_sem,
    *, imgs, bands,
):
    img, band = lax.axis_index("img"), lax.axis_index("band")
    qkv_part, out_part = qkv_ref.shape[0] // imgs, out_ref.shape[0] // imgs
    both = own.shape[1]
    depth, width = wide_ref.shape
    row_block = back_ref.shape[1]
    half = first_x.shape[1]
    lanes = 128
    beside_x, beside_y, sibling = flip(img, 2), flip(img, 4), flip(img, 1)
    chips = (img, beside_x, beside_y, flip(beside_x, 4))
    upper, lower = pl.ds(0, half), pl.ds(half, both - half)
    spans = (pl.ds(0, qkv_part), pl.ds(qkv_part, out_part))

    barrier = pltpu.get_barrier_semaphore()
    for step in range(1, imgs):
        other = lax.rem(img + step, imgs)
        pl.semaphore_signal(barrier, inc=1, device_id={"img": other}, device_id_type=MESH)
    for step in range(1, bands):
        pl.semaphore_signal(
            barrier, inc=1, device_id={"band": lax.rem(band + step, bands)}, device_id_type=MESH
        )
    pl.semaphore_wait(barrier, imgs + bands - 2)

    def grad_rows(kind, owner):
        source, count = ((qkv_ref, qkv_part), (out_ref, out_part))[kind]
        return source.at[pl.ds(pl.multiple_of(owner * count, 16), count), :]

    def core_copy(kind, at):
        return pltpu.make_async_remote_copy(
            src_ref=grad_rows(kind, flip(chips[at], 1)), dst_ref=from_core.at[at, spans[kind]],
            send_sem=core_send.at[kind, at], recv_sem=core_recv.at[kind, at],
            device_id={"img": sibling}, device_id_type=MESH,
        )

    def own_copy(kind, at):
        return pltpu.make_async_copy(
            grad_rows(kind, chips[at]), own.at[at, spans[kind]], local_sem.at[4 * kind + at]
        )

    plan = (
        (own.at[1, upper], first_x.at[0], beside_x),
        (own.at[3, upper], first_x.at[1], beside_x),
        (own.at[2, lower], first_y.at[0], beside_y),
        (own.at[3, lower], first_y.at[1], beside_y),
        (own.at[2, upper], last_y, beside_y),
        (own.at[1, lower], last_x, beside_x),
    )

    def flat_copy(at):
        source, target, toward = plan[at]
        return pltpu.make_async_remote_copy(
            src_ref=source, dst_ref=target, send_sem=flat_send.at[at], recv_sem=flat_recv.at[at],
            device_id={"img": toward}, device_id_type=MESH,
        )

    def row_span(owner):
        return pl.ds(pl.multiple_of(owner * row_block, 16), row_block)

    def row_copy(step):
        target = lax.rem(band + step, bands)
        return pltpu.make_async_remote_copy(
            src_ref=rows_ref.at[row_span(target), :], dst_ref=back_ref.at[band],
            send_sem=row_send.at[step - 1], recv_sem=row_recv.at[step - 1],
            device_id={"band": target}, device_id_type=MESH,
        )

    def row_arrival(step):
        source = lax.rem(band + bands - step, bands)
        return pltpu.make_async_remote_copy(
            src_ref=back_ref.at[source], dst_ref=back_ref.at[source],
            send_sem=row_send.at[step - 1], recv_sem=row_recv.at[step - 1],
            device_id={"band": source}, device_id_type=MESH,
        )

    first = -(-both // lanes) * lanes
    parts = (pl.ds(0, first), pl.ds(first, width - first))

    def piece(part, owner, way=None):
        down = pl.ds(pl.multiple_of(owner * depth, 16), depth)
        return held.at[down, parts[part]] if way is None else held_in.at[way, down, parts[part]]

    def line_copy(part, way, owner, toward):
        return pltpu.make_async_remote_copy(
            src_ref=piece(part, owner), dst_ref=piece(part, owner, way),
            send_sem=line_send.at[part, way, owner], recv_sem=line_recv.at[part, way, owner],
            device_id={"band": toward}, device_id_type=MESH,
        )

    def line_ends(part):
        for step in range(bands - 1):

            @pl.when(band == 0)
            def _():
                line_copy(part, 0, bands - 1 - step, band + 1).start()

            @pl.when(band == bands - 1)
            def _():
                line_copy(part, 1, step, band - 1).start()

    def line_round(part, step):
        for way, owner, sign in ((0, bands - 1 - step, 1), (1, step, -1)):

            @pl.when((sign * (owner - band) > 0) & (band > 0) & (band < bands - 1))
            def _():
                copy = line_copy(part, way, owner, band + sign)
                copy.wait_recv()
                mine = piece(part, owner)
                mine[...] = add_low(mine[...], piece(part, owner, way)[...])
                copy.start()

    def line_finish(part):
        span = parts[part]
        wide_ref[:, span] = piece(part, band)[...].astype(jnp.float32)
        for way, sign in ((0, 1), (1, -1)):

            @pl.when((band - sign >= 0) & (band - sign < bands))
            def _():
                line_copy(part, way, band, band - sign).wait_recv()
                wide_ref[:, span] += piece(part, band, way)[...].astype(jnp.float32)

    def line_sent(part):
        for way, sign in ((0, 1), (1, -1)):
            for owner in range(bands):

                @pl.when(sign * (owner - band) > 0)
                def _():
                    line_copy(part, way, owner, band + sign).wait_send()

    def turn(tile):
        span = pl.ds(pl.multiple_of(tile * lanes, lanes), lanes)
        held[:, span] = turned[span, :].astype(jnp.float32).T.astype(jnp.bfloat16)

    def small_copy(source, target, kind, step, axis, toward):
        return pltpu.make_async_remote_copy(
            src_ref=source, dst_ref=target,
            send_sem=small_send.at[kind, step], recv_sem=small_recv.at[kind, step],
            device_id={axis: toward}, device_id_type=MESH,
        )

    def piece_flat(step):
        other = lax.rem(img + step, imgs)
        return small_copy(pieces_ref.at[other], pieces.at[band, img], 0, step, "img", other)

    def piece_line(step):
        other = lax.rem(band + step, bands)
        return small_copy(pieces.at[band], pieces.at[band], 1, step, "band", other)

    def square_one(step):
        other = lax.rem(img + step, imgs)
        return small_copy(square_flat.at[img], square_flat.at[img], 2, step, "img", other)

    def square_two(step):
        other = lax.rem(band + step, bands)
        return small_copy(square_line.at[band], square_line.at[band], 3, step, "band", other)

    def arrival(view, kind, step, axis):
        me, count = (img, imgs) if axis == "img" else (band, bands)
        small_copy(view, view, kind, step, axis, lax.rem(me + count - step, count)).wait_recv()

    order = (3, 1, 2, 0)
    for step in range(1, imgs):
        piece_flat(step).start()
    keep_piece = pltpu.make_async_copy(pieces_ref.at[img], pieces.at[band, img], local_sem.at[9])
    keep_piece.start()
    for at in order:
        core_copy(0, at).start()
        core_copy(1, at).start()
    for at in order:
        own_copy(0, at).start()
        own_copy(1, at).start()
    keep = pltpu.make_async_copy(rows_ref.at[row_span(band), :], back_ref.at[band], local_sem.at[8])
    keep.start()
    turned[pl.ds(both, width - both), :] = up_ref[...]
    pl.loop(first // lanes, width // lanes)(turn)
    line_ends(1)
    for step in range(1, bands):
        row_copy(step).start()
    for at in order:
        for kind in range(2):
            own_copy(kind, at).wait()
            core_copy(kind, at).wait_recv()
        own[at] = add_low(own[at], from_core[at])
        for ready in {3: (1, 3), 1: (0,), 2: (2,), 0: ()}[at]:
            flat_copy(ready).start()
    keep_piece.wait()
    for step in range(1, imgs):
        arrival(pieces.at[band, lax.rem(img + imgs - step, imgs)], 0, step, "img")
    for step in range(1, bands):
        piece_line(step).start()
    flat_copy(1).wait_recv()
    own[2, upper] = add_low(own[2, upper], first_x[1])
    flat_copy(4).start()
    flat_copy(3).wait_recv()
    own[1, lower] = add_low(own[1, lower], first_y[1])
    flat_copy(5).start()
    line_round(1, 0)
    flat_copy(0).wait_recv()
    flat_copy(2).wait_recv()
    flat_copy(4).wait_recv()
    flat_copy(5).wait_recv()
    turned[upper, :] = (
        own[0, upper].astype(jnp.float32)
        + first_x[0].astype(jnp.float32)
        + last_y[...].astype(jnp.float32)
    ).astype(jnp.bfloat16)
    turned[lower, :] = (
        own[0, lower].astype(jnp.float32)
        + first_y[0].astype(jnp.float32)
        + last_x[...].astype(jnp.float32)
    ).astype(jnp.bfloat16)
    pl.loop(0, first // lanes)(turn)
    line_ends(0)
    for step in range(bands - 1):
        line_round(0, step)
        if step > 0:
            line_round(1, step)
    for step in range(1, bands):
        arrival(pieces.at[lax.rem(band + bands - step, bands)], 1, step, "band")
    for image in range(imgs):
        for at in range(bands):
            terms[pl.ds(image * bands + at, 1), :] = pieces[at, image]
    columns = ada_ref.shape[1]
    ada = lax.dot_general(
        silu_ref[...], terms[:, pl.ds(0, columns)], (((1,), (0,)), ((), ())),
        precision=lax.Precision.HIGHEST, preferred_element_type=jnp.float32,
    )
    ada_ref[...] = ada
    bias_rows, bias_columns = bias_ref.shape
    bias = jnp.sum(terms[:, pl.ds(columns, bias_rows * bias_columns)], axis=0, keepdims=True)
    for at in range(bias_rows):
        bias_ref[pl.ds(at, 1), :] = bias[:, at * bias_columns : (at + 1) * bias_columns]
    squares = jnp.sum(ada * ada, axis=0, keepdims=True)
    squares = jnp.sum(squares, axis=1, keepdims=True)
    squares += jnp.sum(bias * bias, axis=1, keepdims=True) / bands
    line_finish(1)
    line_finish(0)
    rows = jnp.sum(wide_ref[...] * wide_ref[...], axis=0, keepdims=True)
    squares += jnp.sum(rows, axis=1, keepdims=True) + known_ref[0:1, 0:1]
    square_flat[img] = jnp.broadcast_to(squares, square_flat.shape[1:])
    for step in range(1, imgs):
        square_one(step).start()
    for step in range(1, imgs):
        arrival(square_flat.at[lax.rem(img + imgs - step, imgs)], 2, step, "img")
    total = square_flat[0]
    for at in range(1, imgs):
        total += square_flat[at]
    square_line[band] = total
    for step in range(1, bands):
        square_two(step).start()
    for step in range(1, bands):
        arrival(square_line.at[lax.rem(band + bands - step, bands)], 3, step, "band")
    total = square_line[0]
    for at in range(1, bands):
        total += square_line[at]
    squares_ref[...] = total
    line_sent(0)
    line_sent(1)
    for step in range(1, imgs):
        piece_flat(step).wait_send()
        square_one(step).wait_send()
    for step in range(1, bands):
        piece_line(step).wait_send()
        square_two(step).wait_send()
    for at in range(4):
        core_copy(0, at).wait_send()
        core_copy(1, at).wait_send()
    for at in range(6):
        flat_copy(at).wait_send()
    for step in range(1, bands):
        row_copy(step).wait_send()
        row_arrival(step).wait_recv()
    keep.wait()


def tail_exchange(qkv_grad, out_grad, up_sum, rows, pieces, silu, known, bias_shape, bands, imgs):
    low = jnp.bfloat16
    features = qkv_grad.shape[1]
    both = (qkv_grad.shape[0] + out_grad.shape[0]) // imgs
    width = both + up_sum.shape[0]
    half = -(-both // 32) * 16
    ada_columns = pieces.shape[2] - bias_shape[0] * bias_shape[1]
    anywhere, vmem = pl.BlockSpec(memory_space=pl.ANY), pl.BlockSpec(memory_space=pltpu.VMEM)
    return pl.pallas_call(
        functools.partial(tail_kernel, imgs=imgs, bands=bands),
        out_shape=(
            jax.ShapeDtypeStruct((features // bands, width), jnp.float32),
            jax.ShapeDtypeStruct((bands, rows.shape[0] // bands, features), low),
            jax.ShapeDtypeStruct((silu.shape[0], ada_columns), jnp.float32),
            jax.ShapeDtypeStruct(bias_shape, jnp.float32),
            jax.ShapeDtypeStruct((8, 128), jnp.float32),
        ),
        in_specs=[anywhere, anywhere, vmem, anywhere, vmem, vmem, vmem],
        out_specs=(vmem, anywhere, vmem, vmem, vmem),
        scratch_shapes=[
            pltpu.VMEM((bands,) + pieces.shape, jnp.float32),
            pltpu.VMEM((bands * imgs, pieces.shape[2]), jnp.float32),
            pltpu.VMEM((imgs, 8, 128), jnp.float32),
            pltpu.VMEM((bands, 8, 128), jnp.float32),
            pltpu.SemaphoreType.DMA((4, imgs)),
            pltpu.SemaphoreType.DMA((4, imgs)),
            pltpu.VMEM((4, both, features), low),
            pltpu.VMEM((4, both, features), low),
            pltpu.VMEM((2, half, features), low),
            pltpu.VMEM((2, both - half, features), low),
            pltpu.VMEM((both - half, features), low),
            pltpu.VMEM((half, features), low),
            pltpu.VMEM((width, features), low),
            pltpu.VMEM((features, width), low),
            pltpu.VMEM((2, features, width), low),
            pltpu.SemaphoreType.DMA((2, 4)),
            pltpu.SemaphoreType.DMA((2, 4)),
            pltpu.SemaphoreType.DMA((6,)),
            pltpu.SemaphoreType.DMA((6,)),
            pltpu.SemaphoreType.DMA((2, 2, bands)),
            pltpu.SemaphoreType.DMA((2, 2, bands)),
            pltpu.SemaphoreType.DMA((bands - 1,)),
            pltpu.SemaphoreType.DMA((bands - 1,)),
            pltpu.SemaphoreType.DMA((10,)),
        ],
        cost_estimate=expected(TAIL_US),
        compiler_params=pltpu.CompilerParams(
            collective_id=1, has_side_effects=True, vmem_limit_bytes=50 * 2**20
        ),
    )(qkv_grad, out_grad, up_sum, rows, pieces, silu, known)


def adam_kernel(*refs):
    squares_ref, wide_ref, tall_ref, ada_ref, bias_ref = refs[:5]
    sources, results = refs[5:23], refs[23:]
    norm = jnp.sqrt(squares_ref[0:1, 0:1])
    factor = clip_norm / jnp.maximum(norm, clip_norm)
    qkv_part = sources[3].shape[1]
    both = qkv_part + sources[6].shape[1]
    rates = (learn_rate, learn_rate, out_rate, learn_rate, learn_rate, bias_rate)

    def update(which, rows, gradient):
        weight_ref, first_ref, second_ref = sources[3 * which : 3 * which + 3]
        new = adam_update(
            weight_ref[rows, :], first_ref[rows, :], second_ref[rows, :], gradient, factor, rates[which]
        )
        for into, value in zip(results[3 * which : 3 * which + 3], new):
            into[rows, :] = value

    depth = wide_ref.shape[0]
    block = next(rows for rows in (32, 16, 8) if depth % rows == 0)

    @pl.loop(0, depth // block)
    def _(step):
        rows = pl.ds(pl.multiple_of(step * block, block), block)
        update(0, rows, ada_ref[rows, :])
        update(1, rows, wide_ref[rows, :qkv_part])
        update(2, rows, wide_ref[rows, qkv_part:both])
        update(3, rows, wide_ref[rows, both:])

    tall_width = sources[12].shape[0]
    whole = tall_width // 128 * 128

    @pl.loop(0, tall_width // 128)
    def _(step):
        rows = pl.ds(pl.multiple_of(step * 128, 128), 128)
        update(4, rows, tall_ref[:, rows].T)

    if whole < tall_width:
        update(4, pl.ds(whole, tall_width - whole), tall_ref[:, whole:].T)
    update(5, slice(None), bias_ref[...])
    results[18][...] = bias_ref[pl.ds(13, 1), :] * factor


def adam_all(squares, wide, tall, ada, bias, groups):
    flat = [array for group in groups for array in group]
    return pl.pallas_call(
        adam_kernel,
        out_shape=[jax.ShapeDtypeStruct(array.shape, jnp.float32) for array in flat]
        + [jax.ShapeDtypeStruct((1, bias.shape[1]), jnp.float32)],
        compiler_params=pltpu.CompilerParams(vmem_limit_bytes=50 * 2**20),
    )(squares, wide, tall, ada, bias, *flat)


def body(
    inputs,
    condition,
    valid_rows,
    cotangent,
    ada_weight,
    qkv_weight,
    out_weight,
    up_weight,
    down_weight,
    biases,
    ada_first,
    qkv_first,
    out_first,
    up_first,
    down_first,
    bias_first,
    ada_second,
    qkv_second,
    out_second,
    up_second,
    down_second,
    bias_second,
):
    images, local_rows, features = inputs.shape
    length = L
    head_count = HEADS
    head_size = HEAD_DIM
    score_scale = head_size ** (-0.5)
    band_count = lax.axis_size("band")
    img_count = lax.axis_size("img")
    band_rank = lax.axis_index("band")
    img_rank = lax.axis_index("img")
    own = max(1, images // band_count)
    split = max(1, band_count // images)
    mates = band_count // split
    image_rows = length // split
    exchange_groups = None
    share_groups = None
    if split > 1:
        exchange_groups = [[g * mates + m for m in range(mates)] for g in range(split)]
        share_groups = [[g * mates + m for g in range(split)] for m in range(mates)]
    low_type = jnp.bfloat16

    def to_images(rows):
        return lax.all_to_all(rows, "band", split_axis=0, concat_axis=1, axis_index_groups=exchange_groups, tiled=True)

    def to_bands(whole):
        cut = whole.reshape(own, mates, local_rows, features).transpose(1, 0, 2, 3)
        back = lax.all_to_all(
            cut, "band", split_axis=0, concat_axis=0, axis_index_groups=exchange_groups, tiled=True
        )
        return back.reshape(images, local_rows, features)

    def after(value, *earlier):
        return lax.optimization_barrier((value,) + earlier)[0]

    def sum_everywhere(partial):
        sent = jnp.broadcast_to(partial, (img_count * band_count, 128))
        got = lax.all_to_all(sent, ("img", "band"), split_axis=0, concat_axis=0, tiled=True)
        return jnp.sum(got[:, 0])

    qkv_part, out_part = qkv_weight.shape[1], out_weight.shape[1]

    bias_rows, bias_columns = biases.shape
    ada_rows, ada_columns = ada_weight.shape
    silu_own = lax.reduce_precision(jax.nn.silu(condition.astype(jnp.float32)), 8, 7)
    silu_own = lax.dynamic_slice_in_dim(silu_own, band_rank * ada_rows, ada_rows, axis=1)
    told = jnp.concatenate(
        [silu_own.reshape(1, -1), lax.reduce_precision(biases, 8, 7).reshape(1, -1)],
        axis=1,
    )
    ada_low = ada_weight.astype(low_type)
    wide = jnp.concatenate([qkv_weight, out_weight, up_weight], axis=1).astype(low_type)
    tall = down_weight.T.astype(low_type)
    if img_count == 8 and own == 1 and split == 1:
        qkv_full, out_full, up_rows, down_rows, tokens_low, heard, silu_rows, mod_summed = (
            start_exchange(
                wide, tall, inputs, told, ada_low, band_count, img_count, qkv_part, out_part
            )
        )
        tokens_low = tokens_low.reshape(own, image_rows, features)
        mod_summed = mod_summed.reshape(own, img_count * ada_columns)
    else:
        turned = lax.all_gather(wide, "band", axis=0, tiled=True).T
        qkv_full = lax.all_gather(turned[:qkv_part], "img", axis=0, tiled=True)
        out_full = lax.all_gather(
            turned[qkv_part : qkv_part + out_part], "img", axis=0, tiled=True
        )
        up_rows = turned[qkv_part + out_part :]
        down_rows = lax.all_gather(tall, "band", axis=1, tiled=True)
        tokens_low = to_images(inputs)
        heard = lax.all_gather(told, "img", axis=0, tiled=True)
        silu_rows = heard[:, : images * ada_rows].reshape(img_count * images, ada_rows)
        mod_partial = jnp.dot(
            silu_rows.astype(low_type), ada_low, preferred_element_type=jnp.float32
        )
        mod_sent = jnp.tile(
            mod_partial.reshape(img_count, 1, images * ada_columns), (1, split, 1)
        )
        mod_pieces = lax.all_to_all(
            mod_sent.reshape(img_count * band_count, own * ada_columns),
            ("img", "band"),
            split_axis=0,
            concat_axis=0,
            tiled=True,
        ).reshape(img_count, band_count, own, ada_columns)
        mod_summed = (
            jnp.sum(mod_pieces, axis=1).transpose(1, 0, 2).reshape(own, img_count * ada_columns)
        )
    up_full = lax.all_gather(up_rows, "img", axis=0, tiled=True)
    down_full = lax.all_gather(after(down_rows, up_rows), "img", axis=0, tiled=True)
    bias_vals = (
        heard.reshape(img_count, -1)[:, images * ada_rows :]
        .reshape(img_count, bias_rows, bias_columns)
        .transpose(1, 0, 2)
        .reshape(bias_rows, features)
    )
    modulation = mod_summed + bias_vals[0:6].reshape(-1)
    mod_parts = modulation.reshape(own, 6, 1, features)
    shift_one = mod_parts[:, 0]
    scale_one = mod_parts[:, 1]
    gate_one = mod_parts[:, 2]
    shift_two = mod_parts[:, 3]
    scale_two = mod_parts[:, 4]
    gate_two = mod_parts[:, 5]
    valid_own = lax.dynamic_slice_in_dim(valid_rows, lax.rem(band_rank, mates) * own, own, axis=0)
    key_mask = jnp.arange(length, dtype=jnp.int32)[None, :] < valid_own[:, None]
    positions = lax.div(band_rank, mates) * image_rows + jnp.arange(image_rows, dtype=jnp.int32)
    row_mask = (positions[None, :] < valid_own[:, None]).astype(jnp.float32)[:, :, None]
    tokens_in = tokens_low.astype(jnp.float32)
    normed_one, inverse_one = normalize_keep(tokens_in)
    first_in = (normed_one * (1.0 + scale_one) + shift_one).astype(jnp.bfloat16)
    cotangent_low = to_images(after(cotangent, tokens_low))
    grad_out = cotangent_low.astype(jnp.float32) * row_mask
    qkv_bias = jnp.concatenate([bias_vals[6], jnp.zeros((features,), jnp.float32), bias_vals[7]])
    projected = (
        jnp.einsum("ird,ed->ire", first_in, qkv_full, preferred_element_type=jnp.float32) + qkv_bias
    ).astype(jnp.bfloat16)
    key_bias = jnp.where(key_mask, 0.0, very_low).astype(jnp.float32)[:, :, None]
    queries = [projected[i] for i in range(own)]
    if split > 1:
        keys_values = lax.all_gather(
            projected[..., features:], "band", axis=1, axis_index_groups=share_groups, tiled=True
        )
        keys_values = [keys_values[i] for i in range(own)]
        key_shift = 0
    else:
        keys_values = queries
        key_shift = features
    mixed, log_total = zip(
        *[
            attention_forward(queries[i], keys_values[i], key_bias[i], features, key_shift, 512)
            for i in range(own)
        ]
    )
    mixed_parts = mixed
    mixed = jnp.stack(mixed)
    attended = (
        jnp.einsum("ird,ed->ire", mixed, out_full, preferred_element_type=jnp.float32)
        + bias_vals[8]
    )
    middle = tokens_in + gate_one * attended
    normed_two, inverse_two = normalize_keep(middle)
    second_in = (normed_two * (1.0 + scale_two) + shift_two).astype(jnp.bfloat16)
    hidden_pre = jnp.einsum(
        "ird,fd->irf", second_in, up_full, preferred_element_type=jnp.float32
    ) + bias_vals[9:13].reshape(-1)
    hidden, gelu_back = jax.vjp(smooth_gate, hidden_pre)
    hidden_low = hidden.astype(jnp.bfloat16)
    branch = (
        jnp.einsum("irf,df->ird", hidden_low, down_full, preferred_element_type=jnp.float32)
        + bias_vals[13]
    )
    output_low = (middle + gate_two * branch).astype(jnp.bfloat16)
    branch_grad = (gate_two * grad_out).astype(jnp.bfloat16)
    gate_two_grad = jnp.sum(grad_out * branch, axis=1)
    down_grad = jnp.einsum(
        "ird,irf->df", branch_grad, hidden_low, preferred_element_type=jnp.float32
    ).astype(low_type)
    down_sum = lax.psum_scatter(down_grad, "img", scatter_dimension=0, tiled=True)
    hidden_grad = jnp.einsum(
        "ird,df->irf",
        after(branch_grad, down_grad),
        down_full,
        preferred_element_type=jnp.float32,
    )
    pre_grad = gelu_back(hidden_grad)[0].astype(jnp.bfloat16)
    up_grad = jnp.einsum(
        "irf,ird->fd", pre_grad, second_in, preferred_element_type=jnp.float32
    ).astype(low_type)
    up_sum = lax.psum_scatter(up_grad, "img", scatter_dimension=0, tiled=True)
    second_grad = jnp.einsum("irf,fd->ird", after(pre_grad, up_grad), up_full, preferred_element_type=jnp.float32)
    shift_two_grad = jnp.sum(second_grad, axis=1)
    scale_two_grad = jnp.sum(second_grad * normed_two, axis=1)
    middle_grad = grad_out + normalize_back(
        normed_two, inverse_two, second_grad * (1.0 + scale_two)
    )
    attended_grad = (gate_one * middle_grad).astype(jnp.bfloat16)
    gate_one_grad = jnp.sum(middle_grad * attended, axis=1)
    out_grad = jnp.einsum(
        "ire,ird->ed", attended_grad, mixed, preferred_element_type=jnp.float32
    ).astype(low_type)
    mixed_grad = jnp.einsum(
        "ire,ed->ird", after(attended_grad, out_grad), out_full, preferred_element_type=jnp.float32
    ).astype(jnp.bfloat16)
    tall_cut = down_sum.reshape(down_sum.shape[0], band_count, -1).transpose(1, 0, 2)
    tall_shard = jnp.sum(
        lax.all_to_all(tall_cut, "band", split_axis=0, concat_axis=0, tiled=True).astype(jnp.float32),
        axis=0,
    )
    hosted = img_count == 8 and own == 1 and split == 1
    tall_squares = jnp.broadcast_to(jnp.sum(tall_shard * tall_shard), (8, 128))
    attention_grads = [
        attention_backward(
            queries[i], keys_values[i], key_bias[i], mixed_parts[i], mixed_grad[i], log_total[i],
            features, 512, output_low[i] if hosted else None, tall_squares, band_count,
        )
        for i in range(own)
    ]
    if hosted:
        output, tall_squares = attention_grads[0][1:]
    else:
        output = to_bands(output_low)
    if split > 1:
        shared_grads = lax.psum_scatter(
            jnp.stack([pair[1] for pair in attention_grads]),
            "band",
            scatter_dimension=1,
            axis_index_groups=share_groups,
            tiled=True,
        )
        qkv_grad = jnp.concatenate(
            [jnp.stack([pair[0] for pair in attention_grads]), shared_grads], axis=-1
        )
    elif hosted:
        qkv_grad = attention_grads[0][0][None]
    else:
        qkv_grad = jnp.stack([jnp.concatenate(pair, axis=-1) for pair in attention_grads])
    qkv_sums = jnp.sum(qkv_grad.astype(jnp.float32), axis=(0, 1))
    qkv_weight_grad = jnp.einsum(
        "ire,ird->ed", qkv_grad, first_in, preferred_element_type=jnp.float32
    ).astype(low_type)
    first_grad = jnp.einsum("ire,ed->ird", after(qkv_grad, qkv_weight_grad), qkv_full, preferred_element_type=jnp.float32)
    shift_one_grad = jnp.sum(first_grad, axis=1)
    scale_one_grad = jnp.sum(first_grad * normed_one, axis=1)
    input_grad_low = (
        middle_grad + normalize_back(normed_one, inverse_one, first_grad * (1.0 + scale_one))
    ).astype(low_type)
    mod_grad = jnp.stack(
        [
            shift_one_grad,
            scale_one_grad,
            gate_one_grad,
            shift_two_grad,
            scale_two_grad,
            gate_two_grad,
        ],
        axis=1,
    )
    row_sums = jnp.concatenate(
        [
            qkv_sums[:features][None],
            qkv_sums[2 * features :][None],
            jnp.sum(attended_grad.astype(jnp.float32), axis=(0, 1))[None],
            jnp.sum(pre_grad.astype(jnp.float32), axis=(0, 1)).reshape(4, features),
            jnp.sum(branch_grad.astype(jnp.float32), axis=(0, 1))[None],
        ],
        axis=0,
    )
    pieces = jnp.concatenate(
        [
            mod_grad.reshape(own, img_count, ada_columns)
            .transpose(1, 0, 2)
            .reshape(img_count, own * ada_columns),
            jnp.concatenate([jnp.sum(mod_grad, axis=0).reshape(6, features), row_sums], axis=0)
            .reshape(bias_rows, img_count, bias_columns)
            .transpose(1, 0, 2)
            .reshape(img_count, -1),
        ],
        axis=1,
    )
    silu_terms = jnp.tile(
        silu_rows.reshape(img_count, 1, images, ada_rows), (1, split, 1, 1)
    ).reshape(img_count * band_count * own, ada_rows)
    if img_count == 8 and own == 1 and split == 1:
        wide_shard, input_grad_low, ada_shard, bias_total, squares_total = tail_exchange(
            qkv_weight_grad,
            out_grad,
            up_sum,
            input_grad_low[0],
            pieces[:, None],
            silu_terms.T,
            tall_squares,
            biases.shape,
            band_count,
            img_count,
        )
    else:
        sent = jnp.broadcast_to(
            pieces[:, None], (img_count, band_count, pieces.shape[1])
        ).reshape(img_count * band_count, -1)
        got = lax.all_to_all(sent, ("img", "band"), split_axis=0, concat_axis=0, tiled=True)
        ada_shard = jnp.einsum(
            "id,ie->de",
            silu_terms,
            got[:, : own * ada_columns].reshape(-1, ada_columns),
            precision=lax.Precision.HIGHEST,
        )
        bias_total = jnp.sum(got[:, own * ada_columns :], axis=0).reshape(bias_rows, bias_columns)
        qkv_sum = lax.psum_scatter(qkv_weight_grad, "img", scatter_dimension=0, tiled=True)
        out_sum = lax.psum_scatter(out_grad, "img", scatter_dimension=0, tiled=True)
        wide_shard = lax.psum_scatter(
            jnp.concatenate([qkv_sum, out_sum, up_sum], axis=0).T,
            "band",
            scatter_dimension=0,
            tiled=True,
        ).astype(jnp.float32)
        input_grad_low = to_bands(input_grad_low)
        squares = tall_squares[0, 0] + jnp.sum(bias_total * bias_total) / band_count
        for shard_grad in (ada_shard, wide_shard):
            squares = squares + jnp.sum(shard_grad * shard_grad)
        squares_total = jnp.broadcast_to(sum_everywhere(squares), (8, 128))
    input_grad = input_grad_low.astype(jnp.float32)
    grad_norm = jnp.sqrt(squares_total[0, 0])
    groups = (
        (ada_weight, ada_first, ada_second),
        (qkv_weight, qkv_first, qkv_second),
        (out_weight, out_first, out_second),
        (up_weight, up_first, up_second),
        (down_weight, down_first, down_second),
        (biases, bias_first, bias_second),
    )
    updated = adam_all(squares_total, wide_shard, tall_shard, ada_shard, bias_total, groups)
    ada_new, ada_first_new, ada_second_new = updated[0:3]
    qkv_new, qkv_first_new, qkv_second_new = updated[3:6]
    out_new, out_first_new, out_second_new = updated[6:9]
    up_new, up_first_new, up_second_new = updated[9:12]
    down_new, down_first_new, down_second_new = updated[12:15]
    bias_new, bias_first_new, bias_second_new = updated[15:18]
    branch_bias_grad = updated[18][0]
    return (
        output,
        input_grad,
        grad_norm,
        ada_new,
        qkv_new,
        out_new,
        up_new,
        down_new,
        bias_new,
        ada_first_new,
        qkv_first_new,
        out_first_new,
        up_first_new,
        down_first_new,
        bias_first_new,
        ada_second_new,
        qkv_second_new,
        out_second_new,
        up_second_new,
        down_second_new,
        bias_second_new,
        branch_bias_grad,
    )


def solution(mesh):
    return jax.shard_map(
        body,
        mesh=mesh,
        in_specs=(
            P("img", "band", None),
            P("img", None),
            P("img"),
            P("img", "band", None),
            P("band", "img"),
            P("band", "img"),
            P("band", "img"),
            P("band", "img"),
            P("band", "img"),
            P(None, "img"),
            P("band", "img"),
            P("band", "img"),
            P("band", "img"),
            P("band", "img"),
            P("band", "img"),
            P(None, "img"),
            P("band", "img"),
            P("band", "img"),
            P("band", "img"),
            P("band", "img"),
            P("band", "img"),
            P(None, "img"),
        ),
        out_specs=(
            P("img", "band", None),
            P("img", "band", None),
            P(),
            P("band", "img"),
            P("band", "img"),
            P("band", "img"),
            P("band", "img"),
            P("band", "img"),
            P(None, "img"),
            P("band", "img"),
            P("band", "img"),
            P("band", "img"),
            P("band", "img"),
            P("band", "img"),
            P(None, "img"),
            P("band", "img"),
            P("band", "img"),
            P("band", "img"),
            P("band", "img"),
            P("band", "img"),
            P(None, "img"),
            P("img"),
        ),
        check_vma=False,
    )
```

```python
import functools

import jax
import jax.numpy as jnp
from jax import lax
from jax.experimental import pallas as pl
from jax.experimental.pallas import tpu as pltpu
from jax.sharding import PartitionSpec as P

HEADS = 16
HEAD_DIM = 72
L = 1024
STEP = 10


norm_eps = 1e-06
beta_one = 0.9
beta_two = 0.999
adam_eps = 1e-08
learn_rate = 0.03
out_rate = 0.25
bias_rate = 0.4
clip_norm = 1.0
very_low = -1000000000.0


def normalize_keep(values):
    centre = values - jnp.mean(values, axis=-1, keepdims=True)
    inverse = lax.rsqrt(jnp.mean(centre * centre, axis=-1, keepdims=True) + norm_eps)
    return (centre * inverse, inverse)


def normalize_back(normed, inverse, incoming):
    return inverse * (
        incoming
        - jnp.mean(incoming, axis=-1, keepdims=True)
        - normed * jnp.mean(incoming * normed, axis=-1, keepdims=True)
    )


def smooth_gate(values):
    return jax.nn.gelu(values, approximate=True)


def adam_update(weight, first_old, second_old, gradient, factor, rate):
    clipped = gradient * factor
    first_new = beta_one * first_old + (1.0 - beta_one) * clipped
    second_new = beta_two * second_old + (1.0 - beta_two) * clipped * clipped
    first_hat = first_new / (1.0 - beta_one**STEP)
    second_hat = second_new / (1.0 - beta_two**STEP)
    return (weight - rate * first_hat / (jnp.sqrt(second_hat) + adam_eps), first_new, second_new)


WINDOW = 256
CONTRACT_LAST = (((1,), (1,)), ((), ()))
LOG2_E = 1.4426950408889634


FORWARD_US, BACKWARD_US, START_US, TAIL_US = 37, 57, 115, 110


def expected(microseconds):
    moved = int(microseconds * 3.2e6)
    return pl.CostEstimate(flops=0, bytes_accessed=moved, transcendentals=0)


def head_window(head, features):
    start = head * HEAD_DIM
    base = pl.multiple_of(jnp.minimum(start // 128 * 128, features - WINDOW), 128)
    lane = lax.broadcasted_iota(jnp.int32, (1, WINDOW), 1)
    inside = (lane >= start - base) & (lane < start - base + HEAD_DIM)
    return base, inside


def attention_forward_kernel(
    query_ref, keyval_ref, bias_ref, mixed_ref, log_ref, scaled, value_t, mixed_t, *, features, shift, block
):
    length = keyval_ref.shape[0]
    rows = mixed_ref.shape[0]
    scaled[...] = (query_ref[:, :features].astype(jnp.float32) * (HEAD_DIM**-0.5 * LOG2_E)).astype(
        jnp.bfloat16
    )

    @pl.loop(0, features // 128)
    def _(tile):
        columns = pl.ds(pl.multiple_of(tile * 128, 128), 128)
        source = pl.ds(pl.multiple_of(shift + features + tile * 128, 128), 128)
        value_t[columns, :] = keyval_ref[:, source].astype(jnp.float32).T

    @pl.loop(0, HEADS)
    def _(head):
        base, inside = head_window(head, features)
        head_rows = pl.ds(pl.multiple_of(head * HEAD_DIM, 8), HEAD_DIM)
        query = scaled[:, pl.ds(base, WINDOW)]
        ones = jnp.ones((8, block), jnp.float32)
        top = None
        for at in range(0, length, block):
            key = keyval_ref[pl.ds(at, block), pl.ds(pl.multiple_of(base + shift, 128), WINDOW)]
            key = jnp.where(inside, key, jnp.zeros_like(key))
            scores = lax.dot_general(key, query, CONTRACT_LAST, preferred_element_type=jnp.float32)
            if at + block == length:
                scores = scores + bias_ref[pl.ds(at, block), :]
            block_top = jnp.max(scores, axis=0, keepdims=True)
            value = jnp.concatenate([value_t[head_rows, pl.ds(at, block)], ones], axis=0).astype(jnp.bfloat16)
            if top is None:
                top = block_top
                probs = jnp.exp2(scores - top).astype(jnp.bfloat16)
                total = jnp.dot(value, probs, preferred_element_type=jnp.float32)
            else:
                new_top = jnp.maximum(top, block_top)
                fade = jnp.exp2(top - new_top)
                top = new_top
                probs = jnp.exp2(scores - top).astype(jnp.bfloat16)
                total = total * fade + jnp.dot(value, probs, preferred_element_type=jnp.float32)
        weight = total[HEAD_DIM : HEAD_DIM + 1]
        mixed_t[head_rows, :] = total[:HEAD_DIM] * (1.0 / weight)
        log_ref[pl.ds(head, 1), :] = top + jnp.log2(weight)

    @pl.loop(0, features // 128)
    def _(tile):
        columns = pl.ds(pl.multiple_of(tile * 128, 128), 128)
        mixed_ref[:, columns] = mixed_t[columns, :].T.astype(jnp.bfloat16)


def attention_forward(query, keyval, key_bias, features, shift, block):
    rows, length = query.shape[0], keyval.shape[0]
    return pl.pallas_call(
        functools.partial(attention_forward_kernel, features=features, shift=shift, block=block),
        out_shape=(
            jax.ShapeDtypeStruct((rows, features), jnp.bfloat16),
            jax.ShapeDtypeStruct((HEADS, rows), jnp.float32),
        ),
        scratch_shapes=[
            pltpu.VMEM((rows, features), jnp.bfloat16),
            pltpu.VMEM((features, length), jnp.float32),
            pltpu.VMEM((features, rows), jnp.float32),
        ],
        cost_estimate=expected(FORWARD_US),
        compiler_params=pltpu.CompilerParams(vmem_limit_bytes=56 * 2**20),
    )(query, keyval, key_bias)


MESH = pl.DeviceIdType.MESH


def exchange_rows(rows_ref, back_ref, send, recv, local_sem, *, bands):
    band = lax.axis_index("band")
    block = back_ref.shape[1]
    barrier = pltpu.get_barrier_semaphore()
    for step in range(1, bands):
        pl.semaphore_signal(
            barrier, inc=1, device_id={"band": lax.rem(band + step, bands)}, device_id_type=MESH
        )
    pl.semaphore_wait(barrier, bands - 1)

    def span(owner):
        return rows_ref.at[pl.ds(pl.multiple_of(owner * block, 16), block), :]

    def sent(step):
        target = lax.rem(band + step, bands)
        return pltpu.make_async_remote_copy(
            src_ref=span(target), dst_ref=back_ref.at[band],
            send_sem=send.at[step], recv_sem=recv.at[step],
            device_id={"band": target}, device_id_type=MESH,
        )

    keep = pltpu.make_async_copy(span(band), back_ref.at[band], local_sem)
    keep.start()
    for step in range(1, bands):
        sent(step).start()

    def finish():
        keep.wait()
        for step in range(1, bands):
            sent(step).wait_send()
            source = lax.rem(band + bands - step, bands)
            pltpu.make_async_remote_copy(
                src_ref=back_ref.at[source], dst_ref=back_ref.at[source],
                send_sem=send.at[step], recv_sem=recv.at[step],
                device_id={"band": source}, device_id_type=MESH,
            ).wait_recv()

    return finish


def attention_backward_kernel(
    query_ref, keyval_ref, bias_ref, mixed_ref, grad_ref, log_ref, out_ref, keyval_grad_ref,
    scaled, key_t, wide_t, *, features, shift, out_shift, block
):
    length = keyval_ref.shape[0]
    rows = mixed_ref.shape[0]
    scale = HEAD_DIM**-0.5
    scaled[...] = (query_ref[:, :features].astype(jnp.float32) * (scale * LOG2_E)).astype(jnp.bfloat16)

    @pl.loop(0, features // 128)
    def _(tile):
        columns = pl.ds(pl.multiple_of(tile * 128, 128), 128)
        key_t[columns, :] = keyval_ref[:, pl.ds(pl.multiple_of(shift + tile * 128, 128), 128)].astype(jnp.float32).T
        wide_t[columns, :] = (
            mixed_ref[:, columns].astype(jnp.float32) * grad_ref[:, columns].astype(jnp.float32)
        ).T

    @pl.loop(0, HEADS)
    def _(head):
        base, inside = head_window(head, features)
        head_rows = pl.ds(pl.multiple_of(head * HEAD_DIM, 8), HEAD_DIM)
        window = pl.ds(base, WINDOW)
        delta = jnp.sum(wide_t[head_rows, :], axis=0, keepdims=True)
        log_total = log_ref[pl.ds(head, 1), :]
        query = query_ref[:, window]
        query_scaled = scaled[:, window]
        grad = grad_ref[:, window]
        query_grad = None
        for at in range(0, length, block):
            here = pl.ds(at, block)
            key_window = pl.ds(pl.multiple_of(base + shift, 128), WINDOW)
            value_window = pl.ds(pl.multiple_of(base + shift + features, 128), WINDOW)
            key = keyval_ref[here, key_window]
            value = keyval_ref[here, value_window]
            key = jnp.where(inside, key, jnp.zeros_like(key))
            value = jnp.where(inside, value, jnp.zeros_like(value))
            scores = lax.dot_general(key, query_scaled, CONTRACT_LAST, preferred_element_type=jnp.float32)
            if at + block == length:
                scores = scores + bias_ref[here, :]
            probs = jnp.exp2(scores - log_total)
            prob_grad = lax.dot_general(value, grad, CONTRACT_LAST, preferred_element_type=jnp.float32)
            score_grad = (probs * (prob_grad - delta)).astype(jnp.bfloat16)
            value_grad = jnp.dot(probs.astype(jnp.bfloat16), grad, preferred_element_type=jnp.float32)
            key_grad = jnp.dot(score_grad, query, preferred_element_type=jnp.float32) * scale
            key_out = pl.ds(pl.multiple_of(base + out_shift, 128), WINDOW)
            value_out = pl.ds(pl.multiple_of(base + out_shift + features, 128), WINDOW)
            keyval_grad_ref[here, key_out] = jnp.where(inside, key_grad.astype(jnp.bfloat16), keyval_grad_ref[here, key_out])
            keyval_grad_ref[here, value_out] = jnp.where(inside, value_grad.astype(jnp.bfloat16), keyval_grad_ref[here, value_out])
            part = jnp.dot(
                key_t[head_rows, here].astype(jnp.bfloat16), score_grad, preferred_element_type=jnp.float32
            )
            query_grad = part if query_grad is None else query_grad + part
        wide_t[head_rows, :] = query_grad * scale

    @pl.loop(0, features // 128)
    def _(tile):
        columns = pl.ds(pl.multiple_of(tile * 128, 128), 128)
        out_ref[:, columns] = wide_t[columns, :].T.astype(jnp.bfloat16)


def attention_backward(
    query, keyval, key_bias, mixed, grad, log_total, features, block, exchanged, known, bands
):
    rows, length = query.shape[0], keyval.shape[0]
    shared = exchanged is not None
    scratch = [
        pltpu.VMEM((rows, features), jnp.bfloat16),
        pltpu.VMEM((features, length), jnp.float32),
        pltpu.VMEM((features, rows), jnp.float32),
    ]
    params = pltpu.CompilerParams(vmem_limit_bytes=56 * 2**20)
    if shared:

        def shared_kernel(both_ref, bias_ref, mixed_ref, grad_ref, log_ref, rows_ref, known_ref, out_ref, back_ref, kept_ref, *held):
            kept_ref[...] = known_ref[...]
            finish = exchange_rows(rows_ref, back_ref, *held[3:], bands=bands)
            attention_backward_kernel(
                both_ref, both_ref, bias_ref, mixed_ref, grad_ref, log_ref, out_ref, out_ref, *held[:3],
                features=features, shift=features, out_shift=features, block=block,
            )
            finish()

        anywhere, vmem = pl.BlockSpec(memory_space=pl.ANY), pl.BlockSpec(memory_space=pltpu.VMEM)
        return pl.pallas_call(
            shared_kernel,
            out_shape=(
                jax.ShapeDtypeStruct((rows, 3 * features), jnp.bfloat16),
                jax.ShapeDtypeStruct((bands, rows // bands, features), jnp.bfloat16),
                jax.ShapeDtypeStruct(known.shape, jnp.float32),
            ),
            in_specs=[vmem] * 5 + [anywhere, vmem],
            out_specs=(vmem, anywhere, vmem),
            scratch_shapes=scratch
            + [
                pltpu.SemaphoreType.DMA((bands,)),
                pltpu.SemaphoreType.DMA((bands,)),
                pltpu.SemaphoreType.DMA(()),
            ],
            cost_estimate=expected(BACKWARD_US),
            compiler_params=pltpu.CompilerParams(
                collective_id=2, has_side_effects=True, vmem_limit_bytes=56 * 2**20
            ),
        )(query, key_bias, mixed, grad, log_total, exchanged, known)
    return pl.pallas_call(
        functools.partial(
            attention_backward_kernel, features=features, shift=0, out_shift=0, block=block
        ),
        out_shape=(
            jax.ShapeDtypeStruct((rows, features), jnp.bfloat16),
            jax.ShapeDtypeStruct((length, 2 * features), jnp.bfloat16),
        ),
        scratch_shapes=scratch,
        compiler_params=params,
    )(query, keyval, key_bias, mixed, grad, log_total)


def flip(index, bit):
    return index + bit - 2 * bit * lax.rem(lax.div(index, bit), 2)


def start_kernel(
    wide_ref, tall_ref, tokens_ref, told_ref, ada_ref,
    qkv_ref, out_ref, up_ref, down_ref, rows_ref, heard_ref, silu_ref, mod_ref,
    partial, summed, banded, small_send, small_recv,
    held, turned, line_send, line_recv, row_send, row_recv, flat_send, flat_recv, local_sem,
    *, imgs, bands, qkv_part, out_part,
):
    img, band = lax.axis_index("img"), lax.axis_index("band")
    depth, width = wide_ref.shape
    tall_rows, tall_width = tall_ref.shape
    row_block = tokens_ref.shape[1]
    lanes = 128
    first = -(-(qkv_part + out_part) // lanes) * lanes
    beside_x, beside_y, sibling = flip(img, 2), flip(img, 4), flip(img, 1)
    across = flip(beside_x, 4)

    barrier = pltpu.get_barrier_semaphore()
    for step in range(1, imgs):
        other = lax.rem(img + step, imgs)
        pl.semaphore_signal(barrier, inc=1, device_id={"img": other}, device_id_type=MESH)
    for step in range(1, bands):
        pl.semaphore_signal(
            barrier, inc=1, device_id={"band": lax.rem(band + step, bands)}, device_id_type=MESH
        )
    pl.semaphore_wait(barrier, imgs + bands - 2)

    def piece(part, owner):
        if part == 2:
            return down_ref.at[:, pl.ds(pl.multiple_of(owner * tall_width, lanes), tall_width)]
        span = pl.ds(0, first) if part == 0 else pl.ds(first, width - first)
        return held.at[pl.ds(pl.multiple_of(owner * depth, 16), depth), span]

    def line_copy(part, way, step, owner, toward):
        view = piece(part, owner)
        return pltpu.make_async_remote_copy(
            src_ref=view, dst_ref=view,
            send_sem=line_send.at[part, way, step], recv_sem=line_recv.at[part, way, step],
            device_id={"band": toward}, device_id_type=MESH,
        )

    def line_sends(part, step, act):
        for way, sign in ((0, 1), (1, -1)):
            owner, toward = band - sign * step, band + sign

            @pl.when((owner >= 0) & (owner < bands) & (toward >= 0) & (toward < bands))
            def _():
                act(line_copy(part, way, step, owner, toward))

    def line_arrivals(part, step):
        for way, sign in ((0, 1), (1, -1)):
            owner = band - sign * (step + 1)

            @pl.when((owner >= 0) & (owner < bands))
            def _():
                line_copy(part, way, step, owner, band - sign).wait_recv()

    def row_copy(step):
        target = lax.rem(band + step, bands)
        return pltpu.make_async_remote_copy(
            src_ref=tokens_ref.at[target],
            dst_ref=rows_ref.at[pl.ds(pl.multiple_of(band * row_block, 16), row_block), :],
            send_sem=row_send.at[step - 1], recv_sem=row_recv.at[step - 1],
            device_id={"band": target}, device_id_type=MESH,
        )

    def row_arrival(step):
        source = lax.rem(band + bands - step, bands)
        view = rows_ref.at[pl.ds(pl.multiple_of(source * row_block, 16), row_block), :]
        return pltpu.make_async_remote_copy(
            src_ref=view, dst_ref=view,
            send_sem=row_send.at[step - 1], recv_sem=row_recv.at[step - 1],
            device_id={"band": source}, device_id_type=MESH,
        )

    def qkv_rows(owner, start=0, count=qkv_part):
        return qkv_ref.at[pl.ds(pl.multiple_of(owner * qkv_part + start, 16), count), :]

    def out_rows(owner):
        return out_ref.at[pl.ds(pl.multiple_of(owner * out_part, 16), out_part), :]

    half = (qkv_part + out_part) // 2
    own_qkv, own_out = turned.at[pl.ds(0, qkv_part), :], turned.at[pl.ds(qkv_part, out_part), :]
    plan = [
        (own_qkv, qkv_rows(img), beside_x, qkv_rows(beside_x)),
        (own_out, out_rows(img), beside_x, out_rows(beside_x)),
        (own_qkv, qkv_rows(img), beside_y, qkv_rows(beside_y)),
        (own_out, out_rows(img), beside_y, out_rows(beside_y)),
        (own_qkv, qkv_rows(img), sibling, qkv_rows(sibling)),
        (own_out, out_rows(img), sibling, out_rows(sibling)),
    ]
    for owner, toward, whole in ((beside_x, beside_y, True), (beside_y, beside_x, False)):
        if whole:
            view = qkv_rows(owner, 0, half)
            plan.append((view, view, toward, qkv_rows(across, 0, half)))
        else:
            rest = qkv_part - half
            view = qkv_rows(owner, half, rest)
            plan.append((view, view, toward, qkv_rows(across, half, rest)))
            plan.append((out_rows(owner), out_rows(owner), toward, out_rows(across)))
    for owner in (beside_x, beside_y):
        plan.append((qkv_rows(owner), qkv_rows(owner), sibling, qkv_rows(flip(owner, 1))))
        plan.append((out_rows(owner), out_rows(owner), sibling, out_rows(flip(owner, 1))))
    far = flip(across, 1)
    plan.append((qkv_rows(across, 0, half), qkv_rows(across, 0, half), sibling, qkv_rows(far, 0, half)))
    rest = qkv_part - half
    plan.append((qkv_rows(across, half, rest), qkv_rows(across, half, rest), sibling, qkv_rows(far, half, rest)))
    plan.append((out_rows(across), out_rows(across), sibling, out_rows(far)))

    def flat_copy(at):
        source, target, toward, _ = plan[at]
        return pltpu.make_async_remote_copy(
            src_ref=source, dst_ref=target, send_sem=flat_send.at[at], recv_sem=flat_recv.at[at],
            device_id={"img": toward}, device_id_type=MESH,
        )

    def flat_arrival(at):
        landing = plan[at][3]
        pltpu.make_async_remote_copy(
            src_ref=landing, dst_ref=landing, send_sem=flat_send.at[at], recv_sem=flat_recv.at[at],
            device_id={"img": sibling}, device_id_type=MESH,
        ).wait_recv()

    def turn(tile):
        span = pl.ds(pl.multiple_of(tile * lanes, lanes), lanes)
        turned[span, :] = held[:, span].astype(jnp.float32).T.astype(jnp.bfloat16)

    start = lambda copy: copy.start()
    own_rows = pltpu.make_async_copy(
        tokens_ref.at[band],
        rows_ref.at[pl.ds(pl.multiple_of(band * row_block, 16), row_block), :],
        local_sem.at[0],
    )
    own_rows.start()

    def small_copy(source, target, kind, step, axis, toward):
        return pltpu.make_async_remote_copy(
            src_ref=source, dst_ref=target,
            send_sem=small_send.at[kind, step], recv_sem=small_recv.at[kind, step],
            device_id={axis: toward}, device_id_type=MESH,
        )

    def told(step):
        return small_copy(told_ref, heard_ref.at[img], 0, step, "img", lax.rem(img + step, imgs))

    def partial_copy(step):
        other = lax.rem(img + step, imgs)
        return small_copy(partial.at[other], summed.at[img], 1, step, "img", other)

    def banded_copy(step):
        other = lax.rem(band + step, bands)
        return small_copy(summed.at[:, other], banded.at[band], 2, step, "band", other)

    def arrival(view, kind, step, axis):
        me, count = (img, imgs) if axis == "img" else (band, bands)
        small_copy(view, view, kind, step, axis, lax.rem(me + count - step, count)).wait_recv()

    for step in range(1, imgs):
        told(step).start()
    held[pl.ds(pl.multiple_of(band * depth, 16), depth), :] = wide_ref[...]
    down_ref[:, pl.ds(pl.multiple_of(band * tall_width, lanes), tall_width)] = tall_ref[...]
    line_sends(0, 0, start)
    heard_ref[img] = told_ref[...]
    for step in range(bands - 1):
        line_arrivals(0, step)
        if step < bands - 2:
            line_sends(0, step + 1, start)
    line_sends(1, 0, start)
    line_sends(2, 0, start)
    for step in range(1, bands):
        row_copy(step).start()
    pl.loop(0, first // lanes)(turn)
    keep_qkv = pltpu.make_async_copy(own_qkv, qkv_rows(img), local_sem.at[1])
    keep_out = pltpu.make_async_copy(own_out, out_rows(img), local_sem.at[2])
    for at in range(6):
        flat_copy(at).start()
    keep_qkv.start()
    keep_out.start()
    for step in range(1, imgs):
        arrival(heard_ref.at[lax.rem(img + imgs - step, imgs)], 0, step, "img")
    images = partial.shape[1]
    for other in range(imgs):
        for image in range(images):
            silu_ref[pl.ds(other * images + image, 1), :] = heard_ref[
                other, :, pl.ds(image * depth, depth)
            ]
    products = jnp.dot(
        silu_ref[...].astype(jnp.bfloat16), ada_ref[...], preferred_element_type=jnp.float32
    )
    for other in range(imgs):
        for image in range(images):
            at = other * images + image
            partial[other, image] = products[at : at + 1, :]
    for step in range(1, imgs):
        partial_copy(step).start()
    summed[img] = partial[img]
    for step in range(bands - 2):
        for part in (1, 2):
            line_arrivals(part, step)
            line_sends(part, step + 1, start)
    for arrived, sent in (((0, 1), (6, 9, 10)), ((2, 3), (7, 8, 11, 12))):
        for at in arrived:
            flat_arrival(at)
        for at in sent:
            flat_copy(at).start()
    for step in range(1, imgs):
        arrival(summed.at[lax.rem(img + imgs - step, imgs)], 1, step, "img")
    for step in range(1, bands):
        banded_copy(step).start()
    banded[band] = summed[:, band]
    for at in (6, 7, 8):
        flat_arrival(at)
        flat_copy(at + 7).start()
    for part in (1, 2):
        line_arrivals(part, bands - 2)
    pl.loop(first // lanes, width // lanes)(turn)
    up_ref[...] = turned[pl.ds(qkv_part + out_part, width - qkv_part - out_part), :]
    for step in range(1, bands):
        arrival(banded.at[lax.rem(band + bands - step, bands)], 2, step, "band")
    total = banded[0]
    for at in range(1, bands):
        total += banded[at]
    mod_ref[...] = total
    for part in range(3):
        for step in range(bands - 1):
            line_sends(part, step, lambda copy: copy.wait_send())
    for at in (4, 5, 9, 10, 11, 12, 13, 14, 15):
        flat_arrival(at)
    for at in range(16):
        flat_copy(at).wait_send()
    for step in range(1, bands):
        row_copy(step).wait_send()
        row_arrival(step).wait_recv()
        banded_copy(step).wait_send()
    for step in range(1, imgs):
        told(step).wait_send()
        partial_copy(step).wait_send()
    own_rows.wait()
    keep_qkv.wait()
    keep_out.wait()


def start_exchange(wide, tall, tokens, told, ada, bands, imgs, qkv_part, out_part):
    depth, width = wide.shape
    up_part = width - qkv_part - out_part
    low = jnp.bfloat16
    anywhere, vmem = pl.BlockSpec(memory_space=pl.ANY), pl.BlockSpec(memory_space=pltpu.VMEM)
    features = depth * bands
    images = tokens.shape[0]
    ada_columns = ada.shape[1]
    return pl.pallas_call(
        functools.partial(
            start_kernel, imgs=imgs, bands=bands, qkv_part=qkv_part, out_part=out_part
        ),
        out_shape=(
            jax.ShapeDtypeStruct((qkv_part * imgs, features), low),
            jax.ShapeDtypeStruct((out_part * imgs, features), low),
            jax.ShapeDtypeStruct((up_part, features), low),
            jax.ShapeDtypeStruct((tall.shape[0], tall.shape[1] * bands), low),
            jax.ShapeDtypeStruct((tokens.shape[1] * bands, tokens.shape[2]), low),
            jax.ShapeDtypeStruct((imgs,) + told.shape, jnp.float32),
            jax.ShapeDtypeStruct((imgs * images, depth), jnp.float32),
            jax.ShapeDtypeStruct((imgs, 1, ada_columns), jnp.float32),
        ),
        in_specs=[vmem, vmem, anywhere, vmem, vmem],
        out_specs=(anywhere, anywhere, vmem, vmem, anywhere, vmem, vmem, vmem),
        scratch_shapes=[
            pltpu.VMEM((imgs, images, 1, ada_columns), jnp.float32),
            pltpu.VMEM((imgs, images, 1, ada_columns), jnp.float32),
            pltpu.VMEM((bands, imgs, 1, ada_columns), jnp.float32),
            pltpu.SemaphoreType.DMA((3, imgs)),
            pltpu.SemaphoreType.DMA((3, imgs)),
            pltpu.VMEM((features, width), low),
            pltpu.VMEM((width, features), low),
            pltpu.SemaphoreType.DMA((3, 2, bands - 1)),
            pltpu.SemaphoreType.DMA((3, 2, bands - 1)),
            pltpu.SemaphoreType.DMA((bands - 1,)),
            pltpu.SemaphoreType.DMA((bands - 1,)),
            pltpu.SemaphoreType.DMA((16,)),
            pltpu.SemaphoreType.DMA((16,)),
            pltpu.SemaphoreType.DMA((3,)),
        ],
        cost_estimate=expected(START_US),
        compiler_params=pltpu.CompilerParams(
            collective_id=0, has_side_effects=True, vmem_limit_bytes=48 * 2**20
        ),
    )(wide, tall, tokens, told, ada)


def add_low(left, right):
    return (left.astype(jnp.float32) + right.astype(jnp.float32)).astype(jnp.bfloat16)


def tail_kernel(
    qkv_ref, out_ref, up_ref, rows_ref, pieces_ref, silu_ref, known_ref,
    wide_ref, back_ref, ada_ref, bias_ref, squares_ref,
    pieces, terms, square_flat, square_line, small_send, small_recv,
    own, from_core, first_x, first_y, last_x, last_y, turned, held, held_in,
    core_send, core_recv, flat_send, flat_recv, line_send, line_recv, row_send, row_recv, local_sem,
    *, imgs, bands,
):
    img, band = lax.axis_index("img"), lax.axis_index("band")
    qkv_part, out_part = qkv_ref.shape[0] // imgs, out_ref.shape[0] // imgs
    both = own.shape[1]
    depth, width = wide_ref.shape
    row_block = back_ref.shape[1]
    half = first_x.shape[1]
    lanes = 128
    beside_x, beside_y, sibling = flip(img, 2), flip(img, 4), flip(img, 1)
    chips = (img, beside_x, beside_y, flip(beside_x, 4))
    upper, lower = pl.ds(0, half), pl.ds(half, both - half)
    spans = (pl.ds(0, qkv_part), pl.ds(qkv_part, out_part))

    barrier = pltpu.get_barrier_semaphore()
    for step in range(1, imgs):
        other = lax.rem(img + step, imgs)
        pl.semaphore_signal(barrier, inc=1, device_id={"img": other}, device_id_type=MESH)
    for step in range(1, bands):
        pl.semaphore_signal(
            barrier, inc=1, device_id={"band": lax.rem(band + step, bands)}, device_id_type=MESH
        )
    pl.semaphore_wait(barrier, imgs + bands - 2)

    def grad_rows(kind, owner):
        source, count = ((qkv_ref, qkv_part), (out_ref, out_part))[kind]
        return source.at[pl.ds(pl.multiple_of(owner * count, 16), count), :]

    def core_copy(kind, at):
        return pltpu.make_async_remote_copy(
            src_ref=grad_rows(kind, flip(chips[at], 1)), dst_ref=from_core.at[at, spans[kind]],
            send_sem=core_send.at[kind, at], recv_sem=core_recv.at[kind, at],
            device_id={"img": sibling}, device_id_type=MESH,
        )

    def own_copy(kind, at):
        return pltpu.make_async_copy(
            grad_rows(kind, chips[at]), own.at[at, spans[kind]], local_sem.at[4 * kind + at]
        )

    plan = (
        (own.at[1, upper], first_x.at[0], beside_x),
        (own.at[3, upper], first_x.at[1], beside_x),
        (own.at[2, lower], first_y.at[0], beside_y),
        (own.at[3, lower], first_y.at[1], beside_y),
        (own.at[2, upper], last_y, beside_y),
        (own.at[1, lower], last_x, beside_x),
    )

    def flat_copy(at):
        source, target, toward = plan[at]
        return pltpu.make_async_remote_copy(
            src_ref=source, dst_ref=target, send_sem=flat_send.at[at], recv_sem=flat_recv.at[at],
            device_id={"img": toward}, device_id_type=MESH,
        )

    def row_span(owner):
        return pl.ds(pl.multiple_of(owner * row_block, 16), row_block)

    def row_copy(step):
        target = lax.rem(band + step, bands)
        return pltpu.make_async_remote_copy(
            src_ref=rows_ref.at[row_span(target), :], dst_ref=back_ref.at[band],
            send_sem=row_send.at[step - 1], recv_sem=row_recv.at[step - 1],
            device_id={"band": target}, device_id_type=MESH,
        )

    def row_arrival(step):
        source = lax.rem(band + bands - step, bands)
        return pltpu.make_async_remote_copy(
            src_ref=back_ref.at[source], dst_ref=back_ref.at[source],
            send_sem=row_send.at[step - 1], recv_sem=row_recv.at[step - 1],
            device_id={"band": source}, device_id_type=MESH,
        )

    first = -(-both // lanes) * lanes
    parts = (pl.ds(0, first), pl.ds(first, width - first))

    def piece(part, owner, way=None):
        down = pl.ds(pl.multiple_of(owner * depth, 16), depth)
        return held.at[down, parts[part]] if way is None else held_in.at[way, down, parts[part]]

    def line_copy(part, way, owner, toward):
        return pltpu.make_async_remote_copy(
            src_ref=piece(part, owner), dst_ref=piece(part, owner, way),
            send_sem=line_send.at[part, way, owner], recv_sem=line_recv.at[part, way, owner],
            device_id={"band": toward}, device_id_type=MESH,
        )

    def line_ends(part):
        for step in range(bands - 1):

            @pl.when(band == 0)
            def _():
                line_copy(part, 0, bands - 1 - step, band + 1).start()

            @pl.when(band == bands - 1)
            def _():
                line_copy(part, 1, step, band - 1).start()

    def line_round(part, step):
        for way, owner, sign in ((0, bands - 1 - step, 1), (1, step, -1)):

            @pl.when((sign * (owner - band) > 0) & (band > 0) & (band < bands - 1))
            def _():
                copy = line_copy(part, way, owner, band + sign)
                copy.wait_recv()
                mine = piece(part, owner)
                mine[...] = add_low(mine[...], piece(part, owner, way)[...])
                copy.start()

    def line_finish(part):
        span = parts[part]
        wide_ref[:, span] = piece(part, band)[...].astype(jnp.float32)
        for way, sign in ((0, 1), (1, -1)):

            @pl.when((band - sign >= 0) & (band - sign < bands))
            def _():
                line_copy(part, way, band, band - sign).wait_recv()
                wide_ref[:, span] += piece(part, band, way)[...].astype(jnp.float32)

    def line_sent(part):
        for way, sign in ((0, 1), (1, -1)):
            for owner in range(bands):

                @pl.when(sign * (owner - band) > 0)
                def _():
                    line_copy(part, way, owner, band + sign).wait_send()

    def turn(tile):
        span = pl.ds(pl.multiple_of(tile * lanes, lanes), lanes)
        held[:, span] = turned[span, :].astype(jnp.float32).T.astype(jnp.bfloat16)

    def small_copy(source, target, kind, step, axis, toward):
        return pltpu.make_async_remote_copy(
            src_ref=source, dst_ref=target,
            send_sem=small_send.at[kind, step], recv_sem=small_recv.at[kind, step],
            device_id={axis: toward}, device_id_type=MESH,
        )

    def piece_flat(step):
        other = lax.rem(img + step, imgs)
        return small_copy(pieces_ref.at[other], pieces.at[band, img], 0, step, "img", other)

    def piece_line(step):
        other = lax.rem(band + step, bands)
        return small_copy(pieces.at[band], pieces.at[band], 1, step, "band", other)

    def square_one(step):
        other = lax.rem(img + step, imgs)
        return small_copy(square_flat.at[img], square_flat.at[img], 2, step, "img", other)

    def square_two(step):
        other = lax.rem(band + step, bands)
        return small_copy(square_line.at[band], square_line.at[band], 3, step, "band", other)

    def arrival(view, kind, step, axis):
        me, count = (img, imgs) if axis == "img" else (band, bands)
        small_copy(view, view, kind, step, axis, lax.rem(me + count - step, count)).wait_recv()

    order = (3, 1, 2, 0)
    for step in range(1, imgs):
        piece_flat(step).start()
    keep_piece = pltpu.make_async_copy(pieces_ref.at[img], pieces.at[band, img], local_sem.at[9])
    keep_piece.start()
    for at in order:
        core_copy(0, at).start()
        core_copy(1, at).start()
    for at in order:
        own_copy(0, at).start()
        own_copy(1, at).start()
    keep = pltpu.make_async_copy(rows_ref.at[row_span(band), :], back_ref.at[band], local_sem.at[8])
    keep.start()
    turned[pl.ds(both, width - both), :] = up_ref[...]
    pl.loop(first // lanes, width // lanes)(turn)
    line_ends(1)
    for step in range(1, bands):
        row_copy(step).start()
    for at in order:
        for kind in range(2):
            own_copy(kind, at).wait()
            core_copy(kind, at).wait_recv()
        own[at] = add_low(own[at], from_core[at])
        for ready in {3: (1, 3), 1: (0,), 2: (2,), 0: ()}[at]:
            flat_copy(ready).start()
    keep_piece.wait()
    for step in range(1, imgs):
        arrival(pieces.at[band, lax.rem(img + imgs - step, imgs)], 0, step, "img")
    for step in range(1, bands):
        piece_line(step).start()
    flat_copy(1).wait_recv()
    own[2, upper] = add_low(own[2, upper], first_x[1])
    flat_copy(4).start()
    flat_copy(3).wait_recv()
    own[1, lower] = add_low(own[1, lower], first_y[1])
    flat_copy(5).start()
    line_round(1, 0)
    flat_copy(0).wait_recv()
    flat_copy(2).wait_recv()
    flat_copy(4).wait_recv()
    flat_copy(5).wait_recv()
    turned[upper, :] = (
        own[0, upper].astype(jnp.float32)
        + first_x[0].astype(jnp.float32)
        + last_y[...].astype(jnp.float32)
    ).astype(jnp.bfloat16)
    turned[lower, :] = (
        own[0, lower].astype(jnp.float32)
        + first_y[0].astype(jnp.float32)
        + last_x[...].astype(jnp.float32)
    ).astype(jnp.bfloat16)
    pl.loop(0, first // lanes)(turn)
    line_ends(0)
    for step in range(bands - 1):
        line_round(0, step)
        if step > 0:
            line_round(1, step)
    for step in range(1, bands):
        arrival(pieces.at[lax.rem(band + bands - step, bands)], 1, step, "band")
    for image in range(imgs):
        for at in range(bands):
            terms[pl.ds(image * bands + at, 1), :] = pieces[at, image]
    columns = ada_ref.shape[1]
    ada = lax.dot_general(
        silu_ref[...], terms[:, pl.ds(0, columns)], (((1,), (0,)), ((), ())),
        precision=lax.Precision.HIGHEST, preferred_element_type=jnp.float32,
    )
    ada_ref[...] = ada
    bias_rows, bias_columns = bias_ref.shape
    bias = jnp.sum(terms[:, pl.ds(columns, bias_rows * bias_columns)], axis=0, keepdims=True)
    for at in range(bias_rows):
        bias_ref[pl.ds(at, 1), :] = bias[:, at * bias_columns : (at + 1) * bias_columns]
    squares = jnp.sum(ada * ada, axis=0, keepdims=True)
    squares = jnp.sum(squares, axis=1, keepdims=True)
    squares += jnp.sum(bias * bias, axis=1, keepdims=True) / bands
    line_finish(1)
    line_finish(0)
    rows = jnp.sum(wide_ref[...] * wide_ref[...], axis=0, keepdims=True)
    squares += jnp.sum(rows, axis=1, keepdims=True) + known_ref[0:1, 0:1]
    square_flat[img] = jnp.broadcast_to(squares, square_flat.shape[1:])
    for step in range(1, imgs):
        square_one(step).start()
    for step in range(1, imgs):
        arrival(square_flat.at[lax.rem(img + imgs - step, imgs)], 2, step, "img")
    total = square_flat[0]
    for at in range(1, imgs):
        total += square_flat[at]
    square_line[band] = total
    for step in range(1, bands):
        square_two(step).start()
    for step in range(1, bands):
        arrival(square_line.at[lax.rem(band + bands - step, bands)], 3, step, "band")
    total = square_line[0]
    for at in range(1, bands):
        total += square_line[at]
    squares_ref[...] = total
    line_sent(0)
    line_sent(1)
    for step in range(1, imgs):
        piece_flat(step).wait_send()
        square_one(step).wait_send()
    for step in range(1, bands):
        piece_line(step).wait_send()
        square_two(step).wait_send()
    for at in range(4):
        core_copy(0, at).wait_send()
        core_copy(1, at).wait_send()
    for at in range(6):
        flat_copy(at).wait_send()
    for step in range(1, bands):
        row_copy(step).wait_send()
        row_arrival(step).wait_recv()
    keep.wait()


def tail_exchange(qkv_grad, out_grad, up_sum, rows, pieces, silu, known, bias_shape, bands, imgs):
    low = jnp.bfloat16
    features = qkv_grad.shape[1]
    both = (qkv_grad.shape[0] + out_grad.shape[0]) // imgs
    width = both + up_sum.shape[0]
    half = -(-both // 32) * 16
    ada_columns = pieces.shape[2] - bias_shape[0] * bias_shape[1]
    anywhere, vmem = pl.BlockSpec(memory_space=pl.ANY), pl.BlockSpec(memory_space=pltpu.VMEM)
    return pl.pallas_call(
        functools.partial(tail_kernel, imgs=imgs, bands=bands),
        out_shape=(
            jax.ShapeDtypeStruct((features // bands, width), jnp.float32),
            jax.ShapeDtypeStruct((bands, rows.shape[0] // bands, features), low),
            jax.ShapeDtypeStruct((silu.shape[0], ada_columns), jnp.float32),
            jax.ShapeDtypeStruct(bias_shape, jnp.float32),
            jax.ShapeDtypeStruct((8, 128), jnp.float32),
        ),
        in_specs=[anywhere, anywhere, vmem, anywhere, vmem, vmem, vmem],
        out_specs=(vmem, anywhere, vmem, vmem, vmem),
        scratch_shapes=[
            pltpu.VMEM((bands,) + pieces.shape, jnp.float32),
            pltpu.VMEM((bands * imgs, pieces.shape[2]), jnp.float32),
            pltpu.VMEM((imgs, 8, 128), jnp.float32),
            pltpu.VMEM((bands, 8, 128), jnp.float32),
            pltpu.SemaphoreType.DMA((4, imgs)),
            pltpu.SemaphoreType.DMA((4, imgs)),
            pltpu.VMEM((4, both, features), low),
            pltpu.VMEM((4, both, features), low),
            pltpu.VMEM((2, half, features), low),
            pltpu.VMEM((2, both - half, features), low),
            pltpu.VMEM((both - half, features), low),
            pltpu.VMEM((half, features), low),
            pltpu.VMEM((width, features), low),
            pltpu.VMEM((features, width), low),
            pltpu.VMEM((2, features, width), low),
            pltpu.SemaphoreType.DMA((2, 4)),
            pltpu.SemaphoreType.DMA((2, 4)),
            pltpu.SemaphoreType.DMA((6,)),
            pltpu.SemaphoreType.DMA((6,)),
            pltpu.SemaphoreType.DMA((2, 2, bands)),
            pltpu.SemaphoreType.DMA((2, 2, bands)),
            pltpu.SemaphoreType.DMA((bands - 1,)),
            pltpu.SemaphoreType.DMA((bands - 1,)),
            pltpu.SemaphoreType.DMA((10,)),
        ],
        cost_estimate=expected(TAIL_US),
        compiler_params=pltpu.CompilerParams(
            collective_id=1, has_side_effects=True, vmem_limit_bytes=50 * 2**20
        ),
    )(qkv_grad, out_grad, up_sum, rows, pieces, silu, known)


def adam_kernel(*refs):
    squares_ref, wide_ref, tall_ref, ada_ref, bias_ref = refs[:5]
    sources, results = refs[5:23], refs[23:]
    norm = jnp.sqrt(squares_ref[0:1, 0:1])
    factor = clip_norm / jnp.maximum(norm, clip_norm)
    qkv_part = sources[3].shape[1]
    both = qkv_part + sources[6].shape[1]
    rates = (learn_rate, learn_rate, out_rate, learn_rate, learn_rate, bias_rate)

    def update(which, rows, gradient):
        weight_ref, first_ref, second_ref = sources[3 * which : 3 * which + 3]
        new = adam_update(
            weight_ref[rows, :], first_ref[rows, :], second_ref[rows, :], gradient, factor, rates[which]
        )
        for into, value in zip(results[3 * which : 3 * which + 3], new):
            into[rows, :] = value

    depth = wide_ref.shape[0]
    block = next(rows for rows in (32, 16, 8) if depth % rows == 0)

    @pl.loop(0, depth // block)
    def _(step):
        rows = pl.ds(pl.multiple_of(step * block, block), block)
        update(0, rows, ada_ref[rows, :])
        update(1, rows, wide_ref[rows, :qkv_part])
        update(2, rows, wide_ref[rows, qkv_part:both])
        update(3, rows, wide_ref[rows, both:])

    tall_rows = tall_ref.shape[0]
    tall_block = 16 if tall_rows % 16 == 0 else tall_rows
    for start in range(0, tall_rows, tall_block):
        rows = pl.ds(start, tall_block)
        update(4, rows, tall_ref[rows, :])

    update(5, slice(None), bias_ref[...])
    results[18][...] = bias_ref[pl.ds(13, 1), :] * factor


def adam_all(squares, wide, tall, ada, bias, groups):
    flat = [array for group in groups for array in group]
    return pl.pallas_call(
        adam_kernel,
        out_shape=[jax.ShapeDtypeStruct(array.shape, jnp.float32) for array in flat]
        + [jax.ShapeDtypeStruct((1, bias.shape[1]), jnp.float32)],
        compiler_params=pltpu.CompilerParams(vmem_limit_bytes=50 * 2**20),
    )(squares, wide, tall, ada, bias, *flat)


def body(
    inputs,
    condition,
    valid_rows,
    cotangent,
    ada_weight,
    qkv_weight,
    out_weight,
    up_weight,
    down_weight,
    biases,
    ada_first,
    qkv_first,
    out_first,
    up_first,
    down_first,
    bias_first,
    ada_second,
    qkv_second,
    out_second,
    up_second,
    down_second,
    bias_second,
):
    images, local_rows, features = inputs.shape
    length = L
    head_count = HEADS
    head_size = HEAD_DIM
    score_scale = head_size ** (-0.5)
    band_count = lax.axis_size("band")
    img_count = lax.axis_size("img")
    band_rank = lax.axis_index("band")
    img_rank = lax.axis_index("img")
    own = max(1, images // band_count)
    split = max(1, band_count // images)
    mates = band_count // split
    image_rows = length // split
    exchange_groups = None
    share_groups = None
    if split > 1:
        exchange_groups = [[g * mates + m for m in range(mates)] for g in range(split)]
        share_groups = [[g * mates + m for g in range(split)] for m in range(mates)]
    low_type = jnp.bfloat16

    def to_images(rows):
        return lax.all_to_all(rows, "band", split_axis=0, concat_axis=1, axis_index_groups=exchange_groups, tiled=True)

    def to_bands(whole):
        cut = whole.reshape(own, mates, local_rows, features).transpose(1, 0, 2, 3)
        back = lax.all_to_all(
            cut, "band", split_axis=0, concat_axis=0, axis_index_groups=exchange_groups, tiled=True
        )
        return back.reshape(images, local_rows, features)

    def after(value, *earlier):
        return lax.optimization_barrier((value,) + earlier)[0]

    def sum_everywhere(partial):
        sent = jnp.broadcast_to(partial, (img_count * band_count, 128))
        got = lax.all_to_all(sent, ("img", "band"), split_axis=0, concat_axis=0, tiled=True)
        return jnp.sum(got[:, 0])

    qkv_part, out_part = qkv_weight.shape[1], out_weight.shape[1]

    bias_rows, bias_columns = biases.shape
    ada_rows, ada_columns = ada_weight.shape
    silu_own = lax.reduce_precision(jax.nn.silu(condition.astype(jnp.float32)), 8, 7)
    silu_own = lax.dynamic_slice_in_dim(silu_own, band_rank * ada_rows, ada_rows, axis=1)
    told = jnp.concatenate(
        [silu_own.reshape(1, -1), lax.reduce_precision(biases, 8, 7).reshape(1, -1)],
        axis=1,
    )
    ada_low = ada_weight.astype(low_type)
    wide = jnp.concatenate([qkv_weight, out_weight, up_weight], axis=1).astype(low_type)
    tall = down_weight.T.astype(low_type)
    if img_count == 8 and own == 1 and split == 1:
        qkv_full, out_full, up_rows, down_rows, tokens_low, heard, silu_rows, mod_summed = (
            start_exchange(
                wide, tall, inputs, told, ada_low, band_count, img_count, qkv_part, out_part
            )
        )
        tokens_low = tokens_low.reshape(own, image_rows, features)
        mod_summed = mod_summed.reshape(own, img_count * ada_columns)
    else:
        turned = lax.all_gather(wide, "band", axis=0, tiled=True).T
        qkv_full = lax.all_gather(turned[:qkv_part], "img", axis=0, tiled=True)
        out_full = lax.all_gather(
            turned[qkv_part : qkv_part + out_part], "img", axis=0, tiled=True
        )
        up_rows = turned[qkv_part + out_part :]
        down_rows = lax.all_gather(tall, "band", axis=1, tiled=True)
        tokens_low = to_images(inputs)
        heard = lax.all_gather(told, "img", axis=0, tiled=True)
        silu_rows = heard[:, : images * ada_rows].reshape(img_count * images, ada_rows)
        mod_partial = jnp.dot(
            silu_rows.astype(low_type), ada_low, preferred_element_type=jnp.float32
        )
        mod_sent = jnp.tile(
            mod_partial.reshape(img_count, 1, images * ada_columns), (1, split, 1)
        )
        mod_pieces = lax.all_to_all(
            mod_sent.reshape(img_count * band_count, own * ada_columns),
            ("img", "band"),
            split_axis=0,
            concat_axis=0,
            tiled=True,
        ).reshape(img_count, band_count, own, ada_columns)
        mod_summed = (
            jnp.sum(mod_pieces, axis=1).transpose(1, 0, 2).reshape(own, img_count * ada_columns)
        )
    up_full = lax.all_gather(up_rows, "img", axis=0, tiled=True)
    down_full = lax.all_gather(after(down_rows, up_rows), "img", axis=0, tiled=True)
    bias_vals = (
        heard.reshape(img_count, -1)[:, images * ada_rows :]
        .reshape(img_count, bias_rows, bias_columns)
        .transpose(1, 0, 2)
        .reshape(bias_rows, features)
    )
    modulation = mod_summed + bias_vals[0:6].reshape(-1)
    mod_parts = modulation.reshape(own, 6, 1, features)
    shift_one = mod_parts[:, 0]
    scale_one = mod_parts[:, 1]
    gate_one = mod_parts[:, 2]
    shift_two = mod_parts[:, 3]
    scale_two = mod_parts[:, 4]
    gate_two = mod_parts[:, 5]
    valid_own = lax.dynamic_slice_in_dim(valid_rows, lax.rem(band_rank, mates) * own, own, axis=0)
    key_mask = jnp.arange(length, dtype=jnp.int32)[None, :] < valid_own[:, None]
    positions = lax.div(band_rank, mates) * image_rows + jnp.arange(image_rows, dtype=jnp.int32)
    row_mask = (positions[None, :] < valid_own[:, None]).astype(jnp.float32)[:, :, None]
    tokens_in = tokens_low.astype(jnp.float32)
    normed_one, inverse_one = normalize_keep(tokens_in)
    first_in = (normed_one * (1.0 + scale_one) + shift_one).astype(jnp.bfloat16)
    cotangent_low = to_images(after(cotangent, tokens_low))
    grad_out = cotangent_low.astype(jnp.float32) * row_mask
    qkv_bias = jnp.concatenate([bias_vals[6], jnp.zeros((features,), jnp.float32), bias_vals[7]])
    projected = (
        jnp.einsum("ird,ed->ire", first_in, qkv_full, preferred_element_type=jnp.float32) + qkv_bias
    ).astype(jnp.bfloat16)
    key_bias = jnp.where(key_mask, 0.0, very_low).astype(jnp.float32)[:, :, None]
    queries = [projected[i] for i in range(own)]
    if split > 1:
        keys_values = lax.all_gather(
            projected[..., features:], "band", axis=1, axis_index_groups=share_groups, tiled=True
        )
        keys_values = [keys_values[i] for i in range(own)]
        key_shift = 0
    else:
        keys_values = queries
        key_shift = features
    mixed, log_total = zip(
        *[
            attention_forward(queries[i], keys_values[i], key_bias[i], features, key_shift, 512)
            for i in range(own)
        ]
    )
    mixed_parts = mixed
    mixed = jnp.stack(mixed)
    attended = (
        jnp.einsum("ird,ed->ire", mixed, out_full, preferred_element_type=jnp.float32)
        + bias_vals[8]
    )
    middle = tokens_in + gate_one * attended
    normed_two, inverse_two = normalize_keep(middle)
    second_in = (normed_two * (1.0 + scale_two) + shift_two).astype(jnp.bfloat16)
    hidden_pre = jnp.einsum(
        "ird,fd->irf", second_in, up_full, preferred_element_type=jnp.float32
    ) + bias_vals[9:13].reshape(-1)
    hidden, gelu_back = jax.vjp(smooth_gate, hidden_pre)
    hidden_low = hidden.astype(jnp.bfloat16)
    branch = (
        jnp.einsum("irf,df->ird", hidden_low, down_full, preferred_element_type=jnp.float32)
        + bias_vals[13]
    )
    output_low = (middle + gate_two * branch).astype(jnp.bfloat16)
    branch_grad = (gate_two * grad_out).astype(jnp.bfloat16)
    gate_two_grad = jnp.sum(grad_out * branch, axis=1)
    down_grad = jnp.einsum(
        "ird,irf->df", branch_grad, hidden_low, preferred_element_type=jnp.float32
    ).astype(low_type)
    down_sum = lax.psum_scatter(down_grad, "img", scatter_dimension=0, tiled=True)
    hidden_grad = jnp.einsum(
        "ird,df->irf",
        after(branch_grad, down_grad),
        down_full,
        preferred_element_type=jnp.float32,
    )
    pre_grad = gelu_back(hidden_grad)[0].astype(jnp.bfloat16)
    up_grad = jnp.einsum(
        "irf,ird->fd", pre_grad, second_in, preferred_element_type=jnp.float32
    ).astype(low_type)
    up_sum = lax.psum_scatter(up_grad, "img", scatter_dimension=0, tiled=True)
    second_grad = jnp.einsum("irf,fd->ird", after(pre_grad, up_grad), up_full, preferred_element_type=jnp.float32)
    shift_two_grad = jnp.sum(second_grad, axis=1)
    scale_two_grad = jnp.sum(second_grad * normed_two, axis=1)
    middle_grad = grad_out + normalize_back(
        normed_two, inverse_two, second_grad * (1.0 + scale_two)
    )
    attended_grad = (gate_one * middle_grad).astype(jnp.bfloat16)
    gate_one_grad = jnp.sum(middle_grad * attended, axis=1)
    out_grad = jnp.einsum(
        "ire,ird->ed", attended_grad, mixed, preferred_element_type=jnp.float32
    ).astype(low_type)
    mixed_grad = jnp.einsum(
        "ire,ed->ird", after(attended_grad, out_grad), out_full, preferred_element_type=jnp.float32
    ).astype(jnp.bfloat16)
    tall_cut = down_sum.reshape(down_sum.shape[0], band_count, -1).transpose(1, 0, 2)
    tall_shard = jnp.sum(
        lax.all_to_all(tall_cut, "band", split_axis=0, concat_axis=0, tiled=True).astype(jnp.float32),
        axis=0,
    )
    hosted = img_count == 8 and own == 1 and split == 1
    tall_squares = jnp.broadcast_to(jnp.sum(tall_shard * tall_shard), (8, 128))
    attention_grads = [
        attention_backward(
            queries[i], keys_values[i], key_bias[i], mixed_parts[i], mixed_grad[i], log_total[i],
            features, 512, output_low[i] if hosted else None, tall_squares, band_count,
        )
        for i in range(own)
    ]
    if hosted:
        output, tall_squares = attention_grads[0][1:]
    else:
        output = to_bands(output_low)
    if split > 1:
        shared_grads = lax.psum_scatter(
            jnp.stack([pair[1] for pair in attention_grads]),
            "band",
            scatter_dimension=1,
            axis_index_groups=share_groups,
            tiled=True,
        )
        qkv_grad = jnp.concatenate(
            [jnp.stack([pair[0] for pair in attention_grads]), shared_grads], axis=-1
        )
    elif hosted:
        qkv_grad = attention_grads[0][0][None]
    else:
        qkv_grad = jnp.stack([jnp.concatenate(pair, axis=-1) for pair in attention_grads])
    qkv_sums = jnp.sum(qkv_grad.astype(jnp.float32), axis=(0, 1))
    qkv_weight_grad = jnp.einsum(
        "ire,ird->ed", qkv_grad, first_in, preferred_element_type=jnp.float32
    ).astype(low_type)
    first_grad = jnp.einsum("ire,ed->ird", after(qkv_grad, qkv_weight_grad), qkv_full, preferred_element_type=jnp.float32)
    shift_one_grad = jnp.sum(first_grad, axis=1)
    scale_one_grad = jnp.sum(first_grad * normed_one, axis=1)
    input_grad_low = (
        middle_grad + normalize_back(normed_one, inverse_one, first_grad * (1.0 + scale_one))
    ).astype(low_type)
    mod_grad = jnp.stack(
        [
            shift_one_grad,
            scale_one_grad,
            gate_one_grad,
            shift_two_grad,
            scale_two_grad,
            gate_two_grad,
        ],
        axis=1,
    )
    row_sums = jnp.concatenate(
        [
            qkv_sums[:features][None],
            qkv_sums[2 * features :][None],
            jnp.sum(attended_grad.astype(jnp.float32), axis=(0, 1))[None],
            jnp.sum(pre_grad.astype(jnp.float32), axis=(0, 1)).reshape(4, features),
            jnp.sum(branch_grad.astype(jnp.float32), axis=(0, 1))[None],
        ],
        axis=0,
    )
    pieces = jnp.concatenate(
        [
            mod_grad.reshape(own, img_count, ada_columns)
            .transpose(1, 0, 2)
            .reshape(img_count, own * ada_columns),
            jnp.concatenate([jnp.sum(mod_grad, axis=0).reshape(6, features), row_sums], axis=0)
            .reshape(bias_rows, img_count, bias_columns)
            .transpose(1, 0, 2)
            .reshape(img_count, -1),
        ],
        axis=1,
    )
    silu_terms = jnp.tile(
        silu_rows.reshape(img_count, 1, images, ada_rows), (1, split, 1, 1)
    ).reshape(img_count * band_count * own, ada_rows)
    if img_count == 8 and own == 1 and split == 1:
        wide_shard, input_grad_low, ada_shard, bias_total, squares_total = tail_exchange(
            qkv_weight_grad,
            out_grad,
            up_sum,
            input_grad_low[0],
            pieces[:, None],
            silu_terms.T,
            tall_squares,
            biases.shape,
            band_count,
            img_count,
        )
    else:
        sent = jnp.broadcast_to(
            pieces[:, None], (img_count, band_count, pieces.shape[1])
        ).reshape(img_count * band_count, -1)
        got = lax.all_to_all(sent, ("img", "band"), split_axis=0, concat_axis=0, tiled=True)
        ada_shard = jnp.einsum(
            "id,ie->de",
            silu_terms,
            got[:, : own * ada_columns].reshape(-1, ada_columns),
            precision=lax.Precision.HIGHEST,
        )
        bias_total = jnp.sum(got[:, own * ada_columns :], axis=0).reshape(bias_rows, bias_columns)
        qkv_sum = lax.psum_scatter(qkv_weight_grad, "img", scatter_dimension=0, tiled=True)
        out_sum = lax.psum_scatter(out_grad, "img", scatter_dimension=0, tiled=True)
        wide_shard = lax.psum_scatter(
            jnp.concatenate([qkv_sum, out_sum, up_sum], axis=0).T,
            "band",
            scatter_dimension=0,
            tiled=True,
        ).astype(jnp.float32)
        input_grad_low = to_bands(input_grad_low)
        squares = tall_squares[0, 0] + jnp.sum(bias_total * bias_total) / band_count
        for shard_grad in (ada_shard, wide_shard):
            squares = squares + jnp.sum(shard_grad * shard_grad)
        squares_total = jnp.broadcast_to(sum_everywhere(squares), (8, 128))
    input_grad = input_grad_low.astype(jnp.float32)
    grad_norm = jnp.sqrt(squares_total[0, 0])
    groups = (
        (ada_weight, ada_first, ada_second),
        (qkv_weight, qkv_first, qkv_second),
        (out_weight, out_first, out_second),
        (up_weight, up_first, up_second),
        (down_weight.T, down_first.T, down_second.T),
        (biases, bias_first, bias_second),
    )
    updated = adam_all(squares_total, wide_shard, tall_shard, ada_shard, bias_total, groups)
    ada_new, ada_first_new, ada_second_new = updated[0:3]
    qkv_new, qkv_first_new, qkv_second_new = updated[3:6]
    out_new, out_first_new, out_second_new = updated[6:9]
    up_new, up_first_new, up_second_new = updated[9:12]
    down_new, down_first_new, down_second_new = (array.T for array in updated[12:15])
    bias_new, bias_first_new, bias_second_new = updated[15:18]
    branch_bias_grad = updated[18][0]
    return (
        output,
        input_grad,
        grad_norm,
        ada_new,
        qkv_new,
        out_new,
        up_new,
        down_new,
        bias_new,
        ada_first_new,
        qkv_first_new,
        out_first_new,
        up_first_new,
        down_first_new,
        bias_first_new,
        ada_second_new,
        qkv_second_new,
        out_second_new,
        up_second_new,
        down_second_new,
        bias_second_new,
        branch_bias_grad,
    )


def solution(mesh):
    return jax.shard_map(
        body,
        mesh=mesh,
        in_specs=(
            P("img", "band", None),
            P("img", None),
            P("img"),
            P("img", "band", None),
            P("band", "img"),
            P("band", "img"),
            P("band", "img"),
            P("band", "img"),
            P("band", "img"),
            P(None, "img"),
            P("band", "img"),
            P("band", "img"),
            P("band", "img"),
            P("band", "img"),
            P("band", "img"),
            P(None, "img"),
            P("band", "img"),
            P("band", "img"),
            P("band", "img"),
            P("band", "img"),
            P("band", "img"),
            P(None, "img"),
        ),
        out_specs=(
            P("img", "band", None),
            P("img", "band", None),
            P(),
            P("band", "img"),
            P("band", "img"),
            P("band", "img"),
            P("band", "img"),
            P("band", "img"),
            P(None, "img"),
            P("band", "img"),
            P("band", "img"),
            P("band", "img"),
            P("band", "img"),
            P("band", "img"),
            P(None, "img"),
            P("band", "img"),
            P("band", "img"),
            P("band", "img"),
            P("band", "img"),
            P("band", "img"),
            P(None, "img"),
            P("img"),
        ),
        check_vma=False,
    )
```

```python
import functools

import jax
import jax.numpy as jnp
from jax import lax
from jax.experimental import pallas as pl
from jax.experimental.pallas import tpu as pltpu
from jax.sharding import PartitionSpec as P

HEADS = 16
HEAD_DIM = 72
L = 1024
STEP = 10


norm_eps = 1e-06
beta_one = 0.9
beta_two = 0.999
adam_eps = 1e-08
learn_rate = 0.03
out_rate = 0.25
bias_rate = 0.4
clip_norm = 1.0
very_low = -1000000000.0


def normalize_keep(values):
    centre = values - jnp.mean(values, axis=-1, keepdims=True)
    inverse = lax.rsqrt(jnp.mean(centre * centre, axis=-1, keepdims=True) + norm_eps)
    return (centre * inverse, inverse)


def normalize_back(normed, inverse, incoming):
    return inverse * (
        incoming
        - jnp.mean(incoming, axis=-1, keepdims=True)
        - normed * jnp.mean(incoming * normed, axis=-1, keepdims=True)
    )


def smooth_gate(values):
    return jax.nn.gelu(values, approximate=True)


def adam_update(weight, first_old, second_old, gradient, factor, rate):
    clipped = gradient * factor
    first_new = beta_one * first_old + (1.0 - beta_one) * clipped
    second_new = beta_two * second_old + (1.0 - beta_two) * clipped * clipped
    first_hat = first_new / (1.0 - beta_one**STEP)
    second_hat = second_new / (1.0 - beta_two**STEP)
    return (weight - rate * first_hat / (jnp.sqrt(second_hat) + adam_eps), first_new, second_new)


WINDOW = 256
CONTRACT_LAST = (((1,), (1,)), ((), ()))
LOG2_E = 1.4426950408889634


FORWARD_US, BACKWARD_US, START_US, TAIL_US = 37, 57, 115, 110


def expected(microseconds):
    moved = int(microseconds * 3.2e6)
    return pl.CostEstimate(flops=0, bytes_accessed=moved, transcendentals=0)


def head_window(head, features):
    start = head * HEAD_DIM
    base = pl.multiple_of(jnp.minimum(start // 128 * 128, features - WINDOW), 128)
    lane = lax.broadcasted_iota(jnp.int32, (1, WINDOW), 1)
    inside = (lane >= start - base) & (lane < start - base + HEAD_DIM)
    return base, inside


def attention_forward_kernel(
    query_ref, keyval_ref, bias_ref, mixed_ref, log_ref, scaled, value_t, mixed_t, *, features, shift, block
):
    length = keyval_ref.shape[0]
    rows = mixed_ref.shape[0]
    scaled[...] = (query_ref[:, :features].astype(jnp.float32) * (HEAD_DIM**-0.5 * LOG2_E)).astype(
        jnp.bfloat16
    )

    @pl.loop(0, features // 128)
    def _(tile):
        columns = pl.ds(pl.multiple_of(tile * 128, 128), 128)
        source = pl.ds(pl.multiple_of(shift + features + tile * 128, 128), 128)
        value_t[columns, :] = keyval_ref[:, source].astype(jnp.float32).T

    @pl.loop(0, HEADS)
    def _(head):
        base, inside = head_window(head, features)
        head_rows = pl.ds(pl.multiple_of(head * HEAD_DIM, 8), HEAD_DIM)
        query = scaled[:, pl.ds(base, WINDOW)]
        ones = jnp.ones((8, block), jnp.float32)
        top = None
        for at in range(0, length, block):
            key = keyval_ref[pl.ds(at, block), pl.ds(pl.multiple_of(base + shift, 128), WINDOW)]
            key = jnp.where(inside, key, jnp.zeros_like(key))
            scores = lax.dot_general(key, query, CONTRACT_LAST, preferred_element_type=jnp.float32)
            if at + block == length:
                scores = scores + bias_ref[pl.ds(at, block), :]
            block_top = jnp.max(scores, axis=0, keepdims=True)
            value = jnp.concatenate([value_t[head_rows, pl.ds(at, block)], ones], axis=0).astype(jnp.bfloat16)
            if top is None:
                top = block_top
                probs = jnp.exp2(scores - top).astype(jnp.bfloat16)
                total = jnp.dot(value, probs, preferred_element_type=jnp.float32)
            else:
                new_top = jnp.maximum(top, block_top)
                fade = jnp.exp2(top - new_top)
                top = new_top
                probs = jnp.exp2(scores - top).astype(jnp.bfloat16)
                total = total * fade + jnp.dot(value, probs, preferred_element_type=jnp.float32)
        weight = total[HEAD_DIM : HEAD_DIM + 1]
        mixed_t[head_rows, :] = total[:HEAD_DIM] * (1.0 / weight)
        log_ref[pl.ds(head, 1), :] = top + jnp.log2(weight)

    @pl.loop(0, features // 128)
    def _(tile):
        columns = pl.ds(pl.multiple_of(tile * 128, 128), 128)
        mixed_ref[:, columns] = mixed_t[columns, :].T.astype(jnp.bfloat16)


def attention_forward(query, keyval, key_bias, features, shift, block):
    rows, length = query.shape[0], keyval.shape[0]
    return pl.pallas_call(
        functools.partial(attention_forward_kernel, features=features, shift=shift, block=block),
        out_shape=(
            jax.ShapeDtypeStruct((rows, features), jnp.bfloat16),
            jax.ShapeDtypeStruct((HEADS, rows), jnp.float32),
        ),
        scratch_shapes=[
            pltpu.VMEM((rows, features), jnp.bfloat16),
            pltpu.VMEM((features, length), jnp.float32),
            pltpu.VMEM((features, rows), jnp.float32),
        ],
        cost_estimate=expected(FORWARD_US),
        compiler_params=pltpu.CompilerParams(vmem_limit_bytes=56 * 2**20),
    )(query, keyval, key_bias)


MESH = pl.DeviceIdType.MESH


def exchange_rows(rows_ref, back_ref, send, recv, local_sem, *, bands):
    band = lax.axis_index("band")
    block = back_ref.shape[1]
    barrier = pltpu.get_barrier_semaphore()
    for step in range(1, bands):
        pl.semaphore_signal(
            barrier, inc=1, device_id={"band": lax.rem(band + step, bands)}, device_id_type=MESH
        )
    pl.semaphore_wait(barrier, bands - 1)

    def span(owner):
        return rows_ref.at[pl.ds(pl.multiple_of(owner * block, 16), block), :]

    def sent(step):
        target = lax.rem(band + step, bands)
        return pltpu.make_async_remote_copy(
            src_ref=span(target), dst_ref=back_ref.at[band],
            send_sem=send.at[step], recv_sem=recv.at[step],
            device_id={"band": target}, device_id_type=MESH,
        )

    keep = pltpu.make_async_copy(span(band), back_ref.at[band], local_sem)
    keep.start()
    for step in range(1, bands):
        sent(step).start()

    def finish():
        keep.wait()
        for step in range(1, bands):
            sent(step).wait_send()
            source = lax.rem(band + bands - step, bands)
            pltpu.make_async_remote_copy(
                src_ref=back_ref.at[source], dst_ref=back_ref.at[source],
                send_sem=send.at[step], recv_sem=recv.at[step],
                device_id={"band": source}, device_id_type=MESH,
            ).wait_recv()

    return finish


def attention_backward_kernel(
    query_ref, keyval_ref, bias_ref, mixed_ref, grad_ref, log_ref, out_ref, keyval_grad_ref,
    scaled, key_t, wide_t, *, features, shift, out_shift, block
):
    length = keyval_ref.shape[0]
    rows = mixed_ref.shape[0]
    scale = HEAD_DIM**-0.5
    scaled[...] = (query_ref[:, :features].astype(jnp.float32) * (scale * LOG2_E)).astype(jnp.bfloat16)

    @pl.loop(0, features // 128)
    def _(tile):
        columns = pl.ds(pl.multiple_of(tile * 128, 128), 128)
        key_t[columns, :] = keyval_ref[:, pl.ds(pl.multiple_of(shift + tile * 128, 128), 128)].astype(jnp.float32).T
        wide_t[columns, :] = (
            mixed_ref[:, columns].astype(jnp.float32) * grad_ref[:, columns].astype(jnp.float32)
        ).T

    @pl.loop(0, HEADS)
    def _(head):
        base, inside = head_window(head, features)
        head_rows = pl.ds(pl.multiple_of(head * HEAD_DIM, 8), HEAD_DIM)
        window = pl.ds(base, WINDOW)
        delta = jnp.sum(wide_t[head_rows, :], axis=0, keepdims=True)
        log_total = log_ref[pl.ds(head, 1), :]
        query = query_ref[:, window]
        query_scaled = scaled[:, window]
        grad = grad_ref[:, window]
        query_grad = None
        for at in range(0, length, block):
            here = pl.ds(at, block)
            key_window = pl.ds(pl.multiple_of(base + shift, 128), WINDOW)
            value_window = pl.ds(pl.multiple_of(base + shift + features, 128), WINDOW)
            key = keyval_ref[here, key_window]
            value = keyval_ref[here, value_window]
            key = jnp.where(inside, key, jnp.zeros_like(key))
            value = jnp.where(inside, value, jnp.zeros_like(value))
            scores = lax.dot_general(key, query_scaled, CONTRACT_LAST, preferred_element_type=jnp.float32)
            if at + block == length:
                scores = scores + bias_ref[here, :]
            probs = jnp.exp2(scores - log_total)
            prob_grad = lax.dot_general(value, grad, CONTRACT_LAST, preferred_element_type=jnp.float32)
            score_grad = (probs * (prob_grad - delta)).astype(jnp.bfloat16)
            value_grad = jnp.dot(probs.astype(jnp.bfloat16), grad, preferred_element_type=jnp.float32)
            key_grad = jnp.dot(score_grad, query, preferred_element_type=jnp.float32) * scale
            key_out = pl.ds(pl.multiple_of(base + out_shift, 128), WINDOW)
            value_out = pl.ds(pl.multiple_of(base + out_shift + features, 128), WINDOW)
            keyval_grad_ref[here, key_out] = jnp.where(inside, key_grad.astype(jnp.bfloat16), keyval_grad_ref[here, key_out])
            keyval_grad_ref[here, value_out] = jnp.where(inside, value_grad.astype(jnp.bfloat16), keyval_grad_ref[here, value_out])
            part = jnp.dot(
                key_t[head_rows, here].astype(jnp.bfloat16), score_grad, preferred_element_type=jnp.float32
            )
            query_grad = part if query_grad is None else query_grad + part
        wide_t[head_rows, :] = query_grad * scale

    @pl.loop(0, features // 128)
    def _(tile):
        columns = pl.ds(pl.multiple_of(tile * 128, 128), 128)
        out_ref[:, columns] = wide_t[columns, :].T.astype(jnp.bfloat16)


def attention_backward(
    query, keyval, key_bias, mixed, grad, log_total, features, block, exchanged, bands
):
    rows, length = query.shape[0], keyval.shape[0]
    shared = exchanged is not None
    scratch = [
        pltpu.VMEM((rows, features), jnp.bfloat16),
        pltpu.VMEM((features, length), jnp.float32),
        pltpu.VMEM((features, rows), jnp.float32),
    ]
    params = pltpu.CompilerParams(vmem_limit_bytes=56 * 2**20)
    if shared:

        def shared_kernel(both_ref, bias_ref, mixed_ref, grad_ref, log_ref, rows_ref, out_ref, back_ref, *held):
            finish = exchange_rows(rows_ref, back_ref, *held[3:], bands=bands)
            attention_backward_kernel(
                both_ref, both_ref, bias_ref, mixed_ref, grad_ref, log_ref, out_ref, out_ref, *held[:3],
                features=features, shift=features, out_shift=features, block=block,
            )
            finish()

        anywhere, vmem = pl.BlockSpec(memory_space=pl.ANY), pl.BlockSpec(memory_space=pltpu.VMEM)
        return pl.pallas_call(
            shared_kernel,
            out_shape=(
                jax.ShapeDtypeStruct((rows, 3 * features), jnp.bfloat16),
                jax.ShapeDtypeStruct((bands, rows // bands, features), jnp.bfloat16),
            ),
            in_specs=[vmem] * 5 + [anywhere],
            out_specs=(vmem, anywhere),
            scratch_shapes=scratch
            + [
                pltpu.SemaphoreType.DMA((bands,)),
                pltpu.SemaphoreType.DMA((bands,)),
                pltpu.SemaphoreType.DMA(()),
            ],
            cost_estimate=expected(BACKWARD_US),
            compiler_params=pltpu.CompilerParams(
                collective_id=2, has_side_effects=True, vmem_limit_bytes=56 * 2**20
            ),
        )(query, key_bias, mixed, grad, log_total, exchanged)
    return pl.pallas_call(
        functools.partial(
            attention_backward_kernel, features=features, shift=0, out_shift=0, block=block
        ),
        out_shape=(
            jax.ShapeDtypeStruct((rows, features), jnp.bfloat16),
            jax.ShapeDtypeStruct((length, 2 * features), jnp.bfloat16),
        ),
        scratch_shapes=scratch,
        compiler_params=params,
    )(query, keyval, key_bias, mixed, grad, log_total)


def flip(index, bit):
    return index + bit - 2 * bit * lax.rem(lax.div(index, bit), 2)


def start_kernel(
    wide_ref, tall_ref, tokens_ref, told_ref, ada_ref,
    qkv_ref, out_ref, up_ref, down_ref, rows_ref, heard_ref, silu_ref, mod_ref,
    partial, summed, banded, small_send, small_recv,
    held, turned, line_send, line_recv, row_send, row_recv, flat_send, flat_recv, local_sem,
    *, imgs, bands, qkv_part, out_part,
):
    img, band = lax.axis_index("img"), lax.axis_index("band")
    depth, width = wide_ref.shape
    tall_rows, tall_width = tall_ref.shape
    row_block = tokens_ref.shape[1]
    lanes = 128
    first = -(-(qkv_part + out_part) // lanes) * lanes
    beside_x, beside_y, sibling = flip(img, 2), flip(img, 4), flip(img, 1)
    across = flip(beside_x, 4)

    barrier = pltpu.get_barrier_semaphore()
    for step in range(1, imgs):
        other = lax.rem(img + step, imgs)
        pl.semaphore_signal(barrier, inc=1, device_id={"img": other}, device_id_type=MESH)
    for step in range(1, bands):
        pl.semaphore_signal(
            barrier, inc=1, device_id={"band": lax.rem(band + step, bands)}, device_id_type=MESH
        )
    pl.semaphore_wait(barrier, imgs + bands - 2)

    def piece(part, owner):
        if part == 2:
            return down_ref.at[:, pl.ds(pl.multiple_of(owner * tall_width, lanes), tall_width)]
        span = pl.ds(0, first) if part == 0 else pl.ds(first, width - first)
        return held.at[pl.ds(pl.multiple_of(owner * depth, 16), depth), span]

    def line_copy(part, way, step, owner, toward):
        view = piece(part, owner)
        return pltpu.make_async_remote_copy(
            src_ref=view, dst_ref=view,
            send_sem=line_send.at[part, way, step], recv_sem=line_recv.at[part, way, step],
            device_id={"band": toward}, device_id_type=MESH,
        )

    def line_sends(part, step, act):
        for way, sign in ((0, 1), (1, -1)):
            owner, toward = band - sign * step, band + sign

            @pl.when((owner >= 0) & (owner < bands) & (toward >= 0) & (toward < bands))
            def _():
                act(line_copy(part, way, step, owner, toward))

    def line_arrivals(part, step):
        for way, sign in ((0, 1), (1, -1)):
            owner = band - sign * (step + 1)

            @pl.when((owner >= 0) & (owner < bands))
            def _():
                line_copy(part, way, step, owner, band - sign).wait_recv()

    def row_copy(step):
        target = lax.rem(band + step, bands)
        return pltpu.make_async_remote_copy(
            src_ref=tokens_ref.at[target],
            dst_ref=rows_ref.at[pl.ds(pl.multiple_of(band * row_block, 16), row_block), :],
            send_sem=row_send.at[step - 1], recv_sem=row_recv.at[step - 1],
            device_id={"band": target}, device_id_type=MESH,
        )

    def row_arrival(step):
        source = lax.rem(band + bands - step, bands)
        view = rows_ref.at[pl.ds(pl.multiple_of(source * row_block, 16), row_block), :]
        return pltpu.make_async_remote_copy(
            src_ref=view, dst_ref=view,
            send_sem=row_send.at[step - 1], recv_sem=row_recv.at[step - 1],
            device_id={"band": source}, device_id_type=MESH,
        )

    def qkv_rows(owner, start=0, count=qkv_part):
        return qkv_ref.at[pl.ds(pl.multiple_of(owner * qkv_part + start, 16), count), :]

    def out_rows(owner):
        return out_ref.at[pl.ds(pl.multiple_of(owner * out_part, 16), out_part), :]

    half = (qkv_part + out_part) // 2
    own_qkv, own_out = turned.at[pl.ds(0, qkv_part), :], turned.at[pl.ds(qkv_part, out_part), :]
    plan = [
        (own_qkv, qkv_rows(img), beside_x, qkv_rows(beside_x)),
        (own_out, out_rows(img), beside_x, out_rows(beside_x)),
        (own_qkv, qkv_rows(img), beside_y, qkv_rows(beside_y)),
        (own_out, out_rows(img), beside_y, out_rows(beside_y)),
        (own_qkv, qkv_rows(img), sibling, qkv_rows(sibling)),
        (own_out, out_rows(img), sibling, out_rows(sibling)),
    ]
    for owner, toward, whole in ((beside_x, beside_y, True), (beside_y, beside_x, False)):
        if whole:
            view = qkv_rows(owner, 0, half)
            plan.append((view, view, toward, qkv_rows(across, 0, half)))
        else:
            rest = qkv_part - half
            view = qkv_rows(owner, half, rest)
            plan.append((view, view, toward, qkv_rows(across, half, rest)))
            plan.append((out_rows(owner), out_rows(owner), toward, out_rows(across)))
    for owner in (beside_x, beside_y):
        plan.append((qkv_rows(owner), qkv_rows(owner), sibling, qkv_rows(flip(owner, 1))))
        plan.append((out_rows(owner), out_rows(owner), sibling, out_rows(flip(owner, 1))))
    far = flip(across, 1)
    plan.append((qkv_rows(across, 0, half), qkv_rows(across, 0, half), sibling, qkv_rows(far, 0, half)))
    rest = qkv_part - half
    plan.append((qkv_rows(across, half, rest), qkv_rows(across, half, rest), sibling, qkv_rows(far, half, rest)))
    plan.append((out_rows(across), out_rows(across), sibling, out_rows(far)))

    def flat_copy(at):
        source, target, toward, _ = plan[at]
        return pltpu.make_async_remote_copy(
            src_ref=source, dst_ref=target, send_sem=flat_send.at[at], recv_sem=flat_recv.at[at],
            device_id={"img": toward}, device_id_type=MESH,
        )

    def flat_arrival(at):
        landing = plan[at][3]
        pltpu.make_async_remote_copy(
            src_ref=landing, dst_ref=landing, send_sem=flat_send.at[at], recv_sem=flat_recv.at[at],
            device_id={"img": sibling}, device_id_type=MESH,
        ).wait_recv()

    def turn(tile):
        span = pl.ds(pl.multiple_of(tile * lanes, lanes), lanes)
        turned[span, :] = held[:, span].astype(jnp.float32).T.astype(jnp.bfloat16)

    start = lambda copy: copy.start()
    own_rows = pltpu.make_async_copy(
        tokens_ref.at[band],
        rows_ref.at[pl.ds(pl.multiple_of(band * row_block, 16), row_block), :],
        local_sem.at[0],
    )
    own_rows.start()

    def small_copy(source, target, kind, step, axis, toward):
        return pltpu.make_async_remote_copy(
            src_ref=source, dst_ref=target,
            send_sem=small_send.at[kind, step], recv_sem=small_recv.at[kind, step],
            device_id={axis: toward}, device_id_type=MESH,
        )

    def told(step):
        return small_copy(told_ref, heard_ref.at[img], 0, step, "img", lax.rem(img + step, imgs))

    def partial_copy(step):
        other = lax.rem(img + step, imgs)
        return small_copy(partial.at[other], summed.at[img], 1, step, "img", other)

    def banded_copy(step):
        other = lax.rem(band + step, bands)
        return small_copy(summed.at[:, other], banded.at[band], 2, step, "band", other)

    def arrival(view, kind, step, axis):
        me, count = (img, imgs) if axis == "img" else (band, bands)
        small_copy(view, view, kind, step, axis, lax.rem(me + count - step, count)).wait_recv()

    for step in range(1, imgs):
        told(step).start()
    held[pl.ds(pl.multiple_of(band * depth, 16), depth), :] = wide_ref[...]
    down_ref[:, pl.ds(pl.multiple_of(band * tall_width, lanes), tall_width)] = tall_ref[...]
    line_sends(0, 0, start)
    heard_ref[img] = told_ref[...]
    for step in range(bands - 1):
        line_arrivals(0, step)
        if step < bands - 2:
            line_sends(0, step + 1, start)
    line_sends(1, 0, start)
    line_sends(2, 0, start)
    for step in range(1, bands):
        row_copy(step).start()
    pl.loop(0, first // lanes)(turn)
    keep_qkv = pltpu.make_async_copy(own_qkv, qkv_rows(img), local_sem.at[1])
    keep_out = pltpu.make_async_copy(own_out, out_rows(img), local_sem.at[2])
    for at in range(6):
        flat_copy(at).start()
    keep_qkv.start()
    keep_out.start()
    for step in range(1, imgs):
        arrival(heard_ref.at[lax.rem(img + imgs - step, imgs)], 0, step, "img")
    images = partial.shape[1]
    for other in range(imgs):
        for image in range(images):
            silu_ref[pl.ds(other * images + image, 1), :] = heard_ref[
                other, :, pl.ds(image * depth, depth)
            ]
    products = jnp.dot(
        silu_ref[...].astype(jnp.bfloat16), ada_ref[...], preferred_element_type=jnp.float32
    )
    for other in range(imgs):
        for image in range(images):
            at = other * images + image
            partial[other, image] = products[at : at + 1, :]
    for step in range(1, imgs):
        partial_copy(step).start()
    summed[img] = partial[img]
    for step in range(bands - 2):
        for part in (1, 2):
            line_arrivals(part, step)
            line_sends(part, step + 1, start)
    for arrived, sent in (((0, 1), (6, 9, 10)), ((2, 3), (7, 8, 11, 12))):
        for at in arrived:
            flat_arrival(at)
        for at in sent:
            flat_copy(at).start()
    for step in range(1, imgs):
        arrival(summed.at[lax.rem(img + imgs - step, imgs)], 1, step, "img")
    for step in range(1, bands):
        banded_copy(step).start()
    banded[band] = summed[:, band]
    for at in (6, 7, 8):
        flat_arrival(at)
        flat_copy(at + 7).start()
    for part in (1, 2):
        line_arrivals(part, bands - 2)
    pl.loop(first // lanes, width // lanes)(turn)
    up_ref[...] = turned[pl.ds(qkv_part + out_part, width - qkv_part - out_part), :]
    for step in range(1, bands):
        arrival(banded.at[lax.rem(band + bands - step, bands)], 2, step, "band")
    total = banded[0]
    for at in range(1, bands):
        total += banded[at]
    mod_ref[...] = total
    for part in range(3):
        for step in range(bands - 1):
            line_sends(part, step, lambda copy: copy.wait_send())
    for at in (4, 5, 9, 10, 11, 12, 13, 14, 15):
        flat_arrival(at)
    for at in range(16):
        flat_copy(at).wait_send()
    for step in range(1, bands):
        row_copy(step).wait_send()
        row_arrival(step).wait_recv()
        banded_copy(step).wait_send()
    for step in range(1, imgs):
        told(step).wait_send()
        partial_copy(step).wait_send()
    own_rows.wait()
    keep_qkv.wait()
    keep_out.wait()


def start_exchange(wide, tall, tokens, told, ada, bands, imgs, qkv_part, out_part):
    depth, width = wide.shape
    up_part = width - qkv_part - out_part
    low = jnp.bfloat16
    anywhere, vmem = pl.BlockSpec(memory_space=pl.ANY), pl.BlockSpec(memory_space=pltpu.VMEM)
    features = depth * bands
    images = tokens.shape[0]
    ada_columns = ada.shape[1]
    return pl.pallas_call(
        functools.partial(
            start_kernel, imgs=imgs, bands=bands, qkv_part=qkv_part, out_part=out_part
        ),
        out_shape=(
            jax.ShapeDtypeStruct((qkv_part * imgs, features), low),
            jax.ShapeDtypeStruct((out_part * imgs, features), low),
            jax.ShapeDtypeStruct((up_part, features), low),
            jax.ShapeDtypeStruct((tall.shape[0], tall.shape[1] * bands), low),
            jax.ShapeDtypeStruct((tokens.shape[1] * bands, tokens.shape[2]), low),
            jax.ShapeDtypeStruct((imgs,) + told.shape, jnp.float32),
            jax.ShapeDtypeStruct((imgs * images, depth), jnp.float32),
            jax.ShapeDtypeStruct((imgs, 1, ada_columns), jnp.float32),
        ),
        in_specs=[vmem, vmem, anywhere, vmem, vmem],
        out_specs=(anywhere, anywhere, vmem, vmem, anywhere, vmem, vmem, vmem),
        scratch_shapes=[
            pltpu.VMEM((imgs, images, 1, ada_columns), jnp.float32),
            pltpu.VMEM((imgs, images, 1, ada_columns), jnp.float32),
            pltpu.VMEM((bands, imgs, 1, ada_columns), jnp.float32),
            pltpu.SemaphoreType.DMA((3, imgs)),
            pltpu.SemaphoreType.DMA((3, imgs)),
            pltpu.VMEM((features, width), low),
            pltpu.VMEM((width, features), low),
            pltpu.SemaphoreType.DMA((3, 2, bands - 1)),
            pltpu.SemaphoreType.DMA((3, 2, bands - 1)),
            pltpu.SemaphoreType.DMA((bands - 1,)),
            pltpu.SemaphoreType.DMA((bands - 1,)),
            pltpu.SemaphoreType.DMA((16,)),
            pltpu.SemaphoreType.DMA((16,)),
            pltpu.SemaphoreType.DMA((3,)),
        ],
        cost_estimate=expected(START_US),
        compiler_params=pltpu.CompilerParams(
            collective_id=0, has_side_effects=True, vmem_limit_bytes=48 * 2**20
        ),
    )(wide, tall, tokens, told, ada)


def add_low(left, right):
    return (left.astype(jnp.float32) + right.astype(jnp.float32)).astype(jnp.bfloat16)


def tail_kernel(
    qkv_ref, out_ref, up_ref, rows_ref, pieces_ref, silu_ref, known_ref,
    wide_ref, back_ref, ada_ref, bias_ref, squares_ref,
    pieces, terms, square_flat, square_line, small_send, small_recv,
    own, from_core, first_x, first_y, last_x, last_y, turned, held, held_in,
    core_send, core_recv, flat_send, flat_recv, line_send, line_recv, row_send, row_recv, local_sem,
    *, imgs, bands,
):
    img, band = lax.axis_index("img"), lax.axis_index("band")
    qkv_part, out_part = qkv_ref.shape[0] // imgs, out_ref.shape[0] // imgs
    both = own.shape[1]
    depth, width = wide_ref.shape
    row_block = back_ref.shape[1]
    half = first_x.shape[1]
    lanes = 128
    beside_x, beside_y, sibling = flip(img, 2), flip(img, 4), flip(img, 1)
    chips = (img, beside_x, beside_y, flip(beside_x, 4))
    upper, lower = pl.ds(0, half), pl.ds(half, both - half)
    spans = (pl.ds(0, qkv_part), pl.ds(qkv_part, out_part))

    barrier = pltpu.get_barrier_semaphore()
    for step in range(1, imgs):
        other = lax.rem(img + step, imgs)
        pl.semaphore_signal(barrier, inc=1, device_id={"img": other}, device_id_type=MESH)
    for step in range(1, bands):
        pl.semaphore_signal(
            barrier, inc=1, device_id={"band": lax.rem(band + step, bands)}, device_id_type=MESH
        )
    pl.semaphore_wait(barrier, imgs + bands - 2)

    def grad_rows(kind, owner):
        source, count = ((qkv_ref, qkv_part), (out_ref, out_part))[kind]
        return source.at[pl.ds(pl.multiple_of(owner * count, 16), count), :]

    def core_copy(kind, at):
        return pltpu.make_async_remote_copy(
            src_ref=grad_rows(kind, flip(chips[at], 1)), dst_ref=from_core.at[at, spans[kind]],
            send_sem=core_send.at[kind, at], recv_sem=core_recv.at[kind, at],
            device_id={"img": sibling}, device_id_type=MESH,
        )

    def own_copy(kind, at):
        return pltpu.make_async_copy(
            grad_rows(kind, chips[at]), own.at[at, spans[kind]], local_sem.at[4 * kind + at]
        )

    plan = (
        (own.at[1, upper], first_x.at[0], beside_x),
        (own.at[3, upper], first_x.at[1], beside_x),
        (own.at[2, lower], first_y.at[0], beside_y),
        (own.at[3, lower], first_y.at[1], beside_y),
        (own.at[2, upper], last_y, beside_y),
        (own.at[1, lower], last_x, beside_x),
    )

    def flat_copy(at):
        source, target, toward = plan[at]
        return pltpu.make_async_remote_copy(
            src_ref=source, dst_ref=target, send_sem=flat_send.at[at], recv_sem=flat_recv.at[at],
            device_id={"img": toward}, device_id_type=MESH,
        )

    def row_span(owner):
        return pl.ds(pl.multiple_of(owner * row_block, 16), row_block)

    def row_copy(step):
        target = lax.rem(band + step, bands)
        return pltpu.make_async_remote_copy(
            src_ref=rows_ref.at[row_span(target), :], dst_ref=back_ref.at[band],
            send_sem=row_send.at[step - 1], recv_sem=row_recv.at[step - 1],
            device_id={"band": target}, device_id_type=MESH,
        )

    def row_arrival(step):
        source = lax.rem(band + bands - step, bands)
        return pltpu.make_async_remote_copy(
            src_ref=back_ref.at[source], dst_ref=back_ref.at[source],
            send_sem=row_send.at[step - 1], recv_sem=row_recv.at[step - 1],
            device_id={"band": source}, device_id_type=MESH,
        )

    first = -(-both // lanes) * lanes
    parts = (pl.ds(0, first), pl.ds(first, width - first))

    def piece(part, owner, way=None):
        down = pl.ds(pl.multiple_of(owner * depth, 16), depth)
        return held.at[down, parts[part]] if way is None else held_in.at[way, down, parts[part]]

    def line_copy(part, way, owner, toward):
        return pltpu.make_async_remote_copy(
            src_ref=piece(part, owner), dst_ref=piece(part, owner, way),
            send_sem=line_send.at[part, way, owner], recv_sem=line_recv.at[part, way, owner],
            device_id={"band": toward}, device_id_type=MESH,
        )

    def line_ends(part):
        for step in range(bands - 1):

            @pl.when(band == 0)
            def _():
                line_copy(part, 0, bands - 1 - step, band + 1).start()

            @pl.when(band == bands - 1)
            def _():
                line_copy(part, 1, step, band - 1).start()

    def line_round(part, step):
        for way, owner, sign in ((0, bands - 1 - step, 1), (1, step, -1)):

            @pl.when((sign * (owner - band) > 0) & (band > 0) & (band < bands - 1))
            def _():
                copy = line_copy(part, way, owner, band + sign)
                copy.wait_recv()
                mine = piece(part, owner)
                mine[...] = add_low(mine[...], piece(part, owner, way)[...])
                copy.start()

    def line_finish(part):
        span = parts[part]
        wide_ref[:, span] = piece(part, band)[...].astype(jnp.float32)
        for way, sign in ((0, 1), (1, -1)):

            @pl.when((band - sign >= 0) & (band - sign < bands))
            def _():
                line_copy(part, way, band, band - sign).wait_recv()
                wide_ref[:, span] += piece(part, band, way)[...].astype(jnp.float32)

    def line_sent(part):
        for way, sign in ((0, 1), (1, -1)):
            for owner in range(bands):

                @pl.when(sign * (owner - band) > 0)
                def _():
                    line_copy(part, way, owner, band + sign).wait_send()

    def turn(tile):
        span = pl.ds(pl.multiple_of(tile * lanes, lanes), lanes)
        held[:, span] = turned[span, :].astype(jnp.float32).T.astype(jnp.bfloat16)

    def small_copy(source, target, kind, step, axis, toward):
        return pltpu.make_async_remote_copy(
            src_ref=source, dst_ref=target,
            send_sem=small_send.at[kind, step], recv_sem=small_recv.at[kind, step],
            device_id={axis: toward}, device_id_type=MESH,
        )

    def piece_flat(step):
        other = lax.rem(img + step, imgs)
        return small_copy(pieces_ref.at[other], pieces.at[band, img], 0, step, "img", other)

    def piece_line(step):
        other = lax.rem(band + step, bands)
        return small_copy(pieces.at[band], pieces.at[band], 1, step, "band", other)

    def square_one(step):
        other = lax.rem(img + step, imgs)
        return small_copy(square_flat.at[img], square_flat.at[img], 2, step, "img", other)

    def square_two(step):
        other = lax.rem(band + step, bands)
        return small_copy(square_line.at[band], square_line.at[band], 3, step, "band", other)

    def arrival(view, kind, step, axis):
        me, count = (img, imgs) if axis == "img" else (band, bands)
        small_copy(view, view, kind, step, axis, lax.rem(me + count - step, count)).wait_recv()

    order = (3, 1, 2, 0)
    for step in range(1, imgs):
        piece_flat(step).start()
    keep_piece = pltpu.make_async_copy(pieces_ref.at[img], pieces.at[band, img], local_sem.at[9])
    keep_piece.start()
    for at in order:
        core_copy(0, at).start()
        core_copy(1, at).start()
    for at in order:
        own_copy(0, at).start()
        own_copy(1, at).start()
    keep = pltpu.make_async_copy(rows_ref.at[row_span(band), :], back_ref.at[band], local_sem.at[8])
    keep.start()
    turned[pl.ds(both, width - both), :] = up_ref[...]
    pl.loop(first // lanes, width // lanes)(turn)
    line_ends(1)
    for step in range(1, bands):
        row_copy(step).start()
    for at in order:
        for kind in range(2):
            own_copy(kind, at).wait()
            core_copy(kind, at).wait_recv()
        own[at] = add_low(own[at], from_core[at])
        for ready in {3: (1, 3), 1: (0,), 2: (2,), 0: ()}[at]:
            flat_copy(ready).start()
    keep_piece.wait()
    for step in range(1, imgs):
        arrival(pieces.at[band, lax.rem(img + imgs - step, imgs)], 0, step, "img")
    for step in range(1, bands):
        piece_line(step).start()
    flat_copy(1).wait_recv()
    own[2, upper] = add_low(own[2, upper], first_x[1])
    flat_copy(4).start()
    flat_copy(3).wait_recv()
    own[1, lower] = add_low(own[1, lower], first_y[1])
    flat_copy(5).start()
    line_round(1, 0)
    flat_copy(0).wait_recv()
    flat_copy(2).wait_recv()
    flat_copy(4).wait_recv()
    flat_copy(5).wait_recv()
    turned[upper, :] = (
        own[0, upper].astype(jnp.float32)
        + first_x[0].astype(jnp.float32)
        + last_y[...].astype(jnp.float32)
    ).astype(jnp.bfloat16)
    turned[lower, :] = (
        own[0, lower].astype(jnp.float32)
        + first_y[0].astype(jnp.float32)
        + last_x[...].astype(jnp.float32)
    ).astype(jnp.bfloat16)
    pl.loop(0, first // lanes)(turn)
    line_ends(0)
    for step in range(bands - 1):
        line_round(0, step)
        if step > 0:
            line_round(1, step)
    for step in range(1, bands):
        arrival(pieces.at[lax.rem(band + bands - step, bands)], 1, step, "band")
    for image in range(imgs):
        for at in range(bands):
            terms[pl.ds(image * bands + at, 1), :] = pieces[at, image]
    columns = ada_ref.shape[1]
    ada = lax.dot_general(
        silu_ref[...], terms[:, pl.ds(0, columns)], (((1,), (0,)), ((), ())),
        precision=lax.Precision.HIGHEST, preferred_element_type=jnp.float32,
    )
    ada_ref[...] = ada
    bias_rows, bias_columns = bias_ref.shape
    bias = jnp.sum(terms[:, pl.ds(columns, bias_rows * bias_columns)], axis=0, keepdims=True)
    for at in range(bias_rows):
        bias_ref[pl.ds(at, 1), :] = bias[:, at * bias_columns : (at + 1) * bias_columns]
    squares = jnp.sum(ada * ada, axis=0, keepdims=True)
    squares = jnp.sum(squares, axis=1, keepdims=True)
    squares += jnp.sum(bias * bias, axis=1, keepdims=True) / bands
    line_finish(1)
    line_finish(0)
    rows = jnp.sum(wide_ref[...] * wide_ref[...], axis=0, keepdims=True)
    squares += jnp.sum(rows, axis=1, keepdims=True) + known_ref[0:1, 0:1]
    square_flat[img] = jnp.broadcast_to(squares, square_flat.shape[1:])
    for step in range(1, imgs):
        square_one(step).start()
    for step in range(1, imgs):
        arrival(square_flat.at[lax.rem(img + imgs - step, imgs)], 2, step, "img")
    total = square_flat[0]
    for at in range(1, imgs):
        total += square_flat[at]
    square_line[band] = total
    for step in range(1, bands):
        square_two(step).start()
    for step in range(1, bands):
        arrival(square_line.at[lax.rem(band + bands - step, bands)], 3, step, "band")
    total = square_line[0]
    for at in range(1, bands):
        total += square_line[at]
    squares_ref[...] = total
    line_sent(0)
    line_sent(1)
    for step in range(1, imgs):
        piece_flat(step).wait_send()
        square_one(step).wait_send()
    for step in range(1, bands):
        piece_line(step).wait_send()
        square_two(step).wait_send()
    for at in range(4):
        core_copy(0, at).wait_send()
        core_copy(1, at).wait_send()
    for at in range(6):
        flat_copy(at).wait_send()
    for step in range(1, bands):
        row_copy(step).wait_send()
        row_arrival(step).wait_recv()
    keep.wait()


def tail_exchange(qkv_grad, out_grad, up_sum, rows, pieces, silu, known, bias_shape, bands, imgs):
    low = jnp.bfloat16
    features = qkv_grad.shape[1]
    both = (qkv_grad.shape[0] + out_grad.shape[0]) // imgs
    width = both + up_sum.shape[0]
    half = -(-both // 32) * 16
    ada_columns = pieces.shape[2] - bias_shape[0] * bias_shape[1]
    anywhere, vmem = pl.BlockSpec(memory_space=pl.ANY), pl.BlockSpec(memory_space=pltpu.VMEM)
    return pl.pallas_call(
        functools.partial(tail_kernel, imgs=imgs, bands=bands),
        out_shape=(
            jax.ShapeDtypeStruct((features // bands, width), jnp.float32),
            jax.ShapeDtypeStruct((bands, rows.shape[0] // bands, features), low),
            jax.ShapeDtypeStruct((silu.shape[0], ada_columns), jnp.float32),
            jax.ShapeDtypeStruct(bias_shape, jnp.float32),
            jax.ShapeDtypeStruct((8, 128), jnp.float32),
        ),
        in_specs=[anywhere, anywhere, vmem, anywhere, vmem, vmem, vmem],
        out_specs=(vmem, anywhere, vmem, vmem, vmem),
        scratch_shapes=[
            pltpu.VMEM((bands,) + pieces.shape, jnp.float32),
            pltpu.VMEM((bands * imgs, pieces.shape[2]), jnp.float32),
            pltpu.VMEM((imgs, 8, 128), jnp.float32),
            pltpu.VMEM((bands, 8, 128), jnp.float32),
            pltpu.SemaphoreType.DMA((4, imgs)),
            pltpu.SemaphoreType.DMA((4, imgs)),
            pltpu.VMEM((4, both, features), low),
            pltpu.VMEM((4, both, features), low),
            pltpu.VMEM((2, half, features), low),
            pltpu.VMEM((2, both - half, features), low),
            pltpu.VMEM((both - half, features), low),
            pltpu.VMEM((half, features), low),
            pltpu.VMEM((width, features), low),
            pltpu.VMEM((features, width), low),
            pltpu.VMEM((2, features, width), low),
            pltpu.SemaphoreType.DMA((2, 4)),
            pltpu.SemaphoreType.DMA((2, 4)),
            pltpu.SemaphoreType.DMA((6,)),
            pltpu.SemaphoreType.DMA((6,)),
            pltpu.SemaphoreType.DMA((2, 2, bands)),
            pltpu.SemaphoreType.DMA((2, 2, bands)),
            pltpu.SemaphoreType.DMA((bands - 1,)),
            pltpu.SemaphoreType.DMA((bands - 1,)),
            pltpu.SemaphoreType.DMA((10,)),
        ],
        cost_estimate=expected(TAIL_US),
        compiler_params=pltpu.CompilerParams(
            collective_id=1, has_side_effects=True, vmem_limit_bytes=50 * 2**20
        ),
    )(qkv_grad, out_grad, up_sum, rows, pieces, silu, known)


def adam_kernel(*refs):
    squares_ref, wide_ref, tall_ref, ada_ref, bias_ref = refs[:5]
    sources, results = refs[5:23], refs[23:]
    norm = jnp.sqrt(squares_ref[0:1, 0:1])
    factor = clip_norm / jnp.maximum(norm, clip_norm)
    qkv_part = sources[3].shape[1]
    both = qkv_part + sources[6].shape[1]
    rates = (learn_rate, learn_rate, out_rate, learn_rate, learn_rate, bias_rate)

    def update(which, rows, gradient):
        weight_ref, first_ref, second_ref = sources[3 * which : 3 * which + 3]
        new = adam_update(
            weight_ref[rows, :], first_ref[rows, :], second_ref[rows, :], gradient, factor, rates[which]
        )
        for into, value in zip(results[3 * which : 3 * which + 3], new):
            into[rows, :] = value

    depth = wide_ref.shape[0]
    block = next(rows for rows in (32, 16, 8) if depth % rows == 0)

    @pl.loop(0, depth // block)
    def _(step):
        rows = pl.ds(pl.multiple_of(step * block, block), block)
        update(0, rows, ada_ref[rows, :])
        update(1, rows, wide_ref[rows, :qkv_part])
        update(2, rows, wide_ref[rows, qkv_part:both])
        update(3, rows, wide_ref[rows, both:])

    tall_rows = tall_ref.shape[0]
    tall_block = 16 if tall_rows % 16 == 0 else tall_rows
    for start in range(0, tall_rows, tall_block):
        rows = pl.ds(start, tall_block)
        update(4, rows, tall_ref[rows, :])

    update(5, slice(None), bias_ref[...])
    results[18][...] = bias_ref[pl.ds(13, 1), :] * factor


def adam_all(squares, wide, tall, ada, bias, groups):
    flat = [array for group in groups for array in group]
    return pl.pallas_call(
        adam_kernel,
        out_shape=[jax.ShapeDtypeStruct(array.shape, jnp.float32) for array in flat]
        + [jax.ShapeDtypeStruct((1, bias.shape[1]), jnp.float32)],
        compiler_params=pltpu.CompilerParams(vmem_limit_bytes=50 * 2**20),
    )(squares, wide, tall, ada, bias, *flat)


def body(
    inputs,
    condition,
    valid_rows,
    cotangent,
    ada_weight,
    qkv_weight,
    out_weight,
    up_weight,
    down_weight,
    biases,
    ada_first,
    qkv_first,
    out_first,
    up_first,
    down_first,
    bias_first,
    ada_second,
    qkv_second,
    out_second,
    up_second,
    down_second,
    bias_second,
):
    images, local_rows, features = inputs.shape
    length = L
    head_count = HEADS
    head_size = HEAD_DIM
    score_scale = head_size ** (-0.5)
    band_count = lax.axis_size("band")
    img_count = lax.axis_size("img")
    band_rank = lax.axis_index("band")
    img_rank = lax.axis_index("img")
    own = max(1, images // band_count)
    split = max(1, band_count // images)
    mates = band_count // split
    image_rows = length // split
    exchange_groups = None
    share_groups = None
    if split > 1:
        exchange_groups = [[g * mates + m for m in range(mates)] for g in range(split)]
        share_groups = [[g * mates + m for g in range(split)] for m in range(mates)]
    low_type = jnp.bfloat16

    def to_images(rows):
        return lax.all_to_all(rows, "band", split_axis=0, concat_axis=1, axis_index_groups=exchange_groups, tiled=True)

    def to_bands(whole):
        cut = whole.reshape(own, mates, local_rows, features).transpose(1, 0, 2, 3)
        back = lax.all_to_all(
            cut, "band", split_axis=0, concat_axis=0, axis_index_groups=exchange_groups, tiled=True
        )
        return back.reshape(images, local_rows, features)

    def after(value, *earlier):
        return lax.optimization_barrier((value,) + earlier)[0]

    def sum_everywhere(partial):
        sent = jnp.broadcast_to(partial, (img_count * band_count, 128))
        got = lax.all_to_all(sent, ("img", "band"), split_axis=0, concat_axis=0, tiled=True)
        return jnp.sum(got[:, 0])

    qkv_part, out_part = qkv_weight.shape[1], out_weight.shape[1]

    bias_rows, bias_columns = biases.shape
    ada_rows, ada_columns = ada_weight.shape
    silu_own = lax.reduce_precision(jax.nn.silu(condition.astype(jnp.float32)), 8, 7)
    silu_own = lax.dynamic_slice_in_dim(silu_own, band_rank * ada_rows, ada_rows, axis=1)
    told = jnp.concatenate(
        [silu_own.reshape(1, -1), lax.reduce_precision(biases, 8, 7).reshape(1, -1)],
        axis=1,
    )
    ada_low = ada_weight.astype(low_type)
    wide = jnp.concatenate([qkv_weight, out_weight, up_weight], axis=1).astype(low_type)
    tall = down_weight.T.astype(low_type)
    if img_count == 8 and own == 1 and split == 1:
        qkv_full, out_full, up_rows, down_rows, tokens_low, heard, silu_rows, mod_summed = (
            start_exchange(
                wide, tall, inputs, told, ada_low, band_count, img_count, qkv_part, out_part
            )
        )
        tokens_low = tokens_low.reshape(own, image_rows, features)
        mod_summed = mod_summed.reshape(own, img_count * ada_columns)
    else:
        turned = lax.all_gather(wide, "band", axis=0, tiled=True).T
        qkv_full = lax.all_gather(turned[:qkv_part], "img", axis=0, tiled=True)
        out_full = lax.all_gather(
            turned[qkv_part : qkv_part + out_part], "img", axis=0, tiled=True
        )
        up_rows = turned[qkv_part + out_part :]
        down_rows = lax.all_gather(tall, "band", axis=1, tiled=True)
        tokens_low = to_images(inputs)
        heard = lax.all_gather(told, "img", axis=0, tiled=True)
        silu_rows = heard[:, : images * ada_rows].reshape(img_count * images, ada_rows)
        mod_partial = jnp.dot(
            silu_rows.astype(low_type), ada_low, preferred_element_type=jnp.float32
        )
        mod_sent = jnp.tile(
            mod_partial.reshape(img_count, 1, images * ada_columns), (1, split, 1)
        )
        mod_pieces = lax.all_to_all(
            mod_sent.reshape(img_count * band_count, own * ada_columns),
            ("img", "band"),
            split_axis=0,
            concat_axis=0,
            tiled=True,
        ).reshape(img_count, band_count, own, ada_columns)
        mod_summed = (
            jnp.sum(mod_pieces, axis=1).transpose(1, 0, 2).reshape(own, img_count * ada_columns)
        )
    up_full = lax.all_gather(up_rows, "img", axis=0, tiled=True)
    down_full = lax.all_gather(after(down_rows, up_rows), "img", axis=0, tiled=True)
    bias_vals = (
        heard.reshape(img_count, -1)[:, images * ada_rows :]
        .reshape(img_count, bias_rows, bias_columns)
        .transpose(1, 0, 2)
        .reshape(bias_rows, features)
    )
    modulation = mod_summed + bias_vals[0:6].reshape(-1)
    mod_parts = modulation.reshape(own, 6, 1, features)
    shift_one = mod_parts[:, 0]
    scale_one = mod_parts[:, 1]
    gate_one = mod_parts[:, 2]
    shift_two = mod_parts[:, 3]
    scale_two = mod_parts[:, 4]
    gate_two = mod_parts[:, 5]
    valid_own = lax.dynamic_slice_in_dim(valid_rows, lax.rem(band_rank, mates) * own, own, axis=0)
    key_mask = jnp.arange(length, dtype=jnp.int32)[None, :] < valid_own[:, None]
    positions = lax.div(band_rank, mates) * image_rows + jnp.arange(image_rows, dtype=jnp.int32)
    row_mask = (positions[None, :] < valid_own[:, None]).astype(jnp.float32)[:, :, None]
    tokens_in = tokens_low.astype(jnp.float32)
    normed_one, inverse_one = normalize_keep(tokens_in)
    first_in = (normed_one * (1.0 + scale_one) + shift_one).astype(jnp.bfloat16)
    cotangent_low = to_images(after(cotangent, tokens_low))
    grad_out = cotangent_low.astype(jnp.float32) * row_mask
    qkv_bias = jnp.concatenate([bias_vals[6], jnp.zeros((features,), jnp.float32), bias_vals[7]])
    projected = (
        jnp.einsum("ird,ed->ire", first_in, qkv_full, preferred_element_type=jnp.float32) + qkv_bias
    ).astype(jnp.bfloat16)
    key_bias = jnp.where(key_mask, 0.0, very_low).astype(jnp.float32)[:, :, None]
    queries = [projected[i] for i in range(own)]
    if split > 1:
        keys_values = lax.all_gather(
            projected[..., features:], "band", axis=1, axis_index_groups=share_groups, tiled=True
        )
        keys_values = [keys_values[i] for i in range(own)]
        key_shift = 0
    else:
        keys_values = queries
        key_shift = features
    mixed, log_total = zip(
        *[
            attention_forward(queries[i], keys_values[i], key_bias[i], features, key_shift, 512)
            for i in range(own)
        ]
    )
    mixed_parts = mixed
    mixed = jnp.stack(mixed)
    attended = (
        jnp.einsum("ird,ed->ire", mixed, out_full, preferred_element_type=jnp.float32)
        + bias_vals[8]
    )
    middle = tokens_in + gate_one * attended
    normed_two, inverse_two = normalize_keep(middle)
    second_in = (normed_two * (1.0 + scale_two) + shift_two).astype(jnp.bfloat16)
    hidden_pre = jnp.einsum(
        "ird,fd->irf", second_in, up_full, preferred_element_type=jnp.float32
    ) + bias_vals[9:13].reshape(-1)
    hidden, gelu_back = jax.vjp(smooth_gate, hidden_pre)
    hidden_low = hidden.astype(jnp.bfloat16)
    branch = (
        jnp.einsum("irf,df->ird", hidden_low, down_full, preferred_element_type=jnp.float32)
        + bias_vals[13]
    )
    output_low = (middle + gate_two * branch).astype(jnp.bfloat16)
    branch_grad = (gate_two * grad_out).astype(jnp.bfloat16)
    gate_two_grad = jnp.sum(grad_out * branch, axis=1)
    down_grad = jnp.einsum(
        "ird,irf->df", branch_grad, hidden_low, preferred_element_type=jnp.float32
    ).astype(low_type)
    down_sum = lax.psum_scatter(down_grad, "img", scatter_dimension=0, tiled=True)
    hidden_grad = jnp.einsum(
        "ird,df->irf",
        after(branch_grad, down_grad),
        down_full,
        preferred_element_type=jnp.float32,
    )
    pre_grad = gelu_back(hidden_grad)[0].astype(jnp.bfloat16)
    up_grad = jnp.einsum(
        "irf,ird->fd", pre_grad, second_in, preferred_element_type=jnp.float32
    ).astype(low_type)
    up_sum = lax.psum_scatter(up_grad, "img", scatter_dimension=0, tiled=True)
    second_grad = jnp.einsum("irf,fd->ird", after(pre_grad, up_grad), up_full, preferred_element_type=jnp.float32)
    shift_two_grad = jnp.sum(second_grad, axis=1)
    scale_two_grad = jnp.sum(second_grad * normed_two, axis=1)
    middle_grad = grad_out + normalize_back(
        normed_two, inverse_two, second_grad * (1.0 + scale_two)
    )
    attended_grad = (gate_one * middle_grad).astype(jnp.bfloat16)
    gate_one_grad = jnp.sum(middle_grad * attended, axis=1)
    out_grad = jnp.einsum(
        "ire,ird->ed", attended_grad, mixed, preferred_element_type=jnp.float32
    ).astype(low_type)
    mixed_grad = jnp.einsum(
        "ire,ed->ird", after(attended_grad, out_grad), out_full, preferred_element_type=jnp.float32
    ).astype(jnp.bfloat16)
    tall_cut = down_sum.reshape(down_sum.shape[0], band_count, -1).transpose(1, 0, 2)
    tall_shard = jnp.sum(
        lax.all_to_all(tall_cut, "band", split_axis=0, concat_axis=0, tiled=True).astype(jnp.float32),
        axis=0,
    )
    hosted = img_count == 8 and own == 1 and split == 1
    tall_squares = jnp.broadcast_to(jnp.sum(tall_shard * tall_shard), (8, 128))
    attention_grads = [
        attention_backward(
            queries[i], keys_values[i], key_bias[i], mixed_parts[i], mixed_grad[i], log_total[i],
            features, 512, output_low[i] if hosted else None, band_count,
        )
        for i in range(own)
    ]
    if hosted:
        output = attention_grads[0][1]
    else:
        output = to_bands(output_low)
    if split > 1:
        shared_grads = lax.psum_scatter(
            jnp.stack([pair[1] for pair in attention_grads]),
            "band",
            scatter_dimension=1,
            axis_index_groups=share_groups,
            tiled=True,
        )
        qkv_grad = jnp.concatenate(
            [jnp.stack([pair[0] for pair in attention_grads]), shared_grads], axis=-1
        )
    elif hosted:
        qkv_grad = attention_grads[0][0][None]
    else:
        qkv_grad = jnp.stack([jnp.concatenate(pair, axis=-1) for pair in attention_grads])
    qkv_sums = jnp.sum(qkv_grad.astype(jnp.float32), axis=(0, 1))
    qkv_weight_grad = jnp.einsum(
        "ire,ird->ed", after(qkv_grad, tall_shard), first_in, preferred_element_type=jnp.float32
    ).astype(low_type)
    first_grad = jnp.einsum("ire,ed->ird", after(qkv_grad, qkv_weight_grad), qkv_full, preferred_element_type=jnp.float32)
    shift_one_grad = jnp.sum(first_grad, axis=1)
    scale_one_grad = jnp.sum(first_grad * normed_one, axis=1)
    input_grad_low = (
        middle_grad + normalize_back(normed_one, inverse_one, first_grad * (1.0 + scale_one))
    ).astype(low_type)
    mod_grad = jnp.stack(
        [
            shift_one_grad,
            scale_one_grad,
            gate_one_grad,
            shift_two_grad,
            scale_two_grad,
            gate_two_grad,
        ],
        axis=1,
    )
    row_sums = jnp.concatenate(
        [
            qkv_sums[:features][None],
            qkv_sums[2 * features :][None],
            jnp.sum(attended_grad.astype(jnp.float32), axis=(0, 1))[None],
            jnp.sum(pre_grad.astype(jnp.float32), axis=(0, 1)).reshape(4, features),
            jnp.sum(branch_grad.astype(jnp.float32), axis=(0, 1))[None],
        ],
        axis=0,
    )
    pieces = jnp.concatenate(
        [
            mod_grad.reshape(own, img_count, ada_columns)
            .transpose(1, 0, 2)
            .reshape(img_count, own * ada_columns),
            jnp.concatenate([jnp.sum(mod_grad, axis=0).reshape(6, features), row_sums], axis=0)
            .reshape(bias_rows, img_count, bias_columns)
            .transpose(1, 0, 2)
            .reshape(img_count, -1),
        ],
        axis=1,
    )
    silu_terms = jnp.tile(
        silu_rows.reshape(img_count, 1, images, ada_rows), (1, split, 1, 1)
    ).reshape(img_count * band_count * own, ada_rows)
    if img_count == 8 and own == 1 and split == 1:
        wide_shard, input_grad_low, ada_shard, bias_total, squares_total = tail_exchange(
            qkv_weight_grad,
            out_grad,
            up_sum,
            input_grad_low[0],
            pieces[:, None],
            silu_terms.T,
            tall_squares,
            biases.shape,
            band_count,
            img_count,
        )
    else:
        sent = jnp.broadcast_to(
            pieces[:, None], (img_count, band_count, pieces.shape[1])
        ).reshape(img_count * band_count, -1)
        got = lax.all_to_all(sent, ("img", "band"), split_axis=0, concat_axis=0, tiled=True)
        ada_shard = jnp.einsum(
            "id,ie->de",
            silu_terms,
            got[:, : own * ada_columns].reshape(-1, ada_columns),
            precision=lax.Precision.HIGHEST,
        )
        bias_total = jnp.sum(got[:, own * ada_columns :], axis=0).reshape(bias_rows, bias_columns)
        qkv_sum = lax.psum_scatter(qkv_weight_grad, "img", scatter_dimension=0, tiled=True)
        out_sum = lax.psum_scatter(out_grad, "img", scatter_dimension=0, tiled=True)
        wide_shard = lax.psum_scatter(
            jnp.concatenate([qkv_sum, out_sum, up_sum], axis=0).T,
            "band",
            scatter_dimension=0,
            tiled=True,
        ).astype(jnp.float32)
        input_grad_low = to_bands(input_grad_low)
        squares = tall_squares[0, 0] + jnp.sum(bias_total * bias_total) / band_count
        for shard_grad in (ada_shard, wide_shard):
            squares = squares + jnp.sum(shard_grad * shard_grad)
        squares_total = jnp.broadcast_to(sum_everywhere(squares), (8, 128))
    input_grad = input_grad_low.astype(jnp.float32)
    grad_norm = jnp.sqrt(squares_total[0, 0])
    groups = (
        (ada_weight, ada_first, ada_second),
        (qkv_weight, qkv_first, qkv_second),
        (out_weight, out_first, out_second),
        (up_weight, up_first, up_second),
        (down_weight.T, down_first.T, down_second.T),
        (biases, bias_first, bias_second),
    )
    updated = adam_all(squares_total, wide_shard, tall_shard, ada_shard, bias_total, groups)
    ada_new, ada_first_new, ada_second_new = updated[0:3]
    qkv_new, qkv_first_new, qkv_second_new = updated[3:6]
    out_new, out_first_new, out_second_new = updated[6:9]
    up_new, up_first_new, up_second_new = updated[9:12]
    down_new, down_first_new, down_second_new = (array.T for array in updated[12:15])
    bias_new, bias_first_new, bias_second_new = updated[15:18]
    branch_bias_grad = updated[18][0]
    return (
        output,
        input_grad,
        grad_norm,
        ada_new,
        qkv_new,
        out_new,
        up_new,
        down_new,
        bias_new,
        ada_first_new,
        qkv_first_new,
        out_first_new,
        up_first_new,
        down_first_new,
        bias_first_new,
        ada_second_new,
        qkv_second_new,
        out_second_new,
        up_second_new,
        down_second_new,
        bias_second_new,
        branch_bias_grad,
    )


def solution(mesh):
    return jax.shard_map(
        body,
        mesh=mesh,
        in_specs=(
            P("img", "band", None),
            P("img", None),
            P("img"),
            P("img", "band", None),
            P("band", "img"),
            P("band", "img"),
            P("band", "img"),
            P("band", "img"),
            P("band", "img"),
            P(None, "img"),
            P("band", "img"),
            P("band", "img"),
            P("band", "img"),
            P("band", "img"),
            P("band", "img"),
            P(None, "img"),
            P("band", "img"),
            P("band", "img"),
            P("band", "img"),
            P("band", "img"),
            P("band", "img"),
            P(None, "img"),
        ),
        out_specs=(
            P("img", "band", None),
            P("img", "band", None),
            P(),
            P("band", "img"),
            P("band", "img"),
            P("band", "img"),
            P("band", "img"),
            P("band", "img"),
            P(None, "img"),
            P("band", "img"),
            P("band", "img"),
            P("band", "img"),
            P("band", "img"),
            P("band", "img"),
            P(None, "img"),
            P("band", "img"),
            P("band", "img"),
            P("band", "img"),
            P("band", "img"),
            P("band", "img"),
            P(None, "img"),
            P("img"),
        ),
        check_vma=False,
    )
```

```python
import functools

import jax
import jax.numpy as jnp
from jax import lax
from jax.experimental import pallas as pl
from jax.experimental.pallas import tpu as pltpu
from jax.sharding import PartitionSpec as P

HEADS = 16
HEAD_DIM = 72
L = 1024
STEP = 10


norm_eps = 1e-06
beta_one = 0.9
beta_two = 0.999
adam_eps = 1e-08
learn_rate = 0.03
out_rate = 0.25
bias_rate = 0.4
clip_norm = 1.0
very_low = -1000000000.0


def normalize_keep(values):
    centre = values - jnp.mean(values, axis=-1, keepdims=True)
    inverse = lax.rsqrt(jnp.mean(centre * centre, axis=-1, keepdims=True) + norm_eps)
    return (centre * inverse, inverse)


def normalize_back(normed, inverse, incoming):
    return inverse * (
        incoming
        - jnp.mean(incoming, axis=-1, keepdims=True)
        - normed * jnp.mean(incoming * normed, axis=-1, keepdims=True)
    )


def smooth_gate(values):
    return jax.nn.gelu(values, approximate=True)


def adam_update(weight, first_old, second_old, gradient, factor, rate):
    clipped = gradient * factor
    first_new = beta_one * first_old + (1.0 - beta_one) * clipped
    second_new = beta_two * second_old + (1.0 - beta_two) * clipped * clipped
    first_hat = first_new / (1.0 - beta_one**STEP)
    second_hat = second_new / (1.0 - beta_two**STEP)
    return (weight - rate * first_hat / (jnp.sqrt(second_hat) + adam_eps), first_new, second_new)


WINDOW = 256
CONTRACT_LAST = (((1,), (1,)), ((), ()))
LOG2_E = 1.4426950408889634


FORWARD_US, BACKWARD_US, START_US, TAIL_US = 37, 57, 115, 110


def expected(microseconds):
    moved = int(microseconds * 3.2e6)
    return pl.CostEstimate(flops=0, bytes_accessed=moved, transcendentals=0)


def head_window(head, features):
    start = head * HEAD_DIM
    base = pl.multiple_of(jnp.minimum(start // 128 * 128, features - WINDOW), 128)
    lane = lax.broadcasted_iota(jnp.int32, (1, WINDOW), 1)
    inside = (lane >= start - base) & (lane < start - base + HEAD_DIM)
    return base, inside


def attention_forward_kernel(
    query_ref, keyval_ref, bias_ref, mixed_ref, log_ref, scaled, value_t, mixed_t, *, features, shift, block
):
    length = keyval_ref.shape[0]
    rows = mixed_ref.shape[0]
    scaled[...] = (query_ref[:, :features].astype(jnp.float32) * (HEAD_DIM**-0.5 * LOG2_E)).astype(
        jnp.bfloat16
    )

    @pl.loop(0, features // 128)
    def _(tile):
        columns = pl.ds(pl.multiple_of(tile * 128, 128), 128)
        source = pl.ds(pl.multiple_of(shift + features + tile * 128, 128), 128)
        value_t[columns, :] = keyval_ref[:, source].astype(jnp.float32).T

    @pl.loop(0, HEADS)
    def _(head):
        base, inside = head_window(head, features)
        head_rows = pl.ds(pl.multiple_of(head * HEAD_DIM, 8), HEAD_DIM)
        query = scaled[:, pl.ds(base, WINDOW)]
        ones = jnp.ones((8, block), jnp.float32)
        top = None
        for at in range(0, length, block):
            key = keyval_ref[pl.ds(at, block), pl.ds(pl.multiple_of(base + shift, 128), WINDOW)]
            key = jnp.where(inside, key, jnp.zeros_like(key))
            scores = lax.dot_general(key, query, CONTRACT_LAST, preferred_element_type=jnp.float32)
            if at + block == length:
                scores = scores + bias_ref[pl.ds(at, block), :]
            block_top = jnp.max(scores, axis=0, keepdims=True)
            value = jnp.concatenate([value_t[head_rows, pl.ds(at, block)], ones], axis=0).astype(jnp.bfloat16)
            if top is None:
                top = block_top
                probs = jnp.exp2(scores - top).astype(jnp.bfloat16)
                total = jnp.dot(value, probs, preferred_element_type=jnp.float32)
            else:
                new_top = jnp.maximum(top, block_top)
                fade = jnp.exp2(top - new_top)
                top = new_top
                probs = jnp.exp2(scores - top).astype(jnp.bfloat16)
                total = total * fade + jnp.dot(value, probs, preferred_element_type=jnp.float32)
        weight = total[HEAD_DIM : HEAD_DIM + 1]
        mixed_t[head_rows, :] = total[:HEAD_DIM] * (1.0 / weight)
        log_ref[pl.ds(head, 1), :] = top + jnp.log2(weight)

    @pl.loop(0, features // 128)
    def _(tile):
        columns = pl.ds(pl.multiple_of(tile * 128, 128), 128)
        mixed_ref[:, columns] = mixed_t[columns, :].T.astype(jnp.bfloat16)


def attention_forward(query, keyval, key_bias, features, shift, block):
    rows, length = query.shape[0], keyval.shape[0]
    return pl.pallas_call(
        functools.partial(attention_forward_kernel, features=features, shift=shift, block=block),
        out_shape=(
            jax.ShapeDtypeStruct((rows, features), jnp.bfloat16),
            jax.ShapeDtypeStruct((HEADS, rows), jnp.float32),
        ),
        scratch_shapes=[
            pltpu.VMEM((rows, features), jnp.bfloat16),
            pltpu.VMEM((features, length), jnp.float32),
            pltpu.VMEM((features, rows), jnp.float32),
        ],
        cost_estimate=expected(FORWARD_US),
        compiler_params=pltpu.CompilerParams(vmem_limit_bytes=56 * 2**20),
    )(query, keyval, key_bias)


MESH = pl.DeviceIdType.MESH


def exchange_rows(rows_ref, back_ref, send, recv, local_sem, *, bands):
    band = lax.axis_index("band")
    block = back_ref.shape[1]
    barrier = pltpu.get_barrier_semaphore()
    for step in range(1, bands):
        pl.semaphore_signal(
            barrier, inc=1, device_id={"band": lax.rem(band + step, bands)}, device_id_type=MESH
        )
    pl.semaphore_wait(barrier, bands - 1)

    def span(owner):
        return rows_ref.at[pl.ds(pl.multiple_of(owner * block, 16), block), :]

    def sent(step):
        target = lax.rem(band + step, bands)
        return pltpu.make_async_remote_copy(
            src_ref=span(target), dst_ref=back_ref.at[band],
            send_sem=send.at[step], recv_sem=recv.at[step],
            device_id={"band": target}, device_id_type=MESH,
        )

    keep = pltpu.make_async_copy(span(band), back_ref.at[band], local_sem)
    keep.start()
    for step in range(1, bands):
        sent(step).start()

    def finish():
        keep.wait()
        for step in range(1, bands):
            sent(step).wait_send()
            source = lax.rem(band + bands - step, bands)
            pltpu.make_async_remote_copy(
                src_ref=back_ref.at[source], dst_ref=back_ref.at[source],
                send_sem=send.at[step], recv_sem=recv.at[step],
                device_id={"band": source}, device_id_type=MESH,
            ).wait_recv()

    return finish


def attention_backward_kernel(
    query_ref, keyval_ref, bias_ref, mixed_ref, grad_ref, log_ref, out_ref, keyval_grad_ref,
    scaled, key_t, wide_t, *, features, shift, out_shift, block
):
    length = keyval_ref.shape[0]
    rows = mixed_ref.shape[0]
    scale = HEAD_DIM**-0.5
    scaled[...] = (query_ref[:, :features].astype(jnp.float32) * (scale * LOG2_E)).astype(jnp.bfloat16)

    @pl.loop(0, features // 128)
    def _(tile):
        columns = pl.ds(pl.multiple_of(tile * 128, 128), 128)
        key_t[columns, :] = keyval_ref[:, pl.ds(pl.multiple_of(shift + tile * 128, 128), 128)].astype(jnp.float32).T
        wide_t[columns, :] = (
            mixed_ref[:, columns].astype(jnp.float32) * grad_ref[:, columns].astype(jnp.float32)
        ).T

    @pl.loop(0, HEADS)
    def _(head):
        base, inside = head_window(head, features)
        head_rows = pl.ds(pl.multiple_of(head * HEAD_DIM, 8), HEAD_DIM)
        window = pl.ds(base, WINDOW)
        delta = jnp.sum(wide_t[head_rows, :], axis=0, keepdims=True)
        log_total = log_ref[pl.ds(head, 1), :]
        query = query_ref[:, window]
        query_scaled = scaled[:, window]
        grad = grad_ref[:, window]
        query_grad = None
        for at in range(0, length, block):
            here = pl.ds(at, block)
            key_window = pl.ds(pl.multiple_of(base + shift, 128), WINDOW)
            value_window = pl.ds(pl.multiple_of(base + shift + features, 128), WINDOW)
            key = keyval_ref[here, key_window]
            value = keyval_ref[here, value_window]
            key = jnp.where(inside, key, jnp.zeros_like(key))
            value = jnp.where(inside, value, jnp.zeros_like(value))
            scores = lax.dot_general(key, query_scaled, CONTRACT_LAST, preferred_element_type=jnp.float32)
            if at + block == length:
                scores = scores + bias_ref[here, :]
            probs = jnp.exp2(scores - log_total)
            prob_grad = lax.dot_general(value, grad, CONTRACT_LAST, preferred_element_type=jnp.float32)
            score_grad = (probs * (prob_grad - delta)).astype(jnp.bfloat16)
            value_grad = jnp.dot(probs.astype(jnp.bfloat16), grad, preferred_element_type=jnp.float32)
            key_grad = jnp.dot(score_grad, query, preferred_element_type=jnp.float32) * scale
            key_out = pl.ds(pl.multiple_of(base + out_shift, 128), WINDOW)
            value_out = pl.ds(pl.multiple_of(base + out_shift + features, 128), WINDOW)
            keyval_grad_ref[here, key_out] = jnp.where(inside, key_grad.astype(jnp.bfloat16), keyval_grad_ref[here, key_out])
            keyval_grad_ref[here, value_out] = jnp.where(inside, value_grad.astype(jnp.bfloat16), keyval_grad_ref[here, value_out])
            part = jnp.dot(
                key_t[head_rows, here].astype(jnp.bfloat16), score_grad, preferred_element_type=jnp.float32
            )
            query_grad = part if query_grad is None else query_grad + part
        wide_t[head_rows, :] = query_grad * scale

    @pl.loop(0, features // 128)
    def _(tile):
        columns = pl.ds(pl.multiple_of(tile * 128, 128), 128)
        out_ref[:, columns] = wide_t[columns, :].T.astype(jnp.bfloat16)


def attention_backward(
    query, keyval, key_bias, mixed, grad, log_total, features, block, exchanged, known, bands
):
    rows, length = query.shape[0], keyval.shape[0]
    shared = exchanged is not None
    scratch = [
        pltpu.VMEM((rows, features), jnp.bfloat16),
        pltpu.VMEM((features, length), jnp.float32),
        pltpu.VMEM((features, rows), jnp.float32),
    ]
    params = pltpu.CompilerParams(vmem_limit_bytes=56 * 2**20)
    if shared:

        def shared_kernel(both_ref, bias_ref, mixed_ref, grad_ref, log_ref, rows_ref, known_ref, out_ref, back_ref, kept_ref, *held):
            kept_ref[...] = known_ref[...]
            finish = exchange_rows(rows_ref, back_ref, *held[3:], bands=bands)
            attention_backward_kernel(
                both_ref, both_ref, bias_ref, mixed_ref, grad_ref, log_ref, out_ref, out_ref, *held[:3],
                features=features, shift=features, out_shift=features, block=block,
            )
            finish()

        anywhere, vmem = pl.BlockSpec(memory_space=pl.ANY), pl.BlockSpec(memory_space=pltpu.VMEM)
        return pl.pallas_call(
            shared_kernel,
            out_shape=(
                jax.ShapeDtypeStruct((rows, 3 * features), jnp.bfloat16),
                jax.ShapeDtypeStruct((bands, rows // bands, features), jnp.bfloat16),
                jax.ShapeDtypeStruct(known.shape, jnp.float32),
            ),
            in_specs=[vmem] * 5 + [anywhere, vmem],
            out_specs=(vmem, anywhere, vmem),
            scratch_shapes=scratch
            + [
                pltpu.SemaphoreType.DMA((bands,)),
                pltpu.SemaphoreType.DMA((bands,)),
                pltpu.SemaphoreType.DMA(()),
            ],
            cost_estimate=expected(BACKWARD_US),
            compiler_params=pltpu.CompilerParams(
                collective_id=2, has_side_effects=True, vmem_limit_bytes=56 * 2**20
            ),
        )(query, key_bias, mixed, grad, log_total, exchanged, known)
    return pl.pallas_call(
        functools.partial(
            attention_backward_kernel, features=features, shift=0, out_shift=0, block=block
        ),
        out_shape=(
            jax.ShapeDtypeStruct((rows, features), jnp.bfloat16),
            jax.ShapeDtypeStruct((length, 2 * features), jnp.bfloat16),
        ),
        scratch_shapes=scratch,
        compiler_params=params,
    )(query, keyval, key_bias, mixed, grad, log_total)


def flip(index, bit):
    return index + bit - 2 * bit * lax.rem(lax.div(index, bit), 2)


def start_kernel(
    wide_ref, tall_ref, tokens_ref, told_ref, ada_ref,
    qkv_ref, out_ref, up_ref, down_ref, rows_ref, heard_ref, silu_ref, mod_ref,
    partial, summed, banded, small_send, small_recv,
    held, turned, line_send, line_recv, row_send, row_recv, flat_send, flat_recv, local_sem,
    *, imgs, bands, qkv_part, out_part,
):
    img, band = lax.axis_index("img"), lax.axis_index("band")
    depth, width = wide_ref.shape
    tall_rows, tall_width = tall_ref.shape
    row_block = tokens_ref.shape[1]
    lanes = 128
    first = -(-(qkv_part + out_part) // lanes) * lanes
    beside_x, beside_y, sibling = flip(img, 2), flip(img, 4), flip(img, 1)
    across = flip(beside_x, 4)

    barrier = pltpu.get_barrier_semaphore()
    for step in range(1, imgs):
        other = lax.rem(img + step, imgs)
        pl.semaphore_signal(barrier, inc=1, device_id={"img": other}, device_id_type=MESH)
    for step in range(1, bands):
        pl.semaphore_signal(
            barrier, inc=1, device_id={"band": lax.rem(band + step, bands)}, device_id_type=MESH
        )
    pl.semaphore_wait(barrier, imgs + bands - 2)

    def piece(part, owner):
        if part == 2:
            return down_ref.at[:, pl.ds(pl.multiple_of(owner * tall_width, lanes), tall_width)]
        span = pl.ds(0, first) if part == 0 else pl.ds(first, width - first)
        return held.at[pl.ds(pl.multiple_of(owner * depth, 16), depth), span]

    def line_copy(part, way, step, owner, toward):
        view = piece(part, owner)
        return pltpu.make_async_remote_copy(
            src_ref=view, dst_ref=view,
            send_sem=line_send.at[part, way, step], recv_sem=line_recv.at[part, way, step],
            device_id={"band": toward}, device_id_type=MESH,
        )

    def line_sends(part, step, act):
        for way, sign in ((0, 1), (1, -1)):
            owner, toward = band - sign * step, band + sign

            @pl.when((owner >= 0) & (owner < bands) & (toward >= 0) & (toward < bands))
            def _():
                act(line_copy(part, way, step, owner, toward))

    def line_arrivals(part, step):
        for way, sign in ((0, 1), (1, -1)):
            owner = band - sign * (step + 1)

            @pl.when((owner >= 0) & (owner < bands))
            def _():
                line_copy(part, way, step, owner, band - sign).wait_recv()

    def row_copy(step):
        target = lax.rem(band + step, bands)
        return pltpu.make_async_remote_copy(
            src_ref=tokens_ref.at[target],
            dst_ref=rows_ref.at[pl.ds(pl.multiple_of(band * row_block, 16), row_block), :],
            send_sem=row_send.at[step - 1], recv_sem=row_recv.at[step - 1],
            device_id={"band": target}, device_id_type=MESH,
        )

    def row_arrival(step):
        source = lax.rem(band + bands - step, bands)
        view = rows_ref.at[pl.ds(pl.multiple_of(source * row_block, 16), row_block), :]
        return pltpu.make_async_remote_copy(
            src_ref=view, dst_ref=view,
            send_sem=row_send.at[step - 1], recv_sem=row_recv.at[step - 1],
            device_id={"band": source}, device_id_type=MESH,
        )

    def qkv_rows(owner, start=0, count=qkv_part):
        return qkv_ref.at[pl.ds(pl.multiple_of(owner * qkv_part + start, 16), count), :]

    def out_rows(owner):
        return out_ref.at[pl.ds(pl.multiple_of(owner * out_part, 16), out_part), :]

    half = (qkv_part + out_part) // 2
    own_qkv, own_out = turned.at[pl.ds(0, qkv_part), :], turned.at[pl.ds(qkv_part, out_part), :]
    plan = [
        (own_qkv, qkv_rows(img), beside_x, qkv_rows(beside_x)),
        (own_out, out_rows(img), beside_x, out_rows(beside_x)),
        (own_qkv, qkv_rows(img), beside_y, qkv_rows(beside_y)),
        (own_out, out_rows(img), beside_y, out_rows(beside_y)),
        (own_qkv, qkv_rows(img), sibling, qkv_rows(sibling)),
        (own_out, out_rows(img), sibling, out_rows(sibling)),
    ]
    for owner, toward, whole in ((beside_x, beside_y, True), (beside_y, beside_x, False)):
        if whole:
            view = qkv_rows(owner, 0, half)
            plan.append((view, view, toward, qkv_rows(across, 0, half)))
        else:
            rest = qkv_part - half
            view = qkv_rows(owner, half, rest)
            plan.append((view, view, toward, qkv_rows(across, half, rest)))
            plan.append((out_rows(owner), out_rows(owner), toward, out_rows(across)))
    for owner in (beside_x, beside_y):
        plan.append((qkv_rows(owner), qkv_rows(owner), sibling, qkv_rows(flip(owner, 1))))
        plan.append((out_rows(owner), out_rows(owner), sibling, out_rows(flip(owner, 1))))
    far = flip(across, 1)
    plan.append((qkv_rows(across, 0, half), qkv_rows(across, 0, half), sibling, qkv_rows(far, 0, half)))
    rest = qkv_part - half
    plan.append((qkv_rows(across, half, rest), qkv_rows(across, half, rest), sibling, qkv_rows(far, half, rest)))
    plan.append((out_rows(across), out_rows(across), sibling, out_rows(far)))

    def flat_copy(at):
        source, target, toward, _ = plan[at]
        return pltpu.make_async_remote_copy(
            src_ref=source, dst_ref=target, send_sem=flat_send.at[at], recv_sem=flat_recv.at[at],
            device_id={"img": toward}, device_id_type=MESH,
        )

    def flat_arrival(at):
        landing = plan[at][3]
        pltpu.make_async_remote_copy(
            src_ref=landing, dst_ref=landing, send_sem=flat_send.at[at], recv_sem=flat_recv.at[at],
            device_id={"img": sibling}, device_id_type=MESH,
        ).wait_recv()

    def turn(tile):
        span = pl.ds(pl.multiple_of(tile * lanes, lanes), lanes)
        turned[span, :] = held[:, span].astype(jnp.float32).T.astype(jnp.bfloat16)

    start = lambda copy: copy.start()
    own_rows = pltpu.make_async_copy(
        tokens_ref.at[band],
        rows_ref.at[pl.ds(pl.multiple_of(band * row_block, 16), row_block), :],
        local_sem.at[0],
    )
    own_rows.start()

    def small_copy(source, target, kind, step, axis, toward):
        return pltpu.make_async_remote_copy(
            src_ref=source, dst_ref=target,
            send_sem=small_send.at[kind, step], recv_sem=small_recv.at[kind, step],
            device_id={axis: toward}, device_id_type=MESH,
        )

    def told(step):
        return small_copy(told_ref, heard_ref.at[img], 0, step, "img", lax.rem(img + step, imgs))

    def partial_copy(step):
        other = lax.rem(img + step, imgs)
        return small_copy(partial.at[other], summed.at[img], 1, step, "img", other)

    def banded_copy(step):
        other = lax.rem(band + step, bands)
        return small_copy(summed.at[:, other], banded.at[band], 2, step, "band", other)

    def arrival(view, kind, step, axis):
        me, count = (img, imgs) if axis == "img" else (band, bands)
        small_copy(view, view, kind, step, axis, lax.rem(me + count - step, count)).wait_recv()

    for step in range(1, imgs):
        told(step).start()
    held[pl.ds(pl.multiple_of(band * depth, 16), depth), :] = wide_ref[...]
    down_ref[:, pl.ds(pl.multiple_of(band * tall_width, lanes), tall_width)] = tall_ref[...]
    line_sends(0, 0, start)
    heard_ref[img] = told_ref[...]
    for step in range(bands - 1):
        line_arrivals(0, step)
        if step < bands - 2:
            line_sends(0, step + 1, start)
    line_sends(1, 0, start)
    line_sends(2, 0, start)
    for step in range(1, bands):
        row_copy(step).start()
    pl.loop(0, first // lanes)(turn)
    keep_qkv = pltpu.make_async_copy(own_qkv, qkv_rows(img), local_sem.at[1])
    keep_out = pltpu.make_async_copy(own_out, out_rows(img), local_sem.at[2])
    for at in range(6):
        flat_copy(at).start()
    keep_qkv.start()
    keep_out.start()
    for step in range(1, imgs):
        arrival(heard_ref.at[lax.rem(img + imgs - step, imgs)], 0, step, "img")
    images = partial.shape[1]
    for other in range(imgs):
        for image in range(images):
            silu_ref[pl.ds(other * images + image, 1), :] = heard_ref[
                other, :, pl.ds(image * depth, depth)
            ]
    products = jnp.dot(
        silu_ref[...].astype(jnp.bfloat16), ada_ref[...], preferred_element_type=jnp.float32
    )
    for other in range(imgs):
        for image in range(images):
            at = other * images + image
            partial[other, image] = products[at : at + 1, :]
    for step in range(1, imgs):
        partial_copy(step).start()
    summed[img] = partial[img]
    for step in range(bands - 2):
        for part in (1, 2):
            line_arrivals(part, step)
            line_sends(part, step + 1, start)
    for arrived, sent in (((0, 1), (6, 9, 10)), ((2, 3), (7, 8, 11, 12))):
        for at in arrived:
            flat_arrival(at)
        for at in sent:
            flat_copy(at).start()
    for step in range(1, imgs):
        arrival(summed.at[lax.rem(img + imgs - step, imgs)], 1, step, "img")
    for step in range(1, bands):
        banded_copy(step).start()
    banded[band] = summed[:, band]
    for at in (6, 7, 8):
        flat_arrival(at)
        flat_copy(at + 7).start()
    for part in (1, 2):
        line_arrivals(part, bands - 2)
    pl.loop(first // lanes, width // lanes)(turn)
    up_ref[...] = turned[pl.ds(qkv_part + out_part, width - qkv_part - out_part), :]
    for step in range(1, bands):
        arrival(banded.at[lax.rem(band + bands - step, bands)], 2, step, "band")
    total = banded[0]
    for at in range(1, bands):
        total += banded[at]
    mod_ref[...] = total
    for part in range(3):
        for step in range(bands - 1):
            line_sends(part, step, lambda copy: copy.wait_send())
    for at in (4, 5, 9, 10, 11, 12, 13, 14, 15):
        flat_arrival(at)
    for at in range(16):
        flat_copy(at).wait_send()
    for step in range(1, bands):
        row_copy(step).wait_send()
        row_arrival(step).wait_recv()
        banded_copy(step).wait_send()
    for step in range(1, imgs):
        told(step).wait_send()
        partial_copy(step).wait_send()
    own_rows.wait()
    keep_qkv.wait()
    keep_out.wait()


def start_exchange(wide, tall, tokens, told, ada, bands, imgs, qkv_part, out_part):
    depth, width = wide.shape
    up_part = width - qkv_part - out_part
    low = jnp.bfloat16
    anywhere, vmem = pl.BlockSpec(memory_space=pl.ANY), pl.BlockSpec(memory_space=pltpu.VMEM)
    features = depth * bands
    images = tokens.shape[0]
    ada_columns = ada.shape[1]
    return pl.pallas_call(
        functools.partial(
            start_kernel, imgs=imgs, bands=bands, qkv_part=qkv_part, out_part=out_part
        ),
        out_shape=(
            jax.ShapeDtypeStruct((qkv_part * imgs, features), low),
            jax.ShapeDtypeStruct((out_part * imgs, features), low),
            jax.ShapeDtypeStruct((up_part, features), low),
            jax.ShapeDtypeStruct((tall.shape[0], tall.shape[1] * bands), low),
            jax.ShapeDtypeStruct((tokens.shape[1] * bands, tokens.shape[2]), low),
            jax.ShapeDtypeStruct((imgs,) + told.shape, jnp.float32),
            jax.ShapeDtypeStruct((imgs * images, depth), jnp.float32),
            jax.ShapeDtypeStruct((imgs, 1, ada_columns), jnp.float32),
        ),
        in_specs=[vmem, vmem, anywhere, vmem, vmem],
        out_specs=(anywhere, anywhere, vmem, vmem, anywhere, vmem, vmem, vmem),
        scratch_shapes=[
            pltpu.VMEM((imgs, images, 1, ada_columns), jnp.float32),
            pltpu.VMEM((imgs, images, 1, ada_columns), jnp.float32),
            pltpu.VMEM((bands, imgs, 1, ada_columns), jnp.float32),
            pltpu.SemaphoreType.DMA((3, imgs)),
            pltpu.SemaphoreType.DMA((3, imgs)),
            pltpu.VMEM((features, width), low),
            pltpu.VMEM((width, features), low),
            pltpu.SemaphoreType.DMA((3, 2, bands - 1)),
            pltpu.SemaphoreType.DMA((3, 2, bands - 1)),
            pltpu.SemaphoreType.DMA((bands - 1,)),
            pltpu.SemaphoreType.DMA((bands - 1,)),
            pltpu.SemaphoreType.DMA((16,)),
            pltpu.SemaphoreType.DMA((16,)),
            pltpu.SemaphoreType.DMA((3,)),
        ],
        cost_estimate=expected(START_US),
        compiler_params=pltpu.CompilerParams(
            collective_id=0, has_side_effects=True, vmem_limit_bytes=48 * 2**20
        ),
    )(wide, tall, tokens, told, ada)


def add_low(left, right):
    return (left.astype(jnp.float32) + right.astype(jnp.float32)).astype(jnp.bfloat16)


def tail_kernel(
    qkv_ref, out_ref, up_ref, rows_ref, pieces_ref, silu_ref, known_ref,
    wide_ref, back_ref, ada_ref, bias_ref, squares_ref,
    pieces, terms, square_flat, square_line, small_send, small_recv,
    own, from_core, first_x, first_y, last_x, last_y, turned, held, held_in,
    core_send, core_recv, flat_send, flat_recv, line_send, line_recv, row_send, row_recv, local_sem,
    *, imgs, bands,
):
    img, band = lax.axis_index("img"), lax.axis_index("band")
    qkv_part, out_part = qkv_ref.shape[0] // imgs, out_ref.shape[0] // imgs
    both = own.shape[1]
    depth, width = wide_ref.shape
    row_block = back_ref.shape[1]
    half = first_x.shape[1]
    lanes = 128
    beside_x, beside_y, sibling = flip(img, 2), flip(img, 4), flip(img, 1)
    chips = (img, beside_x, beside_y, flip(beside_x, 4))
    upper, lower = pl.ds(0, half), pl.ds(half, both - half)
    spans = (pl.ds(0, qkv_part), pl.ds(qkv_part, out_part))

    barrier = pltpu.get_barrier_semaphore()
    for step in range(1, imgs):
        other = lax.rem(img + step, imgs)
        pl.semaphore_signal(barrier, inc=1, device_id={"img": other}, device_id_type=MESH)
    for step in range(1, bands):
        pl.semaphore_signal(
            barrier, inc=1, device_id={"band": lax.rem(band + step, bands)}, device_id_type=MESH
        )
    pl.semaphore_wait(barrier, imgs + bands - 2)

    def grad_rows(kind, owner):
        source, count = ((qkv_ref, qkv_part), (out_ref, out_part))[kind]
        return source.at[pl.ds(pl.multiple_of(owner * count, 16), count), :]

    def core_copy(kind, at):
        return pltpu.make_async_remote_copy(
            src_ref=grad_rows(kind, flip(chips[at], 1)), dst_ref=from_core.at[at, spans[kind]],
            send_sem=core_send.at[kind, at], recv_sem=core_recv.at[kind, at],
            device_id={"img": sibling}, device_id_type=MESH,
        )

    def own_copy(kind, at):
        return pltpu.make_async_copy(
            grad_rows(kind, chips[at]), own.at[at, spans[kind]], local_sem.at[4 * kind + at]
        )

    plan = (
        (own.at[1, upper], first_x.at[0], beside_x),
        (own.at[3, upper], first_x.at[1], beside_x),
        (own.at[2, lower], first_y.at[0], beside_y),
        (own.at[3, lower], first_y.at[1], beside_y),
        (own.at[2, upper], last_y, beside_y),
        (own.at[1, lower], last_x, beside_x),
    )

    def flat_copy(at):
        source, target, toward = plan[at]
        return pltpu.make_async_remote_copy(
            src_ref=source, dst_ref=target, send_sem=flat_send.at[at], recv_sem=flat_recv.at[at],
            device_id={"img": toward}, device_id_type=MESH,
        )

    def row_span(owner):
        return pl.ds(pl.multiple_of(owner * row_block, 16), row_block)

    def row_copy(step):
        target = lax.rem(band + step, bands)
        return pltpu.make_async_remote_copy(
            src_ref=rows_ref.at[row_span(target), :], dst_ref=back_ref.at[band],
            send_sem=row_send.at[step - 1], recv_sem=row_recv.at[step - 1],
            device_id={"band": target}, device_id_type=MESH,
        )

    def row_arrival(step):
        source = lax.rem(band + bands - step, bands)
        return pltpu.make_async_remote_copy(
            src_ref=back_ref.at[source], dst_ref=back_ref.at[source],
            send_sem=row_send.at[step - 1], recv_sem=row_recv.at[step - 1],
            device_id={"band": source}, device_id_type=MESH,
        )

    first = -(-both // lanes) * lanes
    parts = (pl.ds(0, first), pl.ds(first, width - first))

    def piece(part, owner, way=None):
        down = pl.ds(pl.multiple_of(owner * depth, 16), depth)
        return held.at[down, parts[part]] if way is None else held_in.at[way, down, parts[part]]

    def line_copy(part, way, owner, toward):
        return pltpu.make_async_remote_copy(
            src_ref=piece(part, owner), dst_ref=piece(part, owner, way),
            send_sem=line_send.at[part, way, owner], recv_sem=line_recv.at[part, way, owner],
            device_id={"band": toward}, device_id_type=MESH,
        )

    def line_ends(part):
        for step in range(bands - 1):

            @pl.when(band == 0)
            def _():
                line_copy(part, 0, bands - 1 - step, band + 1).start()

            @pl.when(band == bands - 1)
            def _():
                line_copy(part, 1, step, band - 1).start()

    def line_round(part, step):
        for way, owner, sign in ((0, bands - 1 - step, 1), (1, step, -1)):

            @pl.when((sign * (owner - band) > 0) & (band > 0) & (band < bands - 1))
            def _():
                copy = line_copy(part, way, owner, band + sign)
                copy.wait_recv()
                mine = piece(part, owner)
                mine[...] = add_low(mine[...], piece(part, owner, way)[...])
                copy.start()

    def line_finish(part):
        span = parts[part]
        wide_ref[:, span] = piece(part, band)[...].astype(jnp.float32)
        for way, sign in ((0, 1), (1, -1)):

            @pl.when((band - sign >= 0) & (band - sign < bands))
            def _():
                line_copy(part, way, band, band - sign).wait_recv()
                wide_ref[:, span] += piece(part, band, way)[...].astype(jnp.float32)

    def line_sent(part):
        for way, sign in ((0, 1), (1, -1)):
            for owner in range(bands):

                @pl.when(sign * (owner - band) > 0)
                def _():
                    line_copy(part, way, owner, band + sign).wait_send()

    def turn(tile):
        span = pl.ds(pl.multiple_of(tile * lanes, lanes), lanes)
        held[:, span] = turned[span, :].astype(jnp.float32).T.astype(jnp.bfloat16)

    def small_copy(source, target, kind, step, axis, toward):
        return pltpu.make_async_remote_copy(
            src_ref=source, dst_ref=target,
            send_sem=small_send.at[kind, step], recv_sem=small_recv.at[kind, step],
            device_id={axis: toward}, device_id_type=MESH,
        )

    def piece_flat(step):
        other = lax.rem(img + step, imgs)
        return small_copy(pieces_ref.at[other], pieces.at[band, img], 0, step, "img", other)

    def piece_line(step):
        other = lax.rem(band + step, bands)
        return small_copy(pieces.at[band], pieces.at[band], 1, step, "band", other)

    def square_one(step):
        other = lax.rem(img + step, imgs)
        return small_copy(square_flat.at[img], square_flat.at[img], 2, step, "img", other)

    def square_two(step):
        other = lax.rem(band + step, bands)
        return small_copy(square_line.at[band], square_line.at[band], 3, step, "band", other)

    def arrival(view, kind, step, axis):
        me, count = (img, imgs) if axis == "img" else (band, bands)
        small_copy(view, view, kind, step, axis, lax.rem(me + count - step, count)).wait_recv()

    order = (3, 1, 2, 0)
    for step in range(1, bands):
        row_copy(step).start()
    for step in range(1, imgs):
        piece_flat(step).start()
    keep_piece = pltpu.make_async_copy(pieces_ref.at[img], pieces.at[band, img], local_sem.at[9])
    keep_piece.start()
    for at in order:
        core_copy(0, at).start()
        core_copy(1, at).start()
    for at in order:
        own_copy(0, at).start()
        own_copy(1, at).start()
    keep = pltpu.make_async_copy(rows_ref.at[row_span(band), :], back_ref.at[band], local_sem.at[8])
    keep.start()
    turned[pl.ds(both, width - both), :] = up_ref[...]
    pl.loop(first // lanes, width // lanes)(turn)
    line_ends(1)
    for at in order:
        for kind in range(2):
            own_copy(kind, at).wait()
            core_copy(kind, at).wait_recv()
        own[at] = add_low(own[at], from_core[at])
        for ready in {3: (1, 3), 1: (0,), 2: (2,), 0: ()}[at]:
            flat_copy(ready).start()
    keep_piece.wait()
    for step in range(1, imgs):
        arrival(pieces.at[band, lax.rem(img + imgs - step, imgs)], 0, step, "img")
    for step in range(1, bands):
        piece_line(step).start()
    flat_copy(1).wait_recv()
    own[2, upper] = add_low(own[2, upper], first_x[1])
    flat_copy(4).start()
    flat_copy(3).wait_recv()
    own[1, lower] = add_low(own[1, lower], first_y[1])
    flat_copy(5).start()
    line_round(1, 0)
    flat_copy(0).wait_recv()
    flat_copy(2).wait_recv()
    flat_copy(4).wait_recv()
    flat_copy(5).wait_recv()
    turned[upper, :] = (
        own[0, upper].astype(jnp.float32)
        + first_x[0].astype(jnp.float32)
        + last_y[...].astype(jnp.float32)
    ).astype(jnp.bfloat16)
    turned[lower, :] = (
        own[0, lower].astype(jnp.float32)
        + first_y[0].astype(jnp.float32)
        + last_x[...].astype(jnp.float32)
    ).astype(jnp.bfloat16)
    pl.loop(0, first // lanes)(turn)
    line_ends(0)
    for step in range(bands - 1):
        line_round(0, step)
        if step > 0:
            line_round(1, step)
    for step in range(1, bands):
        arrival(pieces.at[lax.rem(band + bands - step, bands)], 1, step, "band")
    for image in range(imgs):
        for at in range(bands):
            terms[pl.ds(image * bands + at, 1), :] = pieces[at, image]
    columns = ada_ref.shape[1]
    ada = lax.dot_general(
        silu_ref[...], terms[:, pl.ds(0, columns)], (((1,), (0,)), ((), ())),
        precision=lax.Precision.HIGHEST, preferred_element_type=jnp.float32,
    )
    ada_ref[...] = ada
    bias_rows, bias_columns = bias_ref.shape
    bias = jnp.sum(terms[:, pl.ds(columns, bias_rows * bias_columns)], axis=0, keepdims=True)
    for at in range(bias_rows):
        bias_ref[pl.ds(at, 1), :] = bias[:, at * bias_columns : (at + 1) * bias_columns]
    squares = jnp.sum(ada * ada, axis=0, keepdims=True)
    squares = jnp.sum(squares, axis=1, keepdims=True)
    squares += jnp.sum(bias * bias, axis=1, keepdims=True) / bands
    line_finish(1)
    line_finish(0)
    rows = jnp.sum(wide_ref[...] * wide_ref[...], axis=0, keepdims=True)
    squares += jnp.sum(rows, axis=1, keepdims=True) + known_ref[0:1, 0:1]
    square_flat[img] = jnp.broadcast_to(squares, square_flat.shape[1:])
    for step in range(1, imgs):
        square_one(step).start()
    for step in range(1, imgs):
        arrival(square_flat.at[lax.rem(img + imgs - step, imgs)], 2, step, "img")
    total = square_flat[0]
    for at in range(1, imgs):
        total += square_flat[at]
    square_line[band] = total
    for step in range(1, bands):
        square_two(step).start()
    for step in range(1, bands):
        arrival(square_line.at[lax.rem(band + bands - step, bands)], 3, step, "band")
    total = square_line[0]
    for at in range(1, bands):
        total += square_line[at]
    squares_ref[...] = total
    line_sent(0)
    line_sent(1)
    for step in range(1, imgs):
        piece_flat(step).wait_send()
        square_one(step).wait_send()
    for step in range(1, bands):
        piece_line(step).wait_send()
        square_two(step).wait_send()
    for at in range(4):
        core_copy(0, at).wait_send()
        core_copy(1, at).wait_send()
    for at in range(6):
        flat_copy(at).wait_send()
    for step in range(1, bands):
        row_copy(step).wait_send()
        row_arrival(step).wait_recv()
    keep.wait()


def tail_exchange(qkv_grad, out_grad, up_sum, rows, pieces, silu, known, bias_shape, bands, imgs):
    low = jnp.bfloat16
    features = qkv_grad.shape[1]
    both = (qkv_grad.shape[0] + out_grad.shape[0]) // imgs
    width = both + up_sum.shape[0]
    half = -(-both // 32) * 16
    ada_columns = pieces.shape[2] - bias_shape[0] * bias_shape[1]
    anywhere, vmem = pl.BlockSpec(memory_space=pl.ANY), pl.BlockSpec(memory_space=pltpu.VMEM)
    return pl.pallas_call(
        functools.partial(tail_kernel, imgs=imgs, bands=bands),
        out_shape=(
            jax.ShapeDtypeStruct((features // bands, width), jnp.float32),
            jax.ShapeDtypeStruct((bands, rows.shape[0] // bands, features), low),
            jax.ShapeDtypeStruct((silu.shape[0], ada_columns), jnp.float32),
            jax.ShapeDtypeStruct(bias_shape, jnp.float32),
            jax.ShapeDtypeStruct((8, 128), jnp.float32),
        ),
        in_specs=[anywhere, anywhere, vmem, anywhere, vmem, vmem, vmem],
        out_specs=(vmem, anywhere, vmem, vmem, vmem),
        scratch_shapes=[
            pltpu.VMEM((bands,) + pieces.shape, jnp.float32),
            pltpu.VMEM((bands * imgs, pieces.shape[2]), jnp.float32),
            pltpu.VMEM((imgs, 8, 128), jnp.float32),
            pltpu.VMEM((bands, 8, 128), jnp.float32),
            pltpu.SemaphoreType.DMA((4, imgs)),
            pltpu.SemaphoreType.DMA((4, imgs)),
            pltpu.VMEM((4, both, features), low),
            pltpu.VMEM((4, both, features), low),
            pltpu.VMEM((2, half, features), low),
            pltpu.VMEM((2, both - half, features), low),
            pltpu.VMEM((both - half, features), low),
            pltpu.VMEM((half, features), low),
            pltpu.VMEM((width, features), low),
            pltpu.VMEM((features, width), low),
            pltpu.VMEM((2, features, width), low),
            pltpu.SemaphoreType.DMA((2, 4)),
            pltpu.SemaphoreType.DMA((2, 4)),
            pltpu.SemaphoreType.DMA((6,)),
            pltpu.SemaphoreType.DMA((6,)),
            pltpu.SemaphoreType.DMA((2, 2, bands)),
            pltpu.SemaphoreType.DMA((2, 2, bands)),
            pltpu.SemaphoreType.DMA((bands - 1,)),
            pltpu.SemaphoreType.DMA((bands - 1,)),
            pltpu.SemaphoreType.DMA((10,)),
        ],
        cost_estimate=expected(TAIL_US),
        compiler_params=pltpu.CompilerParams(
            collective_id=1, has_side_effects=True, vmem_limit_bytes=50 * 2**20
        ),
    )(qkv_grad, out_grad, up_sum, rows, pieces, silu, known)


def adam_kernel(*refs):
    squares_ref, wide_ref, tall_ref, ada_ref, bias_ref = refs[:5]
    sources, results = refs[5:23], refs[23:]
    norm = jnp.sqrt(squares_ref[0:1, 0:1])
    factor = clip_norm / jnp.maximum(norm, clip_norm)
    qkv_part = sources[3].shape[1]
    both = qkv_part + sources[6].shape[1]
    rates = (learn_rate, learn_rate, out_rate, learn_rate, learn_rate, bias_rate)

    def update(which, rows, gradient):
        weight_ref, first_ref, second_ref = sources[3 * which : 3 * which + 3]
        new = adam_update(
            weight_ref[rows, :], first_ref[rows, :], second_ref[rows, :], gradient, factor, rates[which]
        )
        for into, value in zip(results[3 * which : 3 * which + 3], new):
            into[rows, :] = value

    depth = wide_ref.shape[0]
    block = next(rows for rows in (32, 16, 8) if depth % rows == 0)

    @pl.loop(0, depth // block)
    def _(step):
        rows = pl.ds(pl.multiple_of(step * block, block), block)
        update(0, rows, ada_ref[rows, :])
        update(1, rows, wide_ref[rows, :qkv_part])
        update(2, rows, wide_ref[rows, qkv_part:both])
        update(3, rows, wide_ref[rows, both:])

    tall_rows = tall_ref.shape[0]
    tall_block = 16 if tall_rows % 16 == 0 else tall_rows
    for start in range(0, tall_rows, tall_block):
        rows = pl.ds(start, tall_block)
        update(4, rows, tall_ref[rows, :])

    update(5, slice(None), bias_ref[...])
    results[18][...] = bias_ref[pl.ds(13, 1), :] * factor


def adam_all(squares, wide, tall, ada, bias, groups):
    flat = [array for group in groups for array in group]
    return pl.pallas_call(
        adam_kernel,
        out_shape=[jax.ShapeDtypeStruct(array.shape, jnp.float32) for array in flat]
        + [jax.ShapeDtypeStruct((1, bias.shape[1]), jnp.float32)],
        compiler_params=pltpu.CompilerParams(vmem_limit_bytes=50 * 2**20),
    )(squares, wide, tall, ada, bias, *flat)


def body(
    inputs,
    condition,
    valid_rows,
    cotangent,
    ada_weight,
    qkv_weight,
    out_weight,
    up_weight,
    down_weight,
    biases,
    ada_first,
    qkv_first,
    out_first,
    up_first,
    down_first,
    bias_first,
    ada_second,
    qkv_second,
    out_second,
    up_second,
    down_second,
    bias_second,
):
    images, local_rows, features = inputs.shape
    length = L
    head_count = HEADS
    head_size = HEAD_DIM
    score_scale = head_size ** (-0.5)
    band_count = lax.axis_size("band")
    img_count = lax.axis_size("img")
    band_rank = lax.axis_index("band")
    img_rank = lax.axis_index("img")
    own = max(1, images // band_count)
    split = max(1, band_count // images)
    mates = band_count // split
    image_rows = length // split
    exchange_groups = None
    share_groups = None
    if split > 1:
        exchange_groups = [[g * mates + m for m in range(mates)] for g in range(split)]
        share_groups = [[g * mates + m for g in range(split)] for m in range(mates)]
    low_type = jnp.bfloat16

    def to_images(rows):
        return lax.all_to_all(rows, "band", split_axis=0, concat_axis=1, axis_index_groups=exchange_groups, tiled=True)

    def to_bands(whole):
        cut = whole.reshape(own, mates, local_rows, features).transpose(1, 0, 2, 3)
        back = lax.all_to_all(
            cut, "band", split_axis=0, concat_axis=0, axis_index_groups=exchange_groups, tiled=True
        )
        return back.reshape(images, local_rows, features)

    def after(value, *earlier):
        return lax.optimization_barrier((value,) + earlier)[0]

    def sum_everywhere(partial):
        sent = jnp.broadcast_to(partial, (img_count * band_count, 128))
        got = lax.all_to_all(sent, ("img", "band"), split_axis=0, concat_axis=0, tiled=True)
        return jnp.sum(got[:, 0])

    qkv_part, out_part = qkv_weight.shape[1], out_weight.shape[1]

    bias_rows, bias_columns = biases.shape
    ada_rows, ada_columns = ada_weight.shape
    silu_own = lax.reduce_precision(jax.nn.silu(condition.astype(jnp.float32)), 8, 7)
    silu_own = lax.dynamic_slice_in_dim(silu_own, band_rank * ada_rows, ada_rows, axis=1)
    told = jnp.concatenate(
        [silu_own.reshape(1, -1), lax.reduce_precision(biases, 8, 7).reshape(1, -1)],
        axis=1,
    )
    ada_low = ada_weight.astype(low_type)
    wide = jnp.concatenate([qkv_weight, out_weight, up_weight], axis=1).astype(low_type)
    tall = down_weight.T.astype(low_type)
    if img_count == 8 and own == 1 and split == 1:
        qkv_full, out_full, up_rows, down_rows, tokens_low, heard, silu_rows, mod_summed = (
            start_exchange(
                wide, tall, inputs, told, ada_low, band_count, img_count, qkv_part, out_part
            )
        )
        tokens_low = tokens_low.reshape(own, image_rows, features)
        mod_summed = mod_summed.reshape(own, img_count * ada_columns)
    else:
        turned = lax.all_gather(wide, "band", axis=0, tiled=True).T
        qkv_full = lax.all_gather(turned[:qkv_part], "img", axis=0, tiled=True)
        out_full = lax.all_gather(
            turned[qkv_part : qkv_part + out_part], "img", axis=0, tiled=True
        )
        up_rows = turned[qkv_part + out_part :]
        down_rows = lax.all_gather(tall, "band", axis=1, tiled=True)
        tokens_low = to_images(inputs)
        heard = lax.all_gather(told, "img", axis=0, tiled=True)
        silu_rows = heard[:, : images * ada_rows].reshape(img_count * images, ada_rows)
        mod_partial = jnp.dot(
            silu_rows.astype(low_type), ada_low, preferred_element_type=jnp.float32
        )
        mod_sent = jnp.tile(
            mod_partial.reshape(img_count, 1, images * ada_columns), (1, split, 1)
        )
        mod_pieces = lax.all_to_all(
            mod_sent.reshape(img_count * band_count, own * ada_columns),
            ("img", "band"),
            split_axis=0,
            concat_axis=0,
            tiled=True,
        ).reshape(img_count, band_count, own, ada_columns)
        mod_summed = (
            jnp.sum(mod_pieces, axis=1).transpose(1, 0, 2).reshape(own, img_count * ada_columns)
        )
    up_full = lax.all_gather(up_rows, "img", axis=0, tiled=True)
    down_full = lax.all_gather(after(down_rows, up_rows), "img", axis=0, tiled=True)
    bias_vals = (
        heard.reshape(img_count, -1)[:, images * ada_rows :]
        .reshape(img_count, bias_rows, bias_columns)
        .transpose(1, 0, 2)
        .reshape(bias_rows, features)
    )
    modulation = mod_summed + bias_vals[0:6].reshape(-1)
    mod_parts = modulation.reshape(own, 6, 1, features)
    shift_one = mod_parts[:, 0]
    scale_one = mod_parts[:, 1]
    gate_one = mod_parts[:, 2]
    shift_two = mod_parts[:, 3]
    scale_two = mod_parts[:, 4]
    gate_two = mod_parts[:, 5]
    valid_own = lax.dynamic_slice_in_dim(valid_rows, lax.rem(band_rank, mates) * own, own, axis=0)
    key_mask = jnp.arange(length, dtype=jnp.int32)[None, :] < valid_own[:, None]
    positions = lax.div(band_rank, mates) * image_rows + jnp.arange(image_rows, dtype=jnp.int32)
    row_mask = (positions[None, :] < valid_own[:, None]).astype(jnp.float32)[:, :, None]
    tokens_in = tokens_low.astype(jnp.float32)
    normed_one, inverse_one = normalize_keep(tokens_in)
    first_in = (normed_one * (1.0 + scale_one) + shift_one).astype(jnp.bfloat16)
    cotangent_low = to_images(after(cotangent, tokens_low))
    grad_out = cotangent_low.astype(jnp.float32) * row_mask
    qkv_bias = jnp.concatenate([bias_vals[6], jnp.zeros((features,), jnp.float32), bias_vals[7]])
    projected = (
        jnp.einsum("ird,ed->ire", first_in, qkv_full, preferred_element_type=jnp.float32) + qkv_bias
    ).astype(jnp.bfloat16)
    key_bias = jnp.where(key_mask, 0.0, very_low).astype(jnp.float32)[:, :, None]
    queries = [projected[i] for i in range(own)]
    if split > 1:
        keys_values = lax.all_gather(
            projected[..., features:], "band", axis=1, axis_index_groups=share_groups, tiled=True
        )
        keys_values = [keys_values[i] for i in range(own)]
        key_shift = 0
    else:
        keys_values = queries
        key_shift = features
    mixed, log_total = zip(
        *[
            attention_forward(queries[i], keys_values[i], key_bias[i], features, key_shift, 512)
            for i in range(own)
        ]
    )
    mixed_parts = mixed
    mixed = jnp.stack(mixed)
    attended = (
        jnp.einsum("ird,ed->ire", mixed, out_full, preferred_element_type=jnp.float32)
        + bias_vals[8]
    )
    middle = tokens_in + gate_one * attended
    normed_two, inverse_two = normalize_keep(middle)
    second_in = (normed_two * (1.0 + scale_two) + shift_two).astype(jnp.bfloat16)
    hidden_pre = jnp.einsum(
        "ird,fd->irf", second_in, up_full, preferred_element_type=jnp.float32
    ) + bias_vals[9:13].reshape(-1)
    hidden, gelu_back = jax.vjp(smooth_gate, hidden_pre)
    hidden_low = hidden.astype(jnp.bfloat16)
    branch = (
        jnp.einsum("irf,df->ird", hidden_low, down_full, preferred_element_type=jnp.float32)
        + bias_vals[13]
    )
    output_low = (middle + gate_two * branch).astype(jnp.bfloat16)
    branch_grad = (gate_two * grad_out).astype(jnp.bfloat16)
    gate_two_grad = jnp.sum(grad_out * branch, axis=1)
    down_grad = jnp.einsum(
        "ird,irf->df", branch_grad, hidden_low, preferred_element_type=jnp.float32
    ).astype(low_type)
    down_sum = lax.psum_scatter(down_grad, "img", scatter_dimension=0, tiled=True)
    hidden_grad = jnp.einsum(
        "ird,df->irf",
        after(branch_grad, down_grad),
        down_full,
        preferred_element_type=jnp.float32,
    )
    pre_grad = gelu_back(hidden_grad)[0].astype(jnp.bfloat16)
    up_grad = jnp.einsum(
        "irf,ird->fd", pre_grad, second_in, preferred_element_type=jnp.float32
    ).astype(low_type)
    up_sum = lax.psum_scatter(up_grad, "img", scatter_dimension=0, tiled=True)
    second_grad = jnp.einsum("irf,fd->ird", after(pre_grad, up_grad), up_full, preferred_element_type=jnp.float32)
    shift_two_grad = jnp.sum(second_grad, axis=1)
    scale_two_grad = jnp.sum(second_grad * normed_two, axis=1)
    middle_grad = grad_out + normalize_back(
        normed_two, inverse_two, second_grad * (1.0 + scale_two)
    )
    attended_grad = (gate_one * middle_grad).astype(jnp.bfloat16)
    gate_one_grad = jnp.sum(middle_grad * attended, axis=1)
    out_grad = jnp.einsum(
        "ire,ird->ed", attended_grad, mixed, preferred_element_type=jnp.float32
    ).astype(low_type)
    mixed_grad = jnp.einsum(
        "ire,ed->ird", after(attended_grad, out_grad), out_full, preferred_element_type=jnp.float32
    ).astype(jnp.bfloat16)
    tall_cut = down_sum.reshape(down_sum.shape[0], band_count, -1).transpose(1, 0, 2)
    tall_shard = jnp.sum(
        lax.all_to_all(tall_cut, "band", split_axis=0, concat_axis=0, tiled=True).astype(jnp.float32),
        axis=0,
    )
    hosted = img_count == 8 and own == 1 and split == 1
    tall_squares = jnp.broadcast_to(jnp.sum(tall_shard * tall_shard), (8, 128))
    attention_grads = [
        attention_backward(
            queries[i], keys_values[i], key_bias[i], mixed_parts[i], mixed_grad[i], log_total[i],
            features, 512, output_low[i] if hosted else None, tall_squares, band_count,
        )
        for i in range(own)
    ]
    if hosted:
        output, tall_squares = attention_grads[0][1:]
    else:
        output = to_bands(output_low)
    if split > 1:
        shared_grads = lax.psum_scatter(
            jnp.stack([pair[1] for pair in attention_grads]),
            "band",
            scatter_dimension=1,
            axis_index_groups=share_groups,
            tiled=True,
        )
        qkv_grad = jnp.concatenate(
            [jnp.stack([pair[0] for pair in attention_grads]), shared_grads], axis=-1
        )
    elif hosted:
        qkv_grad = attention_grads[0][0][None]
    else:
        qkv_grad = jnp.stack([jnp.concatenate(pair, axis=-1) for pair in attention_grads])
    qkv_sums = jnp.sum(qkv_grad.astype(jnp.float32), axis=(0, 1))
    qkv_weight_grad = jnp.einsum(
        "ire,ird->ed", qkv_grad, first_in, preferred_element_type=jnp.float32
    ).astype(low_type)
    first_grad = jnp.einsum("ire,ed->ird", after(qkv_grad, qkv_weight_grad), qkv_full, preferred_element_type=jnp.float32)
    shift_one_grad = jnp.sum(first_grad, axis=1)
    scale_one_grad = jnp.sum(first_grad * normed_one, axis=1)
    input_grad_low = (
        middle_grad + normalize_back(normed_one, inverse_one, first_grad * (1.0 + scale_one))
    ).astype(low_type)
    mod_grad = jnp.stack(
        [
            shift_one_grad,
            scale_one_grad,
            gate_one_grad,
            shift_two_grad,
            scale_two_grad,
            gate_two_grad,
        ],
        axis=1,
    )
    row_sums = jnp.concatenate(
        [
            qkv_sums[:features][None],
            qkv_sums[2 * features :][None],
            jnp.sum(attended_grad.astype(jnp.float32), axis=(0, 1))[None],
            jnp.sum(pre_grad.astype(jnp.float32), axis=(0, 1)).reshape(4, features),
            jnp.sum(branch_grad.astype(jnp.float32), axis=(0, 1))[None],
        ],
        axis=0,
    )
    pieces = jnp.concatenate(
        [
            mod_grad.reshape(own, img_count, ada_columns)
            .transpose(1, 0, 2)
            .reshape(img_count, own * ada_columns),
            jnp.concatenate([jnp.sum(mod_grad, axis=0).reshape(6, features), row_sums], axis=0)
            .reshape(bias_rows, img_count, bias_columns)
            .transpose(1, 0, 2)
            .reshape(img_count, -1),
        ],
        axis=1,
    )
    silu_terms = jnp.tile(
        silu_rows.reshape(img_count, 1, images, ada_rows), (1, split, 1, 1)
    ).reshape(img_count * band_count * own, ada_rows)
    if img_count == 8 and own == 1 and split == 1:
        wide_shard, input_grad_low, ada_shard, bias_total, squares_total = tail_exchange(
            qkv_weight_grad,
            out_grad,
            up_sum,
            input_grad_low[0],
            pieces[:, None],
            silu_terms.T,
            tall_squares,
            biases.shape,
            band_count,
            img_count,
        )
    else:
        sent = jnp.broadcast_to(
            pieces[:, None], (img_count, band_count, pieces.shape[1])
        ).reshape(img_count * band_count, -1)
        got = lax.all_to_all(sent, ("img", "band"), split_axis=0, concat_axis=0, tiled=True)
        ada_shard = jnp.einsum(
            "id,ie->de",
            silu_terms,
            got[:, : own * ada_columns].reshape(-1, ada_columns),
            precision=lax.Precision.HIGHEST,
        )
        bias_total = jnp.sum(got[:, own * ada_columns :], axis=0).reshape(bias_rows, bias_columns)
        qkv_sum = lax.psum_scatter(qkv_weight_grad, "img", scatter_dimension=0, tiled=True)
        out_sum = lax.psum_scatter(out_grad, "img", scatter_dimension=0, tiled=True)
        wide_shard = lax.psum_scatter(
            jnp.concatenate([qkv_sum, out_sum, up_sum], axis=0).T,
            "band",
            scatter_dimension=0,
            tiled=True,
        ).astype(jnp.float32)
        input_grad_low = to_bands(input_grad_low)
        squares = tall_squares[0, 0] + jnp.sum(bias_total * bias_total) / band_count
        for shard_grad in (ada_shard, wide_shard):
            squares = squares + jnp.sum(shard_grad * shard_grad)
        squares_total = jnp.broadcast_to(sum_everywhere(squares), (8, 128))
    input_grad = input_grad_low.astype(jnp.float32)
    grad_norm = jnp.sqrt(squares_total[0, 0])
    groups = (
        (ada_weight, ada_first, ada_second),
        (qkv_weight, qkv_first, qkv_second),
        (out_weight, out_first, out_second),
        (up_weight, up_first, up_second),
        (down_weight.T, down_first.T, down_second.T),
        (biases, bias_first, bias_second),
    )
    updated = adam_all(squares_total, wide_shard, tall_shard, ada_shard, bias_total, groups)
    ada_new, ada_first_new, ada_second_new = updated[0:3]
    qkv_new, qkv_first_new, qkv_second_new = updated[3:6]
    out_new, out_first_new, out_second_new = updated[6:9]
    up_new, up_first_new, up_second_new = updated[9:12]
    down_new, down_first_new, down_second_new = (array.T for array in updated[12:15])
    bias_new, bias_first_new, bias_second_new = updated[15:18]
    branch_bias_grad = updated[18][0]
    return (
        output,
        input_grad,
        grad_norm,
        ada_new,
        qkv_new,
        out_new,
        up_new,
        down_new,
        bias_new,
        ada_first_new,
        qkv_first_new,
        out_first_new,
        up_first_new,
        down_first_new,
        bias_first_new,
        ada_second_new,
        qkv_second_new,
        out_second_new,
        up_second_new,
        down_second_new,
        bias_second_new,
        branch_bias_grad,
    )


def solution(mesh):
    return jax.shard_map(
        body,
        mesh=mesh,
        in_specs=(
            P("img", "band", None),
            P("img", None),
            P("img"),
            P("img", "band", None),
            P("band", "img"),
            P("band", "img"),
            P("band", "img"),
            P("band", "img"),
            P("band", "img"),
            P(None, "img"),
            P("band", "img"),
            P("band", "img"),
            P("band", "img"),
            P("band", "img"),
            P("band", "img"),
            P(None, "img"),
            P("band", "img"),
            P("band", "img"),
            P("band", "img"),
            P("band", "img"),
            P("band", "img"),
            P(None, "img"),
        ),
        out_specs=(
            P("img", "band", None),
            P("img", "band", None),
            P(),
            P("band", "img"),
            P("band", "img"),
            P("band", "img"),
            P("band", "img"),
            P("band", "img"),
            P(None, "img"),
            P("band", "img"),
            P("band", "img"),
            P("band", "img"),
            P("band", "img"),
            P("band", "img"),
            P(None, "img"),
            P("band", "img"),
            P("band", "img"),
            P("band", "img"),
            P("band", "img"),
            P("band", "img"),
            P(None, "img"),
            P("img"),
        ),
        check_vma=False,
    )
```
